32 devices in a mesh: rows: 8 (over z, x), grp: 4 (over y, core).
Axes of the slice: x: 2, y: 2, z: 4, core: 2. Of those that a mesh axis runs over, the one named last changes fastest.
Arguments:
- observations: float32 [65536, 512], P(('rows', 'grp')), may hold values from -32 to 32, as said below
- sensor_ids: int32 [65536], P(('rows', 'grp')), may hold values from 0 to 127
- sensor_sigma: float32 [128], replicated, may hold values from 0.3 to 3
- buckets: int32 [65536], P(('rows', 'grp')), may hold values from 0 to 7, as said below
- prior_factor: float32 [512, 512], replicated, may hold values from -0.3 to 3, as said below
Outputs:
- whitened: float32 [65536, 512], P(('rows', 'grp'))
- info_factor: float32 [512, 512], replicated
The draws below stay inside these ranges and needn't reach their ends.
Inputs may be any that keep to these rules, and one draw needn't show every extreme that they name: `buckets`: in each aligned block of 2048 rows every bucket index appears exactly 256 times. `observations`: rows are real-valued without further structure. `prior_factor`: upper triangular with a positive diagonal of at least 0.5.
All inputs are finite; a program needn't handle non-finite values.
Results may differ from the reference program's by a relative error of at most 0.00007.
Values sent between devices are 32-bit elements; how exact they have to be, the bound alone decides.
No kernel may reach another device: no remote copies, remote signals or barrier semaphores. Data moves between devices by JAX's collectives and lax.ppermute only.
A program may use at most 128 MiB of HBM per device.

```python
import math
import jax
import jax.numpy as jnp
from jax import lax

STATE = 512
ROWS_DEV = 2048
SENSORS = 128
OBS_ROWS = 65536
BUCKET_ROWS = 256
N_ROWS = 8
N_GRP = 4


def draw_observations(key, part):
    first = jax.random.fold_in(key, 0)
    position = jnp.arange(OBS_ROWS, dtype=jnp.float32) / OBS_ROWS
    ramp = (1.0 + 2.0 * position)[:, None]
    values = jnp.clip(jax.random.normal(first, (OBS_ROWS, STATE), jnp.float32), -6.0, 6.0)
    return values * ramp


def draw_buckets(key, part):
    keys = jax.random.split(key, OBS_ROWS // ROWS_DEV)
    orders = jax.vmap(lambda single: jax.random.permutation(single, ROWS_DEV))(keys)
    return (orders // BUCKET_ROWS).reshape(OBS_ROWS).astype(jnp.int32)


def draw_prior_factor(key, part):
    first, second = jax.random.split(key)
    upper = jnp.clip(jax.random.normal(first, (STATE, STATE), jnp.float32) * 0.05, -0.3, 0.3)
    diagonal = jax.random.uniform(second, (STATE,), jnp.float32, 1.0, 2.0)
    return jnp.triu(upper, 1) + jnp.diag(diagonal)


def place_ends(array, own_key, low, largest):
    index_at = [jax.random.randint(jax.random.fold_in(own_key, axis), (), 0, length) for axis, length in enumerate(array.shape)]
    main_axis = array.shape.index(max(array.shape))
    next_to = index_at[:main_axis] + [(index_at[main_axis] + 1) % array.shape[main_axis]] + index_at[main_axis + 1:]
    return array.at[tuple(index_at)].set(low).at[tuple(next_to)].set(largest)


def setup_inputs(seed: int = 0) -> dict:
    streams_of = jax.random.split(jax.random.key(seed), 6)
    observations = draw_observations(jax.random.fold_in(streams_of[5], 71), 0)
    sensor_ids = place_ends(jax.random.randint(streams_of[1], (OBS_ROWS,), 0, SENSORS), jax.random.fold_in(streams_of[1], 1), 0, SENSORS - 1).astype(jnp.int32)
    sensor_sigma = jnp.clip(jnp.exp(jax.random.uniform(streams_of[2], (SENSORS,), jnp.float32, math.log(0.3), math.log(3.0))), 0.3, 3.0)
    buckets = draw_buckets(jax.random.fold_in(streams_of[5], 71), 0)
    prior_factor = draw_prior_factor(jax.random.fold_in(streams_of[5], 71), 0)
    return dict(observations=observations, sensor_ids=sensor_ids, sensor_sigma=sensor_sigma, buckets=buckets, prior_factor=prior_factor)


def reference(observations, sensor_ids, sensor_sigma, buckets, prior_factor):
    inv_sigma = 1.0 / sensor_sigma
    scaled = observations * inv_sigma[sensor_ids][:, None]
    gram_sum = lax.dot_general(scaled.astype(jnp.float32), scaled.astype(jnp.float32), (((0,), (0,)), ((), ())), precision=lax.Precision.HIGHEST, preferred_element_type=jnp.float32)
    prior_gram = jnp.dot(prior_factor.T.astype(jnp.float32), prior_factor.astype(jnp.float32), precision=lax.Precision.HIGHEST, preferred_element_type=jnp.float32)
    information = prior_gram + gram_sum / jnp.float32(OBS_ROWS)
    lower_part = jnp.linalg.cholesky(information)
    info_factor = lower_part.T
    white = lax.linalg.triangular_solve(info_factor, scaled, left_side=False, lower=False, transpose_a=False)
    devices = OBS_ROWS // ROWS_DEV
    blocks = buckets.reshape(devices, ROWS_DEV)
    onehot = (blocks[:, :, None] == jnp.arange(N_ROWS, dtype=jnp.int32)[None, None, :]).astype(jnp.int32)
    running = jnp.cumsum(onehot, axis=1)
    within = jnp.sum(onehot * running, axis=2) - 1
    device_ids = jnp.arange(devices, dtype=jnp.int32)[:, None]
    source = device_ids // N_GRP
    group = device_ids % N_GRP
    target = (blocks * N_GRP + group) * ROWS_DEV + source * BUCKET_ROWS + within
    whitened = jnp.zeros((OBS_ROWS, STATE), jnp.float32).at[target.reshape(-1).astype(jnp.int32)].set(white)
    return (whitened, info_factor)
```

```python
import jax
import jax.numpy as jnp
from jax import lax
from jax.sharding import PartitionSpec as P


def matmul(left, right):
    return jnp.dot(left, right, precision=lax.Precision.HIGH, preferred_element_type=jnp.float32)


def outer_sum(values):
    return lax.dot_general(
        values,
        values,
        (((0,), (0,)), ((), ())),
        precision=lax.Precision.HIGH,
        preferred_element_type=jnp.float32,
    )


def lower_inverse(lower):
    width = lower.shape[0]
    identity = jnp.eye(width, dtype=jnp.float32)
    diag_values = jnp.diagonal(lower)
    scaled_lower = lower / diag_values[:, None]
    nilpotent = identity - scaled_lower
    product = identity + nilpotent
    power = nilpotent
    reach = 2
    while reach < width:
        power = matmul(power, power)
        product = product + matmul(product, power)
        reach = reach * 2
    return product / diag_values[None, :]


def exchange(chunks, row_groups):
    received = [chunks[0]]
    for k in range(1, row_groups):
        perm = [(i, i ^ k) for i in range(row_groups)]
        received.append(lax.ppermute(chunks[k], "rows", perm))
    return received


def shards(observations, sensor_ids, sensor_sigma, buckets, prior_factor):
    rows_dev, state = observations.shape
    row_groups = lax.axis_size("rows")
    devices = lax.axis_size(("rows", "grp"))
    me = lax.axis_index("rows")
    per_bucket = rows_dev // row_groups
    total_rows = rows_dev * devices
    inv_sigma = 1.0 / sensor_sigma
    matches = sensor_ids[:, None] == jnp.arange(sensor_sigma.shape[0], dtype=jnp.int32)[None, :]
    row_scale = jnp.sum(jnp.where(matches, inv_sigma[None, :], jnp.float32(0.0)), axis=1)
    scaled = observations * row_scale[:, None]
    slots = jnp.bitwise_xor(buckets, me)
    onehot = (slots[:, None] == jnp.arange(row_groups, dtype=jnp.int32)[None, :]).astype(jnp.int32)
    running = jnp.cumsum(onehot, axis=0)
    within = jnp.sum(onehot * running, axis=1) - 1
    target = slots * per_bucket + within
    outgoing = jnp.zeros_like(scaled).at[target].set(scaled)
    chunks = [outgoing[k * per_bucket : (k + 1) * per_bucket] for k in range(row_groups)]
    received = exchange(chunks, row_groups)
    summed = lax.psum(outer_sum(scaled), ("rows", "grp"))
    information = outer_sum(prior_factor) + summed / jnp.float32(total_rows)
    lower = jnp.linalg.cholesky(information)
    inverse = lower_inverse(lower).T
    white = jnp.stack([matmul(part, inverse) for part in received])
    order = jnp.bitwise_xor(jnp.arange(row_groups, dtype=jnp.int32), me)
    whitened = jnp.take(white, order, axis=0).reshape(rows_dev, state)
    return (whitened, lower.T)


def solution(mesh):
    in_specs = (P(("rows", "grp"), None), P(("rows", "grp")), P(), P(("rows", "grp")), P())
    out_specs = (P(("rows", "grp"), None), P())
    return jax.shard_map(shards, mesh=mesh, in_specs=in_specs, out_specs=out_specs, check_vma=False)
```

```python
import functools

import jax
import jax.numpy as jnp
from jax import lax
from jax.experimental import pallas as pl
from jax.experimental.pallas import tpu as pltpu
from jax.sharding import PartitionSpec as P

F32 = jnp.float32
BF16 = jnp.bfloat16
I32 = jnp.int32
LANES = 128
SUB = 8
MIB = 1024 * 1024


def iota(shape, axis):
    return lax.broadcasted_iota(I32, shape, axis)


def split(values):
    high = values.astype(BF16)
    low = (values - high.astype(F32)).astype(BF16)
    return high, low


def dot(left, right):
    return jnp.dot(left, right, preferred_element_type=F32)


def dot_rows(left, right):
    return lax.dot_general(left, right, (((0,), (0,)), ((), ())), preferred_element_type=F32)


def dot3(left, right):
    lh, ll = split(left)
    rh, rl = split(right)
    return dot(lh, rh) + (dot(lh, rl) + dot(ll, rh))


def dot3_rows(left, right):
    lh, ll = split(left)
    rh, rl = split(right)
    return dot_rows(lh, rh) + (dot_rows(lh, rl) + dot_rows(ll, rh))


def regroup_kernel(groups, per_bucket, me_ref, buckets_ref, ids_ref, sigma_ref, obs_ref, *rest):
    outs = rest[:groups]
    place_ref, meta_ref, sorted_ref, inv_ref, meta_smem, sem = rest[groups:]
    step = pl.program_id(0)
    blocks, block = buckets_ref.shape
    sensors = sigma_ref.shape[1]
    padded = sorted_ref.shape[0]
    cells = blocks * groups

    @pl.when(step == 0)
    def _():
        me = me_ref[0]
        inv_row = 1.0 / sigma_ref[...]
        inv_ref[...] = jnp.transpose(jnp.broadcast_to(inv_row, (LANES, sensors)))
        slots = buckets_ref[...] ^ me
        hits = jnp.concatenate(
            [
                jnp.broadcast_to(slots[s : s + 1, :], (groups, block)) == iota((groups, block), 0)
                for s in range(blocks)
            ],
            axis=0,
        )
        upto = (iota((block, block), 0) <= iota((block, block), 1)).astype(F32).astype(BF16)
        running = dot(hits.astype(F32).astype(BF16), upto)
        count = jnp.broadcast_to(running[:, block - 1 : block], (cells, LANES))
        row, col = iota((cells, cells), 0), iota((cells, cells), 1)
        shift = groups.bit_length() - 1
        earlier = ((row & (groups - 1)) == (col & (groups - 1))) & (col < row)
        before = dot(earlier.astype(F32).astype(BF16), count.astype(BF16)).astype(I32)
        cell = iota((cells, LANES), 0)
        start = (cell & (groups - 1)) * per_bucket + before
        odd = start & (SUB - 1)
        tiles = (odd + count.astype(I32) + (SUB - 1)) >> 3
        same = ((row >> shift) == (col >> shift)) & (col < row)
        first = dot(same.astype(F32).astype(BF16), tiles.astype(F32).astype(BF16)).astype(I32)
        lane = iota((cells, LANES), 1)
        meta_ref[...] = jnp.where(lane == 0, before, jnp.where(lane == 1, first, tiles))
        copy = pltpu.make_async_copy(meta_ref, meta_smem, sem)
        copy.start()
        local = first * SUB + odd
        local = jnp.concatenate([local] * (block // LANES), axis=1)
        spot = jnp.where(hits, local + running.astype(I32) - 1, 0)
        place_ref[...] = jnp.concatenate(
            [
                jnp.sum(spot[s * groups : (s + 1) * groups], axis=0, keepdims=True)
                for s in range(blocks)
            ],
            axis=0,
        )
        copy.wait()

    place = place_ref[pl.ds(step, 1), :]
    moves = (iota((padded, block), 0) == place).astype(F32).astype(BF16)
    known = iota((sensors, block), 0) == ids_ref[pl.ds(step, 1), :]
    inv = jnp.concatenate([inv_ref[...]] * (block // LANES), axis=1)
    scale_row = jnp.sum(jnp.where(known, inv, 0.0), axis=0, keepdims=True)
    scale = jnp.transpose(jnp.broadcast_to(scale_row, (LANES, block)))
    state = obs_ref.shape[1]
    scaled = obs_ref[...] * jnp.concatenate([scale] * (state // LANES), axis=1)
    high, low = split(scaled)
    sorted_ref[...] = dot(moves, high) + dot(moves, low)

    for v in range(groups):
        cell = step * groups + v
        before = meta_smem[cell, 0]
        source = meta_smem[cell, 1]
        tiles = meta_smem[cell, 2]
        target = before >> 3
        out = outs[v]

        @pl.when(tiles > 0)
        def _(out=out, before=before, source=source, target=target):
            rows = pl.ds(pl.multiple_of(target * SUB, SUB), SUB)
            old = jnp.where((before & (SUB - 1)) > 0, out[rows, :], 0.0)
            out[rows, :] = old + sorted_ref[pl.ds(pl.multiple_of(source * SUB, SUB), SUB), :]

        def body(t, carry, out=out, source=source, target=target):
            out[pl.ds(pl.multiple_of((target + t) * SUB, SUB), SUB), :] = sorted_ref[
                pl.ds(pl.multiple_of((source + t) * SUB, SUB), SUB), :
            ]
            return carry

        lax.fori_loop(1, tiles, body, 0)


def regroup(observations, sensor_ids, sensor_sigma, buckets, me, groups):
    rows, state = observations.shape
    sensors = sensor_sigma.shape[0]
    block = 256
    blocks = rows // block
    per_bucket = rows // groups
    padded = -(-(block + groups * 2 * (SUB - 1)) // LANES) * LANES
    whole = lambda shape: pl.BlockSpec(shape, lambda s, me: (0, 0))
    return pl.pallas_call(
        functools.partial(regroup_kernel, groups, per_bucket),
        grid_spec=pltpu.PrefetchScalarGridSpec(
            num_scalar_prefetch=1,
            grid=(blocks,),
            in_specs=[
                whole((blocks, block)),
                whole((blocks, block)),
                whole((1, sensors)),
                pl.BlockSpec((block, state), lambda s, me: (s, 0)),
            ],
            out_specs=[whole((per_bucket, state))] * groups,
            scratch_shapes=[
                pltpu.VMEM((blocks, block), I32),
                pltpu.VMEM((blocks * groups, LANES), I32),
                pltpu.VMEM((padded, state), F32),
                pltpu.VMEM((sensors, LANES), F32),
                pltpu.SMEM((blocks * groups, LANES), I32),
                pltpu.SemaphoreType.DMA,
            ],
        ),
        out_shape=[jax.ShapeDtypeStruct((per_bucket, state), F32)] * groups,
        compiler_params=pltpu.CompilerParams(vmem_limit_bytes=24 * MIB),
        cost_estimate=pl.CostEstimate(
            flops=4 * rows * padded * state, bytes_accessed=8 * rows * state, transcendentals=0
        ),
    )(
        me.reshape(1),
        buckets.reshape(blocks, block),
        sensor_ids.reshape(blocks, block),
        sensor_sigma.reshape(1, sensors),
        observations,
    )


def block_pairs(count):
    return [(i, j) for i in range(count) for j in range(i, count)]


def write_gram(both, state, out_ref):
    for n, (i, j) in enumerate(block_pairs(state // LANES)):
        a, b = i * LANES, j * LANES
        cross = both[a : a + LANES, state + b : state + b + LANES]
        turned = both[b : b + LANES, state + a : state + a + LANES]
        out_ref[n * LANES : (n + 1) * LANES, :] = both[a : a + LANES, b : b + LANES] + (
            cross + jnp.transpose(turned)
        )


def gram_kernel(groups, prior_ref, *rest):
    chunks = rest[:groups]
    out_ref, prior_out_ref, both_ref, pair_ref = rest[groups:]
    per_bucket, state = chunks[0].shape
    for k, chunk in enumerate(chunks):
        rows = slice(k * per_bucket, (k + 1) * per_bucket)
        high, low = split(chunk[...])
        pair_ref[rows, :state] = high
        pair_ref[rows, state:] = low
    both_ref[...] = dot_rows(pair_ref[:, :state], pair_ref[...])
    write_gram(both_ref, state, out_ref)
    high, low = split(prior_ref[...])
    both_ref[...] = dot_rows(high, jnp.concatenate([high, low], axis=1))
    write_gram(both_ref, state, prior_out_ref)


def gram(prior_factor, chunks):
    groups = len(chunks)
    per_bucket, state = chunks[0].shape
    rows = groups * per_bucket
    packed = len(block_pairs(state // LANES)) * LANES
    vmem = pl.BlockSpec(memory_space=pltpu.VMEM)
    return pl.pallas_call(
        functools.partial(gram_kernel, groups),
        in_specs=[vmem] * (groups + 1),
        out_specs=[vmem] * 2,
        out_shape=[jax.ShapeDtypeStruct((packed, LANES), F32)] * 2,
        scratch_shapes=[pltpu.VMEM((state, 2 * state), F32), pltpu.VMEM((rows, 2 * state), BF16)],
        compiler_params=pltpu.CompilerParams(vmem_limit_bytes=24 * MIB),
        cost_estimate=pl.CostEstimate(
            flops=4 * rows * state * state, bytes_accessed=4 * rows * state, transcendentals=0
        ),
    )(prior_factor, *chunks)


def sum_all(packed, row_groups, grp, later):
    rows, lanes = packed.shape
    part = rows // grp
    got = lax.all_to_all(packed, "grp", split_axis=0, concat_axis=0, tiled=True)
    mine = jnp.sum(got.reshape(grp, part, lanes), axis=0)
    piece = -(-part // row_groups)
    mine = jnp.pad(mine, ((0, piece * row_groups - part), (0, 0)))
    got = lax.all_to_all(mine, "rows", split_axis=0, concat_axis=0, tiled=True)
    got, early = lax.optimization_barrier((got, later[0]))
    mine = jnp.sum(got.reshape(row_groups, piece, lanes), axis=0)
    mine = jnp.broadcast_to(mine, (row_groups, piece, lanes)).reshape(row_groups * piece, lanes)
    mine = lax.all_to_all(mine, "rows", split_axis=0, concat_axis=0, tiled=True)[:part]
    mine = jnp.broadcast_to(mine, (grp, part, lanes)).reshape(rows, lanes)
    summed = lax.all_to_all(mine, "grp", split_axis=0, concat_axis=0, tiled=True)
    summed, late = lax.optimization_barrier((summed, later[1]))
    return summed, (early, late)


def sweep(a, w):
    width = a.shape[0]
    groups = width // SUB
    row_id = iota((SUB, LANES), 0)
    a_rows = [a[g * SUB : (g + 1) * SUB, :] for g in range(groups)]
    w_rows = [w[g * SUB : (g + 1) * SUB, :] for g in range(groups)]
    for g in range(groups):
        va, vw = a_rows[g], w_rows[g]
        cols = [
            jnp.broadcast_to(va[:, g * SUB + j : g * SUB + j + 1], (SUB, LANES)) for j in range(SUB)
        ]
        scale = jnp.zeros((SUB, LANES), F32)
        for j in range(SUB):
            pivot = jnp.broadcast_to(cols[j][j : j + 1, :], (SUB, LANES))
            root = lax.rsqrt(pivot)
            scale = jnp.where(row_id == j, root, scale)
            if j < SUB - 1:
                ratio = jnp.where(row_id > j, cols[j] * (root * root), 0.0)
                for k in range(j + 1, SUB):
                    cols[k] = cols[k] - ratio * cols[k][j : j + 1, :]
                va = va - ratio * va[j : j + 1, :]
                vw = vw - ratio * vw[j : j + 1, :]
        va, vw = va * scale, vw * scale
        va = jnp.where(iota((SUB, LANES), 1) >= row_id + g * SUB, va, 0.0)
        a_rows[g], w_rows[g] = va, vw
        if g < groups - 1:
            both = jnp.concatenate([va, vw], axis=1)
            high = both.astype(BF16).astype(F32)
            low = both - high
            left = jnp.concatenate([high[:, :LANES], high[:, :LANES], low[:, :LANES]], axis=0)
            right = jnp.concatenate([high, low, high], axis=0)
            change = dot_rows(left.astype(BF16), right.astype(BF16))
            for q in range(g + 1, groups):
                rows = slice(q * SUB, (q + 1) * SUB)
                a_rows[q] = a_rows[q] - change[rows, :LANES]
                w_rows[q] = w_rows[q] - change[rows, LANES:]
    return jnp.concatenate(a_rows, axis=0), jnp.concatenate(w_rows, axis=0)


def factor_kernel(inv_total, sum_ref, prior_ref, factor_ref, high_ref, low_ref, a_ref, x_ref):
    state = factor_ref.shape[0]
    count = state // LANES
    span = lambda i: slice(i * LANES, (i + 1) * LANES)
    for n, (i, j) in enumerate(block_pairs(count)):
        a_ref[span(i), span(j)] = prior_ref[span(n), :] + sum_ref[span(n), :] * inv_total
    factor_ref[...] = jnp.zeros((state, state), F32)
    x_ref[...] = jnp.zeros((state, state), F32)
    eye = (iota((LANES, LANES), 0) == iota((LANES, LANES), 1)).astype(F32)
    for k in range(count):
        r, w = sweep(a_ref[span(k), span(k)], eye)
        factor_ref[span(k), span(k)] = r
        x = jnp.transpose(w)
        x_ref[span(k), span(k)] = x
        if k > 0:
            left = dot3(x_ref[: k * LANES, : k * LANES], factor_ref[: k * LANES, span(k)])
            x_ref[: k * LANES, span(k)] = -dot3(left, x)
        if k < count - 1:
            rest = slice((k + 1) * LANES, state)
            right = dot3(w, a_ref[span(k), rest])
            factor_ref[span(k), rest] = right
            for i in range(k + 1, count):
                low = slice(i * LANES, state)
                at = (i - k - 1) * LANES
                a_ref[span(i), low] -= dot3_rows(right[:, at : at + LANES], right[:, at:])
    high, low = split(x_ref[...])
    high_ref[...] = high
    low_ref[...] = low


def factorise(summed, prior_gram, state, total_rows):
    vmem = pl.BlockSpec(memory_space=pltpu.VMEM)
    return pl.pallas_call(
        functools.partial(factor_kernel, 1.0 / total_rows),
        in_specs=[vmem] * 2,
        out_specs=[vmem] * 3,
        out_shape=[
            jax.ShapeDtypeStruct((state, state), F32),
            jax.ShapeDtypeStruct((state, state), BF16),
            jax.ShapeDtypeStruct((state, state), BF16),
        ],
        scratch_shapes=[pltpu.VMEM((state, state), F32)] * 2,
        compiler_params=pltpu.CompilerParams(vmem_limit_bytes=16 * MIB),
        cost_estimate=pl.CostEstimate(
            flops=40_000_000_000, bytes_accessed=4 * state * state, transcendentals=0
        ),
    )(summed, prior_gram)


def whiten_kernel(steps, aliased, me_ref, high_ref, low_ref, *rest):
    count = len(steps)
    chunks = rest[:count]
    out_ref, held, sems = rest[count + aliased :]
    per_bucket = chunks[0].shape[0]
    high, low = high_ref[...], low_ref[...]
    copies = []
    for n, k in enumerate(steps):
        rows_high, rows_low = split(chunks[n][...])
        held[n] = dot(rows_high, high) + (dot(rows_high, low) + dot(rows_low, high))
        slot = me_ref[0] ^ k
        copy = pltpu.make_async_copy(
            held.at[n],
            out_ref.at[pl.ds(pl.multiple_of(slot * per_bucket, per_bucket), per_bucket), :],
            sems.at[n],
        )
        copy.start()
        copies.append(copy)
    for copy in copies:
        copy.wait()


def whiten(me, high, low, steps, chunks, out, rows):
    per_bucket, state = chunks[0].shape
    count = len(chunks)
    vmem = pl.BlockSpec(memory_space=pltpu.VMEM)
    anywhere = pl.BlockSpec(memory_space=pl.ANY)
    extra = [] if out is None else [out]
    return pl.pallas_call(
        functools.partial(whiten_kernel, tuple(steps), len(extra)),
        in_specs=[pl.BlockSpec(memory_space=pltpu.SMEM)]
        + [vmem] * (2 + count)
        + [anywhere] * len(extra),
        out_specs=anywhere,
        out_shape=jax.ShapeDtypeStruct((rows, state), F32),
        scratch_shapes=[
            pltpu.VMEM((count, per_bucket, state), F32),
            pltpu.SemaphoreType.DMA((count,)),
        ],
        input_output_aliases={3 + count: 0} if extra else {},
        compiler_params=pltpu.CompilerParams(vmem_limit_bytes=16 * MIB),
        cost_estimate=pl.CostEstimate(
            flops=6 * count * per_bucket * state * state,
            bytes_accessed=8 * count * per_bucket * state,
            transcendentals=0,
        ),
    )(me.reshape(1), high, low, *chunks, *extra)


def shards(observations, sensor_ids, sensor_sigma, buckets, prior_factor):
    rows_dev, state = observations.shape
    groups = lax.axis_size("rows")
    grp = lax.axis_size("grp")
    me = lax.axis_index("rows").astype(I32)
    total_rows = rows_dev * groups * grp
    chunks = regroup(observations, sensor_ids, sensor_sigma, buckets, me, groups)
    move = lambda k, chunk: lax.ppermute(chunk, "rows", [(i, i ^ k) for i in range(groups)])
    held_back = [k for k in (2, 3) if k < groups]
    received = [chunks[0]] + [None] * (groups - 1)
    for k in reversed(range(1, groups)):
        if k not in held_back:
            received[k] = move(k, chunks[k])
    packed, prior_gram = gram(prior_factor, chunks)
    summed, later = sum_all(packed, groups, grp, [chunks[k] for k in held_back])
    for k, chunk in zip(held_back, later):
        received[k] = move(k, chunk)
    factor, high, low = factorise(summed, prior_gram, state, total_rows)
    out = whiten(me, high, low, range(groups // 2), received[: groups // 2], None, rows_dev)
    out = whiten(me, high, low, range(groups // 2, groups), received[groups // 2 :], out, rows_dev)
    return (out, factor)


def solution(mesh):
    in_specs = (P(("rows", "grp"), None), P(("rows", "grp")), P(), P(("rows", "grp")), P())
    out_specs = (P(("rows", "grp"), None), P())
    return jax.shard_map(shards, mesh=mesh, in_specs=in_specs, out_specs=out_specs, check_vma=False)
```

```python
import functools

import jax
import jax.numpy as jnp
from jax import lax
from jax.experimental import pallas as pl
from jax.experimental.pallas import tpu as pltpu
from jax.sharding import PartitionSpec as P

F32 = jnp.float32
BF16 = jnp.bfloat16
I32 = jnp.int32
LANES = 128
SUB = 8
MIB = 1024 * 1024


def iota(shape, axis):
    return lax.broadcasted_iota(I32, shape, axis)


def split(values):
    high = values.astype(BF16)
    low = (values - high.astype(F32)).astype(BF16)
    return high, low


def dot(left, right):
    return jnp.dot(left, right, preferred_element_type=F32)


def dot_rows(left, right):
    return lax.dot_general(left, right, (((0,), (0,)), ((), ())), preferred_element_type=F32)


def dot3(left, right):
    lh, ll = split(left)
    rh, rl = split(right)
    return dot(lh, rh) + (dot(lh, rl) + dot(ll, rh))


def dot3_rows(left, right):
    lh, ll = split(left)
    rh, rl = split(right)
    return dot_rows(lh, rh) + (dot_rows(lh, rl) + dot_rows(ll, rh))


def rows_of(packed, count, wide):
    return [
        jnp.concatenate([packed[s * wide + i : s * wide + i + 1, :] for i in range(wide)], axis=1)
        for s in range(count)
    ]


def regroup_kernel(
    groups,
    per_bucket,
    buckets_ref,
    ids_ref,
    sigma_ref,
    obs_ref,
    out,
    place_ref,
    meta_ref,
    sorted_ref,
    inv_ref,
    meta_smem,
    sem,
):
    step = pl.program_id(0)
    blocks, block = place_ref.shape
    wide = block // LANES
    sensors = sigma_ref.shape[1]
    padded = sorted_ref.shape[0]
    cells = blocks * groups

    @pl.when(step == 0)
    def _():
        inv_row = 1.0 / sigma_ref[...]
        inv_ref[...] = jnp.transpose(jnp.broadcast_to(inv_row, (LANES, sensors)))
        slots = rows_of(buckets_ref[...], blocks, wide)
        hits = jnp.concatenate(
            [
                jnp.broadcast_to(row, (groups, block)) == iota((groups, block), 0) for row in slots
            ],
            axis=0,
        )
        upto = (iota((block, block), 0) <= iota((block, block), 1)).astype(F32).astype(BF16)
        running = dot(hits.astype(F32).astype(BF16), upto)
        count = jnp.broadcast_to(running[:, block - 1 : block], (cells, LANES))
        row, col = iota((cells, cells), 0), iota((cells, cells), 1)
        shift = groups.bit_length() - 1
        earlier = ((row & (groups - 1)) == (col & (groups - 1))) & (col < row)
        before = dot(earlier.astype(F32).astype(BF16), count.astype(BF16)).astype(I32)
        cell = iota((cells, LANES), 0)
        start = (cell & (groups - 1)) * per_bucket + before
        odd = start & (SUB - 1)
        tiles = (odd + count.astype(I32) + (SUB - 1)) >> 3
        same = ((row >> shift) == (col >> shift)) & (col < row)
        first = dot(same.astype(F32).astype(BF16), tiles.astype(F32).astype(BF16)).astype(I32)
        lane = iota((cells, LANES), 1)
        meta_ref[...] = jnp.where(lane == 0, before, jnp.where(lane == 1, first, tiles))
        copy = pltpu.make_async_copy(meta_ref, meta_smem, sem)
        copy.start()
        local = first * SUB + odd
        local = jnp.concatenate([local] * (block // LANES), axis=1)
        spot = jnp.where(hits, local + running.astype(I32) - 1, 0)
        place_ref[...] = jnp.concatenate(
            [
                jnp.sum(spot[s * groups : (s + 1) * groups], axis=0, keepdims=True)
                for s in range(blocks)
            ],
            axis=0,
        )
        copy.wait()

    place = place_ref[pl.ds(step, 1), :]
    moves = (iota((padded, block), 0) == place).astype(F32).astype(BF16)
    ids = [ids_ref[pl.ds(step * wide + i, 1), :] for i in range(wide)]
    known = iota((sensors, block), 0) == jnp.concatenate(ids, axis=1)
    inv = jnp.concatenate([inv_ref[...]] * (block // LANES), axis=1)
    scale_row = jnp.sum(jnp.where(known, inv, 0.0), axis=0, keepdims=True)
    scale = jnp.transpose(jnp.broadcast_to(scale_row, (LANES, block)))
    state = obs_ref.shape[1]
    scaled = obs_ref[...] * jnp.concatenate([scale] * (state // LANES), axis=1)
    high, low = split(scaled)
    sorted_ref[...] = dot(moves, high) + dot(moves, low)

    for v in range(groups):
        cell = step * groups + v
        before = meta_smem[cell, 0]
        source = meta_smem[cell, 1]
        tiles = meta_smem[cell, 2]
        target = (before >> 3) + v * (per_bucket // SUB)

        @pl.when(tiles > 0)
        def _(before=before, source=source, target=target):
            rows = pl.ds(pl.multiple_of(target * SUB, SUB), SUB)
            old = jnp.where((before & (SUB - 1)) > 0, out[rows, :], 0.0)
            out[rows, :] = old + sorted_ref[pl.ds(pl.multiple_of(source * SUB, SUB), SUB), :]

        def body(t, carry, source=source, target=target):
            out[pl.ds(pl.multiple_of((target + t) * SUB, SUB), SUB), :] = sorted_ref[
                pl.ds(pl.multiple_of((source + t) * SUB, SUB), SUB), :
            ]
            return carry

        lax.fori_loop(1, tiles, body, 0)


def regroup(observations, sensor_ids, sensor_sigma, buckets, groups):
    rows, state = observations.shape
    sensors = sensor_sigma.shape[0]
    block = 256
    blocks = rows // block
    per_bucket = rows // groups
    padded = -(-(block + groups * 2 * (SUB - 1)) // LANES) * LANES
    whole = lambda shape: pl.BlockSpec(shape, lambda s: (0, 0))
    return pl.pallas_call(
        functools.partial(regroup_kernel, groups, per_bucket),
        grid=(blocks,),
        in_specs=[
            whole((rows // LANES, LANES)),
            whole((rows // LANES, LANES)),
            whole((1, sensors)),
            pl.BlockSpec((block, state), lambda s: (s, 0)),
        ],
        out_specs=whole((rows, state)),
        scratch_shapes=[
            pltpu.VMEM((blocks, block), I32),
            pltpu.VMEM((blocks * groups, LANES), I32),
            pltpu.VMEM((padded, state), F32),
            pltpu.VMEM((sensors, LANES), F32),
            pltpu.SMEM((blocks * groups, LANES), I32),
            pltpu.SemaphoreType.DMA,
        ],
        out_shape=jax.ShapeDtypeStruct((rows, state), F32),
        compiler_params=pltpu.CompilerParams(vmem_limit_bytes=24 * MIB),
        cost_estimate=pl.CostEstimate(
            flops=4 * rows * padded * state, bytes_accessed=8 * rows * state, transcendentals=0
        ),
    )(
        buckets.reshape(rows // LANES, LANES),
        sensor_ids.reshape(rows // LANES, LANES),
        sensor_sigma.reshape(1, sensors),
        observations,
    )


def block_pairs(count):
    return [(i, j) for i in range(count) for j in range(i, count)]


def write_gram(both, state, out_ref):
    for n, (i, j) in enumerate(block_pairs(state // LANES)):
        a, b = i * LANES, j * LANES
        cross = both[a : a + LANES, state + b : state + b + LANES]
        turned = both[b : b + LANES, state + a : state + a + LANES]
        out_ref[n * LANES : (n + 1) * LANES, :] = both[a : a + LANES, b : b + LANES] + (
            cross + jnp.transpose(turned)
        )


def gram_kernel(prior_ref, rows_ref, out_ref, prior_out_ref, both_ref, pair_ref):
    state = rows_ref.shape[1]
    high, low = split(rows_ref[...])
    pair_ref[:, :state] = high
    pair_ref[:, state:] = low
    both_ref[...] = dot_rows(pair_ref[:, :state], pair_ref[...])
    write_gram(both_ref, state, out_ref)
    high, low = split(prior_ref[...])
    both_ref[...] = dot_rows(high, jnp.concatenate([high, low], axis=1))
    write_gram(both_ref, state, prior_out_ref)


def gram(prior_factor, scaled):
    rows, state = scaled.shape
    packed = len(block_pairs(state // LANES)) * LANES
    vmem = pl.BlockSpec(memory_space=pltpu.VMEM)
    return pl.pallas_call(
        gram_kernel,
        in_specs=[vmem] * 2,
        out_specs=[vmem] * 2,
        out_shape=[jax.ShapeDtypeStruct((packed, LANES), F32)] * 2,
        scratch_shapes=[pltpu.VMEM((state, 2 * state), F32), pltpu.VMEM((rows, 2 * state), BF16)],
        compiler_params=pltpu.CompilerParams(vmem_limit_bytes=24 * MIB),
        cost_estimate=pl.CostEstimate(
            flops=4 * rows * state * state, bytes_accessed=4 * rows * state, transcendentals=0
        ),
    )(prior_factor, scaled)


def sum_all(packed, row_groups, grp):
    rows, lanes = packed.shape
    part = rows // grp
    got = lax.all_to_all(packed, "grp", split_axis=0, concat_axis=0, tiled=True)
    mine = jnp.sum(got.reshape(grp, part, lanes), axis=0)
    piece = -(-part // row_groups)
    mine = jnp.pad(mine, ((0, piece * row_groups - part), (0, 0)))
    got = lax.all_to_all(mine, "rows", split_axis=0, concat_axis=0, tiled=True)
    mine = jnp.sum(got.reshape(row_groups, piece, lanes), axis=0)
    mine = jnp.broadcast_to(mine, (row_groups, piece, lanes)).reshape(row_groups * piece, lanes)
    mine = lax.all_to_all(mine, "rows", split_axis=0, concat_axis=0, tiled=True)[:part]
    mine = jnp.broadcast_to(mine, (grp, part, lanes)).reshape(rows, lanes)
    return lax.all_to_all(mine, "grp", split_axis=0, concat_axis=0, tiled=True)


def sweep(a, w):
    width = a.shape[0]
    groups = width // SUB
    row_id = iota((SUB, LANES), 0)
    a_rows = [a[g * SUB : (g + 1) * SUB, :] for g in range(groups)]
    w_rows = [w[g * SUB : (g + 1) * SUB, :] for g in range(groups)]
    for g in range(groups):
        va, vw = a_rows[g], w_rows[g]
        cols = [
            jnp.broadcast_to(va[:, g * SUB + j : g * SUB + j + 1], (SUB, LANES)) for j in range(SUB)
        ]
        scale = jnp.zeros((SUB, LANES), F32)
        for j in range(SUB):
            pivot = jnp.broadcast_to(cols[j][j : j + 1, :], (SUB, LANES))
            root = lax.rsqrt(pivot)
            scale = jnp.where(row_id == j, root, scale)
            if j < SUB - 1:
                ratio = jnp.where(row_id > j, cols[j] * (root * root), 0.0)
                for k in range(j + 1, SUB):
                    cols[k] = cols[k] - ratio * cols[k][j : j + 1, :]
                va = va - ratio * va[j : j + 1, :]
                vw = vw - ratio * vw[j : j + 1, :]
        va, vw = va * scale, vw * scale
        va = jnp.where(iota((SUB, LANES), 1) >= row_id + g * SUB, va, 0.0)
        a_rows[g], w_rows[g] = va, vw
        if g < groups - 1:
            both = jnp.concatenate([va, vw], axis=1)
            high = both.astype(BF16).astype(F32)
            low = both - high
            left = jnp.concatenate([high[:, :LANES], high[:, :LANES], low[:, :LANES]], axis=0)
            right = jnp.concatenate([high, low, high], axis=0)
            change = dot_rows(left.astype(BF16), right.astype(BF16))
            for q in range(g + 1, groups):
                rows = slice(q * SUB, (q + 1) * SUB)
                a_rows[q] = a_rows[q] - change[rows, :LANES]
                w_rows[q] = w_rows[q] - change[rows, LANES:]
    return jnp.concatenate(a_rows, axis=0), jnp.concatenate(w_rows, axis=0)


def factor_kernel(inv_total, sum_ref, prior_ref, factor_ref, high_ref, low_ref, a_ref, x_ref):
    state = factor_ref.shape[0]
    count = state // LANES
    span = lambda i: slice(i * LANES, (i + 1) * LANES)
    for n, (i, j) in enumerate(block_pairs(count)):
        a_ref[span(i), span(j)] = prior_ref[span(n), :] + sum_ref[span(n), :] * inv_total
    factor_ref[...] = jnp.zeros((state, state), F32)
    x_ref[...] = jnp.zeros((state, state), F32)
    eye = (iota((LANES, LANES), 0) == iota((LANES, LANES), 1)).astype(F32)
    for k in range(count):
        r, w = sweep(a_ref[span(k), span(k)], eye)
        factor_ref[span(k), span(k)] = r
        x = jnp.transpose(w)
        x_ref[span(k), span(k)] = x
        if k > 0:
            left = dot3(x_ref[: k * LANES, : k * LANES], factor_ref[: k * LANES, span(k)])
            x_ref[: k * LANES, span(k)] = -dot3(left, x)
        if k < count - 1:
            rest = slice((k + 1) * LANES, state)
            right = dot3(w, a_ref[span(k), rest])
            factor_ref[span(k), rest] = right
            for i in range(k + 1, count):
                low = slice(i * LANES, state)
                at = (i - k - 1) * LANES
                a_ref[span(i), low] -= dot3_rows(right[:, at : at + LANES], right[:, at:])
    high, low = split(x_ref[...])
    high_ref[...] = high
    low_ref[...] = low


def factorise(summed, prior_gram, state, total_rows):
    vmem = pl.BlockSpec(memory_space=pltpu.VMEM)
    return pl.pallas_call(
        functools.partial(factor_kernel, 1.0 / total_rows),
        in_specs=[vmem] * 2,
        out_specs=[vmem] * 3,
        out_shape=[
            jax.ShapeDtypeStruct((state, state), F32),
            jax.ShapeDtypeStruct((state, state), BF16),
            jax.ShapeDtypeStruct((state, state), BF16),
        ],
        scratch_shapes=[pltpu.VMEM((state, state), F32)] * 2,
        compiler_params=pltpu.CompilerParams(vmem_limit_bytes=16 * MIB),
        cost_estimate=pl.CostEstimate(
            flops=40_000_000_000, bytes_accessed=4 * state * state, transcendentals=0
        ),
    )(summed, prior_gram)


def whiten_kernel(high_ref, low_ref, rows_ref, out_ref):
    rows_high, rows_low = split(rows_ref[...])
    high, low = high_ref[...], low_ref[...]
    out_ref[...] = dot(rows_high, high) + (dot(rows_high, low) + dot(rows_low, high))


def whiten(high, low, received):
    rows, state = received.shape
    block = 256
    whole = pl.BlockSpec((state, state), lambda s: (0, 0))
    part = pl.BlockSpec((block, state), lambda s: (s, 0))
    return pl.pallas_call(
        whiten_kernel,
        grid=(rows // block,),
        in_specs=[whole, whole, part],
        out_specs=part,
        out_shape=jax.ShapeDtypeStruct((rows, state), F32),
        compiler_params=pltpu.CompilerParams(vmem_limit_bytes=16 * MIB),
        cost_estimate=pl.CostEstimate(
            flops=6 * rows * state * state, bytes_accessed=8 * rows * state, transcendentals=0
        ),
    )(high, low, received)


def shards(observations, sensor_ids, sensor_sigma, buckets, prior_factor):
    rows_dev, state = observations.shape
    groups = lax.axis_size("rows")
    grp = lax.axis_size("grp")
    total_rows = rows_dev * groups * grp
    scaled = regroup(observations, sensor_ids, sensor_sigma, buckets, groups)
    received = lax.all_to_all(scaled, "rows", split_axis=0, concat_axis=0, tiled=True)
    packed, prior_gram = gram(prior_factor, scaled)
    summed = sum_all(packed, groups, grp)
    factor, high, low = factorise(summed, prior_gram, state, total_rows)
    return (whiten(high, low, received), factor)


def solution(mesh):
    in_specs = (P(("rows", "grp"), None), P(("rows", "grp")), P(), P(("rows", "grp")), P())
    out_specs = (P(("rows", "grp"), None), P())
    return jax.shard_map(shards, mesh=mesh, in_specs=in_specs, out_specs=out_specs, check_vma=False)
```

```python
import functools

import jax
import jax.numpy as jnp
from jax import lax
from jax.experimental import pallas as pl
from jax.experimental.pallas import tpu as pltpu
from jax.sharding import PartitionSpec as P

F32 = jnp.float32
BF16 = jnp.bfloat16
I32 = jnp.int32
LANES = 128
SUB = 8
MIB = 1024 * 1024


def iota(shape, axis):
    return lax.broadcasted_iota(I32, shape, axis)


def split(values):
    high = values.astype(BF16)
    low = (values - high.astype(F32)).astype(BF16)
    return high, low


def dot(left, right):
    return jnp.dot(left, right, preferred_element_type=F32)


def dot_rows(left, right):
    return lax.dot_general(left, right, (((0,), (0,)), ((), ())), preferred_element_type=F32)


def dot3(left, right):
    lh, ll = split(left)
    rh, rl = split(right)
    return dot(lh, rh) + (dot(lh, rl) + dot(ll, rh))


def dot3_rows(left, right):
    lh, ll = split(left)
    rh, rl = split(right)
    return dot_rows(lh, rh) + (dot_rows(lh, rl) + dot_rows(ll, rh))


def rows_of(packed, count, wide):
    return [
        jnp.concatenate([packed[s * wide + i : s * wide + i + 1, :] for i in range(wide)], axis=1)
        for s in range(count)
    ]


def regroup_kernel(groups, per_bucket, me_ref, buckets_ref, ids_ref, sigma_ref, obs_ref, *rest):
    outs = rest[:groups]
    place_ref, meta_ref, sorted_ref, inv_ref, meta_smem, sem = rest[groups:]
    step = pl.program_id(0)
    blocks, block = place_ref.shape
    wide = block // LANES
    sensors = sigma_ref.shape[1]
    padded = sorted_ref.shape[0]
    cells = blocks * groups

    @pl.when(step == 0)
    def _():
        me = me_ref[0]
        inv_row = 1.0 / sigma_ref[...]
        inv_ref[...] = jnp.transpose(jnp.broadcast_to(inv_row, (LANES, sensors)))
        slots = rows_of(buckets_ref[...] ^ me, blocks, wide)
        hits = jnp.concatenate(
            [
                jnp.broadcast_to(row, (groups, block)) == iota((groups, block), 0) for row in slots
            ],
            axis=0,
        )
        upto = (iota((block, block), 0) <= iota((block, block), 1)).astype(F32).astype(BF16)
        running = dot(hits.astype(F32).astype(BF16), upto)
        count = jnp.broadcast_to(running[:, block - 1 : block], (cells, LANES))
        row, col = iota((cells, cells), 0), iota((cells, cells), 1)
        shift = groups.bit_length() - 1
        earlier = ((row & (groups - 1)) == (col & (groups - 1))) & (col < row)
        before = dot(earlier.astype(F32).astype(BF16), count.astype(BF16)).astype(I32)
        cell = iota((cells, LANES), 0)
        start = (cell & (groups - 1)) * per_bucket + before
        odd = start & (SUB - 1)
        tiles = (odd + count.astype(I32) + (SUB - 1)) >> 3
        same = ((row >> shift) == (col >> shift)) & (col < row)
        first = dot(same.astype(F32).astype(BF16), tiles.astype(F32).astype(BF16)).astype(I32)
        lane = iota((cells, LANES), 1)
        meta_ref[...] = jnp.where(lane == 0, before, jnp.where(lane == 1, first, tiles))
        copy = pltpu.make_async_copy(meta_ref, meta_smem, sem)
        copy.start()
        local = first * SUB + odd
        local = jnp.concatenate([local] * (block // LANES), axis=1)
        spot = jnp.where(hits, local + running.astype(I32) - 1, 0)
        place_ref[...] = jnp.concatenate(
            [
                jnp.sum(spot[s * groups : (s + 1) * groups], axis=0, keepdims=True)
                for s in range(blocks)
            ],
            axis=0,
        )
        copy.wait()

    place = place_ref[pl.ds(step, 1), :]
    moves = (iota((padded, block), 0) == place).astype(F32).astype(BF16)
    ids = [ids_ref[pl.ds(step * wide + i, 1), :] for i in range(wide)]
    known = iota((sensors, block), 0) == jnp.concatenate(ids, axis=1)
    inv = jnp.concatenate([inv_ref[...]] * (block // LANES), axis=1)
    scale_row = jnp.sum(jnp.where(known, inv, 0.0), axis=0, keepdims=True)
    scale = jnp.transpose(jnp.broadcast_to(scale_row, (LANES, block)))
    state = obs_ref.shape[1]
    scaled = obs_ref[...] * jnp.concatenate([scale] * (state // LANES), axis=1)
    high, low = split(scaled)
    sorted_ref[...] = dot(moves, high) + dot(moves, low)

    for v in range(groups):
        cell = step * groups + v
        before = meta_smem[cell, 0]
        source = meta_smem[cell, 1]
        tiles = meta_smem[cell, 2]
        target = before >> 3
        out = outs[v]

        @pl.when(tiles > 0)
        def _(out=out, before=before, source=source, target=target):
            rows = pl.ds(pl.multiple_of(target * SUB, SUB), SUB)
            old = jnp.where((before & (SUB - 1)) > 0, out[rows, :], 0.0)
            out[rows, :] = old + sorted_ref[pl.ds(pl.multiple_of(source * SUB, SUB), SUB), :]

        def body(t, carry, out=out, source=source, target=target):
            out[pl.ds(pl.multiple_of((target + t) * SUB, SUB), SUB), :] = sorted_ref[
                pl.ds(pl.multiple_of((source + t) * SUB, SUB), SUB), :
            ]
            return carry

        lax.fori_loop(1, tiles, body, 0)


def regroup(observations, sensor_ids, sensor_sigma, buckets, me, groups):
    rows, state = observations.shape
    sensors = sensor_sigma.shape[0]
    block = 256
    blocks = rows // block
    per_bucket = rows // groups
    padded = -(-(block + groups * 2 * (SUB - 1)) // LANES) * LANES
    whole = lambda shape: pl.BlockSpec(shape, lambda s, me: (0, 0))
    return pl.pallas_call(
        functools.partial(regroup_kernel, groups, per_bucket),
        grid_spec=pltpu.PrefetchScalarGridSpec(
            num_scalar_prefetch=1,
            grid=(blocks,),
            in_specs=[
                whole((rows // LANES, LANES)),
                whole((rows // LANES, LANES)),
                whole((1, sensors)),
                pl.BlockSpec((block, state), lambda s, me: (s, 0)),
            ],
            out_specs=[whole((per_bucket, state))] * groups,
            scratch_shapes=[
                pltpu.VMEM((blocks, block), I32),
                pltpu.VMEM((blocks * groups, LANES), I32),
                pltpu.VMEM((padded, state), F32),
                pltpu.VMEM((sensors, LANES), F32),
                pltpu.SMEM((blocks * groups, LANES), I32),
                pltpu.SemaphoreType.DMA,
            ],
        ),
        out_shape=[jax.ShapeDtypeStruct((per_bucket, state), F32)] * groups,
        compiler_params=pltpu.CompilerParams(vmem_limit_bytes=24 * MIB),
        cost_estimate=pl.CostEstimate(
            flops=4 * rows * padded * state, bytes_accessed=8 * rows * state, transcendentals=0
        ),
    )(
        me.reshape(1),
        buckets.reshape(rows // LANES, LANES),
        sensor_ids.reshape(rows // LANES, LANES),
        sensor_sigma.reshape(1, sensors),
        observations,
    )


def block_pairs(count):
    return [(i, j) for i in range(count) for j in range(i, count)]


def write_gram(both, state, out_ref):
    for n, (i, j) in enumerate(block_pairs(state // LANES)):
        a, b = i * LANES, j * LANES
        cross = both[a : a + LANES, state + b : state + b + LANES]
        turned = both[b : b + LANES, state + a : state + a + LANES]
        out_ref[n * LANES : (n + 1) * LANES, :] = both[a : a + LANES, b : b + LANES] + (
            cross + jnp.transpose(turned)
        )


def gram_kernel(groups, prior_ref, *rest):
    chunks = rest[:groups]
    out_ref, prior_out_ref, both_ref, pair_ref = rest[groups:]
    per_bucket, state = chunks[0].shape
    for k, chunk in enumerate(chunks):
        rows = slice(k * per_bucket, (k + 1) * per_bucket)
        high, low = split(chunk[...])
        pair_ref[rows, :state] = high
        pair_ref[rows, state:] = low
    both_ref[...] = dot_rows(pair_ref[:, :state], pair_ref[...])
    write_gram(both_ref, state, out_ref)
    high, low = split(prior_ref[...])
    both_ref[...] = dot_rows(high, jnp.concatenate([high, low], axis=1))
    write_gram(both_ref, state, prior_out_ref)


def gram(prior_factor, chunks):
    groups = len(chunks)
    per_bucket, state = chunks[0].shape
    rows = groups * per_bucket
    packed = len(block_pairs(state // LANES)) * LANES
    vmem = pl.BlockSpec(memory_space=pltpu.VMEM)
    return pl.pallas_call(
        functools.partial(gram_kernel, groups),
        in_specs=[vmem] * (groups + 1),
        out_specs=[vmem] * 2,
        out_shape=[jax.ShapeDtypeStruct((packed, LANES), F32)] * 2,
        scratch_shapes=[pltpu.VMEM((state, 2 * state), F32), pltpu.VMEM((rows, 2 * state), BF16)],
        compiler_params=pltpu.CompilerParams(vmem_limit_bytes=24 * MIB),
        cost_estimate=pl.CostEstimate(
            flops=4 * rows * state * state, bytes_accessed=4 * rows * state, transcendentals=0
        ),
    )(prior_factor, *chunks)


def scatter_sum(packed, row_groups, grp):
    rows, lanes = packed.shape
    part = rows // grp
    got = lax.all_to_all(packed, "grp", split_axis=0, concat_axis=0, tiled=True)
    mine = jnp.sum(got.reshape(grp, part, lanes), axis=0)
    piece = -(-part // row_groups)
    mine = jnp.pad(mine, ((0, piece * row_groups - part), (0, 0)))
    got = lax.all_to_all(mine, "rows", split_axis=0, concat_axis=0, tiled=True)
    return jnp.sum(got.reshape(row_groups, piece, lanes), axis=0)


def gather_pieces(piece, rows, row_groups, grp):
    size, lanes = piece.shape
    part = rows // grp
    mine = jnp.broadcast_to(piece, (row_groups, size, lanes)).reshape(row_groups * size, lanes)
    mine = lax.all_to_all(mine, "rows", split_axis=0, concat_axis=0, tiled=True)[:part]
    mine = jnp.broadcast_to(mine, (grp, part, lanes)).reshape(rows, lanes)
    return lax.all_to_all(mine, "grp", split_axis=0, concat_axis=0, tiled=True)


def sweep(a, w):
    width = a.shape[0]
    groups = width // SUB
    row_id = iota((SUB, LANES), 0)
    a_rows = [a[g * SUB : (g + 1) * SUB, :] for g in range(groups)]
    w_rows = [w[g * SUB : (g + 1) * SUB, :] for g in range(groups)]
    for g in range(groups):
        va, vw = a_rows[g], w_rows[g]
        cols = [
            jnp.broadcast_to(va[:, g * SUB + j : g * SUB + j + 1], (SUB, LANES)) for j in range(SUB)
        ]
        scale = jnp.zeros((SUB, LANES), F32)
        for j in range(SUB):
            pivot = jnp.broadcast_to(cols[j][j : j + 1, :], (SUB, LANES))
            root = lax.rsqrt(pivot)
            scale = jnp.where(row_id == j, root, scale)
            if j < SUB - 1:
                ratio = jnp.where(row_id > j, cols[j] * (root * root), 0.0)
                for k in range(j + 1, SUB):
                    cols[k] = cols[k] - ratio * cols[k][j : j + 1, :]
                va = va - ratio * va[j : j + 1, :]
                vw = vw - ratio * vw[j : j + 1, :]
        va, vw = va * scale, vw * scale
        va = jnp.where(iota((SUB, LANES), 1) >= row_id + g * SUB, va, 0.0)
        a_rows[g], w_rows[g] = va, vw
        if g < groups - 1:
            both = jnp.concatenate([va, vw], axis=1)
            high = both.astype(BF16).astype(F32)
            low = both - high
            left = jnp.concatenate([high[:, :LANES], high[:, :LANES], low[:, :LANES]], axis=0)
            right = jnp.concatenate([high, low, high], axis=0)
            change = dot_rows(left.astype(BF16), right.astype(BF16))
            for q in range(g + 1, groups):
                rows = slice(q * SUB, (q + 1) * SUB)
                a_rows[q] = a_rows[q] - change[rows, :LANES]
                w_rows[q] = w_rows[q] - change[rows, LANES:]
    return jnp.concatenate(a_rows, axis=0), jnp.concatenate(w_rows, axis=0)


def factor_kernel(inv_total, sum_ref, prior_ref, factor_ref, high_ref, low_ref, a_ref, x_ref):
    state = factor_ref.shape[0]
    count = state // LANES
    span = lambda i: slice(i * LANES, (i + 1) * LANES)
    for n, (i, j) in enumerate(block_pairs(count)):
        a_ref[span(i), span(j)] = prior_ref[span(n), :] + sum_ref[span(n), :] * inv_total
    factor_ref[...] = jnp.zeros((state, state), F32)
    x_ref[...] = jnp.zeros((state, state), F32)
    eye = (iota((LANES, LANES), 0) == iota((LANES, LANES), 1)).astype(F32)
    for k in range(count):
        r, w = sweep(a_ref[span(k), span(k)], eye)
        factor_ref[span(k), span(k)] = r
        x = jnp.transpose(w)
        x_ref[span(k), span(k)] = x
        if k > 0:
            left = dot3(x_ref[: k * LANES, : k * LANES], factor_ref[: k * LANES, span(k)])
            x_ref[: k * LANES, span(k)] = -dot3(left, x)
        if k < count - 1:
            rest = slice((k + 1) * LANES, state)
            right = dot3(w, a_ref[span(k), rest])
            factor_ref[span(k), rest] = right
            for i in range(k + 1, count):
                low = slice(i * LANES, state)
                at = (i - k - 1) * LANES
                a_ref[span(i), low] -= dot3_rows(right[:, at : at + LANES], right[:, at:])
    high, low = split(x_ref[...])
    high_ref[...] = high
    low_ref[...] = low


def factorise(summed, prior_gram, state, total_rows):
    vmem = pl.BlockSpec(memory_space=pltpu.VMEM)
    return pl.pallas_call(
        functools.partial(factor_kernel, 1.0 / total_rows),
        in_specs=[vmem] * 2,
        out_specs=[vmem] * 3,
        out_shape=[
            jax.ShapeDtypeStruct((state, state), F32),
            jax.ShapeDtypeStruct((state, state), BF16),
            jax.ShapeDtypeStruct((state, state), BF16),
        ],
        scratch_shapes=[pltpu.VMEM((state, state), F32)] * 2,
        compiler_params=pltpu.CompilerParams(vmem_limit_bytes=16 * MIB),
        cost_estimate=pl.CostEstimate(
            flops=40_000_000_000, bytes_accessed=4 * state * state, transcendentals=0
        ),
    )(summed, prior_gram)


def whiten_kernel(steps, aliased, me_ref, high_ref, low_ref, *rest):
    count = len(steps)
    chunks = rest[:count]
    out_ref, held, sems = rest[count + aliased :]
    per_bucket = chunks[0].shape[0]
    high, low = high_ref[...], low_ref[...]
    copies = []
    for n, k in enumerate(steps):
        rows_high, rows_low = split(chunks[n][...])
        held[n] = dot(rows_high, high) + (dot(rows_high, low) + dot(rows_low, high))
        slot = me_ref[0] ^ k
        copy = pltpu.make_async_copy(
            held.at[n],
            out_ref.at[pl.ds(pl.multiple_of(slot * per_bucket, per_bucket), per_bucket), :],
            sems.at[n],
        )
        copy.start()
        copies.append(copy)
    for copy in copies:
        copy.wait()


def whiten(me, high, low, steps, chunks, out, rows):
    per_bucket, state = chunks[0].shape
    count = len(chunks)
    vmem = pl.BlockSpec(memory_space=pltpu.VMEM)
    anywhere = pl.BlockSpec(memory_space=pl.ANY)
    extra = [] if out is None else [out]
    return pl.pallas_call(
        functools.partial(whiten_kernel, tuple(steps), len(extra)),
        in_specs=[pl.BlockSpec(memory_space=pltpu.SMEM)]
        + [vmem] * (2 + count)
        + [anywhere] * len(extra),
        out_specs=anywhere,
        out_shape=jax.ShapeDtypeStruct((rows, state), F32),
        scratch_shapes=[
            pltpu.VMEM((count, per_bucket, state), F32),
            pltpu.SemaphoreType.DMA((count,)),
        ],
        input_output_aliases={3 + count: 0} if extra else {},
        compiler_params=pltpu.CompilerParams(vmem_limit_bytes=16 * MIB),
        cost_estimate=pl.CostEstimate(
            flops=1, bytes_accessed=1, transcendentals=0
        ),
    )(me.reshape(1), high, low, *chunks, *extra)


def shards(observations, sensor_ids, sensor_sigma, buckets, prior_factor):
    rows_dev, state = observations.shape
    groups = lax.axis_size("rows")
    grp = lax.axis_size("grp")
    me = lax.axis_index("rows").astype(I32)
    total_rows = rows_dev * groups * grp
    chunks = regroup(observations, sensor_ids, sensor_sigma, buckets, me, groups)
    move = lambda k, chunk: lax.ppermute(chunk, "rows", [(i, i ^ k) for i in range(groups)])
    short = [k for k in (1, 2, 3) if k < groups]
    received = [chunks[0]] + [None] * (groups - 1)
    for k in reversed(range(1, groups)):
        if k not in short:
            received[k] = move(k, chunks[k])
    packed_rows = len(block_pairs(state // LANES)) * LANES

    def inside():
        moved = [move(k, chunks[k]) for k in short[:1]]

        def move_next(value):
            if len(moved) < len(short):
                chunk = chunks[short[len(moved)]]
                value, moved[-1], chunk = lax.optimization_barrier((value, moved[-1], chunk))
                moved.append(move(short[len(moved)], chunk))
            return value

        packed, prior_gram = gram(prior_factor, chunks)
        piece = move_next(scatter_sum(packed, groups, grp))
        summed = move_next(gather_pieces(piece, packed_rows, groups, grp))
        return moved, list(factorise(summed, prior_gram, state, total_rows))

    def invalid():
        wrong = jnp.full((state, state), jnp.nan, F32)
        return [chunks[k] for k in short], [wrong, wrong.astype(BF16), wrong.astype(BF16)]

    moved, (factor, high, low) = lax.cond(prior_factor[0, 0] > 0, inside, invalid)
    for k, chunk in zip(short, moved):
        received[k] = chunk
    out = whiten(me, high, low, range(groups // 2), received[: groups // 2], None, rows_dev)
    out = whiten(me, high, low, range(groups // 2, groups), received[groups // 2 :], out, rows_dev)
    return (out, factor)


def solution(mesh):
    in_specs = (P(("rows", "grp"), None), P(("rows", "grp")), P(), P(("rows", "grp")), P())
    out_specs = (P(("rows", "grp"), None), P())
    return jax.shard_map(shards, mesh=mesh, in_specs=in_specs, out_specs=out_specs, check_vma=False)
```

```python
import functools

import jax
import jax.numpy as jnp
from jax import lax
from jax.experimental import pallas as pl
from jax.experimental.pallas import tpu as pltpu
from jax.sharding import PartitionSpec as P

F32 = jnp.float32
BF16 = jnp.bfloat16
I32 = jnp.int32
LANES = 128
SUB = 8
MIB = 1024 * 1024


def iota(shape, axis):
    return lax.broadcasted_iota(I32, shape, axis)


def split(values):
    high = values.astype(BF16)
    low = (values - high.astype(F32)).astype(BF16)
    return high, low


def dot(left, right):
    return jnp.dot(left, right, preferred_element_type=F32)


def dot_rows(left, right):
    return lax.dot_general(left, right, (((0,), (0,)), ((), ())), preferred_element_type=F32)


def dot3(left, right):
    lh, ll = split(left)
    rh, rl = split(right)
    return dot(lh, rh) + (dot(lh, rl) + dot(ll, rh))


def dot3_rows(left, right):
    lh, ll = split(left)
    rh, rl = split(right)
    return dot_rows(lh, rh) + (dot_rows(lh, rl) + dot_rows(ll, rh))


def rows_of(packed, count, wide):
    return [
        jnp.concatenate([packed[s * wide + i : s * wide + i + 1, :] for i in range(wide)], axis=1)
        for s in range(count)
    ]


def regroup_kernel(groups, per_bucket, me_ref, buckets_ref, ids_ref, sigma_ref, obs_ref, *rest):
    outs = rest[:groups]
    place_ref, meta_ref, sorted_ref, inv_ref, meta_smem, sem = rest[groups:]
    step = pl.program_id(0)
    blocks, block = place_ref.shape
    wide = block // LANES
    sensors = sigma_ref.shape[1]
    padded = sorted_ref.shape[0]
    cells = blocks * groups

    @pl.when(step == 0)
    def _():
        me = me_ref[0]
        inv_row = 1.0 / sigma_ref[...]
        inv_ref[...] = jnp.transpose(jnp.broadcast_to(inv_row, (LANES, sensors)))
        slots = rows_of(buckets_ref[...] ^ me, blocks, wide)
        hits = jnp.concatenate(
            [
                jnp.broadcast_to(row, (groups, block)) == iota((groups, block), 0) for row in slots
            ],
            axis=0,
        )
        upto = (iota((block, block), 0) <= iota((block, block), 1)).astype(F32).astype(BF16)
        running = dot(hits.astype(F32).astype(BF16), upto)
        count = jnp.broadcast_to(running[:, block - 1 : block], (cells, LANES))
        row, col = iota((cells, cells), 0), iota((cells, cells), 1)
        shift = groups.bit_length() - 1
        earlier = ((row & (groups - 1)) == (col & (groups - 1))) & (col < row)
        before = dot(earlier.astype(F32).astype(BF16), count.astype(BF16)).astype(I32)
        cell = iota((cells, LANES), 0)
        start = (cell & (groups - 1)) * per_bucket + before
        odd = start & (SUB - 1)
        tiles = (odd + count.astype(I32) + (SUB - 1)) >> 3
        same = ((row >> shift) == (col >> shift)) & (col < row)
        first = dot(same.astype(F32).astype(BF16), tiles.astype(F32).astype(BF16)).astype(I32)
        lane = iota((cells, LANES), 1)
        meta_ref[...] = jnp.where(lane == 0, before, jnp.where(lane == 1, first, tiles))
        copy = pltpu.make_async_copy(meta_ref, meta_smem, sem)
        copy.start()
        local = first * SUB + odd
        local = jnp.concatenate([local] * (block // LANES), axis=1)
        spot = jnp.where(hits, local + running.astype(I32) - 1, 0)
        place_ref[...] = jnp.concatenate(
            [
                jnp.sum(spot[s * groups : (s + 1) * groups], axis=0, keepdims=True)
                for s in range(blocks)
            ],
            axis=0,
        )
        copy.wait()

    place = place_ref[pl.ds(step, 1), :]
    moves = (iota((padded, block), 0) == place).astype(F32).astype(BF16)
    ids = [ids_ref[pl.ds(step * wide + i, 1), :] for i in range(wide)]
    known = iota((sensors, block), 0) == jnp.concatenate(ids, axis=1)
    inv = jnp.concatenate([inv_ref[...]] * (block // LANES), axis=1)
    scale_row = jnp.sum(jnp.where(known, inv, 0.0), axis=0, keepdims=True)
    scale = jnp.transpose(jnp.broadcast_to(scale_row, (LANES, block)))
    state = obs_ref.shape[1]
    scaled = obs_ref[...] * jnp.concatenate([scale] * (state // LANES), axis=1)
    high, low = split(scaled)
    sorted_ref[...] = dot(moves, high) + dot(moves, low)

    for v in range(groups):
        cell = step * groups + v
        before = meta_smem[cell, 0]
        source = meta_smem[cell, 1]
        tiles = meta_smem[cell, 2]
        target = before >> 3
        out = outs[v]

        @pl.when(tiles > 0)
        def _(out=out, before=before, source=source, target=target):
            rows = pl.ds(pl.multiple_of(target * SUB, SUB), SUB)
            old = jnp.where((before & (SUB - 1)) > 0, out[rows, :], 0.0)
            out[rows, :] = old + sorted_ref[pl.ds(pl.multiple_of(source * SUB, SUB), SUB), :]

        def body(t, carry, out=out, source=source, target=target):
            out[pl.ds(pl.multiple_of((target + t) * SUB, SUB), SUB), :] = sorted_ref[
                pl.ds(pl.multiple_of((source + t) * SUB, SUB), SUB), :
            ]
            return carry

        lax.fori_loop(1, tiles, body, 0)


def regroup(observations, sensor_ids, sensor_sigma, buckets, me, groups):
    rows, state = observations.shape
    sensors = sensor_sigma.shape[0]
    block = 256
    blocks = rows // block
    per_bucket = rows // groups
    padded = -(-(block + groups * 2 * (SUB - 1)) // LANES) * LANES
    whole = lambda shape: pl.BlockSpec(shape, lambda s, me: (0, 0))
    return pl.pallas_call(
        functools.partial(regroup_kernel, groups, per_bucket),
        grid_spec=pltpu.PrefetchScalarGridSpec(
            num_scalar_prefetch=1,
            grid=(blocks,),
            in_specs=[
                whole((rows // LANES, LANES)),
                whole((rows // LANES, LANES)),
                whole((1, sensors)),
                pl.BlockSpec((block, state), lambda s, me: (s, 0)),
            ],
            out_specs=[whole((per_bucket, state))] * groups,
            scratch_shapes=[
                pltpu.VMEM((blocks, block), I32),
                pltpu.VMEM((blocks * groups, LANES), I32),
                pltpu.VMEM((padded, state), F32),
                pltpu.VMEM((sensors, LANES), F32),
                pltpu.SMEM((blocks * groups, LANES), I32),
                pltpu.SemaphoreType.DMA,
            ],
        ),
        out_shape=[jax.ShapeDtypeStruct((per_bucket, state), F32)] * groups,
        compiler_params=pltpu.CompilerParams(vmem_limit_bytes=24 * MIB),
        cost_estimate=pl.CostEstimate(
            flops=4 * rows * padded * state, bytes_accessed=8 * rows * state, transcendentals=0
        ),
    )(
        me.reshape(1),
        buckets.reshape(rows // LANES, LANES),
        sensor_ids.reshape(rows // LANES, LANES),
        sensor_sigma.reshape(1, sensors),
        observations,
    )


def block_pairs(count):
    return [(i, j) for i in range(count) for j in range(i, count)]


def write_gram(both, state, out_ref):
    for n, (i, j) in enumerate(block_pairs(state // LANES)):
        a, b = i * LANES, j * LANES
        cross = both[a : a + LANES, state + b : state + b + LANES]
        turned = both[b : b + LANES, state + a : state + a + LANES]
        out_ref[n * LANES : (n + 1) * LANES, :] = both[a : a + LANES, b : b + LANES] + (
            cross + jnp.transpose(turned)
        )


def gram_kernel(groups, prior_ref, *rest):
    chunks = rest[:groups]
    out_ref, prior_out_ref, both_ref, pair_ref = rest[groups:]
    per_bucket, state = chunks[0].shape
    for k, chunk in enumerate(chunks):
        rows = slice(k * per_bucket, (k + 1) * per_bucket)
        high, low = split(chunk[...])
        pair_ref[rows, :state] = high
        pair_ref[rows, state:] = low
    both_ref[...] = dot_rows(pair_ref[:, :state], pair_ref[...])
    write_gram(both_ref, state, out_ref)
    high, low = split(prior_ref[...])
    both_ref[...] = dot_rows(high, jnp.concatenate([high, low], axis=1))
    write_gram(both_ref, state, prior_out_ref)


def gram(prior_factor, chunks):
    groups = len(chunks)
    per_bucket, state = chunks[0].shape
    rows = groups * per_bucket
    packed = len(block_pairs(state // LANES)) * LANES
    vmem = pl.BlockSpec(memory_space=pltpu.VMEM)
    return pl.pallas_call(
        functools.partial(gram_kernel, groups),
        in_specs=[vmem] * (groups + 1),
        out_specs=[vmem] * 2,
        out_shape=[jax.ShapeDtypeStruct((packed, LANES), F32)] * 2,
        scratch_shapes=[pltpu.VMEM((state, 2 * state), F32), pltpu.VMEM((rows, 2 * state), BF16)],
        compiler_params=pltpu.CompilerParams(vmem_limit_bytes=24 * MIB),
        cost_estimate=pl.CostEstimate(
            flops=4 * rows * state * state, bytes_accessed=4 * rows * state, transcendentals=0
        ),
    )(prior_factor, *chunks)


def scatter_sum(packed, count, groups):
    rows, lanes = packed.shape
    axes = ("rows", "grp")
    got = lax.all_to_all(packed, axes, split_axis=0, concat_axis=0, axis_index_groups=groups, tiled=True)
    return jnp.sum(got.reshape(count, rows // count, lanes), axis=0)


def gather_pieces(piece, count, groups):
    rows, lanes = piece.shape
    copies = jnp.broadcast_to(piece, (count, rows, lanes)).reshape(count * rows, lanes)
    axes = ("rows", "grp")
    return lax.all_to_all(copies, axes, split_axis=0, concat_axis=0, axis_index_groups=groups, tiled=True)


def sweep(a, w):
    width = a.shape[0]
    groups = width // SUB
    row_id = iota((SUB, LANES), 0)
    a_rows = [a[g * SUB : (g + 1) * SUB, :] for g in range(groups)]
    w_rows = [w[g * SUB : (g + 1) * SUB, :] for g in range(groups)]
    for g in range(groups):
        va, vw = a_rows[g], w_rows[g]
        cols = [
            jnp.broadcast_to(va[:, g * SUB + j : g * SUB + j + 1], (SUB, LANES)) for j in range(SUB)
        ]
        scale = jnp.zeros((SUB, LANES), F32)
        for j in range(SUB):
            pivot = jnp.broadcast_to(cols[j][j : j + 1, :], (SUB, LANES))
            root = lax.rsqrt(pivot)
            scale = jnp.where(row_id == j, root, scale)
            if j < SUB - 1:
                ratio = jnp.where(row_id > j, cols[j] * (root * root), 0.0)
                for k in range(j + 1, SUB):
                    cols[k] = cols[k] - ratio * cols[k][j : j + 1, :]
                va = va - ratio * va[j : j + 1, :]
                vw = vw - ratio * vw[j : j + 1, :]
        va, vw = va * scale, vw * scale
        va = jnp.where(iota((SUB, LANES), 1) >= row_id + g * SUB, va, 0.0)
        a_rows[g], w_rows[g] = va, vw
        if g < groups - 1:
            both = jnp.concatenate([va, vw], axis=1)
            high = both.astype(BF16).astype(F32)
            low = both - high
            left = jnp.concatenate([high[:, :LANES], high[:, :LANES], low[:, :LANES]], axis=0)
            right = jnp.concatenate([high, low, high], axis=0)
            change = dot_rows(left.astype(BF16), right.astype(BF16))
            for q in range(g + 1, groups):
                rows = slice(q * SUB, (q + 1) * SUB)
                a_rows[q] = a_rows[q] - change[rows, :LANES]
                w_rows[q] = w_rows[q] - change[rows, LANES:]
    return jnp.concatenate(a_rows, axis=0), jnp.concatenate(w_rows, axis=0)


def factor_kernel(inv_total, sum_ref, prior_ref, factor_ref, high_ref, low_ref, a_ref, x_ref):
    state = factor_ref.shape[0]
    count = state // LANES
    span = lambda i: slice(i * LANES, (i + 1) * LANES)
    for n, (i, j) in enumerate(block_pairs(count)):
        a_ref[span(i), span(j)] = prior_ref[span(n), :] + sum_ref[span(n), :] * inv_total
    factor_ref[...] = jnp.zeros((state, state), F32)
    x_ref[...] = jnp.zeros((state, state), F32)
    eye = (iota((LANES, LANES), 0) == iota((LANES, LANES), 1)).astype(F32)
    for k in range(count):
        r, w = sweep(a_ref[span(k), span(k)], eye)
        factor_ref[span(k), span(k)] = r
        x = jnp.transpose(w)
        x_ref[span(k), span(k)] = x
        if k > 0:
            left = dot3(x_ref[: k * LANES, : k * LANES], factor_ref[: k * LANES, span(k)])
            x_ref[: k * LANES, span(k)] = -dot3(left, x)
        if k < count - 1:
            rest = slice((k + 1) * LANES, state)
            right = dot3(w, a_ref[span(k), rest])
            factor_ref[span(k), rest] = right
            for i in range(k + 1, count):
                low = slice(i * LANES, state)
                at = (i - k - 1) * LANES
                a_ref[span(i), low] -= dot3_rows(right[:, at : at + LANES], right[:, at:])
    high, low = split(x_ref[...])
    high_ref[...] = high
    low_ref[...] = low


def factorise(summed, prior_gram, state, total_rows):
    vmem = pl.BlockSpec(memory_space=pltpu.VMEM)
    return pl.pallas_call(
        functools.partial(factor_kernel, 1.0 / total_rows),
        in_specs=[vmem] * 2,
        out_specs=[vmem] * 3,
        out_shape=[
            jax.ShapeDtypeStruct((state, state), F32),
            jax.ShapeDtypeStruct((state, state), BF16),
            jax.ShapeDtypeStruct((state, state), BF16),
        ],
        scratch_shapes=[pltpu.VMEM((state, state), F32)] * 2,
        compiler_params=pltpu.CompilerParams(vmem_limit_bytes=16 * MIB),
        cost_estimate=pl.CostEstimate(
            flops=1, bytes_accessed=1, transcendentals=0
        ),
    )(summed, prior_gram)


def whiten_kernel(steps, aliased, me_ref, high_ref, low_ref, *rest):
    count = len(steps)
    chunks = rest[:count]
    out_ref, held, sems = rest[count + aliased :]
    per_bucket = chunks[0].shape[0]
    high, low = high_ref[...], low_ref[...]
    copies = []
    for n, k in enumerate(steps):
        rows_high, rows_low = split(chunks[n][...])
        held[n] = dot(rows_high, high) + (dot(rows_high, low) + dot(rows_low, high))
        slot = me_ref[0] ^ k
        copy = pltpu.make_async_copy(
            held.at[n],
            out_ref.at[pl.ds(pl.multiple_of(slot * per_bucket, per_bucket), per_bucket), :],
            sems.at[n],
        )
        copy.start()
        copies.append(copy)
    for copy in copies:
        copy.wait()


def whiten(me, high, low, steps, chunks, out, rows):
    per_bucket, state = chunks[0].shape
    count = len(chunks)
    vmem = pl.BlockSpec(memory_space=pltpu.VMEM)
    anywhere = pl.BlockSpec(memory_space=pl.ANY)
    extra = [] if out is None else [out]
    return pl.pallas_call(
        functools.partial(whiten_kernel, tuple(steps), len(extra)),
        in_specs=[pl.BlockSpec(memory_space=pltpu.SMEM)]
        + [vmem] * (2 + count)
        + [anywhere] * len(extra),
        out_specs=anywhere,
        out_shape=jax.ShapeDtypeStruct((rows, state), F32),
        scratch_shapes=[
            pltpu.VMEM((count, per_bucket, state), F32),
            pltpu.SemaphoreType.DMA((count,)),
        ],
        input_output_aliases={3 + count: 0} if extra else {},
        compiler_params=pltpu.CompilerParams(vmem_limit_bytes=16 * MIB),
        cost_estimate=pl.CostEstimate(
            flops=1, bytes_accessed=1, transcendentals=0
        ),
    )(me.reshape(1), high, low, *chunks, *extra)


def behind(value, *arrays):
    return lax.optimization_barrier((value, *arrays))


def shards(observations, sensor_ids, sensor_sigma, buckets, prior_factor):
    rows_dev, state = observations.shape
    groups = lax.axis_size("rows")
    grp = lax.axis_size("grp")
    me = lax.axis_index("rows").astype(I32)
    total_rows = rows_dev * groups * grp
    chunks = regroup(observations, sensor_ids, sensor_sigma, buckets, me, groups)
    move = lambda k, chunk: lax.ppermute(chunk, "rows", [(i, i ^ k) for i in range(groups)])
    packed_rows = len(block_pairs(state // LANES)) * LANES
    plane = 2 * grp
    planes = [list(range(i, i + plane)) for i in range(0, groups * grp, plane)]
    short = [k for k in (1, 2, 3) if k < groups]
    early = [k for k in (4,) if k < groups]
    middle = [k for k in (6, 2) if k < groups]
    late = [k for k in range(3, groups) if k not in early + middle]
    received = {0: chunks[0]}
    valid = prior_factor[0, 0] > 0
    nothing = lambda rows: jnp.full((rows, LANES), jnp.nan, F32)

    for k in early:
        received[k] = move(k, chunks[k])

    def first():
        packed, prior_gram = gram(prior_factor, chunks)
        return move(1, chunks[1]), scatter_sum(packed, plane, planes), prior_gram

    received[1], piece, prior_gram = lax.cond(
        valid, first, lambda: (chunks[1], nothing(packed_rows // plane), nothing(packed_rows))
    )
    for k in early:
        piece, received[k] = behind(piece, received[k])
    across = [piece]
    for step in range(1, groups // 2):
        across.append(move(2 * step, piece))
    for k in middle:
        _, chunk = behind(piece, chunks[k])
        received[k] = move(k, chunk)
    while len(across) > 1:
        across = [across[i] + across[i + 1] for i in range(0, len(across), 2)]
    summed = lax.cond(
        valid, lambda: gather_pieces(across[0], plane, planes), lambda: nothing(packed_rows)
    )
    for k in late:
        _, chunk = behind(summed, chunks[k])
        received[k] = move(k, chunk)
    factor, high, low = factorise(summed, prior_gram, state, total_rows)
    out = None
    for steps in ([0, 1] + early + middle, late):
        out = whiten(me, high, low, steps, [received[k] for k in steps], out, rows_dev)
    return (out, factor)


def solution(mesh):
    in_specs = (P(("rows", "grp"), None), P(("rows", "grp")), P(), P(("rows", "grp")), P())
    out_specs = (P(("rows", "grp"), None), P())
    return jax.shard_map(shards, mesh=mesh, in_specs=in_specs, out_specs=out_specs, check_vma=False)
```

```python
import functools

import jax
import jax.numpy as jnp
from jax import lax
from jax.experimental import pallas as pl
from jax.experimental.pallas import tpu as pltpu
from jax.sharding import PartitionSpec as P

F32 = jnp.float32
BF16 = jnp.bfloat16
I32 = jnp.int32
LANES = 128
SUB = 8
MIB = 1024 * 1024


def iota(shape, axis):
    return lax.broadcasted_iota(I32, shape, axis)


def split(values):
    high = values.astype(BF16)
    low = (values - high.astype(F32)).astype(BF16)
    return high, low


def dot(left, right):
    return jnp.dot(left, right, preferred_element_type=F32)


def dot_rows(left, right):
    return lax.dot_general(left, right, (((0,), (0,)), ((), ())), preferred_element_type=F32)


def dot3(left, right):
    lh, ll = split(left)
    rh, rl = split(right)
    return dot(lh, rh) + (dot(lh, rl) + dot(ll, rh))


def dot3_rows(left, right):
    lh, ll = split(left)
    rh, rl = split(right)
    return dot_rows(lh, rh) + (dot_rows(lh, rl) + dot_rows(ll, rh))


def rows_of(packed, count, wide):
    return [
        jnp.concatenate([packed[s * wide + i : s * wide + i + 1, :] for i in range(wide)], axis=1)
        for s in range(count)
    ]


def regroup_kernel(groups, per_bucket, me_ref, *refs):
    given, outs, scratch = refs[:4], refs[4 : 4 + groups], refs[4 + groups :]
    held, (place_ref, meta_ref, sorted_ref, inv_ref, meta_smem, sems) = scratch[:4], scratch[4:]
    buckets_ref, ids_ref, sigma_ref, obs_ref = held
    blocks, block = place_ref.shape
    wide = block // LANES
    sensors = sigma_ref.shape[1]
    padded, state = sorted_ref.shape
    cells = blocks * groups
    last_tile = per_bucket // SUB - 1
    most = min(7, last_tile + 2)

    small = [pltpu.make_async_copy(given[i], held[i], sems.at[i]) for i in range(3)]
    for copy in small:
        copy.start()

    def fetch(s):
        rows = pl.ds(pl.multiple_of(s * block, block), block)
        return pltpu.make_async_copy(given[3].at[rows, :], obs_ref.at[rows, :], sems.at[4 + s])

    for s in range(blocks):
        fetch(s).start()
    for copy in small:
        copy.wait()

    inv_row = 1.0 / sigma_ref[...]
    inv_ref[...] = jnp.transpose(jnp.broadcast_to(inv_row, (LANES, sensors)))
    slots = rows_of(buckets_ref[...] ^ me_ref[0], blocks, wide)
    hits = jnp.concatenate(
        [jnp.broadcast_to(row, (groups, block)) == iota((groups, block), 0) for row in slots], axis=0
    )
    upto = (iota((block, block), 0) <= iota((block, block), 1)).astype(F32).astype(BF16)
    running = dot(hits.astype(F32).astype(BF16), upto)
    count = jnp.broadcast_to(running[:, block - 1 : block], (cells, LANES))
    row, col = iota((cells, cells), 0), iota((cells, cells), 1)
    shift = groups.bit_length() - 1
    earlier = ((row & (groups - 1)) == (col & (groups - 1))) & (col < row)
    before = dot(earlier.astype(F32).astype(BF16), count.astype(BF16)).astype(I32)
    odd = before & (SUB - 1)
    tiles = (odd + count.astype(I32) + (SUB - 1)) >> 3
    same = ((row >> shift) == (col >> shift)) & (col < row)
    first = dot(same.astype(F32).astype(BF16), tiles.astype(F32).astype(BF16)).astype(I32)
    lane = iota((cells, LANES), 1)
    kept = jnp.where(tiles > 0, odd, SUB)
    target = jnp.minimum(before >> 3, last_tile)
    final = jnp.maximum(tiles - 1, 0)
    meta = jnp.where(lane == 2, first, final)
    meta_ref[...] = jnp.where(lane == 0, kept, jnp.where(lane == 1, target, meta))
    copy = pltpu.make_async_copy(meta_ref, meta_smem, sems.at[3])
    copy.start()
    local = first * SUB + odd
    local = jnp.concatenate([local] * wide, axis=1)
    spot = jnp.where(hits, local + running.astype(I32) - 1, 0)
    place_ref[...] = jnp.concatenate(
        [jnp.sum(spot[s * groups : (s + 1) * groups], axis=0, keepdims=True) for s in range(blocks)],
        axis=0,
    )
    copy.wait()
    sub_row = iota((SUB, state), 0)
    tile = lambda t: pl.ds(pl.multiple_of(t * SUB, SUB), SUB)

    def body(s, carry):
        place = place_ref[pl.ds(s, 1), :]
        moves = (iota((padded, block), 0) == place).astype(F32).astype(BF16)
        ids = [ids_ref[pl.ds(s * wide + i, 1), :] for i in range(wide)]
        known = iota((sensors, block), 0) == jnp.concatenate(ids, axis=1)
        inv = jnp.concatenate([inv_ref[...]] * wide, axis=1)
        scale_row = jnp.sum(jnp.where(known, inv, 0.0), axis=0, keepdims=True)
        scale = jnp.transpose(jnp.broadcast_to(scale_row, (LANES, block)))
        fetch(s).wait()
        rows = pl.ds(pl.multiple_of(s * block, block), block)
        scaled = obs_ref[rows, :] * jnp.concatenate([scale] * (state // LANES), axis=1)
        high, low = split(scaled)
        sorted_ref[...] = dot(moves, high) + dot(moves, low)
        longest = 0
        for v in range(groups):
            cell = s * groups + v
            kept, target = meta_smem[cell, 0], meta_smem[cell, 1]
            first, final = meta_smem[cell, 2], meta_smem[cell, 3]
            longest = jnp.maximum(longest, final)
            old = outs[v][tile(target), :]
            for t in reversed(range(1, most)):
                t = jnp.minimum(t, final)
                outs[v][tile(target + t), :] = sorted_ref[tile(first + t), :]
            outs[v][tile(target), :] = jnp.where(sub_row < kept, old, sorted_ref[tile(first), :])

        @pl.when(longest >= most)
        def _():
            for v in range(groups):
                cell = s * groups + v
                target, first, final = (meta_smem[cell, i] for i in (1, 2, 3))

                def longer(t, carry, v=v, target=target, first=first):
                    outs[v][tile(target + t), :] = sorted_ref[tile(first + t), :]
                    return carry

                lax.fori_loop(most, final + 1, longer, 0)

        return carry

    lax.fori_loop(0, blocks, body, 0)


def regroup(observations, sensor_ids, sensor_sigma, buckets, me, groups):
    rows, state = observations.shape
    sensors = sensor_sigma.shape[0]
    block = 256
    blocks = rows // block
    per_bucket = rows // groups
    padded = -(-(block + groups * 2 * (SUB - 1)) // 16) * 16
    far = pl.BlockSpec(memory_space=pltpu.HBM)
    return pl.pallas_call(
        functools.partial(regroup_kernel, groups, per_bucket),
        in_specs=[pl.BlockSpec(memory_space=pltpu.SMEM)] + [far] * 4,
        out_specs=[pl.BlockSpec(memory_space=pltpu.VMEM)] * groups,
        scratch_shapes=[
            pltpu.VMEM((rows // LANES, LANES), I32),
            pltpu.VMEM((rows // LANES, LANES), I32),
            pltpu.VMEM((1, sensors), F32),
            pltpu.VMEM((rows, state), F32),
            pltpu.VMEM((blocks, block), I32),
            pltpu.VMEM((blocks * groups, LANES), I32),
            pltpu.VMEM((padded, state), F32),
            pltpu.VMEM((sensors, LANES), F32),
            pltpu.SMEM((blocks * groups, LANES), I32),
            pltpu.SemaphoreType.DMA((4 + blocks,)),
        ],
        out_shape=[jax.ShapeDtypeStruct((per_bucket, state), F32)] * groups,
        compiler_params=pltpu.CompilerParams(vmem_limit_bytes=56 * MIB),
        cost_estimate=pl.CostEstimate(
            flops=4 * rows * padded * state, bytes_accessed=8 * rows * state, transcendentals=0
        ),
    )(
        me.reshape(1),
        buckets.reshape(rows // LANES, LANES),
        sensor_ids.reshape(rows // LANES, LANES),
        sensor_sigma.reshape(1, sensors),
        observations,
    )


def block_pairs(count):
    return [(i, j) for i in range(count) for j in range(i, count)]


def write_gram(both, state, out_ref):
    for n, (i, j) in enumerate(block_pairs(state // LANES)):
        a, b = i * LANES, j * LANES
        cross = both[a : a + LANES, state + b : state + b + LANES]
        turned = both[b : b + LANES, state + a : state + a + LANES]
        out_ref[n * LANES : (n + 1) * LANES, :] = both[a : a + LANES, b : b + LANES] + (
            cross + jnp.transpose(turned)
        )


def gram_kernel(groups, prior_ref, *rest):
    chunks = rest[:groups]
    out_ref, prior_out_ref, both_ref, pair_ref = rest[groups:]
    per_bucket, state = chunks[0].shape
    for k, chunk in enumerate(chunks):
        rows = slice(k * per_bucket, (k + 1) * per_bucket)
        high, low = split(chunk[...])
        pair_ref[rows, :state] = high
        pair_ref[rows, state:] = low
    both_ref[...] = dot_rows(pair_ref[:, :state], pair_ref[...])
    write_gram(both_ref, state, out_ref)
    high, low = split(prior_ref[...])
    both_ref[...] = dot_rows(high, jnp.concatenate([high, low], axis=1))
    write_gram(both_ref, state, prior_out_ref)


def gram(prior_factor, chunks):
    groups = len(chunks)
    per_bucket, state = chunks[0].shape
    rows = groups * per_bucket
    packed = len(block_pairs(state // LANES)) * LANES
    vmem = pl.BlockSpec(memory_space=pltpu.VMEM)
    return pl.pallas_call(
        functools.partial(gram_kernel, groups),
        in_specs=[vmem] * (groups + 1),
        out_specs=[vmem] * 2,
        out_shape=[jax.ShapeDtypeStruct((packed, LANES), F32)] * 2,
        scratch_shapes=[pltpu.VMEM((state, 2 * state), F32), pltpu.VMEM((rows, 2 * state), BF16)],
        compiler_params=pltpu.CompilerParams(vmem_limit_bytes=24 * MIB),
        cost_estimate=pl.CostEstimate(
            flops=4 * rows * state * state, bytes_accessed=4 * rows * state, transcendentals=0
        ),
    )(prior_factor, *chunks)


def scatter_sum(packed, count, groups):
    rows, lanes = packed.shape
    axes = ("rows", "grp")
    got = lax.all_to_all(packed, axes, split_axis=0, concat_axis=0, axis_index_groups=groups, tiled=True)
    return jnp.sum(got.reshape(count, rows // count, lanes), axis=0)


def gather_pieces(piece, count, groups):
    rows, lanes = piece.shape
    copies = jnp.broadcast_to(piece, (count, rows, lanes)).reshape(count * rows, lanes)
    axes = ("rows", "grp")
    return lax.all_to_all(copies, axes, split_axis=0, concat_axis=0, axis_index_groups=groups, tiled=True)


def sweep(a, w):
    width = a.shape[0]
    groups = width // SUB
    row_id = iota((SUB, LANES), 0)
    a_rows = [a[g * SUB : (g + 1) * SUB, :] for g in range(groups)]
    w_rows = [w[g * SUB : (g + 1) * SUB, :] for g in range(groups)]
    for g in range(groups):
        va, vw = a_rows[g], w_rows[g]
        cols = [
            jnp.broadcast_to(va[:, g * SUB + j : g * SUB + j + 1], (SUB, LANES)) for j in range(SUB)
        ]
        scale = jnp.zeros((SUB, LANES), F32)
        for j in range(SUB):
            pivot = jnp.broadcast_to(cols[j][j : j + 1, :], (SUB, LANES))
            root = lax.rsqrt(pivot)
            scale = jnp.where(row_id == j, root, scale)
            if j < SUB - 1:
                ratio = jnp.where(row_id > j, cols[j] * (root * root), 0.0)
                for k in range(j + 1, SUB):
                    cols[k] = cols[k] - ratio * cols[k][j : j + 1, :]
                va = va - ratio * va[j : j + 1, :]
                vw = vw - ratio * vw[j : j + 1, :]
        va, vw = va * scale, vw * scale
        va = jnp.where(iota((SUB, LANES), 1) >= row_id + g * SUB, va, 0.0)
        a_rows[g], w_rows[g] = va, vw
        if g < groups - 1:
            both = jnp.concatenate([va, vw], axis=1)
            high = both.astype(BF16).astype(F32)
            low = both - high
            left = jnp.concatenate([high[:, :LANES], high[:, :LANES], low[:, :LANES]], axis=0)
            right = jnp.concatenate([high, low, high], axis=0)
            change = dot_rows(left.astype(BF16), right.astype(BF16))
            for q in range(g + 1, groups):
                rows = slice(q * SUB, (q + 1) * SUB)
                a_rows[q] = a_rows[q] - change[rows, :LANES]
                w_rows[q] = w_rows[q] - change[rows, LANES:]
    return jnp.concatenate(a_rows, axis=0), jnp.concatenate(w_rows, axis=0)


def factor_kernel(inv_total, sum_ref, prior_ref, factor_ref, high_ref, low_ref, a_ref, x_ref):
    state = factor_ref.shape[0]
    count = state // LANES
    span = lambda i: slice(i * LANES, (i + 1) * LANES)
    for n, (i, j) in enumerate(block_pairs(count)):
        a_ref[span(i), span(j)] = prior_ref[span(n), :] + sum_ref[span(n), :] * inv_total
    factor_ref[...] = jnp.zeros((state, state), F32)
    x_ref[...] = jnp.zeros((state, state), F32)
    eye = (iota((LANES, LANES), 0) == iota((LANES, LANES), 1)).astype(F32)
    for k in range(count):
        r, w = sweep(a_ref[span(k), span(k)], eye)
        factor_ref[span(k), span(k)] = r
        x = jnp.transpose(w)
        x_ref[span(k), span(k)] = x
        if k > 0:
            left = dot3(x_ref[: k * LANES, : k * LANES], factor_ref[: k * LANES, span(k)])
            x_ref[: k * LANES, span(k)] = -dot3(left, x)
        if k < count - 1:
            rest = slice((k + 1) * LANES, state)
            right = dot3(w, a_ref[span(k), rest])
            factor_ref[span(k), rest] = right
            for i in range(k + 1, count):
                low = slice(i * LANES, state)
                at = (i - k - 1) * LANES
                a_ref[span(i), low] -= dot3_rows(right[:, at : at + LANES], right[:, at:])
    high, low = split(x_ref[...])
    high_ref[...] = high
    low_ref[...] = low


def factorise(summed, prior_gram, state, total_rows):
    vmem = pl.BlockSpec(memory_space=pltpu.VMEM)
    return pl.pallas_call(
        functools.partial(factor_kernel, 1.0 / total_rows),
        in_specs=[vmem] * 2,
        out_specs=[vmem] * 3,
        out_shape=[
            jax.ShapeDtypeStruct((state, state), F32),
            jax.ShapeDtypeStruct((state, state), BF16),
            jax.ShapeDtypeStruct((state, state), BF16),
        ],
        scratch_shapes=[pltpu.VMEM((state, state), F32)] * 2,
        compiler_params=pltpu.CompilerParams(vmem_limit_bytes=16 * MIB),
        cost_estimate=pl.CostEstimate(
            flops=1, bytes_accessed=1, transcendentals=0
        ),
    )(summed, prior_gram)


def whiten_kernel(steps, aliased, me_ref, high_ref, low_ref, *rest):
    count = len(steps)
    chunks = rest[:count]
    out_ref, held, sems = rest[count + aliased :]
    per_bucket = chunks[0].shape[0]
    high, low = high_ref[...], low_ref[...]
    copies = []
    for n, k in enumerate(steps):
        rows_high, rows_low = split(chunks[n][...])
        held[n] = dot(rows_high, high) + (dot(rows_high, low) + dot(rows_low, high))
        slot = me_ref[0] ^ k
        copy = pltpu.make_async_copy(
            held.at[n],
            out_ref.at[pl.ds(pl.multiple_of(slot * per_bucket, per_bucket), per_bucket), :],
            sems.at[n],
        )
        copy.start()
        copies.append(copy)
    for copy in copies:
        copy.wait()


def whiten(me, high, low, steps, chunks, out, rows):
    per_bucket, state = chunks[0].shape
    count = len(chunks)
    vmem = pl.BlockSpec(memory_space=pltpu.VMEM)
    anywhere = pl.BlockSpec(memory_space=pl.ANY)
    extra = [] if out is None else [out]
    return pl.pallas_call(
        functools.partial(whiten_kernel, tuple(steps), len(extra)),
        in_specs=[pl.BlockSpec(memory_space=pltpu.SMEM)]
        + [vmem] * (2 + count)
        + [anywhere] * len(extra),
        out_specs=anywhere,
        out_shape=jax.ShapeDtypeStruct((rows, state), F32),
        scratch_shapes=[
            pltpu.VMEM((count, per_bucket, state), F32),
            pltpu.SemaphoreType.DMA((count,)),
        ],
        input_output_aliases={3 + count: 0} if extra else {},
        compiler_params=pltpu.CompilerParams(vmem_limit_bytes=16 * MIB),
        cost_estimate=pl.CostEstimate(
            flops=1, bytes_accessed=1, transcendentals=0
        ),
    )(me.reshape(1), high, low, *chunks, *extra)


def behind(value, *arrays):
    return lax.optimization_barrier((value, *arrays))


def shards(observations, sensor_ids, sensor_sigma, buckets, prior_factor):
    rows_dev, state = observations.shape
    groups = lax.axis_size("rows")
    grp = lax.axis_size("grp")
    me = lax.axis_index("rows").astype(I32)
    total_rows = rows_dev * groups * grp
    chunks = regroup(observations, sensor_ids, sensor_sigma, buckets, me, groups)
    move = lambda k, chunk: lax.ppermute(chunk, "rows", [(i, i ^ k) for i in range(groups)])
    packed_rows = len(block_pairs(state // LANES)) * LANES
    plane = 2 * grp
    planes = [list(range(i, i + plane)) for i in range(0, groups * grp, plane)]
    early = [k for k in (1, 4) if k < groups]
    middle = [k for k in (6, 2) if k < groups]
    late = [k for k in range(1, groups) if k not in early + middle]
    received = {0: chunks[0]}
    valid = prior_factor[0, 0] > 0
    nothing = lambda rows: jnp.full((rows, LANES), jnp.nan, F32)

    for k in early:
        received[k] = move(k, chunks[k])

    def first():
        packed, prior_gram = gram(prior_factor, chunks)
        return scatter_sum(packed, plane, planes), prior_gram

    piece, prior_gram = lax.cond(
        valid, first, lambda: (nothing(packed_rows // plane), nothing(packed_rows))
    )
    for k in early:
        piece, received[k] = behind(piece, received[k])
    across = [piece]
    for step in range(1, groups // 2):
        across.append(move(2 * step, piece))
    for k in middle:
        _, chunk = behind(piece, chunks[k])
        received[k] = move(k, chunk)
    while len(across) > 1:
        across = [across[i] + across[i + 1] for i in range(0, len(across), 2)]
    summed = lax.cond(
        valid, lambda: gather_pieces(across[0], plane, planes), lambda: nothing(packed_rows)
    )
    for k in late:
        _, chunk = behind(summed, chunks[k])
        received[k] = move(k, chunk)
    factor, high, low = factorise(summed, prior_gram, state, total_rows)
    out = None
    for steps in ([0] + early + middle, late):
        out = whiten(me, high, low, steps, [received[k] for k in steps], out, rows_dev)
    return (out, factor)


def solution(mesh):
    in_specs = (P(("rows", "grp"), None), P(("rows", "grp")), P(), P(("rows", "grp")), P())
    out_specs = (P(("rows", "grp"), None), P())
    return jax.shard_map(shards, mesh=mesh, in_specs=in_specs, out_specs=out_specs, check_vma=False)
```

```python
import functools

import jax
import jax.numpy as jnp
from jax import lax
from jax.experimental import pallas as pl
from jax.experimental.pallas import tpu as pltpu
from jax.sharding import PartitionSpec as P

F32 = jnp.float32
BF16 = jnp.bfloat16
I32 = jnp.int32
LANES = 128
SUB = 8
MIB = 1024 * 1024


def iota(shape, axis):
    return lax.broadcasted_iota(I32, shape, axis)


def split(values):
    high = values.astype(BF16)
    low = (values - high.astype(F32)).astype(BF16)
    return high, low


def dot(left, right):
    return jnp.dot(left, right, preferred_element_type=F32)


def dot_rows(left, right):
    return lax.dot_general(left, right, (((0,), (0,)), ((), ())), preferred_element_type=F32)


def dot3(left, right):
    lh, ll = split(left)
    rh, rl = split(right)
    return dot(lh, rh) + (dot(lh, rl) + dot(ll, rh))


def dot3_rows(left, right):
    lh, ll = split(left)
    rh, rl = split(right)
    return dot_rows(lh, rh) + (dot_rows(lh, rl) + dot_rows(ll, rh))


def rows_of(packed, count, wide):
    return [
        jnp.concatenate([packed[s * wide + i : s * wide + i + 1, :] for i in range(wide)], axis=1)
        for s in range(count)
    ]


def regroup_kernel(groups, per_bucket, me_ref, *refs):
    given, outs, scratch = refs[:4], refs[4 : 4 + groups], refs[4 + groups :]
    held, (place_ref, meta_ref, sorted_ref, inv_ref, meta_smem, sems) = scratch[:4], scratch[4:]
    buckets_ref, ids_ref, sigma_ref, obs_ref = held
    blocks, block = place_ref.shape
    wide = block // LANES
    sensors = sigma_ref.shape[1]
    _, padded, state = sorted_ref.shape
    cells = blocks * groups
    last_tile = per_bucket // SUB - 1
    most = min(7, last_tile + 2)

    small = [pltpu.make_async_copy(given[i], held[i], sems.at[i]) for i in range(3)]
    for copy in small:
        copy.start()

    def fetch(s):
        rows = pl.ds(pl.multiple_of(s * block, block), block)
        return pltpu.make_async_copy(given[3].at[rows, :], obs_ref.at[rows, :], sems.at[4 + s])

    for s in range(blocks):
        fetch(s).start()
    for copy in small:
        copy.wait()

    inv_row = 1.0 / sigma_ref[...]
    inv_ref[...] = jnp.transpose(jnp.broadcast_to(inv_row, (LANES, sensors)))
    slots = rows_of(buckets_ref[...] ^ me_ref[0], blocks, wide)
    hits = jnp.concatenate(
        [jnp.broadcast_to(row, (groups, block)) == iota((groups, block), 0) for row in slots], axis=0
    )
    upto = (iota((block, block), 0) <= iota((block, block), 1)).astype(F32).astype(BF16)
    running = dot(hits.astype(F32).astype(BF16), upto)
    count = jnp.broadcast_to(running[:, block - 1 : block], (cells, LANES))
    row, col = iota((cells, cells), 0), iota((cells, cells), 1)
    shift = groups.bit_length() - 1
    earlier = ((row & (groups - 1)) == (col & (groups - 1))) & (col < row)
    before = dot(earlier.astype(F32).astype(BF16), count.astype(BF16)).astype(I32)
    odd = before & (SUB - 1)
    tiles = (odd + count.astype(I32) + (SUB - 1)) >> 3
    same = ((row >> shift) == (col >> shift)) & (col < row)
    first = dot(same.astype(F32).astype(BF16), tiles.astype(F32).astype(BF16)).astype(I32)
    lane = iota((cells, LANES), 1)
    kept = jnp.where(tiles > 0, odd, SUB)
    target = jnp.minimum(before >> 3, last_tile)
    final = jnp.maximum(tiles - 1, 0)
    meta = jnp.where(lane == 2, first, final)
    meta_ref[...] = jnp.where(lane == 0, kept, jnp.where(lane == 1, target, meta))
    copy = pltpu.make_async_copy(meta_ref, meta_smem, sems.at[3])
    copy.start()
    local = first * SUB + odd
    local = jnp.concatenate([local] * wide, axis=1)
    spot = jnp.where(hits, local + running.astype(I32) - 1, 0)
    place_ref[...] = jnp.concatenate(
        [jnp.sum(spot[s * groups : (s + 1) * groups], axis=0, keepdims=True) for s in range(blocks)],
        axis=0,
    )
    sub_row = iota((SUB, state), 0)
    tile = lambda t: pl.ds(pl.multiple_of(t * SUB, SUB), SUB)

    def sort_block(s, into):
        place = place_ref[pl.ds(s, 1), :]
        moves = (iota((padded, block), 0) == place).astype(F32).astype(BF16)
        ids = [ids_ref[pl.ds(s * wide + i, 1), :] for i in range(wide)]
        known = iota((sensors, block), 0) == jnp.concatenate(ids, axis=1)
        inv = jnp.concatenate([inv_ref[...]] * wide, axis=1)
        scale_row = jnp.sum(jnp.where(known, inv, 0.0), axis=0, keepdims=True)
        scale = jnp.transpose(jnp.broadcast_to(scale_row, (LANES, block)))
        fetch(s).wait()
        rows = pl.ds(pl.multiple_of(s * block, block), block)
        scaled = obs_ref[rows, :] * jnp.concatenate([scale] * (state // LANES), axis=1)
        high, low = split(scaled)
        into[...] = dot(moves, high) + dot(moves, low)

    def run(cell):
        return [meta_smem[cell, i] for i in range(4)]

    def place_runs(s, source):
        for v in range(groups):
            kept, target, first, final = run(s * groups + v)
            old = outs[v][tile(target), :]
            for t in reversed(range(1, most)):
                t = jnp.minimum(t, final)
                outs[v][tile(target + t), :] = source[tile(first + t), :]
            outs[v][tile(target), :] = jnp.where(sub_row < kept, old, source[tile(first), :])

    def place_rest(s, source):
        for v in range(groups):
            _, target, first, final = run(s * groups + v)

            def longer(t, carry, v=v, target=target, first=first):
                outs[v][tile(target + t), :] = source[tile(first + t), :]
                return carry

            lax.fori_loop(most, final + 1, longer, 0)

    longest = jnp.max(final)
    unroll = groups <= 8

    @pl.when((longest < most) & unroll)
    def _():
        for s in range(blocks if unroll else 0):
            sort_block(s, sorted_ref.at[s % 2])
            if s == 0:
                copy.wait()
            place_runs(s, sorted_ref.at[s % 2])

    @pl.when((longest >= most) | (not unroll))
    def _():
        copy.wait()

        def body(s, carry):
            sort_block(s, sorted_ref.at[0])
            place_runs(s, sorted_ref.at[0])
            place_rest(s, sorted_ref.at[0])
            return carry

        lax.fori_loop(0, blocks, body, 0)


def regroup(observations, sensor_ids, sensor_sigma, buckets, me, groups):
    rows, state = observations.shape
    sensors = sensor_sigma.shape[0]
    block = 256
    blocks = rows // block
    per_bucket = rows // groups
    padded = -(-(block + groups * 2 * (SUB - 1)) // 16) * 16
    far = pl.BlockSpec(memory_space=pltpu.HBM)
    return pl.pallas_call(
        functools.partial(regroup_kernel, groups, per_bucket),
        in_specs=[pl.BlockSpec(memory_space=pltpu.SMEM)] + [far] * 4,
        out_specs=[pl.BlockSpec(memory_space=pltpu.VMEM)] * groups,
        scratch_shapes=[
            pltpu.VMEM((rows // LANES, LANES), I32),
            pltpu.VMEM((rows // LANES, LANES), I32),
            pltpu.VMEM((1, sensors), F32),
            pltpu.VMEM((rows, state), F32),
            pltpu.VMEM((blocks, block), I32),
            pltpu.VMEM((blocks * groups, LANES), I32),
            pltpu.VMEM((2, padded, state), F32),
            pltpu.VMEM((sensors, LANES), F32),
            pltpu.SMEM((blocks * groups, LANES), I32),
            pltpu.SemaphoreType.DMA((4 + blocks,)),
        ],
        out_shape=[jax.ShapeDtypeStruct((per_bucket, state), F32)] * groups,
        compiler_params=pltpu.CompilerParams(vmem_limit_bytes=56 * MIB),
        cost_estimate=pl.CostEstimate(
            flops=4 * rows * padded * state, bytes_accessed=8 * rows * state, transcendentals=0
        ),
    )(
        me.reshape(1),
        buckets.reshape(rows // LANES, LANES),
        sensor_ids.reshape(rows // LANES, LANES),
        sensor_sigma.reshape(1, sensors),
        observations,
    )


def block_pairs(count):
    return [(i, j) for i in range(count) for j in range(i, count)]


def write_gram(both, state, out_ref):
    for n, (i, j) in enumerate(block_pairs(state // LANES)):
        a, b = i * LANES, j * LANES
        cross = both[a : a + LANES, state + b : state + b + LANES]
        turned = both[b : b + LANES, state + a : state + a + LANES]
        out_ref[n * LANES : (n + 1) * LANES, :] = both[a : a + LANES, b : b + LANES] + (
            cross + jnp.transpose(turned)
        )


def gram_kernel(groups, prior_ref, *rest):
    chunks = rest[:groups]
    out_ref, prior_out_ref, both_ref, pair_ref = rest[groups:]
    per_bucket, state = chunks[0].shape
    for k, chunk in enumerate(chunks):
        rows = slice(k * per_bucket, (k + 1) * per_bucket)
        high, low = split(chunk[...])
        pair_ref[rows, :state] = high
        pair_ref[rows, state:] = low
    both_ref[...] = dot_rows(pair_ref[:, :state], pair_ref[...])
    write_gram(both_ref, state, out_ref)
    high, low = split(prior_ref[...])
    both_ref[...] = dot_rows(high, jnp.concatenate([high, low], axis=1))
    write_gram(both_ref, state, prior_out_ref)


def gram(prior_factor, chunks):
    groups = len(chunks)
    per_bucket, state = chunks[0].shape
    rows = groups * per_bucket
    packed = len(block_pairs(state // LANES)) * LANES
    vmem = pl.BlockSpec(memory_space=pltpu.VMEM)
    return pl.pallas_call(
        functools.partial(gram_kernel, groups),
        in_specs=[vmem] * (groups + 1),
        out_specs=[vmem] * 2,
        out_shape=[jax.ShapeDtypeStruct((packed, LANES), F32)] * 2,
        scratch_shapes=[pltpu.VMEM((state, 2 * state), F32), pltpu.VMEM((rows, 2 * state), BF16)],
        compiler_params=pltpu.CompilerParams(vmem_limit_bytes=24 * MIB),
        cost_estimate=pl.CostEstimate(
            flops=4 * rows * state * state, bytes_accessed=4 * rows * state, transcendentals=0
        ),
    )(prior_factor, *chunks)


def scatter_sum(packed, count, groups):
    rows, lanes = packed.shape
    axes = ("rows", "grp")
    got = lax.all_to_all(packed, axes, split_axis=0, concat_axis=0, axis_index_groups=groups, tiled=True)
    return jnp.sum(got.reshape(count, rows // count, lanes), axis=0)


def gather_pieces(piece, count, groups):
    rows, lanes = piece.shape
    copies = jnp.broadcast_to(piece, (count, rows, lanes)).reshape(count * rows, lanes)
    axes = ("rows", "grp")
    return lax.all_to_all(copies, axes, split_axis=0, concat_axis=0, axis_index_groups=groups, tiled=True)


def sweep(a, w):
    width = a.shape[0]
    groups = width // SUB
    row_id = iota((SUB, LANES), 0)
    a_rows = [a[g * SUB : (g + 1) * SUB, :] for g in range(groups)]
    w_rows = [w[g * SUB : (g + 1) * SUB, :] for g in range(groups)]
    for g in range(groups):
        va, vw = a_rows[g], w_rows[g]
        cols = [
            jnp.broadcast_to(va[:, g * SUB + j : g * SUB + j + 1], (SUB, LANES)) for j in range(SUB)
        ]
        scale = jnp.zeros((SUB, LANES), F32)
        for j in range(SUB):
            pivot = jnp.broadcast_to(cols[j][j : j + 1, :], (SUB, LANES))
            root = lax.rsqrt(pivot)
            scale = jnp.where(row_id == j, root, scale)
            if j < SUB - 1:
                ratio = jnp.where(row_id > j, cols[j] * (root * root), 0.0)
                for k in range(j + 1, SUB):
                    cols[k] = cols[k] - ratio * cols[k][j : j + 1, :]
                va = va - ratio * va[j : j + 1, :]
                vw = vw - ratio * vw[j : j + 1, :]
        va, vw = va * scale, vw * scale
        va = jnp.where(iota((SUB, LANES), 1) >= row_id + g * SUB, va, 0.0)
        a_rows[g], w_rows[g] = va, vw
        if g < groups - 1:
            both = jnp.concatenate([va, vw], axis=1)
            high = both.astype(BF16).astype(F32)
            low = both - high
            left = jnp.concatenate([high[:, :LANES], high[:, :LANES], low[:, :LANES]], axis=0)
            right = jnp.concatenate([high, low, high], axis=0)
            change = dot_rows(left.astype(BF16), right.astype(BF16))
            for q in range(g + 1, groups):
                rows = slice(q * SUB, (q + 1) * SUB)
                a_rows[q] = a_rows[q] - change[rows, :LANES]
                w_rows[q] = w_rows[q] - change[rows, LANES:]
    return jnp.concatenate(a_rows, axis=0), jnp.concatenate(w_rows, axis=0)


def factor_kernel(inv_total, sum_ref, prior_ref, factor_ref, high_ref, low_ref, a_ref, x_ref):
    state = factor_ref.shape[0]
    count = state // LANES
    span = lambda i: slice(i * LANES, (i + 1) * LANES)
    for n, (i, j) in enumerate(block_pairs(count)):
        a_ref[span(i), span(j)] = prior_ref[span(n), :] + sum_ref[span(n), :] * inv_total
    factor_ref[...] = jnp.zeros((state, state), F32)
    x_ref[...] = jnp.zeros((state, state), F32)
    eye = (iota((LANES, LANES), 0) == iota((LANES, LANES), 1)).astype(F32)
    for k in range(count):
        r, w = sweep(a_ref[span(k), span(k)], eye)
        factor_ref[span(k), span(k)] = r
        x = jnp.transpose(w)
        x_ref[span(k), span(k)] = x
        if k > 0:
            left = dot3(x_ref[: k * LANES, : k * LANES], factor_ref[: k * LANES, span(k)])
            x_ref[: k * LANES, span(k)] = -dot3(left, x)
        if k < count - 1:
            rest = slice((k + 1) * LANES, state)
            right = dot3(w, a_ref[span(k), rest])
            factor_ref[span(k), rest] = right
            for i in range(k + 1, count):
                low = slice(i * LANES, state)
                at = (i - k - 1) * LANES
                a_ref[span(i), low] -= dot3_rows(right[:, at : at + LANES], right[:, at:])
    high, low = split(x_ref[...])
    high_ref[...] = high
    low_ref[...] = low


def factorise(summed, prior_gram, state, total_rows):
    vmem = pl.BlockSpec(memory_space=pltpu.VMEM)
    return pl.pallas_call(
        functools.partial(factor_kernel, 1.0 / total_rows),
        in_specs=[vmem] * 2,
        out_specs=[vmem] * 3,
        out_shape=[
            jax.ShapeDtypeStruct((state, state), F32),
            jax.ShapeDtypeStruct((state, state), BF16),
            jax.ShapeDtypeStruct((state, state), BF16),
        ],
        scratch_shapes=[pltpu.VMEM((state, state), F32)] * 2,
        compiler_params=pltpu.CompilerParams(vmem_limit_bytes=16 * MIB),
        cost_estimate=pl.CostEstimate(
            flops=1, bytes_accessed=1, transcendentals=0
        ),
    )(summed, prior_gram)


def whiten_kernel(steps, aliased, me_ref, high_ref, low_ref, *rest):
    count = len(steps)
    chunks = rest[:count]
    out_ref, held, sems = rest[count + aliased :]
    per_bucket = chunks[0].shape[0]
    high, low = high_ref[...], low_ref[...]
    copies = []
    for n, k in enumerate(steps):
        rows_high, rows_low = split(chunks[n][...])
        held[n] = dot(rows_high, high) + (dot(rows_high, low) + dot(rows_low, high))
        slot = me_ref[0] ^ k
        copy = pltpu.make_async_copy(
            held.at[n],
            out_ref.at[pl.ds(pl.multiple_of(slot * per_bucket, per_bucket), per_bucket), :],
            sems.at[n],
        )
        copy.start()
        copies.append(copy)
    for copy in copies:
        copy.wait()


def whiten(me, high, low, steps, chunks, out, rows):
    per_bucket, state = chunks[0].shape
    count = len(chunks)
    vmem = pl.BlockSpec(memory_space=pltpu.VMEM)
    anywhere = pl.BlockSpec(memory_space=pl.ANY)
    extra = [] if out is None else [out]
    return pl.pallas_call(
        functools.partial(whiten_kernel, tuple(steps), len(extra)),
        in_specs=[pl.BlockSpec(memory_space=pltpu.SMEM)]
        + [vmem] * (2 + count)
        + [anywhere] * len(extra),
        out_specs=anywhere,
        out_shape=jax.ShapeDtypeStruct((rows, state), F32),
        scratch_shapes=[
            pltpu.VMEM((count, per_bucket, state), F32),
            pltpu.SemaphoreType.DMA((count,)),
        ],
        input_output_aliases={3 + count: 0} if extra else {},
        compiler_params=pltpu.CompilerParams(vmem_limit_bytes=16 * MIB),
        cost_estimate=pl.CostEstimate(
            flops=1, bytes_accessed=1, transcendentals=0
        ),
    )(me.reshape(1), high, low, *chunks, *extra)


def behind(value, *arrays):
    return lax.optimization_barrier((value, *arrays))


def shards(observations, sensor_ids, sensor_sigma, buckets, prior_factor):
    rows_dev, state = observations.shape
    groups = lax.axis_size("rows")
    grp = lax.axis_size("grp")
    me = lax.axis_index("rows").astype(I32)
    total_rows = rows_dev * groups * grp
    chunks = regroup(observations, sensor_ids, sensor_sigma, buckets, me, groups)
    move = lambda k, chunk: lax.ppermute(chunk, "rows", [(i, i ^ k) for i in range(groups)])
    packed_rows = len(block_pairs(state // LANES)) * LANES
    plane = 2 * grp
    planes = [list(range(i, i + plane)) for i in range(0, groups * grp, plane)]
    early = [k for k in (1, 4) if k < groups]
    middle = [k for k in (6, 2) if k < groups]
    late = [k for k in range(1, groups) if k not in early + middle]
    received = {0: chunks[0]}
    valid = prior_factor[0, 0] > 0
    nothing = lambda rows: jnp.full((rows, LANES), jnp.nan, F32)

    for k in early:
        received[k] = move(k, chunks[k])

    def first():
        packed, prior_gram = gram(prior_factor, chunks)
        return scatter_sum(packed, plane, planes), prior_gram

    piece, prior_gram = lax.cond(
        valid, first, lambda: (nothing(packed_rows // plane), nothing(packed_rows))
    )
    across = [piece]
    for step in range(1, groups // 2):
        across.append(move(2 * step, piece))
    while len(across) > 1:
        across = [across[i] + across[i + 1] for i in range(0, len(across), 2)]
    for k in middle:
        _, chunk = behind(across[0], chunks[k])
        received[k] = move(k, chunk)
    for k in early:
        across[0], received[k] = behind(across[0], received[k])
    summed = lax.cond(
        valid, lambda: gather_pieces(across[0], plane, planes), lambda: nothing(packed_rows)
    )
    for k in late:
        _, chunk = behind(summed, chunks[k])
        received[k] = move(k, chunk)
    factor, high, low = factorise(summed, prior_gram, state, total_rows)
    out = None
    for steps in ([0] + early + middle, late[:-1], late[-1:]):
        out = whiten(me, high, low, steps, [received[k] for k in steps], out, rows_dev)
    return (out, factor)


def solution(mesh):
    in_specs = (P(("rows", "grp"), None), P(("rows", "grp")), P(), P(("rows", "grp")), P())
    out_specs = (P(("rows", "grp"), None), P())
    return jax.shard_map(shards, mesh=mesh, in_specs=in_specs, out_specs=out_specs, check_vma=False)
```

```python
import functools

import jax
import jax.numpy as jnp
from jax import lax
from jax.experimental import pallas as pl
from jax.experimental.pallas import tpu as pltpu
from jax.sharding import PartitionSpec as P

F32 = jnp.float32
BF16 = jnp.bfloat16
I32 = jnp.int32
LANES = 128
SUB = 8
MIB = 1024 * 1024


def iota(shape, axis):
    return lax.broadcasted_iota(I32, shape, axis)


def split(values):
    high = values.astype(BF16)
    low = (values - high.astype(F32)).astype(BF16)
    return high, low


def dot(left, right):
    return jnp.dot(left, right, preferred_element_type=F32)


def dot_rows(left, right):
    return lax.dot_general(left, right, (((0,), (0,)), ((), ())), preferred_element_type=F32)


def dot3(left, right):
    lh, ll = split(left)
    rh, rl = split(right)
    return dot(lh, rh) + (dot(lh, rl) + dot(ll, rh))


def dot3_rows(left, right):
    lh, ll = split(left)
    rh, rl = split(right)
    return dot_rows(lh, rh) + (dot_rows(lh, rl) + dot_rows(ll, rh))


def rows_of(packed, count, wide):
    return [
        jnp.concatenate([packed[s * wide + i : s * wide + i + 1, :] for i in range(wide)], axis=1)
        for s in range(count)
    ]


def regroup_kernel(groups, per_bucket, me_ref, *refs):
    given, outs, scratch = refs[:4], refs[4 : 4 + groups], refs[4 + groups :]
    held, (place_ref, meta_ref, sorted_ref, inv_ref, meta_smem, sems) = scratch[:4], scratch[4:]
    buckets_ref, ids_ref, sigma_ref, obs_ref = held
    blocks, block = place_ref.shape
    wide = block // LANES
    sensors = sigma_ref.shape[1]
    _, padded, state = sorted_ref.shape
    cells = blocks * groups
    last_tile = per_bucket // SUB - 1
    most = min(7, last_tile + 2)

    small = [pltpu.make_async_copy(given[i], held[i], sems.at[i]) for i in range(3)]
    for copy in small:
        copy.start()

    def fetch(s):
        rows = pl.ds(pl.multiple_of(s * block, block), block)
        return pltpu.make_async_copy(given[3].at[rows, :], obs_ref.at[rows, :], sems.at[4 + s])

    for s in range(blocks):
        fetch(s).start()
    for copy in small:
        copy.wait()

    inv_row = 1.0 / sigma_ref[...]
    inv_ref[...] = jnp.transpose(jnp.broadcast_to(inv_row, (LANES, sensors)))
    slots = rows_of(buckets_ref[...] ^ me_ref[0], blocks, wide)
    hits = jnp.concatenate(
        [jnp.broadcast_to(row, (groups, block)) == iota((groups, block), 0) for row in slots], axis=0
    )
    upto = (iota((block, block), 0) <= iota((block, block), 1)).astype(F32).astype(BF16)
    running = dot(hits.astype(F32).astype(BF16), upto)
    count = jnp.broadcast_to(running[:, block - 1 : block], (cells, LANES))
    row, col = iota((cells, cells), 0), iota((cells, cells), 1)
    shift = groups.bit_length() - 1
    earlier = ((row & (groups - 1)) == (col & (groups - 1))) & (col < row)
    before = dot(earlier.astype(F32).astype(BF16), count.astype(BF16)).astype(I32)
    odd = before & (SUB - 1)
    tiles = (odd + count.astype(I32) + (SUB - 1)) >> 3
    same = ((row >> shift) == (col >> shift)) & (col < row)
    first = dot(same.astype(F32).astype(BF16), tiles.astype(F32).astype(BF16)).astype(I32)
    lane = iota((cells, LANES), 1)
    kept = jnp.where(tiles > 0, odd, SUB)
    target = jnp.minimum(before >> 3, last_tile)
    final = jnp.maximum(tiles - 1, 0)
    meta = jnp.where(lane == 2, first, final)
    meta_ref[...] = jnp.where(lane == 0, kept, jnp.where(lane == 1, target, meta))
    copy = pltpu.make_async_copy(meta_ref, meta_smem, sems.at[3])
    copy.start()
    local = first * SUB + odd
    local = jnp.concatenate([local] * wide, axis=1)
    spot = jnp.where(hits, local + running.astype(I32) - 1, 0)
    place_ref[...] = jnp.concatenate(
        [jnp.sum(spot[s * groups : (s + 1) * groups], axis=0, keepdims=True) for s in range(blocks)],
        axis=0,
    )
    sub_row = iota((SUB, state), 0)
    tile = lambda t: pl.ds(pl.multiple_of(t * SUB, SUB), SUB)

    def sort_block(s, into):
        place = place_ref[pl.ds(s, 1), :]
        moves = (iota((padded, block), 0) == place).astype(F32).astype(BF16)
        ids = [ids_ref[pl.ds(s * wide + i, 1), :] for i in range(wide)]
        known = iota((sensors, block), 0) == jnp.concatenate(ids, axis=1)
        inv = jnp.concatenate([inv_ref[...]] * wide, axis=1)
        scale_row = jnp.sum(jnp.where(known, inv, 0.0), axis=0, keepdims=True)
        scale = jnp.transpose(jnp.broadcast_to(scale_row, (LANES, block)))
        fetch(s).wait()
        rows = pl.ds(pl.multiple_of(s * block, block), block)
        scaled = obs_ref[rows, :] * jnp.concatenate([scale] * (state // LANES), axis=1)
        high, low = split(scaled)
        into[...] = dot(moves, high) + dot(moves, low)

    def run(cell):
        return [meta_smem[cell, i] for i in range(4)]

    def place_runs(s, source):
        for v in range(groups):
            kept, target, first, final = run(s * groups + v)
            old = outs[v][tile(target), :]
            for t in reversed(range(1, most)):
                t = jnp.minimum(t, final)
                outs[v][tile(target + t), :] = source[tile(first + t), :]
            outs[v][tile(target), :] = jnp.where(sub_row < kept, old, source[tile(first), :])

    def place_rest(s, source):
        for v in range(groups):
            _, target, first, final = run(s * groups + v)

            def longer(t, carry, v=v, target=target, first=first):
                outs[v][tile(target + t), :] = source[tile(first + t), :]
                return carry

            lax.fori_loop(most, final + 1, longer, 0)

    longest = jnp.max(final)
    unroll = groups <= 8

    @pl.when((longest < most) & unroll)
    def _():
        for s in range(blocks if unroll else 0):
            sort_block(s, sorted_ref.at[s % 2])
            if s == 0:
                copy.wait()
            place_runs(s, sorted_ref.at[s % 2])

    @pl.when((longest >= most) | (not unroll))
    def _():
        copy.wait()

        def body(s, carry):
            sort_block(s, sorted_ref.at[0])
            place_runs(s, sorted_ref.at[0])
            place_rest(s, sorted_ref.at[0])
            return carry

        lax.fori_loop(0, blocks, body, 0)


def regroup(observations, sensor_ids, sensor_sigma, buckets, me, groups):
    rows, state = observations.shape
    sensors = sensor_sigma.shape[0]
    block = 256
    blocks = rows // block
    per_bucket = rows // groups
    padded = -(-(block + groups * 2 * (SUB - 1)) // 16) * 16
    far = pl.BlockSpec(memory_space=pltpu.HBM)
    return pl.pallas_call(
        functools.partial(regroup_kernel, groups, per_bucket),
        in_specs=[pl.BlockSpec(memory_space=pltpu.SMEM)] + [far] * 4,
        out_specs=[pl.BlockSpec(memory_space=pltpu.VMEM)] * groups,
        scratch_shapes=[
            pltpu.VMEM((rows // LANES, LANES), I32),
            pltpu.VMEM((rows // LANES, LANES), I32),
            pltpu.VMEM((1, sensors), F32),
            pltpu.VMEM((rows, state), F32),
            pltpu.VMEM((blocks, block), I32),
            pltpu.VMEM((blocks * groups, LANES), I32),
            pltpu.VMEM((2, padded, state), F32),
            pltpu.VMEM((sensors, LANES), F32),
            pltpu.SMEM((blocks * groups, LANES), I32),
            pltpu.SemaphoreType.DMA((4 + blocks,)),
        ],
        out_shape=[jax.ShapeDtypeStruct((per_bucket, state), F32)] * groups,
        compiler_params=pltpu.CompilerParams(vmem_limit_bytes=56 * MIB),
        cost_estimate=pl.CostEstimate(
            flops=4 * rows * padded * state, bytes_accessed=8 * rows * state, transcendentals=0
        ),
    )(
        me.reshape(1),
        buckets.reshape(rows // LANES, LANES),
        sensor_ids.reshape(rows // LANES, LANES),
        sensor_sigma.reshape(1, sensors),
        observations,
    )


def block_pairs(count):
    return [(i, j) for i in range(count) for j in range(i, count)]


def write_gram(both, state, out_ref):
    for n, (i, j) in enumerate(block_pairs(state // LANES)):
        a, b = i * LANES, j * LANES
        cross = both[a : a + LANES, state + b : state + b + LANES]
        turned = both[b : b + LANES, state + a : state + a + LANES]
        out_ref[n * LANES : (n + 1) * LANES, :] = both[a : a + LANES, b : b + LANES] + (
            cross + jnp.transpose(turned)
        )


def fetch_all(sources, held, sems):
    copies = []
    for n, source in enumerate(sources):
        copy = pltpu.make_async_copy(source, held.at[n], sems.at[n])
        copy.start()
        copies.append(copy)
    return copies


def gram_kernel(groups, prior_ref, *rest):
    chunks = rest[:groups]
    out_ref, prior_out_ref, both_ref, pair_ref, held, sems = rest[groups:]
    per_bucket, state = chunks[0].shape
    copies = fetch_all(chunks, held, sems)
    high, low = split(prior_ref[...])
    both_ref[...] = dot_rows(high, jnp.concatenate([high, low], axis=1))
    write_gram(both_ref, state, prior_out_ref)
    for k, copy in enumerate(copies):
        rows = slice(k * per_bucket, (k + 1) * per_bucket)
        copy.wait()
        high, low = split(held[k])
        pair_ref[rows, :state] = high
        pair_ref[rows, state:] = low
    both_ref[...] = dot_rows(pair_ref[:, :state], pair_ref[...])
    write_gram(both_ref, state, out_ref)


def gram(prior_factor, chunks):
    groups = len(chunks)
    per_bucket, state = chunks[0].shape
    rows = groups * per_bucket
    packed = len(block_pairs(state // LANES)) * LANES
    vmem = pl.BlockSpec(memory_space=pltpu.VMEM)
    return pl.pallas_call(
        functools.partial(gram_kernel, groups),
        in_specs=[vmem] + [pl.BlockSpec(memory_space=pl.ANY)] * groups,
        out_specs=[vmem] * 2,
        out_shape=[jax.ShapeDtypeStruct((packed, LANES), F32)] * 2,
        scratch_shapes=[
            pltpu.VMEM((state, 2 * state), F32),
            pltpu.VMEM((rows, 2 * state), BF16),
            pltpu.VMEM((groups, per_bucket, state), F32),
            pltpu.SemaphoreType.DMA((groups,)),
        ],
        compiler_params=pltpu.CompilerParams(vmem_limit_bytes=24 * MIB),
        cost_estimate=pl.CostEstimate(
            flops=4 * rows * state * state, bytes_accessed=4 * rows * state, transcendentals=0
        ),
    )(prior_factor, *chunks)


def scatter_sum(packed, count, groups):
    rows, lanes = packed.shape
    axes = ("rows", "grp")
    got = lax.all_to_all(packed, axes, split_axis=0, concat_axis=0, axis_index_groups=groups, tiled=True)
    return jnp.sum(got.reshape(count, rows // count, lanes), axis=0)


def gather_pieces(piece, count, groups):
    rows, lanes = piece.shape
    copies = jnp.broadcast_to(piece, (count, rows, lanes)).reshape(count * rows, lanes)
    axes = ("rows", "grp")
    return lax.all_to_all(copies, axes, split_axis=0, concat_axis=0, axis_index_groups=groups, tiled=True)


def sweep(a, w):
    width = a.shape[0]
    groups = width // SUB
    row_id = iota((SUB, LANES), 0)
    a_rows = [a[g * SUB : (g + 1) * SUB, :] for g in range(groups)]
    w_rows = [w[g * SUB : (g + 1) * SUB, :] for g in range(groups)]
    for g in range(groups):
        va, vw = a_rows[g], w_rows[g]
        cols = [
            jnp.broadcast_to(va[:, g * SUB + j : g * SUB + j + 1], (SUB, LANES)) for j in range(SUB)
        ]
        scale = jnp.zeros((SUB, LANES), F32)
        for j in range(SUB):
            pivot = jnp.broadcast_to(cols[j][j : j + 1, :], (SUB, LANES))
            root = lax.rsqrt(pivot)
            scale = jnp.where(row_id == j, root, scale)
            if j < SUB - 1:
                ratio = jnp.where(row_id > j, cols[j] * (root * root), 0.0)
                for k in range(j + 1, SUB):
                    cols[k] = cols[k] - ratio * cols[k][j : j + 1, :]
                va = va - ratio * va[j : j + 1, :]
                vw = vw - ratio * vw[j : j + 1, :]
        va, vw = va * scale, vw * scale
        va = jnp.where(iota((SUB, LANES), 1) >= row_id + g * SUB, va, 0.0)
        a_rows[g], w_rows[g] = va, vw
        if g < groups - 1:
            both = jnp.concatenate([va, vw], axis=1)
            high = both.astype(BF16).astype(F32)
            low = both - high
            left = jnp.concatenate([high[:, :LANES], high[:, :LANES], low[:, :LANES]], axis=0)
            right = jnp.concatenate([high, low, high], axis=0)
            change = dot_rows(left.astype(BF16), right.astype(BF16))
            for q in range(g + 1, groups):
                rows = slice(q * SUB, (q + 1) * SUB)
                a_rows[q] = a_rows[q] - change[rows, :LANES]
                w_rows[q] = w_rows[q] - change[rows, LANES:]
    return jnp.concatenate(a_rows, axis=0), jnp.concatenate(w_rows, axis=0)


def factor_kernel(inv_total, sum_ref, prior_ref, factor_ref, high_ref, low_ref, a_ref, x_ref):
    state = factor_ref.shape[0]
    count = state // LANES
    span = lambda i: slice(i * LANES, (i + 1) * LANES)
    for n, (i, j) in enumerate(block_pairs(count)):
        a_ref[span(i), span(j)] = prior_ref[span(n), :] + sum_ref[span(n), :] * inv_total
    factor_ref[...] = jnp.zeros((state, state), F32)
    x_ref[...] = jnp.zeros((state, state), F32)
    eye = (iota((LANES, LANES), 0) == iota((LANES, LANES), 1)).astype(F32)
    for k in range(count):
        r, w = sweep(a_ref[span(k), span(k)], eye)
        factor_ref[span(k), span(k)] = r
        x = jnp.transpose(w)
        x_ref[span(k), span(k)] = x
        if k > 0:
            left = dot3(x_ref[: k * LANES, : k * LANES], factor_ref[: k * LANES, span(k)])
            x_ref[: k * LANES, span(k)] = -dot3(left, x)
        if k < count - 1:
            rest = slice((k + 1) * LANES, state)
            right = dot3(w, a_ref[span(k), rest])
            factor_ref[span(k), rest] = right
            for i in range(k + 1, count):
                low = slice(i * LANES, state)
                at = (i - k - 1) * LANES
                a_ref[span(i), low] -= dot3_rows(right[:, at : at + LANES], right[:, at:])
    high, low = split(x_ref[...])
    high_ref[...] = high
    low_ref[...] = low


def factorise(summed, prior_gram, state, total_rows):
    vmem = pl.BlockSpec(memory_space=pltpu.VMEM)
    return pl.pallas_call(
        functools.partial(factor_kernel, 1.0 / total_rows),
        in_specs=[vmem] * 2,
        out_specs=[vmem] * 3,
        out_shape=[
            jax.ShapeDtypeStruct((state, state), F32),
            jax.ShapeDtypeStruct((state, state), BF16),
            jax.ShapeDtypeStruct((state, state), BF16),
        ],
        scratch_shapes=[pltpu.VMEM((state, state), F32)] * 2,
        compiler_params=pltpu.CompilerParams(vmem_limit_bytes=16 * MIB),
        cost_estimate=pl.CostEstimate(
            flops=1, bytes_accessed=1, transcendentals=0
        ),
    )(summed, prior_gram)


def whiten_kernel(steps, aliased, me_ref, high_ref, low_ref, *rest):
    count = len(steps)
    chunks = rest[:count]
    out_ref, held, given, sems, given_sems = rest[count + aliased :]
    per_bucket = chunks[0].shape[0]
    fetches = fetch_all(chunks, given, given_sems)
    copies = []
    for n, k in enumerate(steps):
        fetches[n].wait()
        rows_high, rows_low = split(given[n])
        high, low = high_ref[...], low_ref[...]
        held[n] = dot(rows_high, high) + (dot(rows_high, low) + dot(rows_low, high))
        slot = me_ref[0] ^ k
        copy = pltpu.make_async_copy(
            held.at[n],
            out_ref.at[pl.ds(pl.multiple_of(slot * per_bucket, per_bucket), per_bucket), :],
            sems.at[n],
        )
        copy.start()
        copies.append(copy)
    for copy in copies:
        copy.wait()


def whiten(me, high, low, steps, chunks, out, rows):
    per_bucket, state = chunks[0].shape
    count = len(chunks)
    vmem = pl.BlockSpec(memory_space=pltpu.VMEM)
    anywhere = pl.BlockSpec(memory_space=pl.ANY)
    extra = [] if out is None else [out]
    return pl.pallas_call(
        functools.partial(whiten_kernel, tuple(steps), len(extra)),
        in_specs=[pl.BlockSpec(memory_space=pltpu.SMEM), vmem, vmem]
        + [anywhere] * (count + len(extra)),
        out_specs=anywhere,
        out_shape=jax.ShapeDtypeStruct((rows, state), F32),
        scratch_shapes=[
            pltpu.VMEM((count, per_bucket, state), F32),
            pltpu.VMEM((count, per_bucket, state), F32),
            pltpu.SemaphoreType.DMA((count,)),
            pltpu.SemaphoreType.DMA((count,)),
        ],
        input_output_aliases={3 + count: 0} if extra else {},
        compiler_params=pltpu.CompilerParams(vmem_limit_bytes=16 * MIB),
        cost_estimate=pl.CostEstimate(flops=1, bytes_accessed=1, transcendentals=0),
    )(me.reshape(1), high, low, *chunks, *extra)


def behind(value, *arrays):
    return lax.optimization_barrier((value, *arrays))


def shards(observations, sensor_ids, sensor_sigma, buckets, prior_factor):
    rows_dev, state = observations.shape
    groups = lax.axis_size("rows")
    grp = lax.axis_size("grp")
    me = lax.axis_index("rows").astype(I32)
    total_rows = rows_dev * groups * grp
    chunks = regroup(observations, sensor_ids, sensor_sigma, buckets, me, groups)
    move = lambda k, chunk: lax.ppermute(chunk, "rows", [(i, i ^ k) for i in range(groups)])
    packed_rows = len(block_pairs(state // LANES)) * LANES
    plane = 2 * grp
    planes = [list(range(i, i + plane)) for i in range(0, groups * grp, plane)]
    early = [k for k in (1, 4) if k < groups]
    middle = [k for k in (2, 6) if k < groups]
    late = [k for k in (5, 3, *range(7, groups)) if k < groups and k not in early + middle]
    received = {0: chunks[0]}
    valid = prior_factor[0, 0] > 0
    nothing = lambda rows: jnp.full((rows, LANES), jnp.nan, F32)

    for k in early:
        received[k] = move(k, chunks[k])

    def first():
        packed, prior_gram = gram(prior_factor, chunks)
        return scatter_sum(packed, plane, planes), prior_gram

    piece, prior_gram = lax.cond(
        valid, first, lambda: (nothing(packed_rows // plane), nothing(packed_rows))
    )
    across = [piece]
    for step in range(1, groups // 2):
        across.append(move(2 * step, piece))
    while len(across) > 1:
        across = [across[i] + across[i + 1] for i in range(0, len(across), 2)]
    for k in middle:
        _, chunk = behind(across[0], chunks[k])
        received[k] = move(k, chunk)
    for k in early:
        across[0], received[k] = behind(across[0], received[k])
    summed = lax.cond(
        valid, lambda: gather_pieces(across[0], plane, planes), lambda: nothing(packed_rows)
    )
    for k in late:
        _, chunk = behind(summed, chunks[k])
        received[k] = move(k, chunk)
    factor, high, low = factorise(summed, prior_gram, state, total_rows)
    out = None
    for steps in ([0] + early + middle, late[:-1], late[-1:]):
        out = whiten(me, high, low, steps, [received[k] for k in steps], out, rows_dev)
    return (out, factor)


def solution(mesh):
    in_specs = (P(("rows", "grp"), None), P(("rows", "grp")), P(), P(("rows", "grp")), P())
    out_specs = (P(("rows", "grp"), None), P())
    return jax.shard_map(shards, mesh=mesh, in_specs=in_specs, out_specs=out_specs, check_vma=False)
```

```python
import functools

import jax
import jax.numpy as jnp
from jax import lax
from jax.experimental import pallas as pl
from jax.experimental.pallas import tpu as pltpu
from jax.sharding import PartitionSpec as P

F32 = jnp.float32
BF16 = jnp.bfloat16
I32 = jnp.int32
LANES = 128
SUB = 8
MIB = 1024 * 1024


def iota(shape, axis):
    return lax.broadcasted_iota(I32, shape, axis)


def split(values):
    high = values.astype(BF16)
    low = (values - high.astype(F32)).astype(BF16)
    return high, low


def dot(left, right):
    return jnp.dot(left, right, preferred_element_type=F32)


def dot_rows(left, right):
    return lax.dot_general(left, right, (((0,), (0,)), ((), ())), preferred_element_type=F32)


def dot3(left, right):
    lh, ll = split(left)
    rh, rl = split(right)
    return dot(lh, rh) + (dot(lh, rl) + dot(ll, rh))


def dot3_rows(left, right):
    lh, ll = split(left)
    rh, rl = split(right)
    return dot_rows(lh, rh) + (dot_rows(lh, rl) + dot_rows(ll, rh))


def rows_of(packed, count, wide):
    return [
        jnp.concatenate([packed[s * wide + i : s * wide + i + 1, :] for i in range(wide)], axis=1)
        for s in range(count)
    ]


def tile(t):
    return pl.ds(pl.multiple_of(t * SUB, SUB), SUB)


class Runs:
    def __init__(self, table, groups, per_bucket, state):
        self.table, self.groups = table, groups
        self.most = min(7, per_bucket // SUB + 1)
        self.sub_row = iota((SUB, state), 0)

    def get(self, s, v):
        return [self.table[s * self.groups + v, i] for i in range(4)]

    def place(self, s, v, out, source, base=None):
        kept, target, first, final = self.get(s, v)
        first = first if base is None else base
        old = out[tile(target), :]
        for t in reversed(range(1, self.most)):
            t = jnp.minimum(t, final)
            out[tile(target + t), :] = source[tile(first + t), :]
        out[tile(target), :] = jnp.where(self.sub_row < kept, old, source[tile(first), :])

    def place_rest(self, s, v, out, source):
        _, target, first, final = self.get(s, v)

        def longer(t, carry):
            out[tile(target + t), :] = source[tile(first + t), :]
            return carry

        lax.fori_loop(self.most, final + 1, longer, 0)


def lead_kernel(groups, per_bucket, lead, me_ref, *refs):
    given, (out, pair_ref, place_ref, meta_ref), scratch = refs[:4], refs[4:8], refs[8:]
    held, (sorted_ref, small_a, small_b, inv_ref, table, sems) = scratch[:4], scratch[4:]
    buckets_ref, ids_ref, sigma_ref, obs_ref = held
    blocks, block = place_ref.shape
    wide = block // LANES
    sensors = sigma_ref.shape[1]
    padded, state = sorted_ref.shape
    cells = blocks * groups
    last_tile = per_bucket // SUB - 1
    runs = Runs(table, groups, per_bucket, state)

    small = [pltpu.make_async_copy(given[i], held[i], sems.at[i]) for i in range(3)]
    for copy in small:
        copy.start()

    def fetch(s):
        rows = pl.ds(pl.multiple_of(s * block, block), block)
        return pltpu.make_async_copy(given[3].at[rows, :], obs_ref.at[rows, :], sems.at[4 + s])

    for s in range(blocks):
        fetch(s).start()
    for copy in small:
        copy.wait()

    inv_row = 1.0 / sigma_ref[...]
    inv_ref[...] = jnp.transpose(jnp.broadcast_to(inv_row, (LANES, sensors)))
    slots = rows_of(buckets_ref[...] ^ me_ref[0], blocks, wide)
    hits = jnp.concatenate(
        [jnp.broadcast_to(row, (groups, block)) == iota((groups, block), 0) for row in slots], axis=0
    )
    upto = (iota((block, block), 0) <= iota((block, block), 1)).astype(F32).astype(BF16)
    running = dot(hits.astype(F32).astype(BF16), upto)
    count = jnp.broadcast_to(running[:, block - 1 : block], (cells, LANES))
    row, col = iota((cells, cells), 0), iota((cells, cells), 1)
    shift = groups.bit_length() - 1
    earlier = ((row & (groups - 1)) == (col & (groups - 1))) & (col < row)
    before = dot(earlier.astype(F32).astype(BF16), count.astype(BF16)).astype(I32)
    odd = before & (SUB - 1)
    tiles = (odd + count.astype(I32) + (SUB - 1)) >> 3
    same = ((row >> shift) == (col >> shift)) & (col < row)
    first = dot(same.astype(F32).astype(BF16), tiles.astype(F32).astype(BF16)).astype(I32)
    lane = iota((cells, LANES), 1)
    kept = jnp.where(tiles > 0, odd, SUB)
    target = jnp.minimum(before >> 3, last_tile)
    final = jnp.maximum(tiles - 1, 0)
    meta = jnp.where(lane == 2, first, final)
    meta_ref[...] = jnp.where(lane == 0, kept, jnp.where(lane == 1, target, meta))
    copy = pltpu.make_async_copy(meta_ref, table, sems.at[3])
    copy.start()
    local = first * SUB + odd
    local = jnp.concatenate([local] * wide, axis=1)
    spot = jnp.where(hits, local + running.astype(I32) - 1, 0)
    place_ref[...] = jnp.concatenate(
        [jnp.sum(spot[s * groups : (s + 1) * groups], axis=0, keepdims=True) for s in range(blocks)],
        axis=0,
    )
    of_lead = (iota((cells, LANES), 0) & (groups - 1)) == lead
    longest = jnp.max(jnp.where(of_lead, final, 0))

    def scale_block(s):
        ids = [ids_ref[pl.ds(s * wide + i, 1), :] for i in range(wide)]
        known = iota((sensors, block), 0) == jnp.concatenate(ids, axis=1)
        inv = jnp.concatenate([inv_ref[...]] * wide, axis=1)
        scale_row = jnp.sum(jnp.where(known, inv, 0.0), axis=0, keepdims=True)
        scale = jnp.transpose(jnp.broadcast_to(scale_row, (LANES, block)))
        fetch(s).wait()
        rows = pl.ds(pl.multiple_of(s * block, block), block)
        high, low = split(obs_ref[rows, :] * jnp.concatenate([scale] * (state // LANES), axis=1))
        pair_ref[rows, :state] = high
        pair_ref[rows, state:] = low
        return high, low

    def moves(s, shape, base):
        spots = place_ref[pl.ds(s, 1), :] - base
        return (iota(shape, 0) == spots).astype(F32).astype(BF16)

    copy.wait()
    unroll = groups <= 8

    @pl.when((longest < runs.most) & unroll)
    def _():
        for s in range(blocks if unroll else 0):
            into = (small_a, small_b)[s % 2]
            high, low = scale_block(s)
            picked = moves(s, (into.shape[0], block), runs.get(s, lead)[2] * SUB)
            into[...] = dot(picked, high) + dot(picked, low)
            runs.place(s, lead, out, into, 0)

    @pl.when((longest >= runs.most) | (not unroll))
    def _():
        def body(s, carry):
            high, low = scale_block(s)
            picked = moves(s, (padded, block), 0)
            sorted_ref[...] = dot(picked, high) + dot(picked, low)
            runs.place(s, lead, out, sorted_ref)
            runs.place_rest(s, lead, out, sorted_ref)
            return carry

        lax.fori_loop(0, blocks, body, 0)


def rest_kernel(groups, per_bucket, others, table, place_ref, pair_ref, *refs):
    outs, (sorted_a, sorted_b) = refs[: len(others)], refs[len(others) :]
    blocks, block = place_ref.shape
    padded, state = sorted_a.shape
    runs = Runs(table, groups, per_bucket, state)

    def sort_block(s, into):
        picked = (iota((padded, block), 0) == place_ref[pl.ds(s, 1), :]).astype(F32).astype(BF16)
        rows = pl.ds(pl.multiple_of(s * block, block), block)
        both = dot(picked, pair_ref[rows, :])
        into[...] = both[:, :state] + both[:, state:]

    longest = 0
    for s in range(blocks):
        for v in range(groups):
            longest = jnp.maximum(longest, table[s * groups + v, 3])
    unroll = groups <= 8

    @pl.when((longest < runs.most) & unroll)
    def _():
        for s in range(blocks if unroll else 0):
            into = (sorted_a, sorted_b)[s % 2]
            sort_block(s, into)
            for v, out in zip(others, outs):
                runs.place(s, v, out, into)

    @pl.when((longest >= runs.most) | (not unroll))
    def _():
        def body(s, carry):
            sort_block(s, sorted_a)
            for v, out in zip(others, outs):
                runs.place(s, v, out, sorted_a)
                runs.place_rest(s, v, out, sorted_a)
            return carry

        lax.fori_loop(0, blocks, body, 0)


def sorted_rows(block, groups):
    return -(-(block + groups * 2 * (SUB - 1)) // 16) * 16


def regroup_lead(observations, sensor_ids, sensor_sigma, buckets, me, groups, lead):
    rows, state = observations.shape
    sensors = sensor_sigma.shape[0]
    block = 256
    blocks = rows // block
    cells = blocks * groups
    per_bucket = rows // groups
    far = pl.BlockSpec(memory_space=pltpu.HBM)
    return pl.pallas_call(
        functools.partial(lead_kernel, groups, per_bucket, lead),
        in_specs=[pl.BlockSpec(memory_space=pltpu.SMEM)] + [far] * 4,
        out_specs=[pl.BlockSpec(memory_space=pltpu.VMEM)] * 4,
        scratch_shapes=[
            pltpu.VMEM((rows // LANES, LANES), I32),
            pltpu.VMEM((rows // LANES, LANES), I32),
            pltpu.VMEM((1, sensors), F32),
            pltpu.VMEM((rows, state), F32),
            pltpu.VMEM((sorted_rows(block, groups), state), F32),
            pltpu.VMEM((64, state), F32),
            pltpu.VMEM((64, state), F32),
            pltpu.VMEM((sensors, LANES), F32),
            pltpu.SMEM((cells, LANES), I32),
            pltpu.SemaphoreType.DMA((4 + blocks,)),
        ],
        out_shape=[
            jax.ShapeDtypeStruct((per_bucket, state), F32),
            jax.ShapeDtypeStruct((rows, 2 * state), BF16),
            jax.ShapeDtypeStruct((blocks, block), I32),
            jax.ShapeDtypeStruct((cells, LANES), I32),
        ],
        compiler_params=pltpu.CompilerParams(vmem_limit_bytes=56 * MIB),
        cost_estimate=pl.CostEstimate(
            flops=rows * state, bytes_accessed=8 * rows * state, transcendentals=0
        ),
    )(
        me.reshape(1),
        buckets.reshape(rows // LANES, LANES),
        sensor_ids.reshape(rows // LANES, LANES),
        sensor_sigma.reshape(1, sensors),
        observations,
    )


def regroup_rest(table, place, pair, groups, others):
    rows, state = pair.shape[0], pair.shape[1] // 2
    per_bucket = rows // groups
    padded = sorted_rows(place.shape[1], groups)
    vmem = pl.BlockSpec(memory_space=pltpu.VMEM)
    return pl.pallas_call(
        functools.partial(rest_kernel, groups, per_bucket, tuple(others)),
        in_specs=[pl.BlockSpec(memory_space=pltpu.SMEM), vmem, vmem],
        out_specs=[vmem] * len(others),
        scratch_shapes=[pltpu.VMEM((padded, state), F32)] * 2,
        out_shape=[jax.ShapeDtypeStruct((per_bucket, state), F32)] * len(others),
        compiler_params=pltpu.CompilerParams(vmem_limit_bytes=24 * MIB),
        cost_estimate=pl.CostEstimate(
            flops=8 * rows * padded * state, bytes_accessed=8 * rows * state, transcendentals=0
        ),
    )(table, place, pair)


def block_pairs(count):
    return [(i, j) for i in range(count) for j in range(i, count)]


def write_gram(both, state, out_ref):
    for n, (i, j) in enumerate(block_pairs(state // LANES)):
        a, b = i * LANES, j * LANES
        cross = both[a : a + LANES, state + b : state + b + LANES]
        turned = both[b : b + LANES, state + a : state + a + LANES]
        out_ref[n * LANES : (n + 1) * LANES, :] = both[a : a + LANES, b : b + LANES] + (
            cross + jnp.transpose(turned)
        )


def gram_kernel(prior_ref, pair_ref, out_ref, prior_out_ref, both_ref):
    state = prior_ref.shape[0]
    both_ref[...] = dot_rows(pair_ref[:, :state], pair_ref[...])
    write_gram(both_ref, state, out_ref)
    high, low = split(prior_ref[...])
    both_ref[...] = dot_rows(high, jnp.concatenate([high, low], axis=1))
    write_gram(both_ref, state, prior_out_ref)


def gram(prior_factor, pair):
    rows, state = pair.shape[0], pair.shape[1] // 2
    packed = len(block_pairs(state // LANES)) * LANES
    vmem = pl.BlockSpec(memory_space=pltpu.VMEM)
    return pl.pallas_call(
        gram_kernel,
        in_specs=[vmem] * 2,
        out_specs=[vmem] * 2,
        out_shape=[jax.ShapeDtypeStruct((packed, LANES), F32)] * 2,
        scratch_shapes=[pltpu.VMEM((state, 2 * state), F32)],
        compiler_params=pltpu.CompilerParams(vmem_limit_bytes=24 * MIB),
        cost_estimate=pl.CostEstimate(
            flops=4 * rows * state * state, bytes_accessed=4 * rows * state, transcendentals=0
        ),
    )(prior_factor, pair)


def scatter_sum(packed, count, groups):
    rows, lanes = packed.shape
    axes = ("rows", "grp")
    got = lax.all_to_all(packed, axes, split_axis=0, concat_axis=0, axis_index_groups=groups, tiled=True)
    return jnp.sum(got.reshape(count, rows // count, lanes), axis=0)


def gather_pieces(piece, count, groups):
    rows, lanes = piece.shape
    copies = jnp.broadcast_to(piece, (count, rows, lanes)).reshape(count * rows, lanes)
    axes = ("rows", "grp")
    return lax.all_to_all(copies, axes, split_axis=0, concat_axis=0, axis_index_groups=groups, tiled=True)


def sweep(a, w):
    width = a.shape[0]
    groups = width // SUB
    row_id = iota((SUB, LANES), 0)
    a_rows = [a[g * SUB : (g + 1) * SUB, :] for g in range(groups)]
    w_rows = [w[g * SUB : (g + 1) * SUB, :] for g in range(groups)]
    for g in range(groups):
        va, vw = a_rows[g], w_rows[g]
        cols = [
            jnp.broadcast_to(va[:, g * SUB + j : g * SUB + j + 1], (SUB, LANES)) for j in range(SUB)
        ]
        scale = jnp.zeros((SUB, LANES), F32)
        for j in range(SUB):
            pivot = jnp.broadcast_to(cols[j][j : j + 1, :], (SUB, LANES))
            root = lax.rsqrt(pivot)
            scale = jnp.where(row_id == j, root, scale)
            if j < SUB - 1:
                ratio = jnp.where(row_id > j, cols[j] * (root * root), 0.0)
                for k in range(j + 1, SUB):
                    cols[k] = cols[k] - ratio * cols[k][j : j + 1, :]
                va = va - ratio * va[j : j + 1, :]
                vw = vw - ratio * vw[j : j + 1, :]
        va, vw = va * scale, vw * scale
        va = jnp.where(iota((SUB, LANES), 1) >= row_id + g * SUB, va, 0.0)
        a_rows[g], w_rows[g] = va, vw
        if g < groups - 1:
            both = jnp.concatenate([va, vw], axis=1)
            high = both.astype(BF16).astype(F32)
            low = both - high
            left = jnp.concatenate([high[:, :LANES], high[:, :LANES], low[:, :LANES]], axis=0)
            right = jnp.concatenate([high, low, high], axis=0)
            change = dot_rows(left.astype(BF16), right.astype(BF16))
            for q in range(g + 1, groups):
                rows = slice(q * SUB, (q + 1) * SUB)
                a_rows[q] = a_rows[q] - change[rows, :LANES]
                w_rows[q] = w_rows[q] - change[rows, LANES:]
    return jnp.concatenate(a_rows, axis=0), jnp.concatenate(w_rows, axis=0)


def factor_kernel(inv_total, sum_ref, prior_ref, factor_ref, high_ref, low_ref, a_ref, x_ref):
    state = factor_ref.shape[0]
    count = state // LANES
    span = lambda i: slice(i * LANES, (i + 1) * LANES)
    for n, (i, j) in enumerate(block_pairs(count)):
        a_ref[span(i), span(j)] = prior_ref[span(n), :] + sum_ref[span(n), :] * inv_total
    factor_ref[...] = jnp.zeros((state, state), F32)
    x_ref[...] = jnp.zeros((state, state), F32)
    eye = (iota((LANES, LANES), 0) == iota((LANES, LANES), 1)).astype(F32)
    for k in range(count):
        r, w = sweep(a_ref[span(k), span(k)], eye)
        factor_ref[span(k), span(k)] = r
        x = jnp.transpose(w)
        x_ref[span(k), span(k)] = x
        if k > 0:
            left = dot3(x_ref[: k * LANES, : k * LANES], factor_ref[: k * LANES, span(k)])
            x_ref[: k * LANES, span(k)] = -dot3(left, x)
        if k < count - 1:
            rest = slice((k + 1) * LANES, state)
            right = dot3(w, a_ref[span(k), rest])
            factor_ref[span(k), rest] = right
            for i in range(k + 1, count):
                low = slice(i * LANES, state)
                at = (i - k - 1) * LANES
                a_ref[span(i), low] -= dot3_rows(right[:, at : at + LANES], right[:, at:])
    high, low = split(x_ref[...])
    high_ref[...] = high
    low_ref[...] = low


def factorise(summed, prior_gram, state, total_rows):
    vmem = pl.BlockSpec(memory_space=pltpu.VMEM)
    return pl.pallas_call(
        functools.partial(factor_kernel, 1.0 / total_rows),
        in_specs=[vmem] * 2,
        out_specs=[vmem] * 3,
        out_shape=[
            jax.ShapeDtypeStruct((state, state), F32),
            jax.ShapeDtypeStruct((state, state), BF16),
            jax.ShapeDtypeStruct((state, state), BF16),
        ],
        scratch_shapes=[pltpu.VMEM((state, state), F32)] * 2,
        compiler_params=pltpu.CompilerParams(vmem_limit_bytes=16 * MIB),
        cost_estimate=pl.CostEstimate(
            flops=1, bytes_accessed=1, transcendentals=0
        ),
    )(summed, prior_gram)


def whiten_kernel(steps, aliased, me_ref, high_ref, low_ref, *rest):
    count = len(steps)
    chunks = rest[:count]
    out_ref, held, sems = rest[count + aliased :]
    per_bucket = chunks[0].shape[0]
    high, low = high_ref[...], low_ref[...]
    copies = []
    for n, k in enumerate(steps):
        rows_high, rows_low = split(chunks[n][...])
        held[n] = dot(rows_high, high) + (dot(rows_high, low) + dot(rows_low, high))
        slot = me_ref[0] ^ k
        copy = pltpu.make_async_copy(
            held.at[n],
            out_ref.at[pl.ds(pl.multiple_of(slot * per_bucket, per_bucket), per_bucket), :],
            sems.at[n],
        )
        copy.start()
        copies.append(copy)
    for copy in copies:
        copy.wait()


def whiten(me, high, low, steps, chunks, out, rows):
    per_bucket, state = chunks[0].shape
    count = len(chunks)
    vmem = pl.BlockSpec(memory_space=pltpu.VMEM)
    anywhere = pl.BlockSpec(memory_space=pl.ANY)
    extra = [] if out is None else [out]
    return pl.pallas_call(
        functools.partial(whiten_kernel, tuple(steps), len(extra)),
        in_specs=[pl.BlockSpec(memory_space=pltpu.SMEM)]
        + [vmem] * (2 + count)
        + [anywhere] * len(extra),
        out_specs=anywhere,
        out_shape=jax.ShapeDtypeStruct((rows, state), F32),
        scratch_shapes=[
            pltpu.VMEM((count, per_bucket, state), F32),
            pltpu.SemaphoreType.DMA((count,)),
        ],
        input_output_aliases={3 + count: 0} if extra else {},
        compiler_params=pltpu.CompilerParams(vmem_limit_bytes=16 * MIB),
        cost_estimate=pl.CostEstimate(
            flops=1, bytes_accessed=1, transcendentals=0
        ),
    )(me.reshape(1), high, low, *chunks, *extra)


def behind(value, *arrays):
    return lax.optimization_barrier((value, *arrays))


def shards(observations, sensor_ids, sensor_sigma, buckets, prior_factor):
    rows_dev, state = observations.shape
    groups = lax.axis_size("rows")
    grp = lax.axis_size("grp")
    me = lax.axis_index("rows").astype(I32)
    total_rows = rows_dev * groups * grp
    lead = 4 if groups > 4 else 0
    others = [k for k in range(groups) if k != lead]
    chunk, pair, place, table = regroup_lead(
        observations, sensor_ids, sensor_sigma, buckets, me, groups, lead
    )
    move = lambda k, chunk: lax.ppermute(chunk, "rows", [(i, i ^ k) for i in range(groups)])
    received = {lead: move(lead, chunk) if lead else chunk}
    packed_rows = len(block_pairs(state // LANES)) * LANES
    plane = 2 * grp
    planes = [list(range(i, i + plane)) for i in range(0, groups * grp, plane)]
    side = [k for k in (1,) if k < groups]
    middle = [k for k in (2, 6) if k < groups]
    late = [k for k in (5, 3, *range(7, groups)) if k < groups]
    valid = prior_factor[0, 0] > 0
    nothing = lambda rows: jnp.full((rows, LANES), jnp.nan, F32)

    def first():
        packed, prior_gram = gram(prior_factor, pair)
        rest = list(regroup_rest(table, place, pair, groups, others))
        return scatter_sum(packed, plane, planes), prior_gram, rest

    def wrong():
        return nothing(packed_rows // plane), nothing(packed_rows), [chunk] * len(others)

    piece, prior_gram, rest = lax.cond(valid, first, wrong)
    chunks = {**dict(zip(others, rest)), lead: chunk}
    if lead:
        received[0] = chunks[0]
    across = [piece]
    for step in range(1, groups // 2):
        across.append(move(2 * step, piece))
    for k in side:
        received[k] = move(k, chunks[k])
    while len(across) > 1:
        across = [across[i] + across[i + 1] for i in range(0, len(across), 2)]
    for k in middle:
        _, chunk = behind(across[0], chunks[k])
        received[k] = move(k, chunk)
    across[0], received[lead] = behind(across[0], received[lead])
    summed = lax.cond(
        valid, lambda: gather_pieces(across[0], plane, planes), lambda: nothing(packed_rows)
    )
    for k in side:
        summed, received[k] = behind(summed, received[k])
    for k in late:
        _, chunk = behind(summed, chunks[k])
        received[k] = move(k, chunk)
    factor, high, low = factorise(summed, prior_gram, state, total_rows)
    out = None
    soon = sorted({0, lead, *side, *middle})
    for steps in (soon, late[:-1], late[-1:]):
        if not steps:
            continue
        out = whiten(me, high, low, steps, [received[k] for k in steps], out, rows_dev)
    return (out, factor)


def solution(mesh):
    in_specs = (P(("rows", "grp"), None), P(("rows", "grp")), P(), P(("rows", "grp")), P())
    out_specs = (P(("rows", "grp"), None), P())
    return jax.shard_map(shards, mesh=mesh, in_specs=in_specs, out_specs=out_specs, check_vma=False)
```

```python
import functools

import jax
import jax.numpy as jnp
from jax import lax
from jax.experimental import pallas as pl
from jax.experimental.pallas import tpu as pltpu
from jax.sharding import PartitionSpec as P

F32 = jnp.float32
BF16 = jnp.bfloat16
I32 = jnp.int32
LANES = 128
SUB = 8
MIB = 1024 * 1024


def iota(shape, axis):
    return lax.broadcasted_iota(I32, shape, axis)


def split(values):
    high = values.astype(BF16)
    low = (values - high.astype(F32)).astype(BF16)
    return high, low


def dot(left, right):
    return jnp.dot(left, right, preferred_element_type=F32)


def dot_rows(left, right):
    return lax.dot_general(left, right, (((0,), (0,)), ((), ())), preferred_element_type=F32)


def dot3(left, right):
    lh, ll = split(left)
    rh, rl = split(right)
    return dot(lh, rh) + (dot(lh, rl) + dot(ll, rh))


def dot3_rows(left, right):
    lh, ll = split(left)
    rh, rl = split(right)
    return dot_rows(lh, rh) + (dot_rows(lh, rl) + dot_rows(ll, rh))


def rows_of(packed, count, wide):
    return [
        jnp.concatenate([packed[s * wide + i : s * wide + i + 1, :] for i in range(wide)], axis=1)
        for s in range(count)
    ]


def tile(t):
    return pl.ds(pl.multiple_of(t * SUB, SUB), SUB)


class Runs:
    def __init__(self, table, groups, per_bucket, state):
        self.table, self.groups = table, groups
        self.most = min(7, per_bucket // SUB + 1)
        self.sub_row = iota((SUB, state), 0)

    def get(self, s, v):
        return [self.table[s * self.groups + v, i] for i in range(4)]

    def place(self, s, v, out, source, base=None):
        kept, target, first, final = self.get(s, v)
        first = first if base is None else base
        old = out[tile(target), :]
        for t in reversed(range(1, self.most)):
            t = jnp.minimum(t, final)
            out[tile(target + t), :] = source[tile(first + t), :]
        out[tile(target), :] = jnp.where(self.sub_row < kept, old, source[tile(first), :])

    def place_rest(self, s, v, out, source):
        _, target, first, final = self.get(s, v)

        def longer(t, carry):
            out[tile(target + t), :] = source[tile(first + t), :]
            return carry

        lax.fori_loop(self.most, final + 1, longer, 0)


def lead_kernel(groups, per_bucket, leads, me_ref, *refs):
    given, outs, refs = refs[:4], refs[4 : 4 + len(leads)], refs[4 + len(leads) :]
    (pair_ref, place_ref, meta_ref), held, scratch = refs[:3], refs[3:7], refs[7:]
    sorted_ref, small_a, small_b, inv_ref, table, sems = scratch
    buckets_ref, ids_ref, sigma_ref, obs_ref = held
    blocks, block = place_ref.shape
    wide = block // LANES
    sensors = sigma_ref.shape[1]
    padded, state = sorted_ref.shape
    cells = blocks * groups
    last_tile = per_bucket // SUB - 1
    runs = Runs(table, groups, per_bucket, state)

    small = [pltpu.make_async_copy(given[i], held[i], sems.at[i]) for i in range(3)]
    for copy in small:
        copy.start()

    def fetch(s):
        rows = pl.ds(pl.multiple_of(s * block, block), block)
        return pltpu.make_async_copy(given[3].at[rows, :], obs_ref.at[rows, :], sems.at[4 + s])

    for s in range(blocks):
        fetch(s).start()
    for copy in small:
        copy.wait()

    inv_row = 1.0 / sigma_ref[...]
    inv_ref[...] = jnp.transpose(jnp.broadcast_to(inv_row, (LANES, sensors)))
    slots = rows_of(buckets_ref[...] ^ me_ref[0], blocks, wide)
    hits = jnp.concatenate(
        [jnp.broadcast_to(row, (groups, block)) == iota((groups, block), 0) for row in slots], axis=0
    )
    upto = (iota((block, block), 0) <= iota((block, block), 1)).astype(F32).astype(BF16)
    running = dot(hits.astype(F32).astype(BF16), upto)
    count = jnp.broadcast_to(running[:, block - 1 : block], (cells, LANES))
    row, col = iota((cells, cells), 0), iota((cells, cells), 1)
    shift = groups.bit_length() - 1
    earlier = ((row & (groups - 1)) == (col & (groups - 1))) & (col < row)
    before = dot(earlier.astype(F32).astype(BF16), count.astype(BF16)).astype(I32)
    odd = before & (SUB - 1)
    tiles = (odd + count.astype(I32) + (SUB - 1)) >> 3
    same = ((row >> shift) == (col >> shift)) & (col < row)
    first = dot(same.astype(F32).astype(BF16), tiles.astype(F32).astype(BF16)).astype(I32)
    lane = iota((cells, LANES), 1)
    kept = jnp.where(tiles > 0, odd, SUB)
    target = jnp.minimum(before >> 3, last_tile)
    final = jnp.maximum(tiles - 1, 0)
    meta = jnp.where(lane == 2, first, final)
    meta_ref[...] = jnp.where(lane == 0, kept, jnp.where(lane == 1, target, meta))
    copy = pltpu.make_async_copy(meta_ref, table, sems.at[3])
    copy.start()
    local = first * SUB + odd
    local = jnp.concatenate([local] * wide, axis=1)
    spot = jnp.where(hits, local + running.astype(I32) - 1, 0)
    place_ref[...] = jnp.concatenate(
        [jnp.sum(spot[s * groups : (s + 1) * groups], axis=0, keepdims=True) for s in range(blocks)],
        axis=0,
    )
    slot = iota((cells, LANES), 0) & (groups - 1)
    of_lead = functools.reduce(jnp.logical_or, [slot == v for v in leads])
    longest = jnp.max(jnp.where(of_lead, final, 0))
    inv = jnp.concatenate([inv_ref[...]] * wide, axis=1)
    block_rows = lambda s: pl.ds(pl.multiple_of(s * block, block), block)

    for s in range(blocks):
        ids = [ids_ref[s * wide + i : s * wide + i + 1, :] for i in range(wide)]
        known = iota((sensors, block), 0) == jnp.concatenate(ids, axis=1)
        scale_row = jnp.sum(jnp.where(known, inv, 0.0), axis=0, keepdims=True)
        scale = jnp.transpose(jnp.broadcast_to(scale_row, (LANES, block)))
        fetch(s).wait()
        rows = block_rows(s)
        high, low = split(obs_ref[rows, :] * jnp.concatenate([scale] * (state // LANES), axis=1))
        pair_ref[rows, :state] = high
        pair_ref[rows, state:] = low

    def sort_block(s, into, base):
        spots = place_ref[pl.ds(s, 1), :] - base
        picked = (iota((into.shape[0], block), 0) == spots).astype(F32).astype(BF16)
        both = dot(picked, pair_ref[block_rows(s), :])
        into[...] = both[:, :state] + both[:, state:]

    copy.wait()
    unroll = groups <= 8

    @pl.when((longest < runs.most) & unroll)
    def _():
        for s in range(blocks if unroll else 0):
            for n, v in enumerate(leads):
                into = (small_a, small_b)[(s * len(leads) + n) % 2]
                sort_block(s, into, runs.get(s, v)[2] * SUB)
                runs.place(s, v, outs[n], into, 0)

    @pl.when((longest >= runs.most) | (not unroll))
    def _():
        def body(s, carry):
            sort_block(s, sorted_ref, 0)
            for v, out in zip(leads, outs):
                runs.place(s, v, out, sorted_ref)
                runs.place_rest(s, v, out, sorted_ref)
            return carry

        lax.fori_loop(0, blocks, body, 0)


def rest_kernel(groups, per_bucket, others, table, place_ref, pair_ref, *refs):
    outs, (sorted_a, sorted_b) = refs[: len(others)], refs[len(others) :]
    blocks, block = place_ref.shape
    padded, state = sorted_a.shape
    runs = Runs(table, groups, per_bucket, state)

    def sort_block(s, into):
        picked = (iota((padded, block), 0) == place_ref[pl.ds(s, 1), :]).astype(F32).astype(BF16)
        rows = pl.ds(pl.multiple_of(s * block, block), block)
        both = dot(picked, pair_ref[rows, :])
        into[...] = both[:, :state] + both[:, state:]

    longest = 0
    for s in range(blocks):
        for v in range(groups):
            longest = jnp.maximum(longest, table[s * groups + v, 3])
    unroll = groups <= 8

    @pl.when((longest < runs.most) & unroll)
    def _():
        for s in range(blocks if unroll else 0):
            into = (sorted_a, sorted_b)[s % 2]
            sort_block(s, into)
            for v, out in zip(others, outs):
                runs.place(s, v, out, into)

    @pl.when((longest >= runs.most) | (not unroll))
    def _():
        def body(s, carry):
            sort_block(s, sorted_a)
            for v, out in zip(others, outs):
                runs.place(s, v, out, sorted_a)
                runs.place_rest(s, v, out, sorted_a)
            return carry

        lax.fori_loop(0, blocks, body, 0)


def sorted_rows(block, groups):
    return -(-(block + groups * 2 * (SUB - 1)) // 16) * 16


def regroup_lead(observations, sensor_ids, sensor_sigma, buckets, me, groups, leads):
    rows, state = observations.shape
    sensors = sensor_sigma.shape[0]
    block = 256
    blocks = rows // block
    cells = blocks * groups
    per_bucket = rows // groups
    far = pl.BlockSpec(memory_space=pltpu.HBM)
    return pl.pallas_call(
        functools.partial(lead_kernel, groups, per_bucket, tuple(leads)),
        in_specs=[pl.BlockSpec(memory_space=pltpu.SMEM)] + [far] * 4,
        out_specs=[pl.BlockSpec(memory_space=pltpu.VMEM)] * (len(leads) + 3),
        scratch_shapes=[
            pltpu.VMEM((rows // LANES, LANES), I32),
            pltpu.VMEM((rows // LANES, LANES), I32),
            pltpu.VMEM((1, sensors), F32),
            pltpu.VMEM((rows, state), F32),
            pltpu.VMEM((sorted_rows(block, groups), state), F32),
            pltpu.VMEM((64, state), F32),
            pltpu.VMEM((64, state), F32),
            pltpu.VMEM((sensors, LANES), F32),
            pltpu.SMEM((cells, LANES), I32),
            pltpu.SemaphoreType.DMA((4 + blocks,)),
        ],
        out_shape=[jax.ShapeDtypeStruct((per_bucket, state), F32)] * len(leads)
        + [
            jax.ShapeDtypeStruct((rows, 2 * state), BF16),
            jax.ShapeDtypeStruct((blocks, block), I32),
            jax.ShapeDtypeStruct((cells, LANES), I32),
        ],
        compiler_params=pltpu.CompilerParams(vmem_limit_bytes=56 * MIB),
        cost_estimate=pl.CostEstimate(
            flops=rows * state, bytes_accessed=8 * rows * state, transcendentals=0
        ),
    )(
        me.reshape(1),
        buckets.reshape(rows // LANES, LANES),
        sensor_ids.reshape(rows // LANES, LANES),
        sensor_sigma.reshape(1, sensors),
        observations,
    )


def regroup_rest(table, place, pair, groups, others):
    rows, state = pair.shape[0], pair.shape[1] // 2
    per_bucket = rows // groups
    padded = sorted_rows(place.shape[1], groups)
    vmem = pl.BlockSpec(memory_space=pltpu.VMEM)
    return pl.pallas_call(
        functools.partial(rest_kernel, groups, per_bucket, tuple(others)),
        in_specs=[pl.BlockSpec(memory_space=pltpu.SMEM), vmem, vmem],
        out_specs=[vmem] * len(others),
        scratch_shapes=[pltpu.VMEM((padded, state), F32)] * 2,
        out_shape=[jax.ShapeDtypeStruct((per_bucket, state), F32)] * len(others),
        compiler_params=pltpu.CompilerParams(vmem_limit_bytes=14 * MIB),
        cost_estimate=pl.CostEstimate(
            flops=8 * rows * padded * state, bytes_accessed=8 * rows * state, transcendentals=0
        ),
    )(table, place, pair)


def block_pairs(count):
    return [(i, j) for i in range(count) for j in range(i, count)]


def write_gram(both, state, out_ref):
    for n, (i, j) in enumerate(block_pairs(state // LANES)):
        a, b = i * LANES, j * LANES
        cross = both[a : a + LANES, state + b : state + b + LANES]
        turned = both[b : b + LANES, state + a : state + a + LANES]
        out_ref[n * LANES : (n + 1) * LANES, :] = both[a : a + LANES, b : b + LANES] + (
            cross + jnp.transpose(turned)
        )


def gram_kernel(prior_ref, pair_ref, out_ref, prior_out_ref, both_ref):
    state = prior_ref.shape[0]
    both_ref[...] = dot_rows(pair_ref[:, :state], pair_ref[...])
    write_gram(both_ref, state, out_ref)
    high, low = split(prior_ref[...])
    both_ref[...] = dot_rows(high, jnp.concatenate([high, low], axis=1))
    write_gram(both_ref, state, prior_out_ref)


def gram(prior_factor, pair):
    rows, state = pair.shape[0], pair.shape[1] // 2
    packed = len(block_pairs(state // LANES)) * LANES
    vmem = pl.BlockSpec(memory_space=pltpu.VMEM)
    return pl.pallas_call(
        gram_kernel,
        in_specs=[vmem] * 2,
        out_specs=[vmem] * 2,
        out_shape=[jax.ShapeDtypeStruct((packed, LANES), F32)] * 2,
        scratch_shapes=[pltpu.VMEM((state, 2 * state), F32)],
        compiler_params=pltpu.CompilerParams(vmem_limit_bytes=10 * MIB),
        cost_estimate=pl.CostEstimate(
            flops=4 * rows * state * state, bytes_accessed=4 * rows * state, transcendentals=0
        ),
    )(prior_factor, pair)


def scatter_sum(packed, count, groups):
    rows, lanes = packed.shape
    axes = ("rows", "grp")
    got = lax.all_to_all(packed, axes, split_axis=0, concat_axis=0, axis_index_groups=groups, tiled=True)
    return jnp.sum(got.reshape(count, rows // count, lanes), axis=0)


def gather_pieces(piece, count, groups):
    rows, lanes = piece.shape
    copies = jnp.broadcast_to(piece, (count, rows, lanes)).reshape(count * rows, lanes)
    axes = ("rows", "grp")
    return lax.all_to_all(copies, axes, split_axis=0, concat_axis=0, axis_index_groups=groups, tiled=True)


def sweep(a, w):
    width = a.shape[0]
    groups = width // SUB
    row_id = iota((SUB, LANES), 0)
    a_rows = [a[g * SUB : (g + 1) * SUB, :] for g in range(groups)]
    w_rows = [w[g * SUB : (g + 1) * SUB, :] for g in range(groups)]
    for g in range(groups):
        va, vw = a_rows[g], w_rows[g]
        cols = [
            jnp.broadcast_to(va[:, g * SUB + j : g * SUB + j + 1], (SUB, LANES)) for j in range(SUB)
        ]
        scale = jnp.zeros((SUB, LANES), F32)
        for j in range(SUB):
            pivot = jnp.broadcast_to(cols[j][j : j + 1, :], (SUB, LANES))
            root = lax.rsqrt(pivot)
            scale = jnp.where(row_id == j, root, scale)
            if j < SUB - 1:
                ratio = jnp.where(row_id > j, cols[j] * (root * root), 0.0)
                for k in range(j + 1, SUB):
                    cols[k] = cols[k] - ratio * cols[k][j : j + 1, :]
                va = va - ratio * va[j : j + 1, :]
                vw = vw - ratio * vw[j : j + 1, :]
        va, vw = va * scale, vw * scale
        va = jnp.where(iota((SUB, LANES), 1) >= row_id + g * SUB, va, 0.0)
        a_rows[g], w_rows[g] = va, vw
        if g < groups - 1:
            both = jnp.concatenate([va, vw], axis=1)
            high = both.astype(BF16).astype(F32)
            low = both - high
            left = jnp.concatenate([high[:, :LANES], high[:, :LANES], low[:, :LANES]], axis=0)
            right = jnp.concatenate([high, low, high], axis=0)
            change = dot_rows(left.astype(BF16), right.astype(BF16))
            for q in range(g + 1, groups):
                rows = slice(q * SUB, (q + 1) * SUB)
                a_rows[q] = a_rows[q] - change[rows, :LANES]
                w_rows[q] = w_rows[q] - change[rows, LANES:]
    return jnp.concatenate(a_rows, axis=0), jnp.concatenate(w_rows, axis=0)


def factor_kernel(inv_total, sum_ref, prior_ref, factor_ref, high_ref, low_ref, a_ref, x_ref):
    state = factor_ref.shape[0]
    count = state // LANES
    span = lambda i: slice(i * LANES, (i + 1) * LANES)
    for n, (i, j) in enumerate(block_pairs(count)):
        a_ref[span(i), span(j)] = prior_ref[span(n), :] + sum_ref[span(n), :] * inv_total
    factor_ref[...] = jnp.zeros((state, state), F32)
    x_ref[...] = jnp.zeros((state, state), F32)
    eye = (iota((LANES, LANES), 0) == iota((LANES, LANES), 1)).astype(F32)
    for k in range(count):
        r, w = sweep(a_ref[span(k), span(k)], eye)
        factor_ref[span(k), span(k)] = r
        x = jnp.transpose(w)
        x_ref[span(k), span(k)] = x
        if k > 0:
            left = dot3(x_ref[: k * LANES, : k * LANES], factor_ref[: k * LANES, span(k)])
            x_ref[: k * LANES, span(k)] = -dot3(left, x)
        if k < count - 1:
            rest = slice((k + 1) * LANES, state)
            right = dot3(w, a_ref[span(k), rest])
            factor_ref[span(k), rest] = right
            for i in range(k + 1, count):
                low = slice(i * LANES, state)
                at = (i - k - 1) * LANES
                a_ref[span(i), low] -= dot3_rows(right[:, at : at + LANES], right[:, at:])
    high, low = split(x_ref[...])
    high_ref[...] = high
    low_ref[...] = low


def factorise(summed, prior_gram, state, total_rows):
    vmem = pl.BlockSpec(memory_space=pltpu.VMEM)
    return pl.pallas_call(
        functools.partial(factor_kernel, 1.0 / total_rows),
        in_specs=[vmem] * 2,
        out_specs=[vmem] * 3,
        out_shape=[
            jax.ShapeDtypeStruct((state, state), F32),
            jax.ShapeDtypeStruct((state, state), BF16),
            jax.ShapeDtypeStruct((state, state), BF16),
        ],
        scratch_shapes=[pltpu.VMEM((state, state), F32)] * 2,
        compiler_params=pltpu.CompilerParams(vmem_limit_bytes=16 * MIB),
        cost_estimate=pl.CostEstimate(
            flops=1, bytes_accessed=1, transcendentals=0
        ),
    )(summed, prior_gram)


def whiten_kernel(steps, aliased, me_ref, high_ref, low_ref, *rest):
    count = len(steps)
    chunks = rest[:count]
    out_ref, held, sems = rest[count + aliased :]
    per_bucket = chunks[0].shape[0]
    high, low = high_ref[...], low_ref[...]
    copies = []
    for n, k in enumerate(steps):
        rows_high, rows_low = split(chunks[n][...])
        held[n] = dot(rows_high, high) + (dot(rows_high, low) + dot(rows_low, high))
        slot = me_ref[0] ^ k
        copy = pltpu.make_async_copy(
            held.at[n],
            out_ref.at[pl.ds(pl.multiple_of(slot * per_bucket, per_bucket), per_bucket), :],
            sems.at[n],
        )
        copy.start()
        copies.append(copy)
    for copy in copies:
        copy.wait()


def whiten(me, high, low, steps, chunks, out, rows):
    per_bucket, state = chunks[0].shape
    count = len(chunks)
    vmem = pl.BlockSpec(memory_space=pltpu.VMEM)
    anywhere = pl.BlockSpec(memory_space=pl.ANY)
    extra = [] if out is None else [out]
    return pl.pallas_call(
        functools.partial(whiten_kernel, tuple(steps), len(extra)),
        in_specs=[pl.BlockSpec(memory_space=pltpu.SMEM)]
        + [vmem] * (2 + count)
        + [anywhere] * len(extra),
        out_specs=anywhere,
        out_shape=jax.ShapeDtypeStruct((rows, state), F32),
        scratch_shapes=[
            pltpu.VMEM((count, per_bucket, state), F32),
            pltpu.SemaphoreType.DMA((count,)),
        ],
        input_output_aliases={3 + count: 0} if extra else {},
        compiler_params=pltpu.CompilerParams(vmem_limit_bytes=16 * MIB),
        cost_estimate=pl.CostEstimate(
            flops=1, bytes_accessed=1, transcendentals=0
        ),
    )(me.reshape(1), high, low, *chunks, *extra)


def behind(value, *arrays):
    return lax.optimization_barrier((value, *arrays))


def shards(observations, sensor_ids, sensor_sigma, buckets, prior_factor):
    rows_dev, state = observations.shape
    groups = lax.axis_size("rows")
    grp = lax.axis_size("grp")
    me = lax.axis_index("rows").astype(I32)
    total_rows = rows_dev * groups * grp
    leads = [k for k in (4, 1) if k < groups]
    others = [k for k in range(groups) if k not in leads]
    *chunks, pair, place, table = regroup_lead(
        observations, sensor_ids, sensor_sigma, buckets, me, groups, leads
    )
    move = lambda k, chunk: lax.ppermute(chunk, "rows", [(i, i ^ k) for i in range(groups)])
    received = {k: move(k, chunk) for k, chunk in zip(leads, chunks)}
    packed_rows = len(block_pairs(state // LANES)) * LANES
    plane = 2 * grp
    planes = [list(range(i, i + plane)) for i in range(0, groups * grp, plane)]
    middle = [k for k in (2, 6) if k < groups]
    late = [k for k in (5, 3, *range(7, groups)) if k < groups]
    valid = sensor_sigma[0] > 0
    nothing = lambda rows: jnp.full((rows, LANES), jnp.nan, F32)

    def first():
        packed, prior_gram = gram(prior_factor, pair)
        rest = list(regroup_rest(table, place, pair, groups, others))
        return scatter_sum(packed, plane, planes), prior_gram, rest

    def wrong():
        return nothing(packed_rows // plane), nothing(packed_rows), [chunks[0]] * len(others)

    piece, prior_gram, rest = lax.cond(valid, first, wrong)
    rest = dict(zip(others, rest))
    received[0] = rest[0]
    for k in leads[1:]:
        piece, received[k] = behind(piece, received[k])
    across = [piece]
    for step in range(1, groups // 2):
        across.append(move(2 * step, piece))
    for k in middle[:1]:
        received[k] = move(k, behind(piece, rest[k])[1])
    while len(across) > 1:
        across = [across[i] + across[i + 1] for i in range(0, len(across), 2)]
    for k in middle[1:]:
        received[leads[0]], chunk = behind(received[leads[0]], rest[k])
        received[k] = move(k, chunk)
    across[0], received[leads[0]] = behind(across[0], received[leads[0]])
    summed = lax.cond(
        valid, lambda: gather_pieces(across[0], plane, planes), lambda: nothing(packed_rows)
    )
    for k in late:
        received[k] = move(k, behind(summed, rest[k])[1])
    factor, high, low = factorise(summed, prior_gram, state, total_rows)
    out = None
    soon = [0, *leads, *middle]
    for steps in (soon, late[:-1], late[-1:]):
        if not steps:
            continue
        out = whiten(me, high, low, steps, [received[k] for k in steps], out, rows_dev)
    return (out, factor)


def solution(mesh):
    in_specs = (P(("rows", "grp"), None), P(("rows", "grp")), P(), P(("rows", "grp")), P())
    out_specs = (P(("rows", "grp"), None), P())
    return jax.shard_map(shards, mesh=mesh, in_specs=in_specs, out_specs=out_specs, check_vma=False)
```

```python
import functools

import jax
import jax.numpy as jnp
from jax import lax
from jax.experimental import pallas as pl
from jax.experimental.pallas import tpu as pltpu
from jax.sharding import PartitionSpec as P

F32 = jnp.float32
BF16 = jnp.bfloat16
I32 = jnp.int32
LANES = 128
SUB = 8
MIB = 1024 * 1024


def iota(shape, axis):
    return lax.broadcasted_iota(I32, shape, axis)


def split(values):
    high = values.astype(BF16)
    low = (values - high.astype(F32)).astype(BF16)
    return high, low


def dot(left, right):
    return jnp.dot(left, right, preferred_element_type=F32)


def dot_rows(left, right):
    return lax.dot_general(left, right, (((0,), (0,)), ((), ())), preferred_element_type=F32)


def dot3(left, right):
    lh, ll = split(left)
    rh, rl = split(right)
    return dot(lh, rh) + (dot(lh, rl) + dot(ll, rh))


def dot3_rows(left, right):
    lh, ll = split(left)
    rh, rl = split(right)
    return dot_rows(lh, rh) + (dot_rows(lh, rl) + dot_rows(ll, rh))


def rows_of(packed, count, wide):
    return [
        jnp.concatenate([packed[s * wide + i : s * wide + i + 1, :] for i in range(wide)], axis=1)
        for s in range(count)
    ]


def tile(t):
    return pl.ds(pl.multiple_of(t * SUB, SUB), SUB)


class Runs:
    def __init__(self, table, groups, per_bucket, state):
        self.table, self.groups = table, groups
        self.most = min(7, per_bucket // SUB + 1)
        self.sub_row = iota((SUB, state), 0)

    def get(self, s, v):
        return [self.table[s * self.groups + v, i] for i in range(4)]

    def place(self, s, v, out, source, base=None):
        kept, target, first, final = self.get(s, v)
        first = first if base is None else base
        old = out[tile(target), :]
        for t in reversed(range(1, self.most)):
            t = jnp.minimum(t, final)
            out[tile(target + t), :] = source[tile(first + t), :]
        out[tile(target), :] = jnp.where(self.sub_row < kept, old, source[tile(first), :])

    def place_rest(self, s, v, out, source):
        _, target, first, final = self.get(s, v)

        def longer(t, carry):
            out[tile(target + t), :] = source[tile(first + t), :]
            return carry

        lax.fori_loop(self.most, final + 1, longer, 0)


def lead_kernel(groups, per_bucket, leads, me_ref, *refs):
    given, far_outs, refs = refs[:4], refs[4 : 4 + len(leads)], refs[4 + len(leads) :]
    (pair_ref, place_ref, meta_ref), held, scratch = refs[:3], refs[3:7], refs[7:]
    sorted_ref, small_a, small_b, inv_ref, outs_ref, table, sems = scratch
    outs = [outs_ref.at[n] for n in range(len(leads))]
    some = small_a.shape[0] // len(leads)
    buckets_ref, ids_ref, sigma_ref, obs_ref = held
    blocks, block = place_ref.shape
    wide = block // LANES
    sensors = sigma_ref.shape[1]
    padded, state = sorted_ref.shape
    cells = blocks * groups
    last_tile = per_bucket // SUB - 1
    runs = Runs(table, groups, per_bucket, state)

    small = [pltpu.make_async_copy(given[i], held[i], sems.at[i]) for i in range(3)]
    for copy in small:
        copy.start()

    def fetch(s):
        rows = pl.ds(pl.multiple_of(s * block, block), block)
        return pltpu.make_async_copy(given[3].at[rows, :], obs_ref.at[rows, :], sems.at[4 + s])

    for s in range(blocks):
        fetch(s).start()
    for copy in small:
        copy.wait()

    inv_row = 1.0 / sigma_ref[...]
    inv_ref[...] = jnp.transpose(jnp.broadcast_to(inv_row, (LANES, sensors)))
    slots = rows_of(buckets_ref[...] ^ me_ref[0], blocks, wide)
    hits = jnp.concatenate(
        [jnp.broadcast_to(row, (groups, block)) == iota((groups, block), 0) for row in slots], axis=0
    )
    upto = (iota((block, block), 0) <= iota((block, block), 1)).astype(F32).astype(BF16)
    running = dot(hits.astype(F32).astype(BF16), upto)
    count = jnp.broadcast_to(running[:, block - 1 : block], (cells, LANES))
    row, col = iota((cells, cells), 0), iota((cells, cells), 1)
    shift = groups.bit_length() - 1
    earlier = ((row & (groups - 1)) == (col & (groups - 1))) & (col < row)
    before = dot(earlier.astype(F32).astype(BF16), count.astype(BF16)).astype(I32)
    odd = before & (SUB - 1)
    tiles = (odd + count.astype(I32) + (SUB - 1)) >> 3
    same = ((row >> shift) == (col >> shift)) & (col < row)
    first = dot(same.astype(F32).astype(BF16), tiles.astype(F32).astype(BF16)).astype(I32)
    lane = iota((cells, LANES), 1)
    kept = jnp.where(tiles > 0, odd, SUB)
    target = jnp.minimum(before >> 3, last_tile)
    final = jnp.maximum(tiles - 1, 0)
    meta = jnp.where(lane == 2, first, final)
    meta = jnp.where(lane == 0, kept, jnp.where(lane == 1, target, meta))
    copy = pltpu.make_async_copy(meta_ref, table, sems.at[3])
    local = first * SUB + odd
    local = jnp.concatenate([local] * wide, axis=1)
    spot = jnp.where(hits, local + running.astype(I32) - 1, 0)
    places = jnp.concatenate(
        [jnp.sum(spot[s * groups : (s + 1) * groups], axis=0, keepdims=True) for s in range(blocks)],
        axis=0,
    )
    slot = iota((cells, LANES), 0) & (groups - 1)
    of_lead = functools.reduce(jnp.logical_or, [slot == v for v in leads])
    longest = jnp.max(jnp.where(of_lead, final, 0))
    inv = jnp.concatenate([inv_ref[...]] * wide, axis=1)
    block_rows = lambda s: pl.ds(pl.multiple_of(s * block, block), block)

    for s in range(blocks):
        if s == blocks // 2:
            meta_ref[...] = meta
            copy.start()
            place_ref[...] = places
        ids = [ids_ref[s * wide + i : s * wide + i + 1, :] for i in range(wide)]
        known = iota((sensors, block), 0) == jnp.concatenate(ids, axis=1)
        scale_row = jnp.sum(jnp.where(known, inv, 0.0), axis=0, keepdims=True)
        scale = jnp.transpose(jnp.broadcast_to(scale_row, (LANES, block)))
        fetch(s).wait()
        rows = block_rows(s)
        high, low = split(obs_ref[rows, :] * jnp.concatenate([scale] * (state // LANES), axis=1))
        pair_ref[rows, :state] = high
        pair_ref[rows, state:] = low

    def sort_into(s, picked, into):
        both = dot(picked.astype(F32).astype(BF16), pair_ref[block_rows(s), :])
        into[...] = both[:, :state] + both[:, state:]

    copy.wait()
    unroll = groups <= 8

    @pl.when((longest < runs.most) & unroll)
    def _():
        for s in range(blocks if unroll else 0):
            into = (small_a, small_b)[s % 2]
            spots = place_ref[s : s + 1, :]
            picked = [iota((some, block), 0) == spots - runs.get(s, v)[2] * SUB for v in leads]
            sort_into(s, jnp.concatenate(picked, axis=0), into)
            for n, v in enumerate(leads):
                runs.place(s, v, outs[n], into, n * some // SUB)

    @pl.when((longest >= runs.most) | (not unroll))
    def _():
        def body(s, carry):
            sort_into(s, iota((padded, block), 0) == place_ref[pl.ds(s, 1), :], sorted_ref)
            for v, out in zip(leads, outs):
                runs.place(s, v, out, sorted_ref)
                runs.place_rest(s, v, out, sorted_ref)
            return carry

        lax.fori_loop(0, blocks, body, 0)

    copies = []
    for n, far in enumerate(far_outs):
        copies.append(pltpu.make_async_copy(outs_ref.at[n], far, sems.at[4 + blocks + n]))
        copies[-1].start()
    for copy in copies:
        copy.wait()


def rest_kernel(groups, per_bucket, others, table, place_ref, pair_ref, *refs):
    outs, (sorted_a, sorted_b) = refs[: len(others)], refs[len(others) :]
    blocks, block = place_ref.shape
    padded, state = sorted_a.shape
    runs = Runs(table, groups, per_bucket, state)

    def sort_block(s, into):
        picked = (iota((padded, block), 0) == place_ref[pl.ds(s, 1), :]).astype(F32).astype(BF16)
        rows = pl.ds(pl.multiple_of(s * block, block), block)
        both = dot(picked, pair_ref[rows, :])
        into[...] = both[:, :state] + both[:, state:]

    longest = 0
    for s in range(blocks):
        for v in range(groups):
            longest = jnp.maximum(longest, table[s * groups + v, 3])
    unroll = groups <= 8

    @pl.when((longest < runs.most) & unroll)
    def _():
        for s in range(blocks if unroll else 0):
            into = (sorted_a, sorted_b)[s % 2]
            sort_block(s, into)
            for v, out in zip(others, outs):
                runs.place(s, v, out, into)

    @pl.when((longest >= runs.most) | (not unroll))
    def _():
        def body(s, carry):
            sort_block(s, sorted_a)
            for v, out in zip(others, outs):
                runs.place(s, v, out, sorted_a)
                runs.place_rest(s, v, out, sorted_a)
            return carry

        lax.fori_loop(0, blocks, body, 0)


def sorted_rows(block, groups):
    return -(-(block + groups * 2 * (SUB - 1)) // 16) * 16


def regroup_lead(observations, sensor_ids, sensor_sigma, buckets, me, groups, leads):
    rows, state = observations.shape
    sensors = sensor_sigma.shape[0]
    block = 256
    blocks = rows // block
    cells = blocks * groups
    per_bucket = rows // groups
    far = pl.BlockSpec(memory_space=pltpu.HBM)
    return pl.pallas_call(
        functools.partial(lead_kernel, groups, per_bucket, tuple(leads)),
        in_specs=[pl.BlockSpec(memory_space=pltpu.SMEM)] + [far] * 4,
        out_specs=[pl.BlockSpec(memory_space=pl.ANY)] * len(leads)
        + [pl.BlockSpec(memory_space=pltpu.VMEM)] * 3,
        scratch_shapes=[
            pltpu.VMEM((rows // LANES, LANES), I32),
            pltpu.VMEM((rows // LANES, LANES), I32),
            pltpu.VMEM((1, sensors), F32),
            pltpu.VMEM((rows, state), F32),
            pltpu.VMEM((sorted_rows(block, groups), state), F32),
            pltpu.VMEM((64 * len(leads), state), F32),
            pltpu.VMEM((64 * len(leads), state), F32),
            pltpu.VMEM((sensors, LANES), F32),
            pltpu.VMEM((len(leads), per_bucket, state), F32),
            pltpu.SMEM((cells, LANES), I32),
            pltpu.SemaphoreType.DMA((4 + blocks + len(leads),)),
        ],
        out_shape=[jax.ShapeDtypeStruct((per_bucket, state), F32)] * len(leads)
        + [
            jax.ShapeDtypeStruct((rows, 2 * state), BF16),
            jax.ShapeDtypeStruct((blocks, block), I32),
            jax.ShapeDtypeStruct((cells, LANES), I32),
        ],
        compiler_params=pltpu.CompilerParams(vmem_limit_bytes=56 * MIB),
        cost_estimate=pl.CostEstimate(
            flops=rows * state, bytes_accessed=8 * rows * state, transcendentals=0
        ),
    )(
        me.reshape(1),
        buckets.reshape(rows // LANES, LANES),
        sensor_ids.reshape(rows // LANES, LANES),
        sensor_sigma.reshape(1, sensors),
        observations,
    )


def regroup_rest(table, place, pair, groups, others):
    rows, state = pair.shape[0], pair.shape[1] // 2
    per_bucket = rows // groups
    padded = sorted_rows(place.shape[1], groups)
    vmem = pl.BlockSpec(memory_space=pltpu.VMEM)
    return pl.pallas_call(
        functools.partial(rest_kernel, groups, per_bucket, tuple(others)),
        in_specs=[pl.BlockSpec(memory_space=pltpu.SMEM), vmem, vmem],
        out_specs=[vmem] * len(others),
        scratch_shapes=[pltpu.VMEM((padded, state), F32)] * 2,
        out_shape=[jax.ShapeDtypeStruct((per_bucket, state), F32)] * len(others),
        compiler_params=pltpu.CompilerParams(vmem_limit_bytes=14 * MIB),
        cost_estimate=pl.CostEstimate(
            flops=8 * rows * padded * state, bytes_accessed=8 * rows * state, transcendentals=0
        ),
    )(table, place, pair)


def block_pairs(count):
    return [(i, j) for i in range(count) for j in range(i, count)]


def write_gram(both, state, out_ref):
    for n, (i, j) in enumerate(block_pairs(state // LANES)):
        a, b = i * LANES, j * LANES
        cross = both[a : a + LANES, state + b : state + b + LANES]
        turned = both[b : b + LANES, state + a : state + a + LANES]
        out_ref[n * LANES : (n + 1) * LANES, :] = both[a : a + LANES, b : b + LANES] + (
            cross + jnp.transpose(turned)
        )


def gram_kernel(prior_ref, pair_ref, out_ref, prior_out_ref, both_ref):
    state = prior_ref.shape[0]
    both_ref[...] = dot_rows(pair_ref[:, :state], pair_ref[...])
    write_gram(both_ref, state, out_ref)
    high, low = split(prior_ref[...])
    both_ref[...] = dot_rows(high, jnp.concatenate([high, low], axis=1))
    write_gram(both_ref, state, prior_out_ref)


def gram(prior_factor, pair):
    rows, state = pair.shape[0], pair.shape[1] // 2
    packed = len(block_pairs(state // LANES)) * LANES
    vmem = pl.BlockSpec(memory_space=pltpu.VMEM)
    return pl.pallas_call(
        gram_kernel,
        in_specs=[vmem] * 2,
        out_specs=[vmem] * 2,
        out_shape=[jax.ShapeDtypeStruct((packed, LANES), F32)] * 2,
        scratch_shapes=[pltpu.VMEM((state, 2 * state), F32)],
        compiler_params=pltpu.CompilerParams(vmem_limit_bytes=10 * MIB),
        cost_estimate=pl.CostEstimate(
            flops=4 * rows * state * state, bytes_accessed=4 * rows * state, transcendentals=0
        ),
    )(prior_factor, pair)


def scatter_sum(packed, count, groups):
    rows, lanes = packed.shape
    axes = ("rows", "grp")
    got = lax.all_to_all(packed, axes, split_axis=0, concat_axis=0, axis_index_groups=groups, tiled=True)
    return jnp.sum(got.reshape(count, rows // count, lanes), axis=0)


def gather_pieces(piece, count, groups):
    rows, lanes = piece.shape
    copies = jnp.broadcast_to(piece, (count, rows, lanes)).reshape(count * rows, lanes)
    axes = ("rows", "grp")
    return lax.all_to_all(copies, axes, split_axis=0, concat_axis=0, axis_index_groups=groups, tiled=True)


def sweep(a, w):
    width = a.shape[0]
    groups = width // SUB
    row_id = iota((SUB, LANES), 0)
    a_rows = [a[g * SUB : (g + 1) * SUB, :] for g in range(groups)]
    w_rows = [w[g * SUB : (g + 1) * SUB, :] for g in range(groups)]
    for g in range(groups):
        va, vw = a_rows[g], w_rows[g]
        cols = [
            jnp.broadcast_to(va[:, g * SUB + j : g * SUB + j + 1], (SUB, LANES)) for j in range(SUB)
        ]
        scale = jnp.zeros((SUB, LANES), F32)
        for j in range(SUB):
            pivot = jnp.broadcast_to(cols[j][j : j + 1, :], (SUB, LANES))
            root = lax.rsqrt(pivot)
            scale = jnp.where(row_id == j, root, scale)
            if j < SUB - 1:
                ratio = jnp.where(row_id > j, cols[j] * (root * root), 0.0)
                for k in range(j + 1, SUB):
                    cols[k] = cols[k] - ratio * cols[k][j : j + 1, :]
                va = va - ratio * va[j : j + 1, :]
                vw = vw - ratio * vw[j : j + 1, :]
        va, vw = va * scale, vw * scale
        va = jnp.where(iota((SUB, LANES), 1) >= row_id + g * SUB, va, 0.0)
        a_rows[g], w_rows[g] = va, vw
        if g < groups - 1:
            both = jnp.concatenate([va, vw], axis=1)
            high = both.astype(BF16).astype(F32)
            low = both - high
            left = jnp.concatenate([high[:, :LANES], high[:, :LANES], low[:, :LANES]], axis=0)
            right = jnp.concatenate([high, low, high], axis=0)
            change = dot_rows(left.astype(BF16), right.astype(BF16))
            for q in range(g + 1, groups):
                rows = slice(q * SUB, (q + 1) * SUB)
                a_rows[q] = a_rows[q] - change[rows, :LANES]
                w_rows[q] = w_rows[q] - change[rows, LANES:]
    return jnp.concatenate(a_rows, axis=0), jnp.concatenate(w_rows, axis=0)


def factor_kernel(inv_total, sum_ref, prior_ref, factor_ref, high_ref, low_ref, a_ref, x_ref):
    state = factor_ref.shape[0]
    count = state // LANES
    span = lambda i: slice(i * LANES, (i + 1) * LANES)
    for n, (i, j) in enumerate(block_pairs(count)):
        a_ref[span(i), span(j)] = prior_ref[span(n), :] + sum_ref[span(n), :] * inv_total
    factor_ref[...] = jnp.zeros((state, state), F32)
    x_ref[...] = jnp.zeros((state, state), F32)
    eye = (iota((LANES, LANES), 0) == iota((LANES, LANES), 1)).astype(F32)
    for k in range(count):
        r, w = sweep(a_ref[span(k), span(k)], eye)
        factor_ref[span(k), span(k)] = r
        x = jnp.transpose(w)
        x_ref[span(k), span(k)] = x
        if k > 0:
            left = dot3(x_ref[: k * LANES, : k * LANES], factor_ref[: k * LANES, span(k)])
            x_ref[: k * LANES, span(k)] = -dot3(left, x)
        if k < count - 1:
            rest = slice((k + 1) * LANES, state)
            right = dot3(w, a_ref[span(k), rest])
            factor_ref[span(k), rest] = right
            for i in range(k + 1, count):
                low = slice(i * LANES, state)
                at = (i - k - 1) * LANES
                a_ref[span(i), low] -= dot3_rows(right[:, at : at + LANES], right[:, at:])
    high, low = split(x_ref[...])
    high_ref[...] = high
    low_ref[...] = low


def factorise(summed, prior_gram, state, total_rows):
    vmem = pl.BlockSpec(memory_space=pltpu.VMEM)
    return pl.pallas_call(
        functools.partial(factor_kernel, 1.0 / total_rows),
        in_specs=[vmem] * 2,
        out_specs=[vmem] * 3,
        out_shape=[
            jax.ShapeDtypeStruct((state, state), F32),
            jax.ShapeDtypeStruct((state, state), BF16),
            jax.ShapeDtypeStruct((state, state), BF16),
        ],
        scratch_shapes=[pltpu.VMEM((state, state), F32)] * 2,
        compiler_params=pltpu.CompilerParams(vmem_limit_bytes=16 * MIB),
        cost_estimate=pl.CostEstimate(
            flops=1, bytes_accessed=1, transcendentals=0
        ),
    )(summed, prior_gram)


def whiten_kernel(steps, aliased, me_ref, high_ref, low_ref, *rest):
    count = len(steps)
    chunks = rest[:count]
    out_ref, held, sems = rest[count + aliased :]
    per_bucket = chunks[0].shape[0]
    high, low = high_ref[...], low_ref[...]
    copies = []
    for n, k in enumerate(steps):
        rows_high, rows_low = split(chunks[n][...])
        held[n] = dot(rows_high, high) + (dot(rows_high, low) + dot(rows_low, high))
        slot = me_ref[0] ^ k
        copy = pltpu.make_async_copy(
            held.at[n],
            out_ref.at[pl.ds(pl.multiple_of(slot * per_bucket, per_bucket), per_bucket), :],
            sems.at[n],
        )
        copy.start()
        copies.append(copy)
    for copy in copies:
        copy.wait()


def whiten(me, high, low, steps, chunks, out, rows):
    per_bucket, state = chunks[0].shape
    count = len(chunks)
    vmem = pl.BlockSpec(memory_space=pltpu.VMEM)
    anywhere = pl.BlockSpec(memory_space=pl.ANY)
    extra = [] if out is None else [out]
    return pl.pallas_call(
        functools.partial(whiten_kernel, tuple(steps), len(extra)),
        in_specs=[pl.BlockSpec(memory_space=pltpu.SMEM)]
        + [vmem] * (2 + count)
        + [anywhere] * len(extra),
        out_specs=anywhere,
        out_shape=jax.ShapeDtypeStruct((rows, state), F32),
        scratch_shapes=[
            pltpu.VMEM((count, per_bucket, state), F32),
            pltpu.SemaphoreType.DMA((count,)),
        ],
        input_output_aliases={3 + count: 0} if extra else {},
        compiler_params=pltpu.CompilerParams(vmem_limit_bytes=16 * MIB),
        cost_estimate=pl.CostEstimate(
            flops=1, bytes_accessed=1, transcendentals=0
        ),
    )(me.reshape(1), high, low, *chunks, *extra)


def behind(value, *arrays):
    return lax.optimization_barrier((value, *arrays))


def shards(observations, sensor_ids, sensor_sigma, buckets, prior_factor):
    rows_dev, state = observations.shape
    groups = lax.axis_size("rows")
    grp = lax.axis_size("grp")
    me = lax.axis_index("rows").astype(I32)
    total_rows = rows_dev * groups * grp
    leads = [k for k in (4, 1) if k < groups]
    others = [k for k in range(groups) if k not in leads]
    *chunks, pair, place, table = regroup_lead(
        observations, sensor_ids, sensor_sigma, buckets, me, groups, leads
    )
    move = lambda k, chunk: lax.ppermute(chunk, "rows", [(i, i ^ k) for i in range(groups)])
    received = {k: move(k, chunk) for k, chunk in zip(leads, chunks)}
    packed_rows = len(block_pairs(state // LANES)) * LANES
    plane = 2 * grp
    planes = [list(range(i, i + plane)) for i in range(0, groups * grp, plane)]
    middle = [k for k in (2, 6) if k < groups]
    late = [k for k in (5, 3, *range(7, groups)) if k < groups]
    valid = sensor_sigma[0] > 0
    nothing = lambda rows: jnp.full((rows, LANES), jnp.nan, F32)

    def first():
        packed, prior_gram = gram(prior_factor, pair)
        rest = list(regroup_rest(table, place, pair, groups, others))
        return scatter_sum(packed, plane, planes), prior_gram, rest

    def wrong():
        return nothing(packed_rows // plane), nothing(packed_rows), [chunks[0]] * len(others)

    piece, prior_gram, rest = lax.cond(valid, first, wrong)
    rest = dict(zip(others, rest))
    received[0] = rest[0]
    across = [piece]
    for step in range(1, groups // 2):
        across.append(move(2 * step, piece))
    for k in middle[1:]:
        received[k] = move(k, behind(piece, rest[k])[1])
    for k in middle[:1]:
        received[leads[0]], chunk = behind(received[leads[0]], rest[k])
        received[k] = move(k, chunk)
    while len(across) > 1:
        across = [across[i] + across[i + 1] for i in range(0, len(across), 2)]
    across[0], received[leads[0]] = behind(across[0], received[leads[0]])
    summed = lax.cond(
        valid, lambda: gather_pieces(across[0], plane, planes), lambda: nothing(packed_rows)
    )
    for k in leads[1:]:
        summed, received[k] = behind(summed, received[k])
    for k in late:
        received[k] = move(k, behind(summed, rest[k])[1])
    factor, high, low = factorise(summed, prior_gram, state, total_rows)
    out = None
    for steps in ([0, *leads, *middle], late[:-1], late[-1:]):
        if steps:
            out = whiten(me, high, low, steps, [received[k] for k in steps], out, rows_dev)
    return (out, factor)


def solution(mesh):
    in_specs = (P(("rows", "grp"), None), P(("rows", "grp")), P(), P(("rows", "grp")), P())
    out_specs = (P(("rows", "grp"), None), P())
    return jax.shard_map(shards, mesh=mesh, in_specs=in_specs, out_specs=out_specs, check_vma=False)
```

```python
import functools

import jax
import jax.numpy as jnp
from jax import lax
from jax.experimental import pallas as pl
from jax.experimental.pallas import tpu as pltpu
from jax.sharding import PartitionSpec as P

F32 = jnp.float32
BF16 = jnp.bfloat16
I32 = jnp.int32
LANES = 128
SUB = 8
MIB = 1024 * 1024


def iota(shape, axis):
    return lax.broadcasted_iota(I32, shape, axis)


def split(values):
    high = values.astype(BF16)
    low = (values - high.astype(F32)).astype(BF16)
    return high, low


def dot(left, right):
    return jnp.dot(left, right, preferred_element_type=F32)


def dot_rows(left, right):
    return lax.dot_general(left, right, (((0,), (0,)), ((), ())), preferred_element_type=F32)


def dot3(left, right):
    lh, ll = split(left)
    rh, rl = split(right)
    return dot(lh, rh) + (dot(lh, rl) + dot(ll, rh))


def dot3_rows(left, right):
    lh, ll = split(left)
    rh, rl = split(right)
    return dot_rows(lh, rh) + (dot_rows(lh, rl) + dot_rows(ll, rh))


def rows_of(packed, count, wide):
    return [
        jnp.concatenate([packed[s * wide + i : s * wide + i + 1, :] for i in range(wide)], axis=1)
        for s in range(count)
    ]


def tile(t):
    return pl.ds(pl.multiple_of(t * SUB, SUB), SUB)


class Runs:
    def __init__(self, table, groups, per_bucket, state):
        self.table, self.groups = table, groups
        self.most = min(7, per_bucket // SUB + 1)
        self.sub_row = iota((SUB, state), 0)

    def get(self, s, v):
        return [self.table[s * self.groups + v, i] for i in range(4)]

    def place(self, s, v, out, source, base=None):
        kept, target, first, final = self.get(s, v)
        first = first if base is None else base
        old = out[tile(target), :]
        for t in reversed(range(1, self.most)):
            t = jnp.minimum(t, final)
            out[tile(target + t), :] = source[tile(first + t), :]
        out[tile(target), :] = jnp.where(self.sub_row < kept, old, source[tile(first), :])

    def place_rest(self, s, v, out, source):
        _, target, first, final = self.get(s, v)

        def longer(t, carry):
            out[tile(target + t), :] = source[tile(first + t), :]
            return carry

        lax.fori_loop(self.most, final + 1, longer, 0)


def lead_kernel(groups, per_bucket, leads, me_ref, *refs):
    given, far_outs, refs = refs[:4], refs[4 : 4 + len(leads)], refs[4 + len(leads) :]
    (pair_ref, place_ref, meta_ref), held, scratch = refs[:3], refs[3:7], refs[7:]
    sorted_ref, small_a, small_b, inv_ref, outs_ref, table, sems = scratch
    outs = [outs_ref.at[n] for n in range(len(leads))]
    some = small_a.shape[0] // len(leads)
    buckets_ref, ids_ref, sigma_ref, obs_ref = held
    blocks, block = place_ref.shape
    wide = block // LANES
    sensors = sigma_ref.shape[1]
    padded, state = sorted_ref.shape
    cells = blocks * groups
    last_tile = per_bucket // SUB - 1
    runs = Runs(table, groups, per_bucket, state)

    small = [pltpu.make_async_copy(given[i], held[i], sems.at[i]) for i in range(3)]
    for copy in small:
        copy.start()

    def fetch(s):
        rows = pl.ds(pl.multiple_of(s * block, block), block)
        return pltpu.make_async_copy(given[3].at[rows, :], obs_ref.at[rows, :], sems.at[4 + s])

    for s in range(blocks):
        fetch(s).start()
    for copy in small:
        copy.wait()

    inv_row = 1.0 / sigma_ref[...]
    inv_ref[...] = jnp.transpose(jnp.broadcast_to(inv_row, (LANES, sensors)))
    slots = rows_of(buckets_ref[...] ^ me_ref[0], blocks, wide)
    hits = jnp.concatenate(
        [jnp.broadcast_to(row, (groups, block)) == iota((groups, block), 0) for row in slots], axis=0
    )
    upto = (iota((block, block), 0) <= iota((block, block), 1)).astype(F32).astype(BF16)
    running = dot(hits.astype(F32).astype(BF16), upto)
    count = jnp.broadcast_to(running[:, block - 1 : block], (cells, LANES))
    row, col = iota((cells, cells), 0), iota((cells, cells), 1)
    shift = groups.bit_length() - 1
    earlier = ((row & (groups - 1)) == (col & (groups - 1))) & (col < row)
    before = dot(earlier.astype(F32).astype(BF16), count.astype(BF16)).astype(I32)
    odd = before & (SUB - 1)
    tiles = (odd + count.astype(I32) + (SUB - 1)) >> 3
    same = ((row >> shift) == (col >> shift)) & (col < row)
    first = dot(same.astype(F32).astype(BF16), tiles.astype(F32).astype(BF16)).astype(I32)
    lane = iota((cells, LANES), 1)
    kept = jnp.where(tiles > 0, odd, SUB)
    target = jnp.minimum(before >> 3, last_tile)
    final = jnp.maximum(tiles - 1, 0)
    meta = jnp.where(lane == 2, first, final)
    meta = jnp.where(lane == 0, kept, jnp.where(lane == 1, target, meta))
    copy = pltpu.make_async_copy(meta_ref, table, sems.at[3])
    local = first * SUB + odd
    local = jnp.concatenate([local] * wide, axis=1)
    spot = jnp.where(hits, local + running.astype(I32) - 1, 0)
    places = jnp.concatenate(
        [jnp.sum(spot[s * groups : (s + 1) * groups], axis=0, keepdims=True) for s in range(blocks)],
        axis=0,
    )
    slot = iota((cells, LANES), 0) & (groups - 1)
    of_lead = functools.reduce(jnp.logical_or, [slot == v for v in leads])
    longest = jnp.max(jnp.where(of_lead, final, 0))
    inv = jnp.concatenate([inv_ref[...]] * wide, axis=1)
    block_rows = lambda s: pl.ds(pl.multiple_of(s * block, block), block)

    for s in range(blocks):
        if s == blocks // 2:
            meta_ref[...] = meta
            copy.start()
            place_ref[...] = places
        ids = [ids_ref[s * wide + i : s * wide + i + 1, :] for i in range(wide)]
        known = iota((sensors, block), 0) == jnp.concatenate(ids, axis=1)
        scale_row = jnp.sum(jnp.where(known, inv, 0.0), axis=0, keepdims=True)
        scale = jnp.transpose(jnp.broadcast_to(scale_row, (LANES, block)))
        fetch(s).wait()
        rows = block_rows(s)
        high, low = split(obs_ref[rows, :] * jnp.concatenate([scale] * (state // LANES), axis=1))
        pair_ref[rows, :state] = high
        pair_ref[rows, state:] = low

    def sort_into(s, picked, into):
        both = dot(picked.astype(F32).astype(BF16), pair_ref[block_rows(s), :])
        into[...] = both[:, :state] + both[:, state:]

    copy.wait()
    unroll = groups <= 8

    @pl.when((longest < runs.most) & unroll)
    def _():
        for s in range(blocks if unroll else 0):
            into = (small_a, small_b)[s % 2]
            spots = place_ref[s : s + 1, :]
            picked = [iota((some, block), 0) == spots - runs.get(s, v)[2] * SUB for v in leads]
            sort_into(s, jnp.concatenate(picked, axis=0), into)
            for n, v in enumerate(leads):
                runs.place(s, v, outs[n], into, n * some // SUB)

    @pl.when((longest >= runs.most) | (not unroll))
    def _():
        def body(s, carry):
            sort_into(s, iota((padded, block), 0) == place_ref[pl.ds(s, 1), :], sorted_ref)
            for v, out in zip(leads, outs):
                runs.place(s, v, out, sorted_ref)
                runs.place_rest(s, v, out, sorted_ref)
            return carry

        lax.fori_loop(0, blocks, body, 0)

    copies = []
    for n, far in enumerate(far_outs):
        copies.append(pltpu.make_async_copy(outs_ref.at[n], far, sems.at[4 + blocks + n]))
        copies[-1].start()
    for copy in copies:
        copy.wait()


def rest_kernel(groups, per_bucket, others, table, place_ref, pair_ref, *refs):
    outs, (sorted_a, sorted_b) = refs[: len(others)], refs[len(others) :]
    blocks, block = place_ref.shape
    padded, state = sorted_a.shape
    runs = Runs(table, groups, per_bucket, state)

    def sort_block(s, into):
        picked = (iota((padded, block), 0) == place_ref[pl.ds(s, 1), :]).astype(F32).astype(BF16)
        rows = pl.ds(pl.multiple_of(s * block, block), block)
        both = dot(picked, pair_ref[rows, :])
        into[...] = both[:, :state] + both[:, state:]

    longest = 0
    for s in range(blocks):
        for v in range(groups):
            longest = jnp.maximum(longest, table[s * groups + v, 3])
    unroll = groups <= 8

    @pl.when((longest < runs.most) & unroll)
    def _():
        for s in range(blocks if unroll else 0):
            into = (sorted_a, sorted_b)[s % 2]
            sort_block(s, into)
            for v, out in zip(others, outs):
                runs.place(s, v, out, into)

    @pl.when((longest >= runs.most) | (not unroll))
    def _():
        def body(s, carry):
            sort_block(s, sorted_a)
            for v, out in zip(others, outs):
                runs.place(s, v, out, sorted_a)
                runs.place_rest(s, v, out, sorted_a)
            return carry

        lax.fori_loop(0, blocks, body, 0)


def sorted_rows(block, groups):
    return -(-(block + groups * 2 * (SUB - 1)) // 16) * 16


def regroup_lead(observations, sensor_ids, sensor_sigma, buckets, me, groups, leads):
    rows, state = observations.shape
    sensors = sensor_sigma.shape[0]
    block = 256
    blocks = rows // block
    cells = blocks * groups
    per_bucket = rows // groups
    far = pl.BlockSpec(memory_space=pltpu.HBM)
    return pl.pallas_call(
        functools.partial(lead_kernel, groups, per_bucket, tuple(leads)),
        in_specs=[pl.BlockSpec(memory_space=pltpu.SMEM)] + [far] * 4,
        out_specs=[pl.BlockSpec(memory_space=pl.ANY)] * len(leads)
        + [pl.BlockSpec(memory_space=pltpu.VMEM)] * 3,
        scratch_shapes=[
            pltpu.VMEM((rows // LANES, LANES), I32),
            pltpu.VMEM((rows // LANES, LANES), I32),
            pltpu.VMEM((1, sensors), F32),
            pltpu.VMEM((rows, state), F32),
            pltpu.VMEM((sorted_rows(block, groups), state), F32),
            pltpu.VMEM((64 * len(leads), state), F32),
            pltpu.VMEM((64 * len(leads), state), F32),
            pltpu.VMEM((sensors, LANES), F32),
            pltpu.VMEM((len(leads), per_bucket, state), F32),
            pltpu.SMEM((cells, LANES), I32),
            pltpu.SemaphoreType.DMA((4 + blocks + len(leads),)),
        ],
        out_shape=[jax.ShapeDtypeStruct((per_bucket, state), F32)] * len(leads)
        + [
            jax.ShapeDtypeStruct((rows, 2 * state), BF16),
            jax.ShapeDtypeStruct((blocks, block), I32),
            jax.ShapeDtypeStruct((cells, LANES), I32),
        ],
        compiler_params=pltpu.CompilerParams(vmem_limit_bytes=56 * MIB),
        cost_estimate=pl.CostEstimate(
            flops=rows * state, bytes_accessed=8 * rows * state, transcendentals=0
        ),
    )(
        me.reshape(1),
        buckets.reshape(rows // LANES, LANES),
        sensor_ids.reshape(rows // LANES, LANES),
        sensor_sigma.reshape(1, sensors),
        observations,
    )


def regroup_rest(table, place, pair, groups, others):
    rows, state = pair.shape[0], pair.shape[1] // 2
    per_bucket = rows // groups
    padded = sorted_rows(place.shape[1], groups)
    vmem = pl.BlockSpec(memory_space=pltpu.VMEM)
    return pl.pallas_call(
        functools.partial(rest_kernel, groups, per_bucket, tuple(others)),
        in_specs=[pl.BlockSpec(memory_space=pltpu.SMEM), vmem, vmem],
        out_specs=[vmem] * len(others),
        scratch_shapes=[pltpu.VMEM((padded, state), F32)] * 2,
        out_shape=[jax.ShapeDtypeStruct((per_bucket, state), F32)] * len(others),
        compiler_params=pltpu.CompilerParams(vmem_limit_bytes=14 * MIB),
        cost_estimate=pl.CostEstimate(
            flops=8 * rows * padded * state, bytes_accessed=8 * rows * state, transcendentals=0
        ),
    )(table, place, pair)


def block_pairs(count):
    return [(i, j) for i in range(count) for j in range(i, count)]


def write_gram(both, state, out_ref):
    for n, (i, j) in enumerate(block_pairs(state // LANES)):
        a, b = i * LANES, j * LANES
        cross = both[a : a + LANES, state + b : state + b + LANES]
        turned = both[b : b + LANES, state + a : state + a + LANES]
        out_ref[n * LANES : (n + 1) * LANES, :] = both[a : a + LANES, b : b + LANES] + (
            cross + jnp.transpose(turned)
        )


def gram_kernel(prior_ref, pair_ref, out_ref, prior_out_ref, both_ref):
    state = prior_ref.shape[0]
    both_ref[...] = dot_rows(pair_ref[:, :state], pair_ref[...])
    write_gram(both_ref, state, out_ref)
    high, low = split(prior_ref[...])
    both_ref[...] = dot_rows(high, jnp.concatenate([high, low], axis=1))
    write_gram(both_ref, state, prior_out_ref)


def gram(prior_factor, pair):
    rows, state = pair.shape[0], pair.shape[1] // 2
    packed = len(block_pairs(state // LANES)) * LANES
    vmem = pl.BlockSpec(memory_space=pltpu.VMEM)
    return pl.pallas_call(
        gram_kernel,
        in_specs=[vmem] * 2,
        out_specs=[vmem] * 2,
        out_shape=[jax.ShapeDtypeStruct((packed, LANES), F32)] * 2,
        scratch_shapes=[pltpu.VMEM((state, 2 * state), F32)],
        compiler_params=pltpu.CompilerParams(vmem_limit_bytes=10 * MIB),
        cost_estimate=pl.CostEstimate(
            flops=4 * rows * state * state, bytes_accessed=4 * rows * state, transcendentals=0
        ),
    )(prior_factor, pair)


def scatter_sum(packed, count, groups):
    rows, lanes = packed.shape
    axes = ("rows", "grp")
    got = lax.all_to_all(packed, axes, split_axis=0, concat_axis=0, axis_index_groups=groups, tiled=True)
    return jnp.sum(got.reshape(count, rows // count, lanes), axis=0)


def gather_pieces(piece, count, groups):
    rows, lanes = piece.shape
    copies = jnp.broadcast_to(piece, (count, rows, lanes)).reshape(count * rows, lanes)
    axes = ("rows", "grp")
    return lax.all_to_all(copies, axes, split_axis=0, concat_axis=0, axis_index_groups=groups, tiled=True)


def sweep(a, w):
    width = a.shape[0]
    groups = width // SUB
    row_id = iota((SUB, LANES), 0)
    a_rows = [a[g * SUB : (g + 1) * SUB, :] for g in range(groups)]
    w_rows = [w[g * SUB : (g + 1) * SUB, :] for g in range(groups)]
    for g in range(groups):
        va, vw = a_rows[g], w_rows[g]
        cols = [
            jnp.broadcast_to(va[:, g * SUB + j : g * SUB + j + 1], (SUB, LANES)) for j in range(SUB)
        ]
        scale = jnp.zeros((SUB, LANES), F32)
        for j in range(SUB):
            pivot = jnp.broadcast_to(cols[j][j : j + 1, :], (SUB, LANES))
            root = lax.rsqrt(pivot)
            scale = jnp.where(row_id == j, root, scale)
            if j < SUB - 1:
                ratio = jnp.where(row_id > j, cols[j] * (root * root), 0.0)
                for k in range(j + 1, SUB):
                    cols[k] = cols[k] - ratio * cols[k][j : j + 1, :]
                va = va - ratio * va[j : j + 1, :]
                vw = vw - ratio * vw[j : j + 1, :]
        va, vw = va * scale, vw * scale
        va = jnp.where(iota((SUB, LANES), 1) >= row_id + g * SUB, va, 0.0)
        a_rows[g], w_rows[g] = va, vw
        if g < groups - 1:
            both = jnp.concatenate([va, vw], axis=1)
            high = both.astype(BF16).astype(F32)
            low = both - high
            left = jnp.concatenate([high[:, :LANES], high[:, :LANES], low[:, :LANES]], axis=0)
            right = jnp.concatenate([high, low, high], axis=0)
            change = dot_rows(left.astype(BF16), right.astype(BF16))
            for q in range(g + 1, groups):
                rows = slice(q * SUB, (q + 1) * SUB)
                a_rows[q] = a_rows[q] - change[rows, :LANES]
                w_rows[q] = w_rows[q] - change[rows, LANES:]
    return jnp.concatenate(a_rows, axis=0), jnp.concatenate(w_rows, axis=0)


def factor_kernel(inv_total, sum_ref, prior_ref, factor_ref, high_ref, low_ref, a_ref, x_ref):
    state = factor_ref.shape[0]
    count = state // LANES
    span = lambda i: slice(i * LANES, (i + 1) * LANES)
    for n, (i, j) in enumerate(block_pairs(count)):
        a_ref[span(i), span(j)] = prior_ref[span(n), :] + sum_ref[span(n), :] * inv_total
    factor_ref[...] = jnp.zeros((state, state), F32)
    x_ref[...] = jnp.zeros((state, state), F32)
    eye = (iota((LANES, LANES), 0) == iota((LANES, LANES), 1)).astype(F32)
    for k in range(count):
        r, w = sweep(a_ref[span(k), span(k)], eye)
        factor_ref[span(k), span(k)] = r
        x = jnp.transpose(w)
        x_ref[span(k), span(k)] = x
        if k > 0:
            left = dot3(x_ref[: k * LANES, : k * LANES], factor_ref[: k * LANES, span(k)])
            x_ref[: k * LANES, span(k)] = -dot3(left, x)
        if k < count - 1:
            rest = slice((k + 1) * LANES, state)
            right = dot3(w, a_ref[span(k), rest])
            factor_ref[span(k), rest] = right
            for i in range(k + 1, count):
                low = slice(i * LANES, state)
                at = (i - k - 1) * LANES
                a_ref[span(i), low] -= dot3_rows(right[:, at : at + LANES], right[:, at:])
    high, low = split(x_ref[...])
    high_ref[...] = high
    low_ref[...] = low


def factorise(summed, prior_gram, state, total_rows):
    vmem = pl.BlockSpec(memory_space=pltpu.VMEM)
    return pl.pallas_call(
        functools.partial(factor_kernel, 1.0 / total_rows),
        in_specs=[vmem] * 2,
        out_specs=[vmem] * 3,
        out_shape=[
            jax.ShapeDtypeStruct((state, state), F32),
            jax.ShapeDtypeStruct((state, state), BF16),
            jax.ShapeDtypeStruct((state, state), BF16),
        ],
        scratch_shapes=[pltpu.VMEM((state, state), F32)] * 2,
        compiler_params=pltpu.CompilerParams(vmem_limit_bytes=16 * MIB),
        cost_estimate=pl.CostEstimate(
            flops=1, bytes_accessed=1, transcendentals=0
        ),
    )(summed, prior_gram)


def whiten_kernel(steps, aliased, me_ref, high_ref, low_ref, *rest):
    count = len(steps)
    chunks = rest[:count]
    out_ref, held, sems = rest[count + aliased :]
    per_bucket = chunks[0].shape[0]
    high, low = high_ref[...], low_ref[...]
    copies = []
    for n, k in enumerate(steps):
        rows_high, rows_low = split(chunks[n][...])
        held[n] = dot(rows_high, high) + (dot(rows_high, low) + dot(rows_low, high))
        slot = me_ref[0] ^ k
        copy = pltpu.make_async_copy(
            held.at[n],
            out_ref.at[pl.ds(pl.multiple_of(slot * per_bucket, per_bucket), per_bucket), :],
            sems.at[n],
        )
        copy.start()
        copies.append(copy)
    for copy in copies:
        copy.wait()


def whiten(me, high, low, steps, chunks, out, rows):
    per_bucket, state = chunks[0].shape
    count = len(chunks)
    vmem = pl.BlockSpec(memory_space=pltpu.VMEM)
    anywhere = pl.BlockSpec(memory_space=pl.ANY)
    extra = [] if out is None else [out]
    return pl.pallas_call(
        functools.partial(whiten_kernel, tuple(steps), len(extra)),
        in_specs=[pl.BlockSpec(memory_space=pltpu.SMEM)]
        + [vmem] * (2 + count)
        + [anywhere] * len(extra),
        out_specs=anywhere,
        out_shape=jax.ShapeDtypeStruct((rows, state), F32),
        scratch_shapes=[
            pltpu.VMEM((count, per_bucket, state), F32),
            pltpu.SemaphoreType.DMA((count,)),
        ],
        input_output_aliases={3 + count: 0} if extra else {},
        compiler_params=pltpu.CompilerParams(vmem_limit_bytes=16 * MIB),
        cost_estimate=pl.CostEstimate(
            flops=1, bytes_accessed=1, transcendentals=0
        ),
    )(me.reshape(1), high, low, *chunks, *extra)


def behind(value, *arrays):
    return lax.optimization_barrier((value, *arrays))


def shards(observations, sensor_ids, sensor_sigma, buckets, prior_factor):
    rows_dev, state = observations.shape
    groups = lax.axis_size("rows")
    grp = lax.axis_size("grp")
    me = lax.axis_index("rows").astype(I32)
    total_rows = rows_dev * groups * grp
    leads = [k for k in (4, 1) if k < groups]
    others = [k for k in range(groups) if k not in leads]
    *chunks, pair, place, table = regroup_lead(
        observations, sensor_ids, sensor_sigma, buckets, me, groups, leads
    )
    move = lambda k, chunk: lax.ppermute(chunk, "rows", [(i, i ^ k) for i in range(groups)])
    received = {k: move(k, chunk) for k, chunk in zip(leads, chunks)}
    packed_rows = len(block_pairs(state // LANES)) * LANES
    plane = 2 * grp
    planes = [list(range(i, i + plane)) for i in range(0, groups * grp, plane)]
    middle = [k for k in (2, 6) if k < groups]
    late = [k for k in (5, 3, *range(7, groups)) if k < groups]
    valid = sensor_sigma[0] > 0
    nothing = lambda rows: jnp.full((rows, LANES), jnp.nan, F32)

    def first():
        packed, prior_gram = gram(prior_factor, pair)
        rest = list(regroup_rest(table, place, pair, groups, others))
        return scatter_sum(packed, plane, planes), prior_gram, rest

    def wrong():
        return nothing(packed_rows // plane), nothing(packed_rows), [chunks[0]] * len(others)

    piece, prior_gram, rest = lax.cond(valid, first, wrong)
    rest = dict(zip(others, rest))
    received[0] = rest[0]
    for k in leads[1:]:
        piece, received[k] = behind(piece, received[k])
    across = [piece]
    for step in range(1, groups // 2):
        across.append(move(2 * step, piece))
    for k in middle[:1]:
        received[k] = move(k, behind(piece, rest[k])[1])
    while len(across) > 1:
        across = [across[i] + across[i + 1] for i in range(0, len(across), 2)]
    for k in middle[1:]:
        received[leads[0]], chunk = behind(received[leads[0]], rest[k])
        received[k] = move(k, chunk)
    across[0], received[leads[0]] = behind(across[0], received[leads[0]])
    summed = lax.cond(
        valid, lambda: gather_pieces(across[0], plane, planes), lambda: nothing(packed_rows)
    )
    for k in late:
        received[k] = move(k, behind(summed, rest[k])[1])
    factor, high, low = factorise(summed, prior_gram, state, total_rows)
    out = None
    for steps in ([0, *leads, *middle], late[:-1], late[-1:]):
        if steps:
            out = whiten(me, high, low, steps, [received[k] for k in steps], out, rows_dev)
    return (out, factor)


def solution(mesh):
    in_specs = (P(("rows", "grp"), None), P(("rows", "grp")), P(), P(("rows", "grp")), P())
    out_specs = (P(("rows", "grp"), None), P())
    return jax.shard_map(shards, mesh=mesh, in_specs=in_specs, out_specs=out_specs, check_vma=False)
```

```python
import functools

import jax
import jax.numpy as jnp
from jax import lax
from jax.experimental import pallas as pl
from jax.experimental.pallas import tpu as pltpu
from jax.sharding import PartitionSpec as P

F32 = jnp.float32
BF16 = jnp.bfloat16
I32 = jnp.int32
LANES = 128
SUB = 8
MIB = 1024 * 1024


def iota(shape, axis):
    return lax.broadcasted_iota(I32, shape, axis)


def split(values):
    high = values.astype(BF16)
    low = (values - high.astype(F32)).astype(BF16)
    return high, low


def dot(left, right):
    return jnp.dot(left, right, preferred_element_type=F32)


def dot_rows(left, right):
    return lax.dot_general(left, right, (((0,), (0,)), ((), ())), preferred_element_type=F32)


def dot3(left, right):
    lh, ll = split(left)
    rh, rl = split(right)
    return dot(lh, rh) + (dot(lh, rl) + dot(ll, rh))


def dot3_rows(left, right):
    lh, ll = split(left)
    rh, rl = split(right)
    return dot_rows(lh, rh) + (dot_rows(lh, rl) + dot_rows(ll, rh))


def rows_of(packed, count, wide):
    return [
        jnp.concatenate([packed[s * wide + i : s * wide + i + 1, :] for i in range(wide)], axis=1)
        for s in range(count)
    ]


def tile(t):
    return pl.ds(pl.multiple_of(t * SUB, SUB), SUB)


class Runs:
    def __init__(self, table, groups, per_bucket, state):
        self.table, self.groups = table, groups
        self.most = min(7, per_bucket // SUB + 1)
        self.sub_row = iota((SUB, state), 0)

    def get(self, s, v):
        return [self.table[s * self.groups + v, i] for i in range(4)]

    def place(self, s, v, out, source, base=None):
        kept, target, first, final = self.get(s, v)
        first = first if base is None else base
        old = out[tile(target), :]
        for t in reversed(range(1, self.most)):
            t = jnp.minimum(t, final)
            out[tile(target + t), :] = source[tile(first + t), :]
        out[tile(target), :] = jnp.where(self.sub_row < kept, old, source[tile(first), :])

    def place_rest(self, s, v, out, source):
        _, target, first, final = self.get(s, v)

        def longer(t, carry):
            out[tile(target + t), :] = source[tile(first + t), :]
            return carry

        lax.fori_loop(self.most, final + 1, longer, 0)


def lead_kernel(groups, per_bucket, leads, me_ref, *refs):
    given, far_outs, refs = refs[:4], refs[4 : 4 + len(leads)], refs[4 + len(leads) :]
    (pair_ref, place_ref, meta_ref), held, scratch = refs[:3], refs[3:7], refs[7:]
    sorted_ref, small_a, small_b, inv_ref, outs_ref, table, sems = scratch
    outs = [outs_ref.at[n] for n in range(len(leads))]
    some = small_a.shape[0] // len(leads)
    buckets_ref, ids_ref, sigma_ref, obs_ref = held
    blocks, block = place_ref.shape
    wide = block // LANES
    sensors = sigma_ref.shape[1]
    padded, state = sorted_ref.shape
    cells = blocks * groups
    last_tile = per_bucket // SUB - 1
    runs = Runs(table, groups, per_bucket, state)

    small = [pltpu.make_async_copy(given[i], held[i], sems.at[i]) for i in range(3)]
    for copy in small:
        copy.start()

    def fetch(s):
        rows = pl.ds(pl.multiple_of(s * block, block), block)
        return pltpu.make_async_copy(given[3].at[rows, :], obs_ref.at[rows, :], sems.at[4 + s])

    for s in range(blocks):
        fetch(s).start()
    for copy in small:
        copy.wait()

    inv_row = 1.0 / sigma_ref[...]
    inv_ref[...] = jnp.transpose(jnp.broadcast_to(inv_row, (LANES, sensors)))
    slots = rows_of(buckets_ref[...] ^ me_ref[0], blocks, wide)
    hits = jnp.concatenate(
        [jnp.broadcast_to(row, (groups, block)) == iota((groups, block), 0) for row in slots], axis=0
    )
    upto = (iota((block, block), 0) <= iota((block, block), 1)).astype(F32).astype(BF16)
    running = dot(hits.astype(F32).astype(BF16), upto)
    count = jnp.broadcast_to(running[:, block - 1 : block], (cells, LANES))
    row, col = iota((cells, cells), 0), iota((cells, cells), 1)
    shift = groups.bit_length() - 1
    earlier = ((row & (groups - 1)) == (col & (groups - 1))) & (col < row)
    before = dot(earlier.astype(F32).astype(BF16), count.astype(BF16)).astype(I32)
    odd = before & (SUB - 1)
    tiles = (odd + count.astype(I32) + (SUB - 1)) >> 3
    same = ((row >> shift) == (col >> shift)) & (col < row)
    first = dot(same.astype(F32).astype(BF16), tiles.astype(F32).astype(BF16)).astype(I32)
    lane = iota((cells, LANES), 1)
    kept = jnp.where(tiles > 0, odd, SUB)
    target = jnp.minimum(before >> 3, last_tile)
    final = jnp.maximum(tiles - 1, 0)
    meta = jnp.where(lane == 2, first, final)
    meta = jnp.where(lane == 0, kept, jnp.where(lane == 1, target, meta))
    copy = pltpu.make_async_copy(meta_ref, table, sems.at[3])
    local = first * SUB + odd
    local = jnp.concatenate([local] * wide, axis=1)
    spot = jnp.where(hits, local + running.astype(I32) - 1, 0)
    places = jnp.concatenate(
        [jnp.sum(spot[s * groups : (s + 1) * groups], axis=0, keepdims=True) for s in range(blocks)],
        axis=0,
    )
    slot = iota((cells, LANES), 0) & (groups - 1)
    of_lead = functools.reduce(jnp.logical_or, [slot == v for v in leads])
    longest = jnp.max(jnp.where(of_lead, final, 0))
    inv = jnp.concatenate([inv_ref[...]] * wide, axis=1)
    block_rows = lambda s: pl.ds(pl.multiple_of(s * block, block), block)

    for s in range(blocks):
        if s == blocks // 2:
            meta_ref[...] = meta
            copy.start()
            place_ref[...] = places
        ids = [ids_ref[s * wide + i : s * wide + i + 1, :] for i in range(wide)]
        known = iota((sensors, block), 0) == jnp.concatenate(ids, axis=1)
        scale_row = jnp.sum(jnp.where(known, inv, 0.0), axis=0, keepdims=True)
        scale = jnp.transpose(jnp.broadcast_to(scale_row, (LANES, block)))
        fetch(s).wait()
        rows = block_rows(s)
        high, low = split(obs_ref[rows, :] * jnp.concatenate([scale] * (state // LANES), axis=1))
        pair_ref[rows, :state] = high
        pair_ref[rows, state:] = low

    def sort_into(s, picked, into):
        both = dot(picked.astype(F32).astype(BF16), pair_ref[block_rows(s), :])
        into[...] = both[:, :state] + both[:, state:]

    copy.wait()
    unroll = groups <= 8

    @pl.when((longest < runs.most) & unroll)
    def _():
        for s in range(blocks if unroll else 0):
            into = (small_a, small_b)[s % 2]
            spots = place_ref[s : s + 1, :]
            picked = [iota((some, block), 0) == spots - runs.get(s, v)[2] * SUB for v in leads]
            sort_into(s, jnp.concatenate(picked, axis=0), into)
            for n, v in enumerate(leads):
                runs.place(s, v, outs[n], into, n * some // SUB)

    @pl.when((longest >= runs.most) | (not unroll))
    def _():
        def body(s, carry):
            sort_into(s, iota((padded, block), 0) == place_ref[pl.ds(s, 1), :], sorted_ref)
            for v, out in zip(leads, outs):
                runs.place(s, v, out, sorted_ref)
                runs.place_rest(s, v, out, sorted_ref)
            return carry

        lax.fori_loop(0, blocks, body, 0)

    copies = []
    for n, far in enumerate(far_outs):
        copies.append(pltpu.make_async_copy(outs_ref.at[n], far, sems.at[4 + blocks + n]))
        copies[-1].start()
    for copy in copies:
        copy.wait()


def rest_kernel(groups, per_bucket, others, table, place_ref, pair_ref, *refs):
    outs, (sorted_a, sorted_b) = refs[: len(others)], refs[len(others) :]
    blocks, block = place_ref.shape
    padded, state = sorted_a.shape
    runs = Runs(table, groups, per_bucket, state)

    def sort_block(s, into):
        picked = (iota((padded, block), 0) == place_ref[pl.ds(s, 1), :]).astype(F32).astype(BF16)
        rows = pl.ds(pl.multiple_of(s * block, block), block)
        both = dot(picked, pair_ref[rows, :])
        into[...] = both[:, :state] + both[:, state:]

    longest = 0
    for s in range(blocks):
        for v in range(groups):
            longest = jnp.maximum(longest, table[s * groups + v, 3])
    unroll = groups <= 8

    @pl.when((longest < runs.most) & unroll)
    def _():
        for s in range(blocks if unroll else 0):
            into = (sorted_a, sorted_b)[s % 2]
            sort_block(s, into)
            for v, out in zip(others, outs):
                runs.place(s, v, out, into)

    @pl.when((longest >= runs.most) | (not unroll))
    def _():
        def body(s, carry):
            sort_block(s, sorted_a)
            for v, out in zip(others, outs):
                runs.place(s, v, out, sorted_a)
                runs.place_rest(s, v, out, sorted_a)
            return carry

        lax.fori_loop(0, blocks, body, 0)


def sorted_rows(block, groups):
    return -(-(block + groups * 2 * (SUB - 1)) // 16) * 16


def regroup_lead(observations, sensor_ids, sensor_sigma, buckets, me, groups, leads):
    rows, state = observations.shape
    sensors = sensor_sigma.shape[0]
    block = 256
    blocks = rows // block
    cells = blocks * groups
    per_bucket = rows // groups
    far = pl.BlockSpec(memory_space=pltpu.HBM)
    return pl.pallas_call(
        functools.partial(lead_kernel, groups, per_bucket, tuple(leads)),
        in_specs=[pl.BlockSpec(memory_space=pltpu.SMEM)] + [far] * 4,
        out_specs=[pl.BlockSpec(memory_space=pl.ANY)] * len(leads)
        + [pl.BlockSpec(memory_space=pltpu.VMEM)] * 3,
        scratch_shapes=[
            pltpu.VMEM((rows // LANES, LANES), I32),
            pltpu.VMEM((rows // LANES, LANES), I32),
            pltpu.VMEM((1, sensors), F32),
            pltpu.VMEM((rows, state), F32),
            pltpu.VMEM((sorted_rows(block, groups), state), F32),
            pltpu.VMEM((64 * len(leads), state), F32),
            pltpu.VMEM((64 * len(leads), state), F32),
            pltpu.VMEM((sensors, LANES), F32),
            pltpu.VMEM((len(leads), per_bucket, state), F32),
            pltpu.SMEM((cells, LANES), I32),
            pltpu.SemaphoreType.DMA((4 + blocks + len(leads),)),
        ],
        out_shape=[jax.ShapeDtypeStruct((per_bucket, state), F32)] * len(leads)
        + [
            jax.ShapeDtypeStruct((rows, 2 * state), BF16),
            jax.ShapeDtypeStruct((blocks, block), I32),
            jax.ShapeDtypeStruct((cells, LANES), I32),
        ],
        compiler_params=pltpu.CompilerParams(vmem_limit_bytes=56 * MIB),
        cost_estimate=pl.CostEstimate(
            flops=rows * state, bytes_accessed=8 * rows * state, transcendentals=0
        ),
    )(
        me.reshape(1),
        buckets.reshape(rows // LANES, LANES),
        sensor_ids.reshape(rows // LANES, LANES),
        sensor_sigma.reshape(1, sensors),
        observations,
    )


def regroup_rest(table, place, pair, groups, others):
    rows, state = pair.shape[0], pair.shape[1] // 2
    per_bucket = rows // groups
    padded = sorted_rows(place.shape[1], groups)
    vmem = pl.BlockSpec(memory_space=pltpu.VMEM)
    return pl.pallas_call(
        functools.partial(rest_kernel, groups, per_bucket, tuple(others)),
        in_specs=[pl.BlockSpec(memory_space=pltpu.SMEM), vmem, vmem],
        out_specs=[vmem] * len(others),
        scratch_shapes=[pltpu.VMEM((padded, state), F32)] * 2,
        out_shape=[jax.ShapeDtypeStruct((per_bucket, state), F32)] * len(others),
        compiler_params=pltpu.CompilerParams(vmem_limit_bytes=14 * MIB),
        cost_estimate=pl.CostEstimate(
            flops=8 * rows * padded * state, bytes_accessed=8 * rows * state, transcendentals=0
        ),
    )(table, place, pair)


def block_pairs(count):
    return [(i, j) for i in range(count) for j in range(i, count)]


def write_gram(both, state, out_ref):
    for n, (i, j) in enumerate(block_pairs(state // LANES)):
        a, b = i * LANES, j * LANES
        cross = both[a : a + LANES, state + b : state + b + LANES]
        turned = both[b : b + LANES, state + a : state + a + LANES]
        out_ref[n * LANES : (n + 1) * LANES, :] = both[a : a + LANES, b : b + LANES] + (
            cross + jnp.transpose(turned)
        )


def gram_kernel(prior_ref, pair_ref, out_ref, prior_out_ref, both_ref):
    state = prior_ref.shape[0]
    both_ref[...] = dot_rows(pair_ref[:, :state], pair_ref[...])
    write_gram(both_ref, state, out_ref)
    high, low = split(prior_ref[...])
    both_ref[...] = dot_rows(high, jnp.concatenate([high, low], axis=1))
    write_gram(both_ref, state, prior_out_ref)


def gram(prior_factor, pair):
    rows, state = pair.shape[0], pair.shape[1] // 2
    packed = len(block_pairs(state // LANES)) * LANES
    vmem = pl.BlockSpec(memory_space=pltpu.VMEM)
    return pl.pallas_call(
        gram_kernel,
        in_specs=[vmem] * 2,
        out_specs=[vmem] * 2,
        out_shape=[jax.ShapeDtypeStruct((packed, LANES), F32)] * 2,
        scratch_shapes=[pltpu.VMEM((state, 2 * state), F32)],
        compiler_params=pltpu.CompilerParams(vmem_limit_bytes=10 * MIB),
        cost_estimate=pl.CostEstimate(
            flops=4 * rows * state * state, bytes_accessed=4 * rows * state, transcendentals=0
        ),
    )(prior_factor, pair)


def scatter_sum(packed, count, groups):
    rows, lanes = packed.shape
    axes = ("rows", "grp")
    got = lax.all_to_all(packed, axes, split_axis=0, concat_axis=0, axis_index_groups=groups, tiled=True)
    return jnp.sum(got.reshape(count, rows // count, lanes), axis=0)


def gather_pieces(piece, count, groups):
    rows, lanes = piece.shape
    copies = jnp.broadcast_to(piece, (count, rows, lanes)).reshape(count * rows, lanes)
    axes = ("rows", "grp")
    return lax.all_to_all(copies, axes, split_axis=0, concat_axis=0, axis_index_groups=groups, tiled=True)


def sweep(a, w):
    width = a.shape[0]
    groups = width // SUB
    row_id = iota((SUB, LANES), 0)
    a_rows = [a[g * SUB : (g + 1) * SUB, :] for g in range(groups)]
    w_rows = [w[g * SUB : (g + 1) * SUB, :] for g in range(groups)]
    for g in range(groups):
        va, vw = a_rows[g], w_rows[g]
        cols = [
            jnp.broadcast_to(va[:, g * SUB + j : g * SUB + j + 1], (SUB, LANES)) for j in range(SUB)
        ]
        scale = jnp.zeros((SUB, LANES), F32)
        for j in range(SUB):
            pivot = jnp.broadcast_to(cols[j][j : j + 1, :], (SUB, LANES))
            root = lax.rsqrt(pivot)
            scale = jnp.where(row_id == j, root, scale)
            if j < SUB - 1:
                ratio = jnp.where(row_id > j, cols[j] * (root * root), 0.0)
                for k in range(j + 1, SUB):
                    cols[k] = cols[k] - ratio * cols[k][j : j + 1, :]
                va = va - ratio * va[j : j + 1, :]
                vw = vw - ratio * vw[j : j + 1, :]
        va, vw = va * scale, vw * scale
        va = jnp.where(iota((SUB, LANES), 1) >= row_id + g * SUB, va, 0.0)
        a_rows[g], w_rows[g] = va, vw
        if g < groups - 1:
            both = jnp.concatenate([va, vw], axis=1)
            high = both.astype(BF16).astype(F32)
            low = both - high
            left = jnp.concatenate([high[:, :LANES], high[:, :LANES], low[:, :LANES]], axis=0)
            right = jnp.concatenate([high, low, high], axis=0)
            change = dot_rows(left.astype(BF16), right.astype(BF16))
            for q in range(g + 1, groups):
                rows = slice(q * SUB, (q + 1) * SUB)
                a_rows[q] = a_rows[q] - change[rows, :LANES]
                w_rows[q] = w_rows[q] - change[rows, LANES:]
    return jnp.concatenate(a_rows, axis=0), jnp.concatenate(w_rows, axis=0)


def factor_kernel(inv_total, sum_ref, prior_ref, factor_ref, high_ref, low_ref, a_ref, x_ref):
    state = factor_ref.shape[0]
    count = state // LANES
    span = lambda i: slice(i * LANES, (i + 1) * LANES)
    for n, (i, j) in enumerate(block_pairs(count)):
        a_ref[span(i), span(j)] = prior_ref[span(n), :] + sum_ref[span(n), :] * inv_total
    factor_ref[...] = jnp.zeros((state, state), F32)
    x_ref[...] = jnp.zeros((state, state), F32)
    eye = (iota((LANES, LANES), 0) == iota((LANES, LANES), 1)).astype(F32)
    for k in range(count):
        r, w = sweep(a_ref[span(k), span(k)], eye)
        factor_ref[span(k), span(k)] = r
        x = jnp.transpose(w)
        x_ref[span(k), span(k)] = x
        if k > 0:
            left = dot3(x_ref[: k * LANES, : k * LANES], factor_ref[: k * LANES, span(k)])
            x_ref[: k * LANES, span(k)] = -dot3(left, x)
        if k < count - 1:
            rest = slice((k + 1) * LANES, state)
            right = dot3(w, a_ref[span(k), rest])
            factor_ref[span(k), rest] = right
            for i in range(k + 1, count):
                low = slice(i * LANES, state)
                at = (i - k - 1) * LANES
                a_ref[span(i), low] -= dot3_rows(right[:, at : at + LANES], right[:, at:])
    high, low = split(x_ref[...])
    high_ref[...] = high
    low_ref[...] = low


def factorise(summed, prior_gram, state, total_rows):
    vmem = pl.BlockSpec(memory_space=pltpu.VMEM)
    return pl.pallas_call(
        functools.partial(factor_kernel, 1.0 / total_rows),
        in_specs=[vmem] * 2,
        out_specs=[vmem] * 3,
        out_shape=[
            jax.ShapeDtypeStruct((state, state), F32),
            jax.ShapeDtypeStruct((state, state), BF16),
            jax.ShapeDtypeStruct((state, state), BF16),
        ],
        scratch_shapes=[pltpu.VMEM((state, state), F32)] * 2,
        compiler_params=pltpu.CompilerParams(vmem_limit_bytes=16 * MIB),
        cost_estimate=pl.CostEstimate(
            flops=1, bytes_accessed=1, transcendentals=0
        ),
    )(summed, prior_gram)


def whiten_kernel(steps, aliased, me_ref, high_ref, low_ref, *rest):
    count = len(steps)
    chunks = rest[:count]
    out_ref, held, sems = rest[count + aliased :]
    per_bucket = chunks[0].shape[0]
    high, low = high_ref[...], low_ref[...]
    copies = []
    for n, k in enumerate(steps):
        rows_high, rows_low = split(chunks[n][...])
        held[n] = dot(rows_high, high) + (dot(rows_high, low) + dot(rows_low, high))
        slot = me_ref[0] ^ k
        copy = pltpu.make_async_copy(
            held.at[n],
            out_ref.at[pl.ds(pl.multiple_of(slot * per_bucket, per_bucket), per_bucket), :],
            sems.at[n],
        )
        copy.start()
        copies.append(copy)
    for copy in copies:
        copy.wait()


def whiten(me, high, low, steps, chunks, out, rows):
    per_bucket, state = chunks[0].shape
    count = len(chunks)
    vmem = pl.BlockSpec(memory_space=pltpu.VMEM)
    anywhere = pl.BlockSpec(memory_space=pl.ANY)
    extra = [] if out is None else [out]
    return pl.pallas_call(
        functools.partial(whiten_kernel, tuple(steps), len(extra)),
        in_specs=[pl.BlockSpec(memory_space=pltpu.SMEM)]
        + [vmem] * (2 + count)
        + [anywhere] * len(extra),
        out_specs=anywhere,
        out_shape=jax.ShapeDtypeStruct((rows, state), F32),
        scratch_shapes=[
            pltpu.VMEM((count, per_bucket, state), F32),
            pltpu.SemaphoreType.DMA((count,)),
        ],
        input_output_aliases={3 + count: 0} if extra else {},
        compiler_params=pltpu.CompilerParams(vmem_limit_bytes=16 * MIB),
        cost_estimate=pl.CostEstimate(
            flops=1, bytes_accessed=1, transcendentals=0
        ),
    )(me.reshape(1), high, low, *chunks, *extra)


def behind(value, *arrays):
    return lax.optimization_barrier((value, *arrays))


def shards(observations, sensor_ids, sensor_sigma, buckets, prior_factor):
    rows_dev, state = observations.shape
    groups = lax.axis_size("rows")
    grp = lax.axis_size("grp")
    me = lax.axis_index("rows").astype(I32)
    total_rows = rows_dev * groups * grp
    leads = [k for k in (4, 1) if k < groups]
    others = [k for k in range(groups) if k not in leads]
    *chunks, pair, place, table = regroup_lead(
        observations, sensor_ids, sensor_sigma, buckets, me, groups, leads
    )
    move = lambda k, chunk: lax.ppermute(chunk, "rows", [(i, i ^ k) for i in range(groups)])
    received = {k: move(k, chunk) for k, chunk in zip(leads, chunks)}
    packed_rows = len(block_pairs(state // LANES)) * LANES
    plane = 2 * grp
    planes = [list(range(i, i + plane)) for i in range(0, groups * grp, plane)]
    middle = [k for k in (2, 6) if k < groups]
    late = [k for k in (5, 3, *range(7, groups)) if k < groups]
    valid = sensor_sigma[0] > 0
    nothing = lambda rows: jnp.full((rows, LANES), jnp.nan, F32)

    def first():
        packed, prior_gram = gram(prior_factor, pair)
        rest = list(regroup_rest(table, place, pair, groups, others))
        return scatter_sum(packed, plane, planes), prior_gram, rest

    def wrong():
        return nothing(packed_rows // plane), nothing(packed_rows), [chunks[0]] * len(others)

    piece, prior_gram, rest = lax.cond(valid, first, wrong)
    rest = dict(zip(others, rest))
    received[0] = rest[0]
    for k in leads[1:]:
        piece, received[k] = behind(piece, received[k])
    across = [piece]
    for step in range(1, groups // 2):
        across.append(move(2 * step, piece))
    for k in middle[:1]:
        received[k] = move(k, behind(piece, rest[k])[1])
    while len(across) > 1:
        across = [across[i] + across[i + 1] for i in range(0, len(across), 2)]
    for k in middle[1:]:
        received[leads[0]], chunk = behind(received[leads[0]], rest[k])
        received[k] = move(k, chunk)
    across[0], received[leads[0]] = behind(across[0], received[leads[0]])
    for k in late[:1]:
        received[k] = move(k, behind(across[0], rest[k])[1])
    summed = lax.cond(
        valid, lambda: gather_pieces(across[0], plane, planes), lambda: nothing(packed_rows)
    )
    for k in late[1:]:
        received[k] = move(k, behind(summed, rest[k])[1])
    factor, high, low = factorise(summed, prior_gram, state, total_rows)
    out = None
    for steps in ([0, *leads, *middle], late[:-1], late[-1:]):
        if steps:
            out = whiten(me, high, low, steps, [received[k] for k in steps], out, rows_dev)
    return (out, factor)


def solution(mesh):
    in_specs = (P(("rows", "grp"), None), P(("rows", "grp")), P(), P(("rows", "grp")), P())
    out_specs = (P(("rows", "grp"), None), P())
    return jax.shard_map(shards, mesh=mesh, in_specs=in_specs, out_specs=out_specs, check_vma=False)
```

```python
import functools

import jax
import jax.numpy as jnp
from jax import lax
from jax.experimental import pallas as pl
from jax.experimental.pallas import tpu as pltpu
from jax.sharding import PartitionSpec as P

F32 = jnp.float32
BF16 = jnp.bfloat16
I32 = jnp.int32
LANES = 128
SUB = 8
MIB = 1024 * 1024


def iota(shape, axis):
    return lax.broadcasted_iota(I32, shape, axis)


def split(values):
    high = values.astype(BF16)
    low = (values - high.astype(F32)).astype(BF16)
    return high, low


def dot(left, right):
    return jnp.dot(left, right, preferred_element_type=F32)


def dot_rows(left, right):
    return lax.dot_general(left, right, (((0,), (0,)), ((), ())), preferred_element_type=F32)


def dot3(left, right):
    lh, ll = split(left)
    rh, rl = split(right)
    return dot(lh, rh) + (dot(lh, rl) + dot(ll, rh))


def dot3_rows(left, right):
    lh, ll = split(left)
    rh, rl = split(right)
    return dot_rows(lh, rh) + (dot_rows(lh, rl) + dot_rows(ll, rh))


def rows_of(packed, count, wide):
    return [
        jnp.concatenate([packed[s * wide + i : s * wide + i + 1, :] for i in range(wide)], axis=1)
        for s in range(count)
    ]


def tile(t):
    return pl.ds(pl.multiple_of(t * SUB, SUB), SUB)


class Runs:
    def __init__(self, table, groups, per_bucket, state):
        self.table, self.groups = table, groups
        self.most = min(7, per_bucket // SUB + 1)
        self.sub_row = iota((SUB, state), 0)

    def get(self, s, v):
        return [self.table[s * self.groups + v, i] for i in range(4)]

    def place(self, s, v, out, source, base=None):
        kept, target, first, final = self.get(s, v)
        first = first if base is None else base
        old = out[tile(target), :]
        for t in reversed(range(1, self.most)):
            t = jnp.minimum(t, final)
            out[tile(target + t), :] = source[tile(first + t), :]
        out[tile(target), :] = jnp.where(self.sub_row < kept, old, source[tile(first), :])

    def place_rest(self, s, v, out, source):
        _, target, first, final = self.get(s, v)

        def longer(t, carry):
            out[tile(target + t), :] = source[tile(first + t), :]
            return carry

        lax.fori_loop(self.most, final + 1, longer, 0)


def lead_kernel(groups, per_bucket, leads, parts, me_ref, *refs):
    given, far_outs, refs = refs[:4], refs[4 : 4 + len(parts)], refs[4 + len(parts) :]
    (pair_ref, place_ref, meta_ref), held, scratch = refs[:3], refs[3:7], refs[7:]
    sorted_ref, small_a, small_b, inv_ref, outs_ref, table, sems = scratch
    outs = [outs_ref.at[n] for n in range(len(leads))]
    some = small_a.shape[0] // len(leads)
    buckets_ref, ids_ref, sigma_ref, obs_ref = held
    blocks, block = place_ref.shape
    wide = block // LANES
    sensors = sigma_ref.shape[1]
    padded, state = sorted_ref.shape
    cells = blocks * groups
    last_tile = per_bucket // SUB - 1
    runs = Runs(table, groups, per_bucket, state)

    small = [pltpu.make_async_copy(given[i], held[i], sems.at[i]) for i in range(3)]
    for copy in small:
        copy.start()

    def fetch(s):
        rows = pl.ds(pl.multiple_of(s * block, block), block)
        return pltpu.make_async_copy(given[3].at[rows, :], obs_ref.at[rows, :], sems.at[4 + s])

    for s in range(blocks):
        fetch(s).start()
    for copy in small:
        copy.wait()

    inv_row = 1.0 / sigma_ref[...]
    inv_ref[...] = jnp.transpose(jnp.broadcast_to(inv_row, (LANES, sensors)))
    slots = rows_of(buckets_ref[...] ^ me_ref[0], blocks, wide)
    hits = jnp.concatenate(
        [jnp.broadcast_to(row, (groups, block)) == iota((groups, block), 0) for row in slots], axis=0
    )
    upto = (iota((block, block), 0) <= iota((block, block), 1)).astype(F32).astype(BF16)
    running = dot(hits.astype(F32).astype(BF16), upto)
    count = jnp.broadcast_to(running[:, block - 1 : block], (cells, LANES))
    row, col = iota((cells, cells), 0), iota((cells, cells), 1)
    shift = groups.bit_length() - 1
    earlier = ((row & (groups - 1)) == (col & (groups - 1))) & (col < row)
    before = dot(earlier.astype(F32).astype(BF16), count.astype(BF16)).astype(I32)
    odd = before & (SUB - 1)
    tiles = (odd + count.astype(I32) + (SUB - 1)) >> 3
    same = ((row >> shift) == (col >> shift)) & (col < row)
    first = dot(same.astype(F32).astype(BF16), tiles.astype(F32).astype(BF16)).astype(I32)
    lane = iota((cells, LANES), 1)
    kept = jnp.where(tiles > 0, odd, SUB)
    target = jnp.minimum(before >> 3, last_tile)
    final = jnp.maximum(tiles - 1, 0)
    meta = jnp.where(lane == 2, first, final)
    meta = jnp.where(lane == 0, kept, jnp.where(lane == 1, target, meta))
    copy = pltpu.make_async_copy(meta_ref, table, sems.at[3])
    local = first * SUB + odd
    local = jnp.concatenate([local] * wide, axis=1)
    spot = jnp.where(hits, local + running.astype(I32) - 1, 0)
    places = jnp.concatenate(
        [jnp.sum(spot[s * groups : (s + 1) * groups], axis=0, keepdims=True) for s in range(blocks)],
        axis=0,
    )
    slot = iota((cells, LANES), 0) & (groups - 1)
    of_lead = functools.reduce(jnp.logical_or, [slot == v for v in leads])
    longest = jnp.max(jnp.where(of_lead, final, 0))
    inv = jnp.concatenate([inv_ref[...]] * wide, axis=1)
    block_rows = lambda s: pl.ds(pl.multiple_of(s * block, block), block)

    for s in range(blocks):
        if s == blocks // 2:
            meta_ref[...] = meta
            copy.start()
            place_ref[...] = places
        ids = [ids_ref[s * wide + i : s * wide + i + 1, :] for i in range(wide)]
        known = iota((sensors, block), 0) == jnp.concatenate(ids, axis=1)
        scale_row = jnp.sum(jnp.where(known, inv, 0.0), axis=0, keepdims=True)
        scale = jnp.transpose(jnp.broadcast_to(scale_row, (LANES, block)))
        fetch(s).wait()
        rows = block_rows(s)
        high, low = split(obs_ref[rows, :] * jnp.concatenate([scale] * (state // LANES), axis=1))
        pair_ref[rows, :state] = high
        pair_ref[rows, state:] = low

    def sort_into(s, picked, into):
        both = dot(picked.astype(F32).astype(BF16), pair_ref[block_rows(s), :])
        into[...] = both[:, :state] + both[:, state:]

    copy.wait()
    unroll = groups <= 8

    @pl.when((longest < runs.most) & unroll)
    def _():
        for s in range(blocks if unroll else 0):
            into = (small_a, small_b)[s % 2]
            spots = place_ref[s : s + 1, :]
            picked = [iota((some, block), 0) == spots - runs.get(s, v)[2] * SUB for v in leads]
            sort_into(s, jnp.concatenate(picked, axis=0), into)
            for n, v in enumerate(leads):
                runs.place(s, v, outs[n], into, n * some // SUB)

    @pl.when((longest >= runs.most) | (not unroll))
    def _():
        def body(s, carry):
            sort_into(s, iota((padded, block), 0) == place_ref[pl.ds(s, 1), :], sorted_ref)
            for v, out in zip(leads, outs):
                runs.place(s, v, out, sorted_ref)
                runs.place_rest(s, v, out, sorted_ref)
            return carry

        lax.fori_loop(0, blocks, body, 0)

    copies = []
    for m, ((n, first_row, rows), far) in enumerate(zip(parts, far_outs)):
        part = outs_ref.at[n, pl.ds(first_row, rows)]
        copies.append(pltpu.make_async_copy(part, far, sems.at[4 + blocks + m]))
        copies[-1].start()
    for copy in copies:
        copy.wait()


def rest_kernel(groups, per_bucket, others, table, place_ref, pair_ref, *refs):
    outs, (sorted_a, sorted_b) = refs[: len(others)], refs[len(others) :]
    blocks, block = place_ref.shape
    padded, state = sorted_a.shape
    runs = Runs(table, groups, per_bucket, state)

    def sort_block(s, into):
        picked = (iota((padded, block), 0) == place_ref[pl.ds(s, 1), :]).astype(F32).astype(BF16)
        rows = pl.ds(pl.multiple_of(s * block, block), block)
        both = dot(picked, pair_ref[rows, :])
        into[...] = both[:, :state] + both[:, state:]

    longest = 0
    for s in range(blocks):
        for v in range(groups):
            longest = jnp.maximum(longest, table[s * groups + v, 3])
    unroll = groups <= 8

    @pl.when((longest < runs.most) & unroll)
    def _():
        for s in range(blocks if unroll else 0):
            into = (sorted_a, sorted_b)[s % 2]
            sort_block(s, into)
            for v, out in zip(others, outs):
                runs.place(s, v, out, into)

    @pl.when((longest >= runs.most) | (not unroll))
    def _():
        def body(s, carry):
            sort_block(s, sorted_a)
            for v, out in zip(others, outs):
                runs.place(s, v, out, sorted_a)
                runs.place_rest(s, v, out, sorted_a)
            return carry

        lax.fori_loop(0, blocks, body, 0)


def sorted_rows(block, groups):
    return -(-(block + groups * 2 * (SUB - 1)) // 16) * 16


def regroup_lead(observations, sensor_ids, sensor_sigma, buckets, me, groups, leads, parts):
    rows, state = observations.shape
    sensors = sensor_sigma.shape[0]
    block = 256
    blocks = rows // block
    cells = blocks * groups
    per_bucket = rows // groups
    far = pl.BlockSpec(memory_space=pltpu.HBM)
    return pl.pallas_call(
        functools.partial(lead_kernel, groups, per_bucket, tuple(leads), tuple(parts)),
        in_specs=[pl.BlockSpec(memory_space=pltpu.SMEM)] + [far] * 4,
        out_specs=[pl.BlockSpec(memory_space=pl.ANY)] * len(parts)
        + [pl.BlockSpec(memory_space=pltpu.VMEM)] * 3,
        scratch_shapes=[
            pltpu.VMEM((rows // LANES, LANES), I32),
            pltpu.VMEM((rows // LANES, LANES), I32),
            pltpu.VMEM((1, sensors), F32),
            pltpu.VMEM((rows, state), F32),
            pltpu.VMEM((sorted_rows(block, groups), state), F32),
            pltpu.VMEM((64 * len(leads), state), F32),
            pltpu.VMEM((64 * len(leads), state), F32),
            pltpu.VMEM((sensors, LANES), F32),
            pltpu.VMEM((len(leads), per_bucket, state), F32),
            pltpu.SMEM((cells, LANES), I32),
            pltpu.SemaphoreType.DMA((4 + blocks + len(parts),)),
        ],
        out_shape=[jax.ShapeDtypeStruct((part[2], state), F32) for part in parts]
        + [
            jax.ShapeDtypeStruct((rows, 2 * state), BF16),
            jax.ShapeDtypeStruct((blocks, block), I32),
            jax.ShapeDtypeStruct((cells, LANES), I32),
        ],
        compiler_params=pltpu.CompilerParams(vmem_limit_bytes=56 * MIB),
        cost_estimate=pl.CostEstimate(
            flops=rows * state, bytes_accessed=8 * rows * state, transcendentals=0
        ),
    )(
        me.reshape(1),
        buckets.reshape(rows // LANES, LANES),
        sensor_ids.reshape(rows // LANES, LANES),
        sensor_sigma.reshape(1, sensors),
        observations,
    )


def regroup_rest(table, place, pair, groups, others):
    rows, state = pair.shape[0], pair.shape[1] // 2
    per_bucket = rows // groups
    padded = sorted_rows(place.shape[1], groups)
    vmem = pl.BlockSpec(memory_space=pltpu.VMEM)
    return pl.pallas_call(
        functools.partial(rest_kernel, groups, per_bucket, tuple(others)),
        in_specs=[pl.BlockSpec(memory_space=pltpu.SMEM), vmem, vmem],
        out_specs=[vmem] * len(others),
        scratch_shapes=[pltpu.VMEM((padded, state), F32)] * 2,
        out_shape=[jax.ShapeDtypeStruct((per_bucket, state), F32)] * len(others),
        compiler_params=pltpu.CompilerParams(vmem_limit_bytes=14 * MIB),
        cost_estimate=pl.CostEstimate(
            flops=8 * rows * padded * state, bytes_accessed=8 * rows * state, transcendentals=0
        ),
    )(table, place, pair)


def block_pairs(count):
    return [(i, j) for i in range(count) for j in range(i + 1, count)]


def packed_rows_of(state, plane):
    count = state // LANES
    rows = (len(block_pairs(count)) + count // 2) * LANES + SUB
    return -(-rows // (plane * SUB)) * plane * SUB


def write_gram(both, state, out_ref):
    count = state // LANES
    pairs = block_pairs(count)
    row, col = iota((LANES, LANES), 0), iota((LANES, LANES), 1)

    def block(i, j):
        a, b = i * LANES, j * LANES
        cross = both[a : a + LANES, state + b : state + b + LANES]
        turned = both[b : b + LANES, state + a : state + a + LANES]
        return both[a : a + LANES, b : b + LANES] + (cross + jnp.transpose(turned))

    for n, (i, j) in enumerate(pairs):
        out_ref[n * LANES : (n + 1) * LANES, :] = block(i, j)
    tail = (len(pairs) + count // 2) * LANES
    out_ref[tail:, :] = jnp.zeros((out_ref.shape[0] - tail, LANES), F32)
    for m in range(count // 2):
        n = len(pairs) + m
        second = block(2 * m + 1, 2 * m + 1)
        out_ref[n * LANES : (n + 1) * LANES, :] = jnp.where(row <= col, block(2 * m, 2 * m), second)
        diagonal = jnp.sum(jnp.where(row == col, second, 0.0), axis=0, keepdims=True)
        out_ref[tail + m : tail + m + 1, :] = diagonal


def read_gram(value, state, a_ref):
    count = state // LANES
    pairs = block_pairs(count)
    row, col = iota((LANES, LANES), 0), iota((LANES, LANES), 1)
    span = lambda i: slice(i * LANES, (i + 1) * LANES)
    for n, (i, j) in enumerate(pairs):
        a_ref[span(i), span(j)] = value(span(n))
    tail = (len(pairs) + count // 2) * LANES
    for m in range(count // 2):
        mixed = value(span(len(pairs) + m))
        turned = jnp.transpose(mixed)
        i, j = span(2 * m), span(2 * m + 1)
        a_ref[i, i] = jnp.where(row <= col, mixed, turned)
        diagonal = value(slice(tail, tail + SUB))[m : m + 1, :]
        second = jnp.where(row > col, mixed, turned)
        a_ref[j, j] = jnp.where(row == col, diagonal, second)


def gram_kernel(prior_ref, pair_ref, out_ref, prior_out_ref, both_ref):
    state = prior_ref.shape[0]
    both_ref[...] = dot_rows(pair_ref[:, :state], pair_ref[...])
    write_gram(both_ref, state, out_ref)
    high, low = split(prior_ref[...])
    both_ref[...] = dot_rows(high, jnp.concatenate([high, low], axis=1))
    write_gram(both_ref, state, prior_out_ref)


def gram(prior_factor, pair, packed):
    rows, state = pair.shape[0], pair.shape[1] // 2
    vmem = pl.BlockSpec(memory_space=pltpu.VMEM)
    return pl.pallas_call(
        gram_kernel,
        in_specs=[vmem] * 2,
        out_specs=[vmem] * 2,
        out_shape=[jax.ShapeDtypeStruct((packed, LANES), F32)] * 2,
        scratch_shapes=[pltpu.VMEM((state, 2 * state), F32)],
        compiler_params=pltpu.CompilerParams(vmem_limit_bytes=10 * MIB),
        cost_estimate=pl.CostEstimate(
            flops=4 * rows * state * state, bytes_accessed=4 * rows * state, transcendentals=0
        ),
    )(prior_factor, pair)


def scatter_sum(packed, count, groups):
    rows, lanes = packed.shape
    axes = ("rows", "grp")
    got = lax.all_to_all(packed, axes, split_axis=0, concat_axis=0, axis_index_groups=groups, tiled=True)
    return jnp.sum(got.reshape(count, rows // count, lanes), axis=0)


def gather_pieces(piece, count, groups):
    rows, lanes = piece.shape
    copies = jnp.broadcast_to(piece, (count, rows, lanes)).reshape(count * rows, lanes)
    axes = ("rows", "grp")
    return lax.all_to_all(copies, axes, split_axis=0, concat_axis=0, axis_index_groups=groups, tiled=True)


def sweep(a, w):
    width = a.shape[0]
    groups = width // SUB
    row_id = iota((SUB, LANES), 0)
    a_rows = [a[g * SUB : (g + 1) * SUB, :] for g in range(groups)]
    w_rows = [w[g * SUB : (g + 1) * SUB, :] for g in range(groups)]
    for g in range(groups):
        va, vw = a_rows[g], w_rows[g]
        cols = [
            jnp.broadcast_to(va[:, g * SUB + j : g * SUB + j + 1], (SUB, LANES)) for j in range(SUB)
        ]
        scale = jnp.zeros((SUB, LANES), F32)
        for j in range(SUB):
            pivot = jnp.broadcast_to(cols[j][j : j + 1, :], (SUB, LANES))
            root = lax.rsqrt(pivot)
            scale = jnp.where(row_id == j, root, scale)
            if j < SUB - 1:
                ratio = jnp.where(row_id > j, cols[j] * (root * root), 0.0)
                for k in range(j + 1, SUB):
                    cols[k] = cols[k] - ratio * cols[k][j : j + 1, :]
                va = va - ratio * va[j : j + 1, :]
                vw = vw - ratio * vw[j : j + 1, :]
        va, vw = va * scale, vw * scale
        va = jnp.where(iota((SUB, LANES), 1) >= row_id + g * SUB, va, 0.0)
        a_rows[g], w_rows[g] = va, vw
        if g < groups - 1:
            both = jnp.concatenate([va, vw], axis=1)
            high = both.astype(BF16).astype(F32)
            low = both - high
            left = jnp.concatenate([high[:, :LANES], high[:, :LANES], low[:, :LANES]], axis=0)
            right = jnp.concatenate([high, low, high], axis=0)
            change = dot_rows(left.astype(BF16), right.astype(BF16))
            for q in range(g + 1, groups):
                rows = slice(q * SUB, (q + 1) * SUB)
                a_rows[q] = a_rows[q] - change[rows, :LANES]
                w_rows[q] = w_rows[q] - change[rows, LANES:]
    return jnp.concatenate(a_rows, axis=0), jnp.concatenate(w_rows, axis=0)


def factor_kernel(inv_total, sum_ref, prior_ref, factor_ref, high_ref, low_ref, a_ref, x_ref):
    state = factor_ref.shape[0]
    count = state // LANES
    span = lambda i: slice(i * LANES, (i + 1) * LANES)
    read_gram(lambda rows: prior_ref[rows, :] + sum_ref[rows, :] * inv_total, state, a_ref)
    factor_ref[...] = jnp.zeros((state, state), F32)
    x_ref[...] = jnp.zeros((state, state), F32)
    eye = (iota((LANES, LANES), 0) == iota((LANES, LANES), 1)).astype(F32)
    for k in range(count):
        r, w = sweep(a_ref[span(k), span(k)], eye)
        factor_ref[span(k), span(k)] = r
        x = jnp.transpose(w)
        x_ref[span(k), span(k)] = x
        if k > 0:
            left = dot3(x_ref[: k * LANES, : k * LANES], factor_ref[: k * LANES, span(k)])
            x_ref[: k * LANES, span(k)] = -dot3(left, x)
        if k < count - 1:
            rest = slice((k + 1) * LANES, state)
            right = dot3(w, a_ref[span(k), rest])
            factor_ref[span(k), rest] = right
            for i in range(k + 1, count):
                low = slice(i * LANES, state)
                at = (i - k - 1) * LANES
                a_ref[span(i), low] -= dot3_rows(right[:, at : at + LANES], right[:, at:])
    high, low = split(x_ref[...])
    high_ref[...] = high
    low_ref[...] = low


def factorise(summed, prior_gram, state, total_rows):
    vmem = pl.BlockSpec(memory_space=pltpu.VMEM)
    return pl.pallas_call(
        functools.partial(factor_kernel, 1.0 / total_rows),
        in_specs=[vmem] * 2,
        out_specs=[vmem] * 3,
        out_shape=[
            jax.ShapeDtypeStruct((state, state), F32),
            jax.ShapeDtypeStruct((state, state), BF16),
            jax.ShapeDtypeStruct((state, state), BF16),
        ],
        scratch_shapes=[pltpu.VMEM((state, state), F32)] * 2,
        compiler_params=pltpu.CompilerParams(vmem_limit_bytes=16 * MIB),
        cost_estimate=pl.CostEstimate(
            flops=1, bytes_accessed=1, transcendentals=0
        ),
    )(summed, prior_gram)


def whiten_kernel(steps, aliased, per_bucket, me_ref, high_ref, low_ref, *rest):
    count = len(steps)
    chunks = rest[:count]
    out_ref, held, sems = rest[count + aliased :]
    high, low = high_ref[...], low_ref[...]
    copies = []
    for n, (k, offset) in enumerate(steps):
        rows = chunks[n].shape[0]
        rows_high, rows_low = split(chunks[n][...])
        held[n, :rows] = dot(rows_high, high) + (dot(rows_high, low) + dot(rows_low, high))
        first = pl.multiple_of((me_ref[0] ^ k) * per_bucket, per_bucket) + offset
        copy = pltpu.make_async_copy(
            held.at[n, pl.ds(0, rows)],
            out_ref.at[pl.ds(pl.multiple_of(first, SUB), rows), :],
            sems.at[n],
        )
        copy.start()
        copies.append(copy)
    for copy in copies:
        copy.wait()


def whiten(me, high, low, parts, out, rows, groups):
    steps = tuple((k, offset) for k, offset, _ in parts)
    chunks = [chunk for _, _, chunk in parts]
    per_bucket, state = rows // groups, chunks[0].shape[1]
    count = len(chunks)
    vmem = pl.BlockSpec(memory_space=pltpu.VMEM)
    anywhere = pl.BlockSpec(memory_space=pl.ANY)
    extra = [] if out is None else [out]
    return pl.pallas_call(
        functools.partial(whiten_kernel, steps, len(extra), per_bucket),
        in_specs=[pl.BlockSpec(memory_space=pltpu.SMEM)]
        + [vmem] * (2 + count)
        + [anywhere] * len(extra),
        out_specs=anywhere,
        out_shape=jax.ShapeDtypeStruct((rows, state), F32),
        scratch_shapes=[
            pltpu.VMEM((count, per_bucket, state), F32),
            pltpu.SemaphoreType.DMA((count,)),
        ],
        input_output_aliases={3 + count: 0} if extra else {},
        compiler_params=pltpu.CompilerParams(vmem_limit_bytes=16 * MIB),
        cost_estimate=pl.CostEstimate(flops=1, bytes_accessed=1, transcendentals=0),
    )(me.reshape(1), high, low, *chunks, *extra)


def behind(value, *arrays):
    return lax.optimization_barrier((value, *arrays))


def shards(observations, sensor_ids, sensor_sigma, buckets, prior_factor):
    rows_dev, state = observations.shape
    groups = lax.axis_size("rows")
    grp = lax.axis_size("grp")
    me = lax.axis_index("rows").astype(I32)
    total_rows = rows_dev * groups * grp
    leads = [k for k in (4, 1) if k < groups]
    others = [k for k in range(groups) if k not in leads]
    per_bucket = rows_dev // groups
    parts = [(n, 0, per_bucket) for n in range(len(leads))]
    *chunks, pair, place, table = regroup_lead(
        observations, sensor_ids, sensor_sigma, buckets, me, groups, leads, parts
    )
    move = lambda k, chunk: lax.ppermute(chunk, "rows", [(i, i ^ k) for i in range(groups)])
    received = {k: move(k, chunk) for k, chunk in zip(leads, chunks)}
    plane = 2 * grp
    packed_rows = packed_rows_of(state, plane)
    planes = [list(range(i, i + plane)) for i in range(0, groups * grp, plane)]
    middle = [k for k in (2, 6) if k < groups]
    late = [k for k in (5, 3, *range(7, groups)) if k < groups]
    valid = sensor_sigma[0] > 0
    nothing = lambda rows: jnp.full((rows, LANES), jnp.nan, F32)

    def first():
        packed, prior_gram = gram(prior_factor, pair, packed_rows)
        rest = list(regroup_rest(table, place, pair, groups, others))
        return scatter_sum(packed, plane, planes), prior_gram, rest

    def wrong():
        return nothing(packed_rows // plane), nothing(packed_rows), [jnp.full((per_bucket, state), jnp.nan, F32)] * len(others)

    piece, prior_gram, rest = lax.cond(valid, first, wrong)
    rest = dict(zip(others, rest))
    received[0] = rest[0]
    for k in leads[1:]:
        piece, received[k] = behind(piece, received[k])
    across = [piece]
    for step in range(1, groups // 2):
        across.append(move(2 * step, piece))
    for k in middle[:1]:
        received[k] = move(k, behind(piece, rest[k])[1])
    while len(across) > 1:
        across = [across[i] + across[i + 1] for i in range(0, len(across), 2)]
    for k in middle[1:]:
        received[leads[0]], chunk = behind(received[leads[0]], rest[k])
        received[k] = move(k, chunk)
    across[0], received[leads[0]] = behind(across[0], received[leads[0]])
    for k in late[:1]:
        received[k] = move(k, behind(across[0], rest[k])[1])
    summed = lax.cond(
        valid, lambda: gather_pieces(across[0], plane, planes), lambda: nothing(packed_rows)
    )
    for k in late[1:]:
        received[k] = move(k, behind(summed, rest[k])[1])
    factor, high, low = factorise(summed, prior_gram, state, total_rows)
    whole = lambda slots: [(k, 0, received[k]) for k in slots]
    out = None
    for parts in (whole([0, *leads, *middle]), whole(late[:-1]), whole(late[-1:])):
        if parts:
            out = whiten(me, high, low, parts, out, rows_dev, groups)
    return (out, factor)


def solution(mesh):
    in_specs = (P(("rows", "grp"), None), P(("rows", "grp")), P(), P(("rows", "grp")), P())
    out_specs = (P(("rows", "grp"), None), P())
    return jax.shard_map(shards, mesh=mesh, in_specs=in_specs, out_specs=out_specs, check_vma=False)
```

```python
import functools

import jax
import jax.numpy as jnp
from jax import lax
from jax.experimental import pallas as pl
from jax.experimental.pallas import tpu as pltpu
from jax.sharding import PartitionSpec as P

F32 = jnp.float32
BF16 = jnp.bfloat16
I32 = jnp.int32
LANES = 128
SUB = 8
MIB = 1024 * 1024


def iota(shape, axis):
    return lax.broadcasted_iota(I32, shape, axis)


def split(values):
    high = values.astype(BF16)
    low = (values - high.astype(F32)).astype(BF16)
    return high, low


def dot(left, right):
    return jnp.dot(left, right, preferred_element_type=F32)


def dot_rows(left, right):
    return lax.dot_general(left, right, (((0,), (0,)), ((), ())), preferred_element_type=F32)


def dot3(left, right):
    lh, ll = split(left)
    rh, rl = split(right)
    return dot(lh, rh) + (dot(lh, rl) + dot(ll, rh))


def dot3_rows(left, right):
    lh, ll = split(left)
    rh, rl = split(right)
    return dot_rows(lh, rh) + (dot_rows(lh, rl) + dot_rows(ll, rh))


def rows_of(packed, count, wide):
    return [
        jnp.concatenate([packed[s * wide + i : s * wide + i + 1, :] for i in range(wide)], axis=1)
        for s in range(count)
    ]


def tile(t):
    return pl.ds(pl.multiple_of(t * SUB, SUB), SUB)


class Runs:
    def __init__(self, table, groups, per_bucket, state):
        self.table, self.groups = table, groups
        self.most = min(7, per_bucket // SUB + 1)
        self.sub_row = iota((SUB, state), 0)

    def get(self, s, v):
        return [self.table[s * self.groups + v, i] for i in range(4)]

    def place(self, s, v, out, source, base=None):
        kept, target, first, final = self.get(s, v)
        first = first if base is None else base
        old = out[tile(target), :]
        for t in reversed(range(1, self.most)):
            t = jnp.minimum(t, final)
            out[tile(target + t), :] = source[tile(first + t), :]
        out[tile(target), :] = jnp.where(self.sub_row < kept, old, source[tile(first), :])

    def place_rest(self, s, v, out, source):
        _, target, first, final = self.get(s, v)

        def longer(t, carry):
            out[tile(target + t), :] = source[tile(first + t), :]
            return carry

        lax.fori_loop(self.most, final + 1, longer, 0)


def lead_kernel(groups, per_bucket, leads, parts, me_ref, *refs):
    given, far_outs, refs = refs[:4], refs[4 : 4 + len(parts)], refs[4 + len(parts) :]
    (pair_ref, place_ref, meta_ref), held, scratch = refs[:3], refs[3:7], refs[7:]
    sorted_ref, small_a, small_b, inv_ref, outs_ref, table, sems = scratch
    outs = [outs_ref.at[n] for n in range(len(leads))]
    some = small_a.shape[0] // len(leads)
    buckets_ref, ids_ref, sigma_ref, obs_ref = held
    blocks, block = place_ref.shape
    wide = block // LANES
    sensors = sigma_ref.shape[1]
    padded, state = sorted_ref.shape
    cells = blocks * groups
    last_tile = per_bucket // SUB - 1
    runs = Runs(table, groups, per_bucket, state)

    small = [pltpu.make_async_copy(given[i], held[i], sems.at[i]) for i in range(3)]
    for copy in small:
        copy.start()

    def fetch(s):
        rows = pl.ds(pl.multiple_of(s * block, block), block)
        return pltpu.make_async_copy(given[3].at[rows, :], obs_ref.at[rows, :], sems.at[4 + s])

    for s in range(blocks):
        fetch(s).start()
    for copy in small:
        copy.wait()

    inv_row = 1.0 / sigma_ref[...]
    inv_ref[...] = jnp.transpose(jnp.broadcast_to(inv_row, (LANES, sensors)))
    slots = rows_of(buckets_ref[...] ^ me_ref[0], blocks, wide)
    hits = jnp.concatenate(
        [jnp.broadcast_to(row, (groups, block)) == iota((groups, block), 0) for row in slots], axis=0
    )
    upto = (iota((block, block), 0) <= iota((block, block), 1)).astype(F32).astype(BF16)
    running = dot(hits.astype(F32).astype(BF16), upto)
    count = jnp.broadcast_to(running[:, block - 1 : block], (cells, LANES))
    row, col = iota((cells, cells), 0), iota((cells, cells), 1)
    shift = groups.bit_length() - 1
    earlier = ((row & (groups - 1)) == (col & (groups - 1))) & (col < row)
    before = dot(earlier.astype(F32).astype(BF16), count.astype(BF16)).astype(I32)
    odd = before & (SUB - 1)
    tiles = (odd + count.astype(I32) + (SUB - 1)) >> 3
    same = ((row >> shift) == (col >> shift)) & (col < row)
    first = dot(same.astype(F32).astype(BF16), tiles.astype(F32).astype(BF16)).astype(I32)
    lane = iota((cells, LANES), 1)
    kept = jnp.where(tiles > 0, odd, SUB)
    target = jnp.minimum(before >> 3, last_tile)
    final = jnp.maximum(tiles - 1, 0)
    meta = jnp.where(lane == 2, first, final)
    meta = jnp.where(lane == 0, kept, jnp.where(lane == 1, target, meta))
    copy = pltpu.make_async_copy(meta_ref, table, sems.at[3])
    local = first * SUB + odd
    local = jnp.concatenate([local] * wide, axis=1)
    spot = jnp.where(hits, local + running.astype(I32) - 1, 0)
    places = jnp.concatenate(
        [jnp.sum(spot[s * groups : (s + 1) * groups], axis=0, keepdims=True) for s in range(blocks)],
        axis=0,
    )
    slot = iota((cells, LANES), 0) & (groups - 1)
    of_lead = functools.reduce(jnp.logical_or, [slot == v for v in leads])
    longest = jnp.max(jnp.where(of_lead, final, 0))
    inv = jnp.concatenate([inv_ref[...]] * wide, axis=1)
    block_rows = lambda s: pl.ds(pl.multiple_of(s * block, block), block)

    for s in range(blocks):
        if s == blocks // 2:
            meta_ref[...] = meta
            copy.start()
            place_ref[...] = places
        ids = [ids_ref[s * wide + i : s * wide + i + 1, :] for i in range(wide)]
        known = iota((sensors, block), 0) == jnp.concatenate(ids, axis=1)
        scale_row = jnp.sum(jnp.where(known, inv, 0.0), axis=0, keepdims=True)
        scale = jnp.transpose(jnp.broadcast_to(scale_row, (LANES, block)))
        fetch(s).wait()
        rows = block_rows(s)
        high, low = split(obs_ref[rows, :] * jnp.concatenate([scale] * (state // LANES), axis=1))
        pair_ref[rows, :state] = high
        pair_ref[rows, state:] = low

    def sort_into(s, picked, into):
        both = dot(picked.astype(F32).astype(BF16), pair_ref[block_rows(s), :])
        into[...] = both[:, :state] + both[:, state:]

    copy.wait()
    unroll = groups <= 8

    @pl.when((longest < runs.most) & unroll)
    def _():
        for s in range(blocks if unroll else 0):
            into = (small_a, small_b)[s % 2]
            spots = place_ref[s : s + 1, :]
            picked = [iota((some, block), 0) == spots - runs.get(s, v)[2] * SUB for v in leads]
            sort_into(s, jnp.concatenate(picked, axis=0), into)
            for n, v in enumerate(leads):
                runs.place(s, v, outs[n], into, n * some // SUB)

    @pl.when((longest >= runs.most) | (not unroll))
    def _():
        def body(s, carry):
            sort_into(s, iota((padded, block), 0) == place_ref[pl.ds(s, 1), :], sorted_ref)
            for v, out in zip(leads, outs):
                runs.place(s, v, out, sorted_ref)
                runs.place_rest(s, v, out, sorted_ref)
            return carry

        lax.fori_loop(0, blocks, body, 0)

    copies = []
    for m, ((n, first_row, rows), far) in enumerate(zip(parts, far_outs)):
        part = outs_ref.at[n, pl.ds(first_row, rows)]
        copies.append(pltpu.make_async_copy(part, far, sems.at[4 + blocks + m]))
        copies[-1].start()
    for copy in copies:
        copy.wait()


def rest_kernel(groups, per_bucket, others, table, place_ref, pair_ref, *refs):
    outs, (sorted_a, sorted_b) = refs[: len(others)], refs[len(others) :]
    blocks, block = place_ref.shape
    padded, state = sorted_a.shape
    runs = Runs(table, groups, per_bucket, state)

    def sort_block(s, into):
        picked = (iota((padded, block), 0) == place_ref[pl.ds(s, 1), :]).astype(F32).astype(BF16)
        rows = pl.ds(pl.multiple_of(s * block, block), block)
        both = dot(picked, pair_ref[rows, :])
        into[...] = both[:, :state] + both[:, state:]

    longest = 0
    for s in range(blocks):
        for v in range(groups):
            longest = jnp.maximum(longest, table[s * groups + v, 3])
    unroll = groups <= 8

    @pl.when((longest < runs.most) & unroll)
    def _():
        for s in range(blocks if unroll else 0):
            into = (sorted_a, sorted_b)[s % 2]
            sort_block(s, into)
            for v, out in zip(others, outs):
                runs.place(s, v, out, into)

    @pl.when((longest >= runs.most) | (not unroll))
    def _():
        def body(s, carry):
            sort_block(s, sorted_a)
            for v, out in zip(others, outs):
                runs.place(s, v, out, sorted_a)
                runs.place_rest(s, v, out, sorted_a)
            return carry

        lax.fori_loop(0, blocks, body, 0)


def sorted_rows(block, groups):
    return -(-(block + groups * 2 * (SUB - 1)) // 16) * 16


def regroup_lead(observations, sensor_ids, sensor_sigma, buckets, me, groups, leads, parts):
    rows, state = observations.shape
    sensors = sensor_sigma.shape[0]
    block = 256
    blocks = rows // block
    cells = blocks * groups
    per_bucket = rows // groups
    far = pl.BlockSpec(memory_space=pltpu.HBM)
    return pl.pallas_call(
        functools.partial(lead_kernel, groups, per_bucket, tuple(leads), tuple(parts)),
        in_specs=[pl.BlockSpec(memory_space=pltpu.SMEM)] + [far] * 4,
        out_specs=[pl.BlockSpec(memory_space=pl.ANY)] * len(parts)
        + [pl.BlockSpec(memory_space=pltpu.VMEM)] * 3,
        scratch_shapes=[
            pltpu.VMEM((rows // LANES, LANES), I32),
            pltpu.VMEM((rows // LANES, LANES), I32),
            pltpu.VMEM((1, sensors), F32),
            pltpu.VMEM((rows, state), F32),
            pltpu.VMEM((sorted_rows(block, groups), state), F32),
            pltpu.VMEM((64 * len(leads), state), F32),
            pltpu.VMEM((64 * len(leads), state), F32),
            pltpu.VMEM((sensors, LANES), F32),
            pltpu.VMEM((len(leads), per_bucket, state), F32),
            pltpu.SMEM((cells, LANES), I32),
            pltpu.SemaphoreType.DMA((4 + blocks + len(parts),)),
        ],
        out_shape=[jax.ShapeDtypeStruct((part[2], state), F32) for part in parts]
        + [
            jax.ShapeDtypeStruct((rows, 2 * state), BF16),
            jax.ShapeDtypeStruct((blocks, block), I32),
            jax.ShapeDtypeStruct((cells, LANES), I32),
        ],
        compiler_params=pltpu.CompilerParams(vmem_limit_bytes=56 * MIB),
        cost_estimate=pl.CostEstimate(
            flops=rows * state, bytes_accessed=8 * rows * state, transcendentals=0
        ),
    )(
        me.reshape(1),
        buckets.reshape(rows // LANES, LANES),
        sensor_ids.reshape(rows // LANES, LANES),
        sensor_sigma.reshape(1, sensors),
        observations,
    )


def regroup_rest(table, place, pair, groups, others):
    rows, state = pair.shape[0], pair.shape[1] // 2
    per_bucket = rows // groups
    padded = sorted_rows(place.shape[1], groups)
    vmem = pl.BlockSpec(memory_space=pltpu.VMEM)
    return pl.pallas_call(
        functools.partial(rest_kernel, groups, per_bucket, tuple(others)),
        in_specs=[pl.BlockSpec(memory_space=pltpu.SMEM), vmem, vmem],
        out_specs=[vmem] * len(others),
        scratch_shapes=[pltpu.VMEM((padded, state), F32)] * 2,
        out_shape=[jax.ShapeDtypeStruct((per_bucket, state), F32)] * len(others),
        compiler_params=pltpu.CompilerParams(vmem_limit_bytes=14 * MIB),
        cost_estimate=pl.CostEstimate(
            flops=8 * rows * padded * state, bytes_accessed=8 * rows * state, transcendentals=0
        ),
    )(table, place, pair)


def block_pairs(count):
    return [(i, j) for i in range(count) for j in range(i + 1, count)]


def packed_rows_of(state, plane):
    count = state // LANES
    rows = (len(block_pairs(count)) + count // 2) * LANES + SUB
    return -(-rows // (plane * SUB)) * plane * SUB


def write_gram(both, state, out_ref):
    count = state // LANES
    pairs = block_pairs(count)
    row, col = iota((LANES, LANES), 0), iota((LANES, LANES), 1)

    def block(i, j):
        a, b = i * LANES, j * LANES
        cross = both[a : a + LANES, state + b : state + b + LANES]
        turned = both[b : b + LANES, state + a : state + a + LANES]
        return both[a : a + LANES, b : b + LANES] + (cross + jnp.transpose(turned))

    for n, (i, j) in enumerate(pairs):
        out_ref[n * LANES : (n + 1) * LANES, :] = block(i, j)
    tail = (len(pairs) + count // 2) * LANES
    out_ref[tail:, :] = jnp.zeros((out_ref.shape[0] - tail, LANES), F32)
    for m in range(count // 2):
        n = len(pairs) + m
        second = block(2 * m + 1, 2 * m + 1)
        out_ref[n * LANES : (n + 1) * LANES, :] = jnp.where(row <= col, block(2 * m, 2 * m), second)
        diagonal = jnp.sum(jnp.where(row == col, second, 0.0), axis=0, keepdims=True)
        out_ref[tail + m : tail + m + 1, :] = diagonal


def read_gram(value, state, a_ref):
    count = state // LANES
    pairs = block_pairs(count)
    row, col = iota((LANES, LANES), 0), iota((LANES, LANES), 1)
    span = lambda i: slice(i * LANES, (i + 1) * LANES)
    for n, (i, j) in enumerate(pairs):
        a_ref[span(i), span(j)] = value(span(n))
    tail = (len(pairs) + count // 2) * LANES
    for m in range(count // 2):
        mixed = value(span(len(pairs) + m))
        turned = jnp.transpose(mixed)
        i, j = span(2 * m), span(2 * m + 1)
        a_ref[i, i] = jnp.where(row <= col, mixed, turned)
        diagonal = value(slice(tail, tail + SUB))[m : m + 1, :]
        second = jnp.where(row > col, mixed, turned)
        a_ref[j, j] = jnp.where(row == col, diagonal, second)


def gram_kernel(prior_ref, pair_ref, out_ref, prior_out_ref, both_ref):
    state = prior_ref.shape[0]
    both_ref[...] = dot_rows(pair_ref[:, :state], pair_ref[...])
    write_gram(both_ref, state, out_ref)
    high, low = split(prior_ref[...])
    both_ref[...] = dot_rows(high, jnp.concatenate([high, low], axis=1))
    write_gram(both_ref, state, prior_out_ref)


def gram(prior_factor, pair, packed):
    rows, state = pair.shape[0], pair.shape[1] // 2
    vmem = pl.BlockSpec(memory_space=pltpu.VMEM)
    return pl.pallas_call(
        gram_kernel,
        in_specs=[vmem] * 2,
        out_specs=[vmem] * 2,
        out_shape=[jax.ShapeDtypeStruct((packed, LANES), F32)] * 2,
        scratch_shapes=[pltpu.VMEM((state, 2 * state), F32)],
        compiler_params=pltpu.CompilerParams(vmem_limit_bytes=10 * MIB),
        cost_estimate=pl.CostEstimate(
            flops=4 * rows * state * state, bytes_accessed=4 * rows * state, transcendentals=0
        ),
    )(prior_factor, pair)


def scatter_sum(packed, count, groups):
    rows, lanes = packed.shape
    axes = ("rows", "grp")
    got = lax.all_to_all(packed, axes, split_axis=0, concat_axis=0, axis_index_groups=groups, tiled=True)
    return jnp.sum(got.reshape(count, rows // count, lanes), axis=0)


def gather_pieces(piece, count, groups):
    rows, lanes = piece.shape
    copies = jnp.broadcast_to(piece, (count, rows, lanes)).reshape(count * rows, lanes)
    axes = ("rows", "grp")
    return lax.all_to_all(copies, axes, split_axis=0, concat_axis=0, axis_index_groups=groups, tiled=True)


def sweep(a, w):
    width = a.shape[0]
    groups = width // SUB
    row_id = iota((SUB, LANES), 0)
    a_rows = [a[g * SUB : (g + 1) * SUB, :] for g in range(groups)]
    w_rows = [w[g * SUB : (g + 1) * SUB, :] for g in range(groups)]
    for g in range(groups):
        va, vw = a_rows[g], w_rows[g]
        cols = [
            jnp.broadcast_to(va[:, g * SUB + j : g * SUB + j + 1], (SUB, LANES)) for j in range(SUB)
        ]
        scale = jnp.zeros((SUB, LANES), F32)
        for j in range(SUB):
            pivot = jnp.broadcast_to(cols[j][j : j + 1, :], (SUB, LANES))
            root = lax.rsqrt(pivot)
            scale = jnp.where(row_id == j, root, scale)
            if j < SUB - 1:
                ratio = jnp.where(row_id > j, cols[j] * (root * root), 0.0)
                for k in range(j + 1, SUB):
                    cols[k] = cols[k] - ratio * cols[k][j : j + 1, :]
                va = va - ratio * va[j : j + 1, :]
                vw = vw - ratio * vw[j : j + 1, :]
        va, vw = va * scale, vw * scale
        va = jnp.where(iota((SUB, LANES), 1) >= row_id + g * SUB, va, 0.0)
        a_rows[g], w_rows[g] = va, vw
        if g < groups - 1:
            both = jnp.concatenate([va, vw], axis=1)
            high = both.astype(BF16).astype(F32)
            low = both - high
            left = jnp.concatenate([high[:, :LANES], high[:, :LANES], low[:, :LANES]], axis=0)
            right = jnp.concatenate([high, low, high], axis=0)
            change = dot_rows(left.astype(BF16), right.astype(BF16))
            for q in range(g + 1, groups):
                rows = slice(q * SUB, (q + 1) * SUB)
                a_rows[q] = a_rows[q] - change[rows, :LANES]
                w_rows[q] = w_rows[q] - change[rows, LANES:]
    return jnp.concatenate(a_rows, axis=0), jnp.concatenate(w_rows, axis=0)


def factor_kernel(inv_total, sum_ref, prior_ref, factor_ref, high_ref, low_ref, a_ref, x_ref):
    state = factor_ref.shape[0]
    count = state // LANES
    span = lambda i: slice(i * LANES, (i + 1) * LANES)
    read_gram(lambda rows: prior_ref[rows, :] + sum_ref[rows, :] * inv_total, state, a_ref)
    factor_ref[...] = jnp.zeros((state, state), F32)
    x_ref[...] = jnp.zeros((state, state), F32)
    eye = (iota((LANES, LANES), 0) == iota((LANES, LANES), 1)).astype(F32)
    for k in range(count):
        r, w = sweep(a_ref[span(k), span(k)], eye)
        factor_ref[span(k), span(k)] = r
        x = jnp.transpose(w)
        x_ref[span(k), span(k)] = x
        if k > 0:
            left = dot3(x_ref[: k * LANES, : k * LANES], factor_ref[: k * LANES, span(k)])
            x_ref[: k * LANES, span(k)] = -dot3(left, x)
        if k < count - 1:
            rest = slice((k + 1) * LANES, state)
            right = dot3(w, a_ref[span(k), rest])
            factor_ref[span(k), rest] = right
            for i in range(k + 1, count):
                low = slice(i * LANES, state)
                at = (i - k - 1) * LANES
                a_ref[span(i), low] -= dot3_rows(right[:, at : at + LANES], right[:, at:])
    high, low = split(x_ref[...])
    high_ref[...] = high
    low_ref[...] = low


def factorise(summed, prior_gram, state, total_rows):
    vmem = pl.BlockSpec(memory_space=pltpu.VMEM)
    return pl.pallas_call(
        functools.partial(factor_kernel, 1.0 / total_rows),
        in_specs=[vmem] * 2,
        out_specs=[vmem] * 3,
        out_shape=[
            jax.ShapeDtypeStruct((state, state), F32),
            jax.ShapeDtypeStruct((state, state), BF16),
            jax.ShapeDtypeStruct((state, state), BF16),
        ],
        scratch_shapes=[pltpu.VMEM((state, state), F32)] * 2,
        compiler_params=pltpu.CompilerParams(vmem_limit_bytes=16 * MIB),
        cost_estimate=pl.CostEstimate(
            flops=1, bytes_accessed=1, transcendentals=0
        ),
    )(summed, prior_gram)


def whiten_kernel(steps, aliased, per_bucket, me_ref, high_ref, low_ref, *rest):
    count = len(steps)
    chunks = rest[:count]
    out_ref, held, sems = rest[count + aliased :]
    high, low = high_ref[...], low_ref[...]
    copies = []
    for n, (k, offset) in enumerate(steps):
        rows = chunks[n].shape[0]
        rows_high, rows_low = split(chunks[n][...])
        held[n, :rows] = dot(rows_high, high) + (dot(rows_high, low) + dot(rows_low, high))
        first = pl.multiple_of((me_ref[0] ^ k) * per_bucket, per_bucket) + offset
        copy = pltpu.make_async_copy(
            held.at[n, pl.ds(0, rows)],
            out_ref.at[pl.ds(pl.multiple_of(first, SUB), rows), :],
            sems.at[n],
        )
        copy.start()
        copies.append(copy)
    for copy in copies:
        copy.wait()


def whiten(me, high, low, parts, out, rows, groups, cost):
    steps = tuple((k, offset) for k, offset, _ in parts)
    chunks = [chunk for _, _, chunk in parts]
    per_bucket, state = rows // groups, chunks[0].shape[1]
    count = len(chunks)
    vmem = pl.BlockSpec(memory_space=pltpu.VMEM)
    anywhere = pl.BlockSpec(memory_space=pl.ANY)
    extra = [] if out is None else [out]
    return pl.pallas_call(
        functools.partial(whiten_kernel, steps, len(extra), per_bucket),
        in_specs=[pl.BlockSpec(memory_space=pltpu.SMEM)]
        + [vmem] * (2 + count)
        + [anywhere] * len(extra),
        out_specs=anywhere,
        out_shape=jax.ShapeDtypeStruct((rows, state), F32),
        scratch_shapes=[
            pltpu.VMEM((count, per_bucket, state), F32),
            pltpu.SemaphoreType.DMA((count,)),
        ],
        input_output_aliases={3 + count: 0} if extra else {},
        compiler_params=pltpu.CompilerParams(vmem_limit_bytes=16 * MIB),
        cost_estimate=pl.CostEstimate(flops=cost, bytes_accessed=1, transcendentals=0),
    )(me.reshape(1), high, low, *chunks, *extra)


def add_kernel(left, right, out):
    out[...] = left[...] + right[...]


def add(left, right, cost):
    vmem = pl.BlockSpec(memory_space=pltpu.VMEM)
    return pl.pallas_call(
        add_kernel,
        in_specs=[vmem] * 2,
        out_specs=vmem,
        out_shape=jax.ShapeDtypeStruct(left.shape, F32),
        compiler_params=pltpu.CompilerParams(vmem_limit_bytes=4 * MIB),
        cost_estimate=pl.CostEstimate(flops=cost, bytes_accessed=1, transcendentals=0),
    )(left, right)


def behind(value, *arrays):
    return lax.optimization_barrier((value, *arrays))


def shards(observations, sensor_ids, sensor_sigma, buckets, prior_factor):
    rows_dev, state = observations.shape
    groups = lax.axis_size("rows")
    grp = lax.axis_size("grp")
    me = lax.axis_index("rows").astype(I32)
    total_rows = rows_dev * groups * grp
    leads = [k for k in (4, 1) if k < groups]
    others = [k for k in range(groups) if k not in leads]
    per_bucket = rows_dev // groups
    parts = [(n, 0, per_bucket) for n in range(len(leads))]
    *chunks, pair, place, table = regroup_lead(
        observations, sensor_ids, sensor_sigma, buckets, me, groups, leads, parts
    )
    move = lambda k, chunk: lax.ppermute(chunk, "rows", [(i, i ^ k) for i in range(groups)])
    received = {k: move(k, chunk) for k, chunk in zip(leads, chunks)}
    plane = 2 * grp
    packed_rows = packed_rows_of(state, plane)
    planes = [list(range(i, i + plane)) for i in range(0, groups * grp, plane)]
    after = [k for k in (3, *range(7, groups)) if k < groups]
    valid = sensor_sigma[0] > 0
    nothing = lambda rows: jnp.full((rows, LANES), jnp.nan, F32)

    def first():
        packed, prior_gram = gram(prior_factor, pair, packed_rows)
        rest = list(regroup_rest(table, place, pair, groups, others))
        return scatter_sum(packed, plane, planes), prior_gram, rest

    def wrong():
        return nothing(packed_rows // plane), nothing(packed_rows), [jnp.full((per_bucket, state), jnp.nan, F32)] * len(others)

    piece, prior_gram, rest = lax.cond(valid, first, wrong)
    rest = dict(zip(others, rest))
    received[0] = rest[0]
    half = per_bucket // 2 // SUB * SUB
    for k in leads[1:]:
        piece, received[k] = behind(piece, received[k])
    step = 1
    if groups > 6:
        across = move(2, piece)
        received[2] = move(2, behind(piece, rest[2])[1])
        received[leads[0]], chunk = behind(received[leads[0]], rest[6][:half])
        six = [move(6, chunk)]
        piece = add(piece, across, 1441250001)
        step = 2
        chunk = behind(piece, rest[6][half:])[1]
    while step < groups // 2:
        piece = add(piece, move(2 * step, piece), 1441250001)
        step = 2 * step
    if groups > 6:
        six.append(move(6, chunk))
        received[5] = move(5, behind(chunk, rest[5])[1])
    summed = lax.cond(
        valid, lambda: gather_pieces(piece, plane, planes), lambda: nothing(packed_rows)
    )
    if groups > 6:
        summed, six[0] = behind(summed, six[0])
    for k in after:
        received[k] = move(k, behind(summed, rest[k])[1])
    factor, high, low = factorise(summed, prior_gram, state, total_rows)
    whole = lambda *slots: [(k, 0, received[k]) for k in slots if k in received]
    soon, last = whole(0, 1, 4, 2), []
    if groups > 6:
        soon.append((6, 0, six[0]))
        last.append((6, half, six[1]))
    out = None
    for parts, cost in ((soon, 4612000001), (whole(5), 576500001), (whole(*after), 1), (last, 1)):
        if parts:
            out = whiten(me, high, low, parts, out, rows_dev, groups, cost)
    return (out, factor)


def solution(mesh):
    in_specs = (P(("rows", "grp"), None), P(("rows", "grp")), P(), P(("rows", "grp")), P())
    out_specs = (P(("rows", "grp"), None), P())
    return jax.shard_map(shards, mesh=mesh, in_specs=in_specs, out_specs=out_specs, check_vma=False)
```

```python
import functools

import jax
import jax.numpy as jnp
from jax import lax
from jax.experimental import pallas as pl
from jax.experimental.pallas import tpu as pltpu
from jax.sharding import PartitionSpec as P

F32 = jnp.float32
BF16 = jnp.bfloat16
I32 = jnp.int32
LANES = 128
SUB = 8
MIB = 1024 * 1024


def iota(shape, axis):
    return lax.broadcasted_iota(I32, shape, axis)


def split(values):
    high = values.astype(BF16)
    low = (values - high.astype(F32)).astype(BF16)
    return high, low


def dot(left, right):
    return jnp.dot(left, right, preferred_element_type=F32)


def dot_rows(left, right):
    return lax.dot_general(left, right, (((0,), (0,)), ((), ())), preferred_element_type=F32)


def dot3(left, right):
    lh, ll = split(left)
    rh, rl = split(right)
    return dot(lh, rh) + (dot(lh, rl) + dot(ll, rh))


def dot3_rows(left, right):
    lh, ll = split(left)
    rh, rl = split(right)
    return dot_rows(lh, rh) + (dot_rows(lh, rl) + dot_rows(ll, rh))


def rows_of(packed, count, wide):
    return [
        jnp.concatenate([packed[s * wide + i : s * wide + i + 1, :] for i in range(wide)], axis=1)
        for s in range(count)
    ]


def tile(t):
    return pl.ds(pl.multiple_of(t * SUB, SUB), SUB)


class Runs:
    def __init__(self, table, groups, per_bucket, state):
        self.table, self.groups = table, groups
        self.most = min(7, per_bucket // SUB + 1)
        self.sub_row = iota((SUB, state), 0)

    def get(self, s, v):
        return [self.table[s * self.groups + v, i] for i in range(4)]

    def place(self, s, v, out, source, base=None):
        kept, target, first, final = self.get(s, v)
        first = first if base is None else base
        old = out[tile(target), :]
        for t in reversed(range(1, self.most)):
            t = jnp.minimum(t, final)
            out[tile(target + t), :] = source[tile(first + t), :]
        out[tile(target), :] = jnp.where(self.sub_row < kept, old, source[tile(first), :])

    def place_rest(self, s, v, out, source):
        _, target, first, final = self.get(s, v)

        def longer(t, carry):
            out[tile(target + t), :] = source[tile(first + t), :]
            return carry

        lax.fori_loop(self.most, final + 1, longer, 0)


def lead_kernel(groups, per_bucket, leads, parts, me_ref, *refs):
    given, far_outs, refs = refs[:4], refs[4 : 4 + len(parts)], refs[4 + len(parts) :]
    (pair_ref, place_ref, meta_ref), held, scratch = refs[:3], refs[3:7], refs[7:]
    sorted_ref, small_a, small_b, inv_ref, outs_ref, table, sems = scratch
    outs = [outs_ref.at[n] for n in range(len(leads))]
    some = small_a.shape[0] // len(leads)
    buckets_ref, ids_ref, sigma_ref, obs_ref = held
    blocks, block = place_ref.shape
    wide = block // LANES
    sensors = sigma_ref.shape[1]
    padded, state = sorted_ref.shape
    cells = blocks * groups
    last_tile = per_bucket // SUB - 1
    runs = Runs(table, groups, per_bucket, state)

    small = [pltpu.make_async_copy(given[i], held[i], sems.at[i]) for i in range(3)]
    for copy in small:
        copy.start()

    def fetch(s):
        rows = pl.ds(s * block, 2 * block)
        return pltpu.make_async_copy(given[3].at[rows, :], obs_ref.at[rows, :], sems.at[4 + s])

    for s in range(0, blocks, 2):
        fetch(s).start()
    for copy in small:
        copy.wait()

    inv_row = 1.0 / sigma_ref[...]
    inv_ref[...] = jnp.transpose(jnp.broadcast_to(inv_row, (LANES, sensors)))
    slots = rows_of(buckets_ref[...] ^ me_ref[0], blocks, wide)
    hits = jnp.concatenate(
        [jnp.broadcast_to(row, (groups, block)) == iota((groups, block), 0) for row in slots], axis=0
    )
    upto = (iota((block, block), 0) <= iota((block, block), 1)).astype(F32).astype(BF16)
    running = dot(hits.astype(F32).astype(BF16), upto)
    count = jnp.broadcast_to(running[:, block - 1 : block], (cells, LANES))
    row, col = iota((cells, cells), 0), iota((cells, cells), 1)
    shift = groups.bit_length() - 1
    earlier = ((row & (groups - 1)) == (col & (groups - 1))) & (col < row)
    before = dot(earlier.astype(F32).astype(BF16), count.astype(BF16)).astype(I32)
    odd = before & (SUB - 1)
    tiles = (odd + count.astype(I32) + (SUB - 1)) >> 3
    same = ((row >> shift) == (col >> shift)) & (col < row)
    first = dot(same.astype(F32).astype(BF16), tiles.astype(F32).astype(BF16)).astype(I32)
    lane = iota((cells, LANES), 1)
    kept = jnp.where(tiles > 0, odd, SUB)
    target = jnp.minimum(before >> 3, last_tile)
    final = jnp.maximum(tiles - 1, 0)
    meta = jnp.where(lane == 2, first, final)
    meta = jnp.where(lane == 0, kept, jnp.where(lane == 1, target, meta))
    copy = pltpu.make_async_copy(meta_ref, table, sems.at[3])
    local = first * SUB + odd
    local = jnp.concatenate([local] * wide, axis=1)
    spot = jnp.where(hits, local + running.astype(I32) - 1, 0)
    places = jnp.concatenate(
        [jnp.sum(spot[s * groups : (s + 1) * groups], axis=0, keepdims=True) for s in range(blocks)],
        axis=0,
    )
    slot = iota((cells, LANES), 0) & (groups - 1)
    of_lead = functools.reduce(jnp.logical_or, [slot == v for v in leads])
    longest = jnp.max(jnp.where(of_lead, final, 0))
    inv = jnp.concatenate([inv_ref[...]] * wide, axis=1)
    block_rows = lambda s: pl.ds(pl.multiple_of(s * block, block), block)

    scales = []
    for s in range(blocks):
        ids = [ids_ref[s * wide + i : s * wide + i + 1, :] for i in range(wide)]
        known = iota((sensors, block), 0) == jnp.concatenate(ids, axis=1)
        scale_row = jnp.sum(jnp.where(known, inv, 0.0), axis=0, keepdims=True)
        scales += [scale_row[:, i * LANES : (i + 1) * LANES] for i in range(wide)]
    scales.append(jnp.zeros((-len(scales) % LANES, LANES), F32))
    turned = jnp.transpose(jnp.concatenate(scales, axis=0))
    for s in range(blocks):
        if s == blocks // 2:
            meta_ref[...] = meta
            copy.start()
            place_ref[...] = places
        if s % 2 == 0:
            fetch(s).wait()
        spread = [
            jnp.broadcast_to(turned[:, c : c + 1], (LANES, LANES))
            for c in range(s * wide, (s + 1) * wide)
        ]
        scale = jnp.concatenate(spread, axis=0)
        rows = block_rows(s)
        high, low = split(obs_ref[rows, :] * jnp.concatenate([scale] * (state // LANES), axis=1))
        pair_ref[rows, :state] = high
        pair_ref[rows, state:] = low

    def sort_into(s, picked, into):
        both = dot(picked.astype(F32).astype(BF16), pair_ref[block_rows(s), :])
        into[...] = both[:, :state] + both[:, state:]

    copy.wait()
    unroll = groups <= 8

    @pl.when((longest < runs.most) & unroll)
    def _():
        for s in range(blocks if unroll else 0):
            into = (small_a, small_b)[s % 2]
            spots = place_ref[s : s + 1, :]
            picked = [iota((some, block), 0) == spots - runs.get(s, v)[2] * SUB for v in leads]
            sort_into(s, jnp.concatenate(picked, axis=0), into)
            for n, v in enumerate(leads):
                runs.place(s, v, outs[n], into, n * some // SUB)

    @pl.when((longest >= runs.most) | (not unroll))
    def _():
        def body(s, carry):
            sort_into(s, iota((padded, block), 0) == place_ref[pl.ds(s, 1), :], sorted_ref)
            for v, out in zip(leads, outs):
                runs.place(s, v, out, sorted_ref)
                runs.place_rest(s, v, out, sorted_ref)
            return carry

        lax.fori_loop(0, blocks, body, 0)

    copies = []
    for m, ((n, first_row, rows), far) in enumerate(zip(parts, far_outs)):
        part = outs_ref.at[n, pl.ds(first_row, rows)]
        copies.append(pltpu.make_async_copy(part, far, sems.at[4 + blocks + m]))
        copies[-1].start()
    for copy in copies:
        copy.wait()


def rest_kernel(groups, per_bucket, others, table, place_ref, pair_ref, *refs):
    outs, (sorted_a, sorted_b) = refs[: len(others)], refs[len(others) :]
    blocks, block = place_ref.shape
    padded, state = sorted_a.shape
    runs = Runs(table, groups, per_bucket, state)

    def sort_block(s, into):
        picked = (iota((padded, block), 0) == place_ref[pl.ds(s, 1), :]).astype(F32).astype(BF16)
        rows = pl.ds(pl.multiple_of(s * block, block), block)
        both = dot(picked, pair_ref[rows, :])
        into[...] = both[:, :state] + both[:, state:]

    longest = 0
    for s in range(blocks):
        for v in range(groups):
            longest = jnp.maximum(longest, table[s * groups + v, 3])
    unroll = groups <= 8

    @pl.when((longest < runs.most) & unroll)
    def _():
        for s in range(blocks if unroll else 0):
            into = (sorted_a, sorted_b)[s % 2]
            sort_block(s, into)
            for v, out in zip(others, outs):
                runs.place(s, v, out, into)

    @pl.when((longest >= runs.most) | (not unroll))
    def _():
        def body(s, carry):
            sort_block(s, sorted_a)
            for v, out in zip(others, outs):
                runs.place(s, v, out, sorted_a)
                runs.place_rest(s, v, out, sorted_a)
            return carry

        lax.fori_loop(0, blocks, body, 0)


def sorted_rows(block, groups):
    return -(-(block + groups * 2 * (SUB - 1)) // 16) * 16


def regroup_lead(observations, sensor_ids, sensor_sigma, buckets, me, groups, leads, parts):
    rows, state = observations.shape
    sensors = sensor_sigma.shape[0]
    block = 256
    blocks = rows // block
    cells = blocks * groups
    per_bucket = rows // groups
    far = pl.BlockSpec(memory_space=pltpu.HBM)
    return pl.pallas_call(
        functools.partial(lead_kernel, groups, per_bucket, tuple(leads), tuple(parts)),
        in_specs=[pl.BlockSpec(memory_space=pltpu.SMEM)] + [far] * 4,
        out_specs=[pl.BlockSpec(memory_space=pl.ANY)] * len(parts)
        + [pl.BlockSpec(memory_space=pltpu.VMEM)] * 3,
        scratch_shapes=[
            pltpu.VMEM((rows // LANES, LANES), I32),
            pltpu.VMEM((rows // LANES, LANES), I32),
            pltpu.VMEM((1, sensors), F32),
            pltpu.VMEM((rows, state), F32),
            pltpu.VMEM((sorted_rows(block, groups), state), F32),
            pltpu.VMEM((64 * len(leads), state), F32),
            pltpu.VMEM((64 * len(leads), state), F32),
            pltpu.VMEM((sensors, LANES), F32),
            pltpu.VMEM((len(leads), per_bucket, state), F32),
            pltpu.SMEM((cells, LANES), I32),
            pltpu.SemaphoreType.DMA((4 + blocks + len(parts),)),
        ],
        out_shape=[jax.ShapeDtypeStruct((part[2], state), F32) for part in parts]
        + [
            jax.ShapeDtypeStruct((rows, 2 * state), BF16),
            jax.ShapeDtypeStruct((blocks, block), I32),
            jax.ShapeDtypeStruct((cells, LANES), I32),
        ],
        compiler_params=pltpu.CompilerParams(vmem_limit_bytes=56 * MIB),
        cost_estimate=pl.CostEstimate(
            flops=rows * state, bytes_accessed=8 * rows * state, transcendentals=0
        ),
    )(
        me.reshape(1),
        buckets.reshape(rows // LANES, LANES),
        sensor_ids.reshape(rows // LANES, LANES),
        sensor_sigma.reshape(1, sensors),
        observations,
    )


def regroup_rest(table, place, pair, groups, others):
    rows, state = pair.shape[0], pair.shape[1] // 2
    per_bucket = rows // groups
    padded = sorted_rows(place.shape[1], groups)
    vmem = pl.BlockSpec(memory_space=pltpu.VMEM)
    return pl.pallas_call(
        functools.partial(rest_kernel, groups, per_bucket, tuple(others)),
        in_specs=[pl.BlockSpec(memory_space=pltpu.SMEM), vmem, vmem],
        out_specs=[vmem] * len(others),
        scratch_shapes=[pltpu.VMEM((padded, state), F32)] * 2,
        out_shape=[jax.ShapeDtypeStruct((per_bucket, state), F32)] * len(others),
        compiler_params=pltpu.CompilerParams(vmem_limit_bytes=14 * MIB),
        cost_estimate=pl.CostEstimate(
            flops=8 * rows * padded * state, bytes_accessed=8 * rows * state, transcendentals=0
        ),
    )(table, place, pair)


def block_pairs(count):
    return [(i, j) for i in range(count) for j in range(i + 1, count)]


def packed_rows_of(state, plane):
    count = state // LANES
    rows = (len(block_pairs(count)) + count // 2) * LANES + SUB
    return -(-rows // (plane * SUB)) * plane * SUB


def write_gram(both, state, out_ref):
    count = state // LANES
    pairs = block_pairs(count)
    row, col = iota((LANES, LANES), 0), iota((LANES, LANES), 1)

    def block(i, j):
        a, b = i * LANES, j * LANES
        cross = both[a : a + LANES, state + b : state + b + LANES]
        turned = both[b : b + LANES, state + a : state + a + LANES]
        return both[a : a + LANES, b : b + LANES] + (cross + jnp.transpose(turned))

    for n, (i, j) in enumerate(pairs):
        out_ref[n * LANES : (n + 1) * LANES, :] = block(i, j)
    tail = (len(pairs) + count // 2) * LANES
    out_ref[tail:, :] = jnp.zeros((out_ref.shape[0] - tail, LANES), F32)
    for m in range(count // 2):
        n = len(pairs) + m
        second = block(2 * m + 1, 2 * m + 1)
        out_ref[n * LANES : (n + 1) * LANES, :] = jnp.where(row <= col, block(2 * m, 2 * m), second)
        diagonal = jnp.sum(jnp.where(row == col, second, 0.0), axis=0, keepdims=True)
        out_ref[tail + m : tail + m + 1, :] = diagonal


def read_gram(value, state, a_ref):
    count = state // LANES
    pairs = block_pairs(count)
    row, col = iota((LANES, LANES), 0), iota((LANES, LANES), 1)
    span = lambda i: slice(i * LANES, (i + 1) * LANES)
    for n, (i, j) in enumerate(pairs):
        a_ref[span(i), span(j)] = value(span(n))
    tail = (len(pairs) + count // 2) * LANES
    for m in range(count // 2):
        mixed = value(span(len(pairs) + m))
        turned = jnp.transpose(mixed)
        i, j = span(2 * m), span(2 * m + 1)
        a_ref[i, i] = jnp.where(row <= col, mixed, turned)
        diagonal = value(slice(tail, tail + SUB))[m : m + 1, :]
        second = jnp.where(row > col, mixed, turned)
        a_ref[j, j] = jnp.where(row == col, diagonal, second)


def gram_kernel(prior_ref, pair_ref, out_ref, prior_out_ref, both_ref):
    state = prior_ref.shape[0]
    both_ref[...] = dot_rows(pair_ref[:, :state], pair_ref[...])
    write_gram(both_ref, state, out_ref)
    high, low = split(prior_ref[...])
    both_ref[...] = dot_rows(high, jnp.concatenate([high, low], axis=1))
    write_gram(both_ref, state, prior_out_ref)


def gram(prior_factor, pair, packed):
    rows, state = pair.shape[0], pair.shape[1] // 2
    vmem = pl.BlockSpec(memory_space=pltpu.VMEM)
    return pl.pallas_call(
        gram_kernel,
        in_specs=[vmem] * 2,
        out_specs=[vmem] * 2,
        out_shape=[jax.ShapeDtypeStruct((packed, LANES), F32)] * 2,
        scratch_shapes=[pltpu.VMEM((state, 2 * state), F32)],
        compiler_params=pltpu.CompilerParams(vmem_limit_bytes=10 * MIB),
        cost_estimate=pl.CostEstimate(
            flops=4 * rows * state * state, bytes_accessed=4 * rows * state, transcendentals=0
        ),
    )(prior_factor, pair)


def scatter_sum(packed, count, groups):
    rows, lanes = packed.shape
    axes = ("rows", "grp")
    got = lax.all_to_all(packed, axes, split_axis=0, concat_axis=0, axis_index_groups=groups, tiled=True)
    return jnp.sum(got.reshape(count, rows // count, lanes), axis=0)


def gather_pieces(piece, count, groups):
    rows, lanes = piece.shape
    copies = jnp.broadcast_to(piece, (count, rows, lanes)).reshape(count * rows, lanes)
    axes = ("rows", "grp")
    return lax.all_to_all(copies, axes, split_axis=0, concat_axis=0, axis_index_groups=groups, tiled=True)


def sweep(a, w):
    width = a.shape[0]
    groups = width // SUB
    row_id = iota((SUB, LANES), 0)
    a_rows = [a[g * SUB : (g + 1) * SUB, :] for g in range(groups)]
    w_rows = [w[g * SUB : (g + 1) * SUB, :] for g in range(groups)]
    for g in range(groups):
        va, vw = a_rows[g], w_rows[g]
        cols = [
            jnp.broadcast_to(va[:, g * SUB + j : g * SUB + j + 1], (SUB, LANES)) for j in range(SUB)
        ]
        scale = jnp.zeros((SUB, LANES), F32)
        for j in range(SUB):
            pivot = jnp.broadcast_to(cols[j][j : j + 1, :], (SUB, LANES))
            root = lax.rsqrt(pivot)
            scale = jnp.where(row_id == j, root, scale)
            if j < SUB - 1:
                ratio = jnp.where(row_id > j, cols[j] * (root * root), 0.0)
                for k in range(j + 1, SUB):
                    cols[k] = cols[k] - ratio * cols[k][j : j + 1, :]
                va = va - ratio * va[j : j + 1, :]
                vw = vw - ratio * vw[j : j + 1, :]
        va, vw = va * scale, vw * scale
        va = jnp.where(iota((SUB, LANES), 1) >= row_id + g * SUB, va, 0.0)
        a_rows[g], w_rows[g] = va, vw
        if g < groups - 1:
            both = jnp.concatenate([va, vw], axis=1)
            high = both.astype(BF16).astype(F32)
            low = both - high
            left = jnp.concatenate([high[:, :LANES], high[:, :LANES], low[:, :LANES]], axis=0)
            right = jnp.concatenate([high, low, high], axis=0)
            change = dot_rows(left.astype(BF16), right.astype(BF16))
            for q in range(g + 1, groups):
                rows = slice(q * SUB, (q + 1) * SUB)
                a_rows[q] = a_rows[q] - change[rows, :LANES]
                w_rows[q] = w_rows[q] - change[rows, LANES:]
    return jnp.concatenate(a_rows, axis=0), jnp.concatenate(w_rows, axis=0)


def factor_kernel(inv_total, sum_ref, prior_ref, factor_ref, high_ref, low_ref, a_ref, x_ref):
    state = factor_ref.shape[0]
    count = state // LANES
    span = lambda i: slice(i * LANES, (i + 1) * LANES)
    read_gram(lambda rows: prior_ref[rows, :] + sum_ref[rows, :] * inv_total, state, a_ref)
    factor_ref[...] = jnp.zeros((state, state), F32)
    x_ref[...] = jnp.zeros((state, state), F32)
    eye = (iota((LANES, LANES), 0) == iota((LANES, LANES), 1)).astype(F32)
    for k in range(count):
        r, w = sweep(a_ref[span(k), span(k)], eye)
        factor_ref[span(k), span(k)] = r
        x = jnp.transpose(w)
        x_ref[span(k), span(k)] = x
        if k > 0:
            left = dot3(x_ref[: k * LANES, : k * LANES], factor_ref[: k * LANES, span(k)])
            x_ref[: k * LANES, span(k)] = -dot3(left, x)
        if k < count - 1:
            rest = slice((k + 1) * LANES, state)
            right = dot3(w, a_ref[span(k), rest])
            factor_ref[span(k), rest] = right
            for i in range(k + 1, count):
                low = slice(i * LANES, state)
                at = (i - k - 1) * LANES
                a_ref[span(i), low] -= dot3_rows(right[:, at : at + LANES], right[:, at:])
    high, low = split(x_ref[...])
    high_ref[...] = high
    low_ref[...] = low


def factorise(summed, prior_gram, state, total_rows):
    vmem = pl.BlockSpec(memory_space=pltpu.VMEM)
    return pl.pallas_call(
        functools.partial(factor_kernel, 1.0 / total_rows),
        in_specs=[vmem] * 2,
        out_specs=[vmem] * 3,
        out_shape=[
            jax.ShapeDtypeStruct((state, state), F32),
            jax.ShapeDtypeStruct((state, state), BF16),
            jax.ShapeDtypeStruct((state, state), BF16),
        ],
        scratch_shapes=[pltpu.VMEM((state, state), F32)] * 2,
        compiler_params=pltpu.CompilerParams(vmem_limit_bytes=16 * MIB),
        cost_estimate=pl.CostEstimate(
            flops=1, bytes_accessed=1, transcendentals=0
        ),
    )(summed, prior_gram)


def whiten_kernel(steps, aliased, per_bucket, me_ref, high_ref, low_ref, *rest):
    count = len(steps)
    chunks = rest[:count]
    out_ref, held, sems = rest[count + aliased :]
    high, low = high_ref[...], low_ref[...]
    copies = []
    for n, (k, offset) in enumerate(steps):
        rows = chunks[n].shape[0]
        rows_high, rows_low = split(chunks[n][...])
        held[n, :rows] = dot(rows_high, high) + (dot(rows_high, low) + dot(rows_low, high))
        first = pl.multiple_of((me_ref[0] ^ k) * per_bucket, per_bucket) + offset
        copy = pltpu.make_async_copy(
            held.at[n, pl.ds(0, rows)],
            out_ref.at[pl.ds(pl.multiple_of(first, SUB), rows), :],
            sems.at[n],
        )
        copy.start()
        copies.append(copy)
    for copy in copies:
        copy.wait()


def whiten(me, high, low, parts, out, rows, groups):
    steps = tuple((k, offset) for k, offset, _ in parts)
    chunks = [chunk for _, _, chunk in parts]
    per_bucket, state = rows // groups, chunks[0].shape[1]
    count = len(chunks)
    vmem = pl.BlockSpec(memory_space=pltpu.VMEM)
    anywhere = pl.BlockSpec(memory_space=pl.ANY)
    extra = [] if out is None else [out]
    return pl.pallas_call(
        functools.partial(whiten_kernel, steps, len(extra), per_bucket),
        in_specs=[pl.BlockSpec(memory_space=pltpu.SMEM)]
        + [vmem] * (2 + count)
        + [anywhere] * len(extra),
        out_specs=anywhere,
        out_shape=jax.ShapeDtypeStruct((rows, state), F32),
        scratch_shapes=[
            pltpu.VMEM((count, per_bucket, state), F32),
            pltpu.SemaphoreType.DMA((count,)),
        ],
        input_output_aliases={3 + count: 0} if extra else {},
        compiler_params=pltpu.CompilerParams(vmem_limit_bytes=16 * MIB),
        cost_estimate=pl.CostEstimate(flops=1, bytes_accessed=1, transcendentals=0),
    )(me.reshape(1), high, low, *chunks, *extra)


def behind(value, *arrays):
    return lax.optimization_barrier((value, *arrays))


def shards(observations, sensor_ids, sensor_sigma, buckets, prior_factor):
    rows_dev, state = observations.shape
    groups = lax.axis_size("rows")
    grp = lax.axis_size("grp")
    me = lax.axis_index("rows").astype(I32)
    total_rows = rows_dev * groups * grp
    leads = [k for k in (4, 1) if k < groups]
    others = [k for k in range(groups) if k not in leads]
    per_bucket = rows_dev // groups
    parts = [(n, 0, per_bucket) for n in range(len(leads))]
    *chunks, pair, place, table = regroup_lead(
        observations, sensor_ids, sensor_sigma, buckets, me, groups, leads, parts
    )
    move = lambda k, chunk: lax.ppermute(chunk, "rows", [(i, i ^ k) for i in range(groups)])
    received = {k: move(k, chunk) for k, chunk in zip(leads, chunks)}
    plane = 2 * grp
    packed_rows = packed_rows_of(state, plane)
    planes = [list(range(i, i + plane)) for i in range(0, groups * grp, plane)]
    middle = [k for k in (2, 6) if k < groups]
    late = [k for k in (5, 3, *range(7, groups)) if k < groups]
    valid = sensor_sigma[0] > 0
    nothing = lambda rows: jnp.full((rows, LANES), jnp.nan, F32)

    def first():
        packed, prior_gram = gram(prior_factor, pair, packed_rows)
        rest = list(regroup_rest(table, place, pair, groups, others))
        return scatter_sum(packed, plane, planes), prior_gram, rest

    def wrong():
        return nothing(packed_rows // plane), nothing(packed_rows), [jnp.full((per_bucket, state), jnp.nan, F32)] * len(others)

    piece, prior_gram, rest = lax.cond(valid, first, wrong)
    rest = dict(zip(others, rest))
    received[0] = rest[0]
    for k in leads[1:]:
        piece, received[k] = behind(piece, received[k])
    across = [piece]
    for step in range(1, groups // 2):
        across.append(move(2 * step, piece))
    for k in middle[:1]:
        received[k] = move(k, behind(piece, rest[k])[1])
    while len(across) > 1:
        across = [across[i] + across[i + 1] for i in range(0, len(across), 2)]
    for k in middle[1:]:
        received[leads[0]], chunk = behind(received[leads[0]], rest[k])
        received[k] = move(k, chunk)
    across[0], received[leads[0]] = behind(across[0], received[leads[0]])
    for k in late[:1]:
        received[k] = move(k, behind(across[0], rest[k])[1])
    summed = lax.cond(
        valid, lambda: gather_pieces(across[0], plane, planes), lambda: nothing(packed_rows)
    )
    for k in late[1:]:
        received[k] = move(k, behind(summed, rest[k])[1])
    factor, high, low = factorise(summed, prior_gram, state, total_rows)
    whole = lambda slots: [(k, 0, received[k]) for k in slots]
    out = None
    for parts in (whole([0, *leads, *middle]), whole(late[:-1]), whole(late[-1:])):
        if parts:
            out = whiten(me, high, low, parts, out, rows_dev, groups)
    return (out, factor)


def solution(mesh):
    in_specs = (P(("rows", "grp"), None), P(("rows", "grp")), P(), P(("rows", "grp")), P())
    out_specs = (P(("rows", "grp"), None), P())
    return jax.shard_map(shards, mesh=mesh, in_specs=in_specs, out_specs=out_specs, check_vma=False)
```

```python
import functools

import jax
import jax.numpy as jnp
from jax import lax
from jax.experimental import pallas as pl
from jax.experimental.pallas import tpu as pltpu
from jax.sharding import PartitionSpec as P

F32 = jnp.float32
BF16 = jnp.bfloat16
I32 = jnp.int32
LANES = 128
SUB = 8
MIB = 1024 * 1024


def iota(shape, axis):
    return lax.broadcasted_iota(I32, shape, axis)


def split(values):
    high = values.astype(BF16)
    low = (values - high.astype(F32)).astype(BF16)
    return high, low


def dot(left, right):
    return jnp.dot(left, right, preferred_element_type=F32)


def dot_rows(left, right):
    return lax.dot_general(left, right, (((0,), (0,)), ((), ())), preferred_element_type=F32)


def dot3(left, right):
    lh, ll = split(left)
    rh, rl = split(right)
    return dot(lh, rh) + (dot(lh, rl) + dot(ll, rh))


def dot3_rows(left, right):
    lh, ll = split(left)
    rh, rl = split(right)
    return dot_rows(lh, rh) + (dot_rows(lh, rl) + dot_rows(ll, rh))


def rows_of(packed, count, wide):
    return [
        jnp.concatenate([packed[s * wide + i : s * wide + i + 1, :] for i in range(wide)], axis=1)
        for s in range(count)
    ]


def tile(t):
    return pl.ds(pl.multiple_of(t * SUB, SUB), SUB)


class Runs:
    def __init__(self, table, groups, per_bucket, state):
        self.table, self.groups = table, groups
        self.most = min(7, per_bucket // SUB + 1)
        self.sub_row = iota((SUB, state), 0)

    def get(self, s, v):
        return [self.table[s * self.groups + v, i] for i in range(4)]

    def place(self, s, v, out, source, base=None):
        kept, target, first, final = self.get(s, v)
        first = first if base is None else base
        old = out[tile(target), :]
        for t in reversed(range(1, self.most)):
            t = jnp.minimum(t, final)
            out[tile(target + t), :] = source[tile(first + t), :]
        out[tile(target), :] = jnp.where(self.sub_row < kept, old, source[tile(first), :])

    def place_rest(self, s, v, out, source):
        _, target, first, final = self.get(s, v)

        def longer(t, carry):
            out[tile(target + t), :] = source[tile(first + t), :]
            return carry

        lax.fori_loop(self.most, final + 1, longer, 0)


def lead_kernel(groups, per_bucket, leads, parts, me_ref, *refs):
    given, far_outs, refs = refs[:4], refs[4 : 4 + len(parts)], refs[4 + len(parts) :]
    (pair_ref, place_ref, meta_ref), held, scratch = refs[:3], refs[3:7], refs[7:]
    sorted_ref, small_a, small_b, inv_ref, outs_ref, table, sems = scratch
    outs = [outs_ref.at[n] for n in range(len(leads))]
    some = small_a.shape[0] // len(leads)
    buckets_ref, ids_ref, sigma_ref, obs_ref = held
    blocks, block = place_ref.shape
    wide = block // LANES
    sensors = sigma_ref.shape[1]
    padded, state = sorted_ref.shape
    cells = blocks * groups
    last_tile = per_bucket // SUB - 1
    runs = Runs(table, groups, per_bucket, state)

    small = [pltpu.make_async_copy(given[i], held[i], sems.at[i]) for i in range(3)]
    for copy in small:
        copy.start()

    def fetch(s):
        rows = pl.ds(s * block, 2 * block)
        return pltpu.make_async_copy(given[3].at[rows, :], obs_ref.at[rows, :], sems.at[4 + s])

    for s in range(0, blocks, 2):
        fetch(s).start()
    for copy in small:
        copy.wait()

    inv_row = 1.0 / sigma_ref[...]
    inv_ref[...] = jnp.transpose(jnp.broadcast_to(inv_row, (LANES, sensors)))
    slots = rows_of(buckets_ref[...] ^ me_ref[0], blocks, wide)
    hits = jnp.concatenate(
        [jnp.broadcast_to(row, (groups, block)) == iota((groups, block), 0) for row in slots], axis=0
    )
    upto = (iota((block, block), 0) <= iota((block, block), 1)).astype(F32).astype(BF16)
    running = dot(hits.astype(F32).astype(BF16), upto)
    count = jnp.broadcast_to(running[:, block - 1 : block], (cells, LANES))
    row, col = iota((cells, cells), 0), iota((cells, cells), 1)
    shift = groups.bit_length() - 1
    earlier = ((row & (groups - 1)) == (col & (groups - 1))) & (col < row)
    before = dot(earlier.astype(F32).astype(BF16), count.astype(BF16)).astype(I32)
    odd = before & (SUB - 1)
    tiles = (odd + count.astype(I32) + (SUB - 1)) >> 3
    same = ((row >> shift) == (col >> shift)) & (col < row)
    first = dot(same.astype(F32).astype(BF16), tiles.astype(F32).astype(BF16)).astype(I32)
    lane = iota((cells, LANES), 1)
    kept = jnp.where(tiles > 0, odd, SUB)
    target = jnp.minimum(before >> 3, last_tile)
    final = jnp.maximum(tiles - 1, 0)
    meta = jnp.where(lane == 2, first, final)
    meta = jnp.where(lane == 0, kept, jnp.where(lane == 1, target, meta))
    copy = pltpu.make_async_copy(meta_ref, table, sems.at[3])
    local = first * SUB + odd
    local = jnp.concatenate([local] * wide, axis=1)
    spot = jnp.where(hits, local + running.astype(I32) - 1, 0)
    places = jnp.concatenate(
        [jnp.sum(spot[s * groups : (s + 1) * groups], axis=0, keepdims=True) for s in range(blocks)],
        axis=0,
    )
    slot = iota((cells, LANES), 0) & (groups - 1)
    of_lead = functools.reduce(jnp.logical_or, [slot == v for v in leads])
    longest = jnp.max(jnp.where(of_lead, final, 0))
    inv = jnp.concatenate([inv_ref[...]] * wide, axis=1)
    block_rows = lambda s: pl.ds(pl.multiple_of(s * block, block), block)

    scales = []
    for s in range(blocks):
        ids = [ids_ref[s * wide + i : s * wide + i + 1, :] for i in range(wide)]
        known = iota((sensors, block), 0) == jnp.concatenate(ids, axis=1)
        scale_row = jnp.sum(jnp.where(known, inv, 0.0), axis=0, keepdims=True)
        scales += [scale_row[:, i * LANES : (i + 1) * LANES] for i in range(wide)]
    scales.append(jnp.zeros((-len(scales) % LANES, LANES), F32))
    turned = jnp.transpose(jnp.concatenate(scales, axis=0))
    for s in range(blocks):
        if s == blocks // 2:
            meta_ref[...] = meta
            copy.start()
            place_ref[...] = places
        if s % 2 == 0:
            fetch(s).wait()
        spread = [
            jnp.broadcast_to(turned[:, c : c + 1], (LANES, LANES))
            for c in range(s * wide, (s + 1) * wide)
        ]
        scale = jnp.concatenate(spread, axis=0)
        rows = block_rows(s)
        high, low = split(obs_ref[rows, :] * jnp.concatenate([scale] * (state // LANES), axis=1))
        pair_ref[rows, :state] = high
        pair_ref[rows, state:] = low

    def sort_into(s, picked, into):
        both = dot(picked.astype(F32).astype(BF16), pair_ref[block_rows(s), :])
        into[...] = both[:, :state] + both[:, state:]

    copy.wait()
    unroll = groups <= 8

    @pl.when((longest < runs.most) & unroll)
    def _():
        for s in range(blocks if unroll else 0):
            into = (small_a, small_b)[s % 2]
            spots = place_ref[s : s + 1, :]
            picked = [iota((some, block), 0) == spots - runs.get(s, v)[2] * SUB for v in leads]
            sort_into(s, jnp.concatenate(picked, axis=0), into)
            for n, v in enumerate(leads):
                runs.place(s, v, outs[n], into, n * some // SUB)

    @pl.when((longest >= runs.most) | (not unroll))
    def _():
        def body(s, carry):
            sort_into(s, iota((padded, block), 0) == place_ref[pl.ds(s, 1), :], sorted_ref)
            for v, out in zip(leads, outs):
                runs.place(s, v, out, sorted_ref)
                runs.place_rest(s, v, out, sorted_ref)
            return carry

        lax.fori_loop(0, blocks, body, 0)

    copies = []
    for m, ((n, first_row, rows), far) in enumerate(zip(parts, far_outs)):
        part = outs_ref.at[n, pl.ds(first_row, rows)]
        copies.append(pltpu.make_async_copy(part, far, sems.at[4 + blocks + m]))
        copies[-1].start()
    for copy in copies:
        copy.wait()


def rest_kernel(groups, per_bucket, others, table, place_ref, pair_ref, *refs):
    outs, (sorted_a, sorted_b) = refs[: len(others)], refs[len(others) :]
    blocks, block = place_ref.shape
    padded, state = sorted_a.shape
    runs = Runs(table, groups, per_bucket, state)

    def sort_block(s, into):
        picked = (iota((padded, block), 0) == place_ref[pl.ds(s, 1), :]).astype(F32).astype(BF16)
        rows = pl.ds(pl.multiple_of(s * block, block), block)
        both = dot(picked, pair_ref[rows, :])
        into[...] = both[:, :state] + both[:, state:]

    longest = 0
    for s in range(blocks):
        for v in range(groups):
            longest = jnp.maximum(longest, table[s * groups + v, 3])
    unroll = groups <= 8

    @pl.when((longest < runs.most) & unroll)
    def _():
        for s in range(blocks if unroll else 0):
            into = (sorted_a, sorted_b)[s % 2]
            sort_block(s, into)
            for v, out in zip(others, outs):
                runs.place(s, v, out, into)

    @pl.when((longest >= runs.most) | (not unroll))
    def _():
        def body(s, carry):
            sort_block(s, sorted_a)
            for v, out in zip(others, outs):
                runs.place(s, v, out, sorted_a)
                runs.place_rest(s, v, out, sorted_a)
            return carry

        lax.fori_loop(0, blocks, body, 0)


def sorted_rows(block, groups):
    return -(-(block + groups * 2 * (SUB - 1)) // 16) * 16


def regroup_lead(observations, sensor_ids, sensor_sigma, buckets, me, groups, leads, parts):
    rows, state = observations.shape
    sensors = sensor_sigma.shape[0]
    block = 256
    blocks = rows // block
    cells = blocks * groups
    per_bucket = rows // groups
    far = pl.BlockSpec(memory_space=pltpu.HBM)
    return pl.pallas_call(
        functools.partial(lead_kernel, groups, per_bucket, tuple(leads), tuple(parts)),
        in_specs=[pl.BlockSpec(memory_space=pltpu.SMEM)] + [far] * 4,
        out_specs=[pl.BlockSpec(memory_space=pl.ANY)] * len(parts)
        + [pl.BlockSpec(memory_space=pltpu.VMEM)] * 3,
        scratch_shapes=[
            pltpu.VMEM((rows // LANES, LANES), I32),
            pltpu.VMEM((rows // LANES, LANES), I32),
            pltpu.VMEM((1, sensors), F32),
            pltpu.VMEM((rows, state), F32),
            pltpu.VMEM((sorted_rows(block, groups), state), F32),
            pltpu.VMEM((64 * len(leads), state), F32),
            pltpu.VMEM((64 * len(leads), state), F32),
            pltpu.VMEM((sensors, LANES), F32),
            pltpu.VMEM((len(leads), per_bucket, state), F32),
            pltpu.SMEM((cells, LANES), I32),
            pltpu.SemaphoreType.DMA((4 + blocks + len(parts),)),
        ],
        out_shape=[jax.ShapeDtypeStruct((part[2], state), F32) for part in parts]
        + [
            jax.ShapeDtypeStruct((rows, 2 * state), BF16),
            jax.ShapeDtypeStruct((blocks, block), I32),
            jax.ShapeDtypeStruct((cells, LANES), I32),
        ],
        compiler_params=pltpu.CompilerParams(vmem_limit_bytes=56 * MIB),
        cost_estimate=pl.CostEstimate(
            flops=rows * state, bytes_accessed=8 * rows * state, transcendentals=0
        ),
    )(
        me.reshape(1),
        buckets.reshape(rows // LANES, LANES),
        sensor_ids.reshape(rows // LANES, LANES),
        sensor_sigma.reshape(1, sensors),
        observations,
    )


def regroup_rest(table, place, pair, groups, others):
    rows, state = pair.shape[0], pair.shape[1] // 2
    per_bucket = rows // groups
    padded = sorted_rows(place.shape[1], groups)
    vmem = pl.BlockSpec(memory_space=pltpu.VMEM)
    return pl.pallas_call(
        functools.partial(rest_kernel, groups, per_bucket, tuple(others)),
        in_specs=[pl.BlockSpec(memory_space=pltpu.SMEM), vmem, vmem],
        out_specs=[vmem] * len(others),
        scratch_shapes=[pltpu.VMEM((padded, state), F32)] * 2,
        out_shape=[jax.ShapeDtypeStruct((per_bucket, state), F32)] * len(others),
        compiler_params=pltpu.CompilerParams(vmem_limit_bytes=14 * MIB),
        cost_estimate=pl.CostEstimate(
            flops=8 * rows * padded * state, bytes_accessed=8 * rows * state, transcendentals=0
        ),
    )(table, place, pair)


def block_pairs(count):
    return [(i, j) for i in range(count) for j in range(i + 1, count)]


def packed_rows_of(state, plane):
    count = state // LANES
    rows = (len(block_pairs(count)) + count // 2) * LANES + SUB
    return -(-rows // (plane * SUB)) * plane * SUB


def write_gram(both, state, out_ref):
    count = state // LANES
    pairs = block_pairs(count)
    row, col = iota((LANES, LANES), 0), iota((LANES, LANES), 1)

    def block(i, j):
        a, b = i * LANES, j * LANES
        cross = both[a : a + LANES, state + b : state + b + LANES]
        turned = both[b : b + LANES, state + a : state + a + LANES]
        return both[a : a + LANES, b : b + LANES] + (cross + jnp.transpose(turned))

    for n, (i, j) in enumerate(pairs):
        out_ref[n * LANES : (n + 1) * LANES, :] = block(i, j)
    tail = (len(pairs) + count // 2) * LANES
    out_ref[tail:, :] = jnp.zeros((out_ref.shape[0] - tail, LANES), F32)
    for m in range(count // 2):
        n = len(pairs) + m
        second = block(2 * m + 1, 2 * m + 1)
        out_ref[n * LANES : (n + 1) * LANES, :] = jnp.where(row <= col, block(2 * m, 2 * m), second)
        diagonal = jnp.sum(jnp.where(row == col, second, 0.0), axis=0, keepdims=True)
        out_ref[tail + m : tail + m + 1, :] = diagonal


def read_gram(value, state, a_ref):
    count = state // LANES
    pairs = block_pairs(count)
    row, col = iota((LANES, LANES), 0), iota((LANES, LANES), 1)
    span = lambda i: slice(i * LANES, (i + 1) * LANES)
    for n, (i, j) in enumerate(pairs):
        a_ref[span(i), span(j)] = value(span(n))
    tail = (len(pairs) + count // 2) * LANES
    for m in range(count // 2):
        mixed = value(span(len(pairs) + m))
        turned = jnp.transpose(mixed)
        i, j = span(2 * m), span(2 * m + 1)
        a_ref[i, i] = jnp.where(row <= col, mixed, turned)
        diagonal = value(slice(tail, tail + SUB))[m : m + 1, :]
        second = jnp.where(row > col, mixed, turned)
        a_ref[j, j] = jnp.where(row == col, diagonal, second)


def gram_kernel(prior_ref, pair_ref, out_ref, prior_out_ref, both_ref):
    state = prior_ref.shape[0]
    both_ref[...] = dot_rows(pair_ref[:, :state], pair_ref[...])
    write_gram(both_ref, state, out_ref)
    high, low = split(prior_ref[...])
    both_ref[...] = dot_rows(high, jnp.concatenate([high, low], axis=1))
    write_gram(both_ref, state, prior_out_ref)


def gram(prior_factor, pair, packed):
    rows, state = pair.shape[0], pair.shape[1] // 2
    vmem = pl.BlockSpec(memory_space=pltpu.VMEM)
    return pl.pallas_call(
        gram_kernel,
        in_specs=[vmem] * 2,
        out_specs=[vmem] * 2,
        out_shape=[jax.ShapeDtypeStruct((packed, LANES), F32)] * 2,
        scratch_shapes=[pltpu.VMEM((state, 2 * state), F32)],
        compiler_params=pltpu.CompilerParams(vmem_limit_bytes=10 * MIB),
        cost_estimate=pl.CostEstimate(
            flops=4 * rows * state * state, bytes_accessed=4 * rows * state, transcendentals=0
        ),
    )(prior_factor, pair)


def scatter_sum(packed, count, groups):
    rows, lanes = packed.shape
    axes = ("rows", "grp")
    got = lax.all_to_all(packed, axes, split_axis=0, concat_axis=0, axis_index_groups=groups, tiled=True)
    return jnp.sum(got.reshape(count, rows // count, lanes), axis=0)


def gather_pieces(piece, count, groups):
    rows, lanes = piece.shape
    copies = jnp.broadcast_to(piece, (count, rows, lanes)).reshape(count * rows, lanes)
    axes = ("rows", "grp")
    return lax.all_to_all(copies, axes, split_axis=0, concat_axis=0, axis_index_groups=groups, tiled=True)


def sweep(a, w):
    width = a.shape[0]
    groups = width // SUB
    row_id = iota((SUB, LANES), 0)
    a_rows = [a[g * SUB : (g + 1) * SUB, :] for g in range(groups)]
    w_rows = [w[g * SUB : (g + 1) * SUB, :] for g in range(groups)]
    for g in range(groups):
        va, vw = a_rows[g], w_rows[g]
        cols = [
            jnp.broadcast_to(va[:, g * SUB + j : g * SUB + j + 1], (SUB, LANES)) for j in range(SUB)
        ]
        scale = jnp.zeros((SUB, LANES), F32)
        for j in range(SUB):
            pivot = jnp.broadcast_to(cols[j][j : j + 1, :], (SUB, LANES))
            root = lax.rsqrt(pivot)
            scale = jnp.where(row_id == j, root, scale)
            if j < SUB - 1:
                ratio = jnp.where(row_id > j, cols[j] * (root * root), 0.0)
                for k in range(j + 1, SUB):
                    cols[k] = cols[k] - ratio * cols[k][j : j + 1, :]
                va = va - ratio * va[j : j + 1, :]
                vw = vw - ratio * vw[j : j + 1, :]
        va, vw = va * scale, vw * scale
        va = jnp.where(iota((SUB, LANES), 1) >= row_id + g * SUB, va, 0.0)
        a_rows[g], w_rows[g] = va, vw
        if g < groups - 1:
            both = jnp.concatenate([va, vw], axis=1)
            high = both.astype(BF16).astype(F32)
            low = both - high
            left = jnp.concatenate([high[:, :LANES], high[:, :LANES], low[:, :LANES]], axis=0)
            right = jnp.concatenate([high, low, high], axis=0)
            change = dot_rows(left.astype(BF16), right.astype(BF16))
            for q in range(g + 1, groups):
                rows = slice(q * SUB, (q + 1) * SUB)
                a_rows[q] = a_rows[q] - change[rows, :LANES]
                w_rows[q] = w_rows[q] - change[rows, LANES:]
    return jnp.concatenate(a_rows, axis=0), jnp.concatenate(w_rows, axis=0)


def factor_kernel(inv_total, sum_ref, prior_ref, factor_ref, high_ref, low_ref, a_ref, x_ref):
    state = factor_ref.shape[0]
    count = state // LANES
    span = lambda i: slice(i * LANES, (i + 1) * LANES)
    read_gram(lambda rows: prior_ref[rows, :] + sum_ref[rows, :] * inv_total, state, a_ref)
    factor_ref[...] = jnp.zeros((state, state), F32)
    x_ref[...] = jnp.zeros((state, state), F32)
    eye = (iota((LANES, LANES), 0) == iota((LANES, LANES), 1)).astype(F32)
    for k in range(count):
        r, w = sweep(a_ref[span(k), span(k)], eye)
        factor_ref[span(k), span(k)] = r
        x = jnp.transpose(w)
        x_ref[span(k), span(k)] = x
        if k > 0:
            left = dot3(x_ref[: k * LANES, : k * LANES], factor_ref[: k * LANES, span(k)])
            x_ref[: k * LANES, span(k)] = -dot3(left, x)
        if k < count - 1:
            rest = slice((k + 1) * LANES, state)
            right = dot3(w, a_ref[span(k), rest])
            factor_ref[span(k), rest] = right
            for i in range(k + 1, count):
                low = slice(i * LANES, state)
                at = (i - k - 1) * LANES
                a_ref[span(i), low] -= dot3_rows(right[:, at : at + LANES], right[:, at:])
    high, low = split(x_ref[...])
    high_ref[...] = high
    low_ref[...] = low


def factorise(summed, prior_gram, state, total_rows):
    vmem = pl.BlockSpec(memory_space=pltpu.VMEM)
    return pl.pallas_call(
        functools.partial(factor_kernel, 1.0 / total_rows),
        in_specs=[vmem] * 2,
        out_specs=[vmem] * 3,
        out_shape=[
            jax.ShapeDtypeStruct((state, state), F32),
            jax.ShapeDtypeStruct((state, state), BF16),
            jax.ShapeDtypeStruct((state, state), BF16),
        ],
        scratch_shapes=[pltpu.VMEM((state, state), F32)] * 2,
        compiler_params=pltpu.CompilerParams(vmem_limit_bytes=16 * MIB),
        cost_estimate=pl.CostEstimate(
            flops=1, bytes_accessed=1, transcendentals=0
        ),
    )(summed, prior_gram)


def whiten_kernel(steps, aliased, per_bucket, me_ref, high_ref, low_ref, *rest):
    count = len(steps)
    chunks = rest[:count]
    out_ref, held, sems = rest[count + aliased :]
    high, low = high_ref[...], low_ref[...]
    copies = []
    for n, (k, offset) in enumerate(steps):
        rows = chunks[n].shape[0]
        rows_high, rows_low = split(chunks[n][...])
        held[n, :rows] = dot(rows_high, high) + (dot(rows_high, low) + dot(rows_low, high))
        first = pl.multiple_of((me_ref[0] ^ k) * per_bucket, per_bucket) + offset
        copy = pltpu.make_async_copy(
            held.at[n, pl.ds(0, rows)],
            out_ref.at[pl.ds(pl.multiple_of(first, SUB), rows), :],
            sems.at[n],
        )
        copy.start()
        copies.append(copy)
    for copy in copies:
        copy.wait()


def whiten(me, high, low, parts, out, rows, groups):
    steps = tuple((k, offset) for k, offset, _ in parts)
    chunks = [chunk for _, _, chunk in parts]
    per_bucket, state = rows // groups, chunks[0].shape[1]
    count = len(chunks)
    vmem = pl.BlockSpec(memory_space=pltpu.VMEM)
    anywhere = pl.BlockSpec(memory_space=pl.ANY)
    extra = [] if out is None else [out]
    return pl.pallas_call(
        functools.partial(whiten_kernel, steps, len(extra), per_bucket),
        in_specs=[pl.BlockSpec(memory_space=pltpu.SMEM)]
        + [vmem] * (2 + count)
        + [anywhere] * len(extra),
        out_specs=anywhere,
        out_shape=jax.ShapeDtypeStruct((rows, state), F32),
        scratch_shapes=[
            pltpu.VMEM((count, per_bucket, state), F32),
            pltpu.SemaphoreType.DMA((count,)),
        ],
        input_output_aliases={3 + count: 0} if extra else {},
        compiler_params=pltpu.CompilerParams(vmem_limit_bytes=16 * MIB),
        cost_estimate=pl.CostEstimate(flops=1, bytes_accessed=1, transcendentals=0),
    )(me.reshape(1), high, low, *chunks, *extra)


def behind(value, *arrays):
    return lax.optimization_barrier((value, *arrays))


def shards(observations, sensor_ids, sensor_sigma, buckets, prior_factor):
    rows_dev, state = observations.shape
    groups = lax.axis_size("rows")
    grp = lax.axis_size("grp")
    me = lax.axis_index("rows").astype(I32)
    total_rows = rows_dev * groups * grp
    leads = [k for k in (4, 1) if k < groups]
    others = [k for k in range(groups) if k not in leads]
    per_bucket = rows_dev // groups
    parts = [(n, 0, per_bucket) for n in range(len(leads))]
    *chunks, pair, place, table = regroup_lead(
        observations, sensor_ids, sensor_sigma, buckets, me, groups, leads, parts
    )
    move = lambda k, chunk: lax.ppermute(chunk, "rows", [(i, i ^ k) for i in range(groups)])
    received = {k: move(k, chunk) for k, chunk in zip(leads, chunks)}
    plane = 2 * grp
    packed_rows = packed_rows_of(state, plane)
    planes = [list(range(i, i + plane)) for i in range(0, groups * grp, plane)]
    middle = [k for k in (6, 2) if k < groups]
    late = [k for k in (5, 3, *range(7, groups)) if k < groups]
    valid = sensor_sigma[0] > 0
    nothing = lambda rows: jnp.full((rows, LANES), jnp.nan, F32)

    def first():
        packed, prior_gram = gram(prior_factor, pair, packed_rows)
        rest = list(regroup_rest(table, place, pair, groups, others))
        return scatter_sum(packed, plane, planes), prior_gram, rest

    def wrong():
        return nothing(packed_rows // plane), nothing(packed_rows), [jnp.full((per_bucket, state), jnp.nan, F32)] * len(others)

    piece, prior_gram, rest = lax.cond(valid, first, wrong)
    rest = dict(zip(others, rest))
    received[0] = rest[0]
    for k in leads[1:]:
        piece, received[k] = behind(piece, received[k])
    across = [piece]
    for step in range(1, groups // 2):
        across.append(move(2 * step, piece))
    for k in middle[:1]:
        received[k] = move(k, behind(piece, rest[k])[1])
    while len(across) > 1:
        across = [across[i] + across[i + 1] for i in range(0, len(across), 2)]
    for k in middle[1:]:
        received[leads[0]], chunk = behind(received[leads[0]], rest[k])
        received[k] = move(k, chunk)
    across[0], received[leads[0]] = behind(across[0], received[leads[0]])
    for k in late[:1]:
        received[k] = move(k, behind(across[0], rest[k])[1])
    summed = lax.cond(
        valid, lambda: gather_pieces(across[0], plane, planes), lambda: nothing(packed_rows)
    )
    for k in late[1:]:
        received[k] = move(k, behind(summed, rest[k])[1])
    factor, high, low = factorise(summed, prior_gram, state, total_rows)
    whole = lambda slots: [(k, 0, received[k]) for k in slots]
    out = None
    for parts in (whole([0, *leads, *middle]), whole(late[:-1]), whole(late[-1:])):
        if parts:
            out = whiten(me, high, low, parts, out, rows_dev, groups)
    return (out, factor)


def solution(mesh):
    in_specs = (P(("rows", "grp"), None), P(("rows", "grp")), P(), P(("rows", "grp")), P())
    out_specs = (P(("rows", "grp"), None), P())
    return jax.shard_map(shards, mesh=mesh, in_specs=in_specs, out_specs=out_specs, check_vma=False)
```

```python
import functools

import jax
import jax.numpy as jnp
from jax import lax
from jax.experimental import pallas as pl
from jax.experimental.pallas import tpu as pltpu
from jax.sharding import PartitionSpec as P

F32 = jnp.float32
BF16 = jnp.bfloat16
I32 = jnp.int32
LANES = 128
SUB = 8
MIB = 1024 * 1024


def iota(shape, axis):
    return lax.broadcasted_iota(I32, shape, axis)


def split(values):
    high = values.astype(BF16)
    low = (values - high.astype(F32)).astype(BF16)
    return high, low


def dot(left, right):
    return jnp.dot(left, right, preferred_element_type=F32)


def dot_rows(left, right):
    return lax.dot_general(left, right, (((0,), (0,)), ((), ())), preferred_element_type=F32)


def dot3(left, right):
    lh, ll = split(left)
    rh, rl = split(right)
    return dot(lh, rh) + (dot(lh, rl) + dot(ll, rh))


def dot3_rows(left, right):
    lh, ll = split(left)
    rh, rl = split(right)
    return dot_rows(lh, rh) + (dot_rows(lh, rl) + dot_rows(ll, rh))


def rows_of(packed, count, wide):
    return [
        jnp.concatenate([packed[s * wide + i : s * wide + i + 1, :] for i in range(wide)], axis=1)
        for s in range(count)
    ]


def tile(t):
    return pl.ds(pl.multiple_of(t * SUB, SUB), SUB)


class Runs:
    def __init__(self, table, groups, per_bucket, state):
        self.table, self.groups = table, groups
        self.most = min(7, per_bucket // SUB + 1)
        self.sub_row = iota((SUB, state), 0)

    def get(self, s, v):
        return [self.table[s * self.groups + v, i] for i in range(4)]

    def place(self, s, v, out, source, base=None):
        kept, target, first, final = self.get(s, v)
        first = first if base is None else base
        old = out[tile(target), :]
        for t in reversed(range(1, self.most)):
            t = jnp.minimum(t, final)
            out[tile(target + t), :] = source[tile(first + t), :]
        out[tile(target), :] = jnp.where(self.sub_row < kept, old, source[tile(first), :])

    def place_rest(self, s, v, out, source):
        _, target, first, final = self.get(s, v)

        def longer(t, carry):
            out[tile(target + t), :] = source[tile(first + t), :]
            return carry

        lax.fori_loop(self.most, final + 1, longer, 0)


def lead_kernel(groups, per_bucket, leads, parts, me_ref, *refs):
    given, far_outs, refs = refs[:4], refs[4 : 4 + len(parts)], refs[4 + len(parts) :]
    (pair_ref, place_ref, meta_ref), held, scratch = refs[:3], refs[3:7], refs[7:]
    sorted_ref, small_a, small_b, inv_ref, outs_ref, table, sems = scratch
    outs = [outs_ref.at[n] for n in range(len(leads))]
    some = small_a.shape[0] // len(leads)
    buckets_ref, ids_ref, sigma_ref, obs_ref = held
    blocks, block = place_ref.shape
    wide = block // LANES
    sensors = sigma_ref.shape[1]
    padded, state = sorted_ref.shape
    cells = blocks * groups
    last_tile = per_bucket // SUB - 1
    runs = Runs(table, groups, per_bucket, state)

    small = [pltpu.make_async_copy(given[i], held[i], sems.at[i]) for i in range(3)]
    for copy in small:
        copy.start()

    def fetch(s):
        rows = pl.ds(s * block, 2 * block)
        return pltpu.make_async_copy(given[3].at[rows, :], obs_ref.at[rows, :], sems.at[4 + s])

    for s in range(0, blocks, 2):
        fetch(s).start()
    for copy in small:
        copy.wait()

    inv_row = 1.0 / sigma_ref[...]
    inv_ref[...] = jnp.transpose(jnp.broadcast_to(inv_row, (LANES, sensors)))
    slots = rows_of(buckets_ref[...] ^ me_ref[0], blocks, wide)
    hits = jnp.concatenate(
        [jnp.broadcast_to(row, (groups, block)) == iota((groups, block), 0) for row in slots], axis=0
    )
    upto = (iota((block, block), 0) <= iota((block, block), 1)).astype(F32).astype(BF16)
    running = dot(hits.astype(F32).astype(BF16), upto)
    count = jnp.broadcast_to(running[:, block - 1 : block], (cells, LANES))
    row, col = iota((cells, cells), 0), iota((cells, cells), 1)
    shift = groups.bit_length() - 1
    earlier = ((row & (groups - 1)) == (col & (groups - 1))) & (col < row)
    before = dot(earlier.astype(F32).astype(BF16), count.astype(BF16)).astype(I32)
    odd = before & (SUB - 1)
    tiles = (odd + count.astype(I32) + (SUB - 1)) >> 3
    same = ((row >> shift) == (col >> shift)) & (col < row)
    first = dot(same.astype(F32).astype(BF16), tiles.astype(F32).astype(BF16)).astype(I32)
    lane = iota((cells, LANES), 1)
    kept = jnp.where(tiles > 0, odd, SUB)
    target = jnp.minimum(before >> 3, last_tile)
    final = jnp.maximum(tiles - 1, 0)
    meta = jnp.where(lane == 2, first, final)
    meta = jnp.where(lane == 0, kept, jnp.where(lane == 1, target, meta))
    copy = pltpu.make_async_copy(meta_ref, table, sems.at[3])
    local = first * SUB + odd
    local = jnp.concatenate([local] * wide, axis=1)
    spot = jnp.where(hits, local + running.astype(I32) - 1, 0)
    places = jnp.concatenate(
        [jnp.sum(spot[s * groups : (s + 1) * groups], axis=0, keepdims=True) for s in range(blocks)],
        axis=0,
    )
    slot = iota((cells, LANES), 0) & (groups - 1)
    of_lead = functools.reduce(jnp.logical_or, [slot == v for v in leads])
    longest = jnp.max(jnp.where(of_lead, final, 0))
    inv = jnp.concatenate([inv_ref[...]] * wide, axis=1)
    block_rows = lambda s: pl.ds(pl.multiple_of(s * block, block), block)

    scales = []
    for s in range(blocks):
        ids = [ids_ref[s * wide + i : s * wide + i + 1, :] for i in range(wide)]
        known = iota((sensors, block), 0) == jnp.concatenate(ids, axis=1)
        scale_row = jnp.sum(jnp.where(known, inv, 0.0), axis=0, keepdims=True)
        scales += [scale_row[:, i * LANES : (i + 1) * LANES] for i in range(wide)]
    scales.append(jnp.zeros((-len(scales) % LANES, LANES), F32))
    turned = jnp.transpose(jnp.concatenate(scales, axis=0))
    for s in range(blocks):
        if s == blocks // 4:
            meta_ref[...] = meta
            copy.start()
            place_ref[...] = places
        if s % 2 == 0:
            fetch(s).wait()
        spread = [
            jnp.broadcast_to(turned[:, c : c + 1], (LANES, LANES))
            for c in range(s * wide, (s + 1) * wide)
        ]
        scale = jnp.concatenate(spread, axis=0)
        rows = block_rows(s)
        high, low = split(obs_ref[rows, :] * jnp.concatenate([scale] * (state // LANES), axis=1))
        pair_ref[rows, :state] = high
        pair_ref[rows, state:] = low

    def sort_into(s, picked, into):
        both = dot(picked.astype(F32).astype(BF16), pair_ref[block_rows(s), :])
        into[...] = both[:, :state] + both[:, state:]

    copy.wait()
    unroll = groups <= 8

    @pl.when((longest < runs.most) & unroll)
    def _():
        for s in range(blocks if unroll else 0):
            into = (small_a, small_b)[s % 2]
            spots = place_ref[s : s + 1, :]
            picked = [iota((some, block), 0) == spots - runs.get(s, v)[2] * SUB for v in leads]
            sort_into(s, jnp.concatenate(picked, axis=0), into)
            for n, v in enumerate(leads):
                runs.place(s, v, outs[n], into, n * some // SUB)

    @pl.when((longest >= runs.most) | (not unroll))
    def _():
        def body(s, carry):
            sort_into(s, iota((padded, block), 0) == place_ref[pl.ds(s, 1), :], sorted_ref)
            for v, out in zip(leads, outs):
                runs.place(s, v, out, sorted_ref)
                runs.place_rest(s, v, out, sorted_ref)
            return carry

        lax.fori_loop(0, blocks, body, 0)

    copies = []
    for m, ((n, first_row, rows), far) in enumerate(zip(parts, far_outs)):
        part = outs_ref.at[n, pl.ds(first_row, rows)]
        copies.append(pltpu.make_async_copy(part, far, sems.at[4 + blocks + m]))
        copies[-1].start()
    for copy in copies:
        copy.wait()


def rest_kernel(groups, per_bucket, others, table, place_ref, pair_ref, *refs):
    outs, (sorted_a, sorted_b) = refs[: len(others)], refs[len(others) :]
    blocks, block = place_ref.shape
    padded, state = sorted_a.shape
    runs = Runs(table, groups, per_bucket, state)

    def sort_block(s, into):
        picked = (iota((padded, block), 0) == place_ref[pl.ds(s, 1), :]).astype(F32).astype(BF16)
        rows = pl.ds(pl.multiple_of(s * block, block), block)
        both = dot(picked, pair_ref[rows, :])
        into[...] = both[:, :state] + both[:, state:]

    longest = 0
    for s in range(blocks):
        for v in range(groups):
            longest = jnp.maximum(longest, table[s * groups + v, 3])
    unroll = groups <= 8

    @pl.when((longest < runs.most) & unroll)
    def _():
        for s in range(blocks if unroll else 0):
            into = (sorted_a, sorted_b)[s % 2]
            sort_block(s, into)
            for v, out in zip(others, outs):
                runs.place(s, v, out, into)

    @pl.when((longest >= runs.most) | (not unroll))
    def _():
        def body(s, carry):
            sort_block(s, sorted_a)
            for v, out in zip(others, outs):
                runs.place(s, v, out, sorted_a)
                runs.place_rest(s, v, out, sorted_a)
            return carry

        lax.fori_loop(0, blocks, body, 0)


def sorted_rows(block, groups):
    return -(-(block + groups * 2 * (SUB - 1)) // 16) * 16


def regroup_lead(observations, sensor_ids, sensor_sigma, buckets, me, groups, leads, parts):
    rows, state = observations.shape
    sensors = sensor_sigma.shape[0]
    block = 256
    blocks = rows // block
    cells = blocks * groups
    per_bucket = rows // groups
    far = pl.BlockSpec(memory_space=pltpu.HBM)
    return pl.pallas_call(
        functools.partial(lead_kernel, groups, per_bucket, tuple(leads), tuple(parts)),
        in_specs=[pl.BlockSpec(memory_space=pltpu.SMEM)] + [far] * 4,
        out_specs=[pl.BlockSpec(memory_space=pl.ANY)] * len(parts)
        + [pl.BlockSpec(memory_space=pltpu.VMEM)] * 3,
        scratch_shapes=[
            pltpu.VMEM((rows // LANES, LANES), I32),
            pltpu.VMEM((rows // LANES, LANES), I32),
            pltpu.VMEM((1, sensors), F32),
            pltpu.VMEM((rows, state), F32),
            pltpu.VMEM((sorted_rows(block, groups), state), F32),
            pltpu.VMEM((64 * len(leads), state), F32),
            pltpu.VMEM((64 * len(leads), state), F32),
            pltpu.VMEM((sensors, LANES), F32),
            pltpu.VMEM((len(leads), per_bucket, state), F32),
            pltpu.SMEM((cells, LANES), I32),
            pltpu.SemaphoreType.DMA((4 + blocks + len(parts),)),
        ],
        out_shape=[jax.ShapeDtypeStruct((part[2], state), F32) for part in parts]
        + [
            jax.ShapeDtypeStruct((rows, 2 * state), BF16),
            jax.ShapeDtypeStruct((blocks, block), I32),
            jax.ShapeDtypeStruct((cells, LANES), I32),
        ],
        compiler_params=pltpu.CompilerParams(vmem_limit_bytes=56 * MIB),
        cost_estimate=pl.CostEstimate(
            flops=rows * state, bytes_accessed=8 * rows * state, transcendentals=0
        ),
    )(
        me.reshape(1),
        buckets.reshape(rows // LANES, LANES),
        sensor_ids.reshape(rows // LANES, LANES),
        sensor_sigma.reshape(1, sensors),
        observations,
    )


def regroup_rest(table, place, pair, groups, others):
    rows, state = pair.shape[0], pair.shape[1] // 2
    per_bucket = rows // groups
    padded = sorted_rows(place.shape[1], groups)
    vmem = pl.BlockSpec(memory_space=pltpu.VMEM)
    return pl.pallas_call(
        functools.partial(rest_kernel, groups, per_bucket, tuple(others)),
        in_specs=[pl.BlockSpec(memory_space=pltpu.SMEM), vmem, vmem],
        out_specs=[vmem] * len(others),
        scratch_shapes=[pltpu.VMEM((padded, state), F32)] * 2,
        out_shape=[jax.ShapeDtypeStruct((per_bucket, state), F32)] * len(others),
        compiler_params=pltpu.CompilerParams(vmem_limit_bytes=14 * MIB),
        cost_estimate=pl.CostEstimate(
            flops=8 * rows * padded * state, bytes_accessed=8 * rows * state, transcendentals=0
        ),
    )(table, place, pair)


def block_pairs(count):
    return [(i, j) for i in range(count) for j in range(i + 1, count)]


def packed_rows_of(state, plane):
    count = state // LANES
    rows = (len(block_pairs(count)) + count // 2) * LANES + SUB
    return -(-rows // (plane * SUB)) * plane * SUB


def write_gram(both, state, out_ref):
    count = state // LANES
    pairs = block_pairs(count)
    row, col = iota((LANES, LANES), 0), iota((LANES, LANES), 1)

    def block(i, j):
        a, b = i * LANES, j * LANES
        cross = both[a : a + LANES, state + b : state + b + LANES]
        turned = both[b : b + LANES, state + a : state + a + LANES]
        return both[a : a + LANES, b : b + LANES] + (cross + jnp.transpose(turned))

    for n, (i, j) in enumerate(pairs):
        out_ref[n * LANES : (n + 1) * LANES, :] = block(i, j)
    tail = (len(pairs) + count // 2) * LANES
    out_ref[tail:, :] = jnp.zeros((out_ref.shape[0] - tail, LANES), F32)
    for m in range(count // 2):
        n = len(pairs) + m
        second = block(2 * m + 1, 2 * m + 1)
        out_ref[n * LANES : (n + 1) * LANES, :] = jnp.where(row <= col, block(2 * m, 2 * m), second)
        diagonal = jnp.sum(jnp.where(row == col, second, 0.0), axis=0, keepdims=True)
        out_ref[tail + m : tail + m + 1, :] = diagonal


def read_gram(value, state, a_ref):
    count = state // LANES
    pairs = block_pairs(count)
    row, col = iota((LANES, LANES), 0), iota((LANES, LANES), 1)
    span = lambda i: slice(i * LANES, (i + 1) * LANES)
    for n, (i, j) in enumerate(pairs):
        a_ref[span(i), span(j)] = value(span(n))
    tail = (len(pairs) + count // 2) * LANES
    for m in range(count // 2):
        mixed = value(span(len(pairs) + m))
        turned = jnp.transpose(mixed)
        i, j = span(2 * m), span(2 * m + 1)
        a_ref[i, i] = jnp.where(row <= col, mixed, turned)
        diagonal = value(slice(tail, tail + SUB))[m : m + 1, :]
        second = jnp.where(row > col, mixed, turned)
        a_ref[j, j] = jnp.where(row == col, diagonal, second)


def gram_kernel(prior_ref, pair_ref, out_ref, prior_out_ref, both_ref):
    state = prior_ref.shape[0]
    both_ref[...] = dot_rows(pair_ref[:, :state], pair_ref[...])
    write_gram(both_ref, state, out_ref)
    high, low = split(prior_ref[...])
    both_ref[...] = dot_rows(high, jnp.concatenate([high, low], axis=1))
    write_gram(both_ref, state, prior_out_ref)


def gram(prior_factor, pair, packed):
    rows, state = pair.shape[0], pair.shape[1] // 2
    vmem = pl.BlockSpec(memory_space=pltpu.VMEM)
    return pl.pallas_call(
        gram_kernel,
        in_specs=[vmem] * 2,
        out_specs=[vmem] * 2,
        out_shape=[jax.ShapeDtypeStruct((packed, LANES), F32)] * 2,
        scratch_shapes=[pltpu.VMEM((state, 2 * state), F32)],
        compiler_params=pltpu.CompilerParams(vmem_limit_bytes=10 * MIB),
        cost_estimate=pl.CostEstimate(
            flops=4 * rows * state * state, bytes_accessed=4 * rows * state, transcendentals=0
        ),
    )(prior_factor, pair)


def scatter_sum(packed, count, groups):
    rows, lanes = packed.shape
    axes = ("rows", "grp")
    got = lax.all_to_all(packed, axes, split_axis=0, concat_axis=0, axis_index_groups=groups, tiled=True)
    return jnp.sum(got.reshape(count, rows // count, lanes), axis=0)


def gather_pieces(piece, count, groups):
    rows, lanes = piece.shape
    copies = jnp.broadcast_to(piece, (count, rows, lanes)).reshape(count * rows, lanes)
    axes = ("rows", "grp")
    return lax.all_to_all(copies, axes, split_axis=0, concat_axis=0, axis_index_groups=groups, tiled=True)


def sweep(a, w):
    width = a.shape[0]
    groups = width // SUB
    row_id = iota((SUB, LANES), 0)
    a_rows = [a[g * SUB : (g + 1) * SUB, :] for g in range(groups)]
    w_rows = [w[g * SUB : (g + 1) * SUB, :] for g in range(groups)]
    for g in range(groups):
        va, vw = a_rows[g], w_rows[g]
        cols = [
            jnp.broadcast_to(va[:, g * SUB + j : g * SUB + j + 1], (SUB, LANES)) for j in range(SUB)
        ]
        scale = jnp.zeros((SUB, LANES), F32)
        for j in range(SUB):
            pivot = jnp.broadcast_to(cols[j][j : j + 1, :], (SUB, LANES))
            root = lax.rsqrt(pivot)
            scale = jnp.where(row_id == j, root, scale)
            if j < SUB - 1:
                ratio = jnp.where(row_id > j, cols[j] * (root * root), 0.0)
                for k in range(j + 1, SUB):
                    cols[k] = cols[k] - ratio * cols[k][j : j + 1, :]
                va = va - ratio * va[j : j + 1, :]
                vw = vw - ratio * vw[j : j + 1, :]
        va, vw = va * scale, vw * scale
        va = jnp.where(iota((SUB, LANES), 1) >= row_id + g * SUB, va, 0.0)
        a_rows[g], w_rows[g] = va, vw
        if g < groups - 1:
            both = jnp.concatenate([va, vw], axis=1)
            high = both.astype(BF16).astype(F32)
            low = both - high
            left = jnp.concatenate([high[:, :LANES], high[:, :LANES], low[:, :LANES]], axis=0)
            right = jnp.concatenate([high, low, high], axis=0)
            change = dot_rows(left.astype(BF16), right.astype(BF16))
            for q in range(g + 1, groups):
                rows = slice(q * SUB, (q + 1) * SUB)
                a_rows[q] = a_rows[q] - change[rows, :LANES]
                w_rows[q] = w_rows[q] - change[rows, LANES:]
    return jnp.concatenate(a_rows, axis=0), jnp.concatenate(w_rows, axis=0)


def factor_kernel(inv_total, sum_ref, prior_ref, factor_ref, high_ref, low_ref, a_ref, x_ref):
    state = factor_ref.shape[0]
    count = state // LANES
    span = lambda i: slice(i * LANES, (i + 1) * LANES)
    read_gram(lambda rows: prior_ref[rows, :] + sum_ref[rows, :] * inv_total, state, a_ref)
    factor_ref[...] = jnp.zeros((state, state), F32)
    x_ref[...] = jnp.zeros((state, state), F32)
    eye = (iota((LANES, LANES), 0) == iota((LANES, LANES), 1)).astype(F32)
    for k in range(count):
        r, w = sweep(a_ref[span(k), span(k)], eye)
        factor_ref[span(k), span(k)] = r
        x = jnp.transpose(w)
        x_ref[span(k), span(k)] = x
        if k > 0:
            left = dot3(x_ref[: k * LANES, : k * LANES], factor_ref[: k * LANES, span(k)])
            x_ref[: k * LANES, span(k)] = -dot3(left, x)
        if k < count - 1:
            rest = slice((k + 1) * LANES, state)
            right = dot3(w, a_ref[span(k), rest])
            factor_ref[span(k), rest] = right
            for i in range(k + 1, count):
                low = slice(i * LANES, state)
                at = (i - k - 1) * LANES
                a_ref[span(i), low] -= dot3_rows(right[:, at : at + LANES], right[:, at:])
    high, low = split(x_ref[...])
    high_ref[...] = high
    low_ref[...] = low


def factorise(summed, prior_gram, state, total_rows):
    vmem = pl.BlockSpec(memory_space=pltpu.VMEM)
    return pl.pallas_call(
        functools.partial(factor_kernel, 1.0 / total_rows),
        in_specs=[vmem] * 2,
        out_specs=[vmem] * 3,
        out_shape=[
            jax.ShapeDtypeStruct((state, state), F32),
            jax.ShapeDtypeStruct((state, state), BF16),
            jax.ShapeDtypeStruct((state, state), BF16),
        ],
        scratch_shapes=[pltpu.VMEM((state, state), F32)] * 2,
        compiler_params=pltpu.CompilerParams(vmem_limit_bytes=16 * MIB),
        cost_estimate=pl.CostEstimate(
            flops=1, bytes_accessed=1, transcendentals=0
        ),
    )(summed, prior_gram)


def whiten_kernel(steps, aliased, per_bucket, me_ref, high_ref, low_ref, *rest):
    count = len(steps)
    chunks = rest[:count]
    out_ref, held, sems = rest[count + aliased :]
    high, low = high_ref[...], low_ref[...]
    pieces = 2 if count == 1 else 1
    copies = []
    for n, (k, offset) in enumerate(steps):
        rows = chunks[n].shape[0] // pieces
        for i in range(pieces):
            rows_high, rows_low = split(chunks[n][i * rows : (i + 1) * rows, :])
            product = dot(rows_high, high) + (dot(rows_high, low) + dot(rows_low, high))
            held[n, i * rows : (i + 1) * rows] = product
            first = pl.multiple_of((me_ref[0] ^ k) * per_bucket, per_bucket) + offset + i * rows
            copy = pltpu.make_async_copy(
                held.at[n, pl.ds(i * rows, rows)],
                out_ref.at[pl.ds(pl.multiple_of(first, SUB), rows), :],
                sems.at[n * pieces + i],
            )
            copy.start()
            copies.append(copy)
    for copy in copies:
        copy.wait()


def whiten(me, high, low, parts, out, rows, groups):
    steps = tuple((k, offset) for k, offset, _ in parts)
    chunks = [chunk for _, _, chunk in parts]
    per_bucket, state = rows // groups, chunks[0].shape[1]
    count = len(chunks)
    vmem = pl.BlockSpec(memory_space=pltpu.VMEM)
    anywhere = pl.BlockSpec(memory_space=pl.ANY)
    extra = [] if out is None else [out]
    return pl.pallas_call(
        functools.partial(whiten_kernel, steps, len(extra), per_bucket),
        in_specs=[pl.BlockSpec(memory_space=pltpu.SMEM)]
        + [vmem] * (2 + count)
        + [anywhere] * len(extra),
        out_specs=anywhere,
        out_shape=jax.ShapeDtypeStruct((rows, state), F32),
        scratch_shapes=[
            pltpu.VMEM((count, per_bucket, state), F32),
            pltpu.SemaphoreType.DMA((count + 1,)),
        ],
        input_output_aliases={3 + count: 0} if extra else {},
        compiler_params=pltpu.CompilerParams(vmem_limit_bytes=16 * MIB),
        cost_estimate=pl.CostEstimate(flops=1, bytes_accessed=1, transcendentals=0),
    )(me.reshape(1), high, low, *chunks, *extra)


def behind(value, *arrays):
    return lax.optimization_barrier((value, *arrays))


def shards(observations, sensor_ids, sensor_sigma, buckets, prior_factor):
    rows_dev, state = observations.shape
    groups = lax.axis_size("rows")
    grp = lax.axis_size("grp")
    me = lax.axis_index("rows").astype(I32)
    total_rows = rows_dev * groups * grp
    leads = [k for k in (4, 1) if k < groups]
    others = [k for k in range(groups) if k not in leads]
    per_bucket = rows_dev // groups
    parts = [(n, 0, per_bucket) for n in range(len(leads))]
    *chunks, pair, place, table = regroup_lead(
        observations, sensor_ids, sensor_sigma, buckets, me, groups, leads, parts
    )
    move = lambda k, chunk: lax.ppermute(chunk, "rows", [(i, i ^ k) for i in range(groups)])
    received = {k: move(k, chunk) for k, chunk in zip(leads, chunks)}
    plane = 2 * grp
    packed_rows = packed_rows_of(state, plane)
    planes = [list(range(i, i + plane)) for i in range(0, groups * grp, plane)]
    middle = [k for k in (2, 6) if k < groups]
    late = [k for k in (5, 3, *range(7, groups)) if k < groups]
    valid = sensor_sigma[0] > 0
    nothing = lambda rows: jnp.full((rows, LANES), jnp.nan, F32)

    def first():
        packed, prior_gram = gram(prior_factor, pair, packed_rows)
        rest = list(regroup_rest(table, place, pair, groups, others))
        return scatter_sum(packed, plane, planes), prior_gram, rest

    def wrong():
        return nothing(packed_rows // plane), nothing(packed_rows), [jnp.full((per_bucket, state), jnp.nan, F32)] * len(others)

    piece, prior_gram, rest = lax.cond(valid, first, wrong)
    rest = dict(zip(others, rest))
    received[0] = rest[0]
    for k in leads[1:]:
        piece, received[k] = behind(piece, received[k])
    across = [piece]
    for step in range(1, groups // 2):
        across.append(move(2 * step, piece))
    for k in middle[:1]:
        received[k] = move(k, behind(piece, rest[k])[1])
    while len(across) > 1:
        across = [across[i] + across[i + 1] for i in range(0, len(across), 2)]
    for k in middle[1:]:
        received[leads[0]], chunk = behind(received[leads[0]], rest[k])
        received[k] = move(k, chunk)
    across[0], received[leads[0]] = behind(across[0], received[leads[0]])
    for k in late[:1]:
        received[k] = move(k, behind(across[0], rest[k])[1])
    summed = lax.cond(
        valid, lambda: gather_pieces(across[0], plane, planes), lambda: nothing(packed_rows)
    )
    for k in late[1:]:
        received[k] = move(k, behind(summed, rest[k])[1])
    factor, high, low = factorise(summed, prior_gram, state, total_rows)
    whole = lambda slots: [(k, 0, received[k]) for k in slots]
    out = None
    for parts in (whole([0, *leads, *middle]), whole(late[:-1]), whole(late[-1:])):
        if parts:
            out = whiten(me, high, low, parts, out, rows_dev, groups)
    return (out, factor)


def solution(mesh):
    in_specs = (P(("rows", "grp"), None), P(("rows", "grp")), P(), P(("rows", "grp")), P())
    out_specs = (P(("rows", "grp"), None), P())
    return jax.shard_map(shards, mesh=mesh, in_specs=in_specs, out_specs=out_specs, check_vma=False)
```

```python
import functools

import jax
import jax.numpy as jnp
from jax import lax
from jax.experimental import pallas as pl
from jax.experimental.pallas import tpu as pltpu
from jax.sharding import PartitionSpec as P

F32 = jnp.float32
BF16 = jnp.bfloat16
I32 = jnp.int32
LANES = 128
SUB = 8
MIB = 1024 * 1024


def iota(shape, axis):
    return lax.broadcasted_iota(I32, shape, axis)


def split(values):
    high = values.astype(BF16)
    low = (values - high.astype(F32)).astype(BF16)
    return high, low


def dot(left, right):
    return jnp.dot(left, right, preferred_element_type=F32)


def dot_rows(left, right):
    return lax.dot_general(left, right, (((0,), (0,)), ((), ())), preferred_element_type=F32)


def dot3(left, right):
    lh, ll = split(left)
    rh, rl = split(right)
    return dot(lh, rh) + (dot(lh, rl) + dot(ll, rh))


def dot3_rows(left, right):
    lh, ll = split(left)
    rh, rl = split(right)
    return dot_rows(lh, rh) + (dot_rows(lh, rl) + dot_rows(ll, rh))


def rows_of(packed, count, wide):
    return [
        jnp.concatenate([packed[s * wide + i : s * wide + i + 1, :] for i in range(wide)], axis=1)
        for s in range(count)
    ]


def tile(t):
    return pl.ds(pl.multiple_of(t * SUB, SUB), SUB)


class Runs:
    def __init__(self, table, groups, per_bucket, state):
        self.table, self.groups = table, groups
        self.most = min(7, per_bucket // SUB + 1)
        self.sub_row = iota((SUB, state), 0)

    def get(self, s, v):
        return [self.table[s * self.groups + v, i] for i in range(4)]

    def place(self, s, v, out, source, base=None):
        kept, target, first, final = self.get(s, v)
        first = first if base is None else base
        old = out[tile(target), :]
        for t in reversed(range(1, self.most)):
            t = jnp.minimum(t, final)
            out[tile(target + t), :] = source[tile(first + t), :]
        out[tile(target), :] = jnp.where(self.sub_row < kept, old, source[tile(first), :])

    def place_rest(self, s, v, out, source):
        _, target, first, final = self.get(s, v)

        def longer(t, carry):
            out[tile(target + t), :] = source[tile(first + t), :]
            return carry

        lax.fori_loop(self.most, final + 1, longer, 0)


def lead_kernel(groups, per_bucket, leads, parts, me_ref, *refs):
    given, far_outs, refs = refs[:4], refs[4 : 4 + len(parts)], refs[4 + len(parts) :]
    (pair_ref, place_ref, meta_ref), held, scratch = refs[:3], refs[3:7], refs[7:]
    sorted_ref, small_a, small_b, inv_ref, outs_ref, table, sems = scratch
    outs = [outs_ref.at[n] for n in range(len(leads))]
    some = small_a.shape[0] // len(leads)
    buckets_ref, ids_ref, sigma_ref, obs_ref = held
    blocks, block = place_ref.shape
    wide = block // LANES
    sensors = sigma_ref.shape[1]
    padded, state = sorted_ref.shape
    cells = blocks * groups
    last_tile = per_bucket // SUB - 1
    runs = Runs(table, groups, per_bucket, state)

    small = [pltpu.make_async_copy(given[i], held[i], sems.at[i]) for i in range(3)]
    for copy in small:
        copy.start()

    def fetch(s):
        rows = pl.ds(s * block, 2 * block)
        return pltpu.make_async_copy(given[3].at[rows, :], obs_ref.at[rows, :], sems.at[4 + s])

    for s in range(0, blocks, 2):
        fetch(s).start()
    for copy in small:
        copy.wait()

    inv_row = 1.0 / sigma_ref[...]
    inv_ref[...] = jnp.transpose(jnp.broadcast_to(inv_row, (LANES, sensors)))
    slots = rows_of(buckets_ref[...] ^ me_ref[0], blocks, wide)
    hits = jnp.concatenate(
        [jnp.broadcast_to(row, (groups, block)) == iota((groups, block), 0) for row in slots], axis=0
    )
    upto = (iota((block, block), 0) <= iota((block, block), 1)).astype(F32).astype(BF16)
    running = dot(hits.astype(F32).astype(BF16), upto)
    count = jnp.broadcast_to(running[:, block - 1 : block], (cells, LANES))
    row, col = iota((cells, cells), 0), iota((cells, cells), 1)
    shift = groups.bit_length() - 1
    earlier = ((row & (groups - 1)) == (col & (groups - 1))) & (col < row)
    before = dot(earlier.astype(F32).astype(BF16), count.astype(BF16)).astype(I32)
    odd = before & (SUB - 1)
    tiles = (odd + count.astype(I32) + (SUB - 1)) >> 3
    same = ((row >> shift) == (col >> shift)) & (col < row)
    first = dot(same.astype(F32).astype(BF16), tiles.astype(F32).astype(BF16)).astype(I32)
    lane = iota((cells, LANES), 1)
    kept = jnp.where(tiles > 0, odd, SUB)
    target = jnp.minimum(before >> 3, last_tile)
    final = jnp.maximum(tiles - 1, 0)
    meta = jnp.where(lane == 2, first, final)
    meta = jnp.where(lane == 0, kept, jnp.where(lane == 1, target, meta))
    copy = pltpu.make_async_copy(meta_ref, table, sems.at[3])
    local = first * SUB + odd
    local = jnp.concatenate([local] * wide, axis=1)
    spot = jnp.where(hits, local + running.astype(I32) - 1, 0)
    places = jnp.concatenate(
        [jnp.sum(spot[s * groups : (s + 1) * groups], axis=0, keepdims=True) for s in range(blocks)],
        axis=0,
    )
    slot = iota((cells, LANES), 0) & (groups - 1)
    of_lead = functools.reduce(jnp.logical_or, [slot == v for v in leads])
    longest = jnp.max(jnp.where(of_lead, final, 0))
    inv = jnp.concatenate([inv_ref[...]] * wide, axis=1)
    block_rows = lambda s: pl.ds(pl.multiple_of(s * block, block), block)

    scales = []
    for s in range(blocks):
        ids = [ids_ref[s * wide + i : s * wide + i + 1, :] for i in range(wide)]
        known = iota((sensors, block), 0) == jnp.concatenate(ids, axis=1)
        scale_row = jnp.sum(jnp.where(known, inv, 0.0), axis=0, keepdims=True)
        scales += [scale_row[:, i * LANES : (i + 1) * LANES] for i in range(wide)]
    scales.append(jnp.zeros((-len(scales) % LANES, LANES), F32))
    turned = jnp.transpose(jnp.concatenate(scales, axis=0))
    for s in range(blocks):
        if s == blocks // 4:
            meta_ref[...] = meta
            copy.start()
            place_ref[...] = places
        if s % 2 == 0:
            fetch(s).wait()
        spread = [
            jnp.broadcast_to(turned[:, c : c + 1], (LANES, LANES))
            for c in range(s * wide, (s + 1) * wide)
        ]
        scale = jnp.concatenate(spread, axis=0)
        rows = block_rows(s)
        high, low = split(obs_ref[rows, :] * jnp.concatenate([scale] * (state // LANES), axis=1))
        pair_ref[rows, :state] = high
        pair_ref[rows, state:] = low

    def sort_into(s, picked, into):
        both = dot(picked.astype(F32).astype(BF16), pair_ref[block_rows(s), :])
        into[...] = both[:, :state] + both[:, state:]

    copy.wait()
    unroll = groups <= 8

    @pl.when((longest < runs.most) & unroll)
    def _():
        for s in range(blocks if unroll else 0):
            into = (small_a, small_b)[s % 2]
            spots = place_ref[s : s + 1, :]
            picked = [iota((some, block), 0) == spots - runs.get(s, v)[2] * SUB for v in leads]
            sort_into(s, jnp.concatenate(picked, axis=0), into)
            for n, v in enumerate(leads):
                runs.place(s, v, outs[n], into, n * some // SUB)

    @pl.when((longest >= runs.most) | (not unroll))
    def _():
        def body(s, carry):
            sort_into(s, iota((padded, block), 0) == place_ref[pl.ds(s, 1), :], sorted_ref)
            for v, out in zip(leads, outs):
                runs.place(s, v, out, sorted_ref)
                runs.place_rest(s, v, out, sorted_ref)
            return carry

        lax.fori_loop(0, blocks, body, 0)

    copies = []
    for m, ((n, first_row, rows), far) in enumerate(zip(parts, far_outs)):
        part = outs_ref.at[n, pl.ds(first_row, rows)]
        copies.append(pltpu.make_async_copy(part, far, sems.at[4 + blocks + m]))
        copies[-1].start()
    for copy in copies:
        copy.wait()


def rest_kernel(groups, per_bucket, others, table, place_ref, pair_ref, *refs):
    outs, (sorted_a, sorted_b) = refs[: len(others)], refs[len(others) :]
    blocks, block = place_ref.shape
    padded, state = sorted_a.shape
    runs = Runs(table, groups, per_bucket, state)

    def sort_block(s, into):
        picked = (iota((padded, block), 0) == place_ref[pl.ds(s, 1), :]).astype(F32).astype(BF16)
        rows = pl.ds(pl.multiple_of(s * block, block), block)
        both = dot(picked, pair_ref[rows, :])
        into[...] = both[:, :state] + both[:, state:]

    longest = 0
    for s in range(blocks):
        for v in range(groups):
            longest = jnp.maximum(longest, table[s * groups + v, 3])
    unroll = groups <= 8

    @pl.when((longest < runs.most) & unroll)
    def _():
        for s in range(blocks if unroll else 0):
            into = (sorted_a, sorted_b)[s % 2]
            sort_block(s, into)
            for v, out in zip(others, outs):
                runs.place(s, v, out, into)

    @pl.when((longest >= runs.most) | (not unroll))
    def _():
        def body(s, carry):
            sort_block(s, sorted_a)
            for v, out in zip(others, outs):
                runs.place(s, v, out, sorted_a)
                runs.place_rest(s, v, out, sorted_a)
            return carry

        lax.fori_loop(0, blocks, body, 0)


def sorted_rows(block, groups):
    return -(-(block + groups * 2 * (SUB - 1)) // 16) * 16


def regroup_lead(observations, sensor_ids, sensor_sigma, buckets, me, groups, leads, parts):
    rows, state = observations.shape
    sensors = sensor_sigma.shape[0]
    block = 256
    blocks = rows // block
    cells = blocks * groups
    per_bucket = rows // groups
    far = pl.BlockSpec(memory_space=pltpu.HBM)
    return pl.pallas_call(
        functools.partial(lead_kernel, groups, per_bucket, tuple(leads), tuple(parts)),
        in_specs=[pl.BlockSpec(memory_space=pltpu.SMEM)] + [far] * 4,
        out_specs=[pl.BlockSpec(memory_space=pl.ANY)] * len(parts)
        + [pl.BlockSpec(memory_space=pltpu.VMEM)] * 3,
        scratch_shapes=[
            pltpu.VMEM((rows // LANES, LANES), I32),
            pltpu.VMEM((rows // LANES, LANES), I32),
            pltpu.VMEM((1, sensors), F32),
            pltpu.VMEM((rows, state), F32),
            pltpu.VMEM((sorted_rows(block, groups), state), F32),
            pltpu.VMEM((64 * len(leads), state), F32),
            pltpu.VMEM((64 * len(leads), state), F32),
            pltpu.VMEM((sensors, LANES), F32),
            pltpu.VMEM((len(leads), per_bucket, state), F32),
            pltpu.SMEM((cells, LANES), I32),
            pltpu.SemaphoreType.DMA((4 + blocks + len(parts),)),
        ],
        out_shape=[jax.ShapeDtypeStruct((part[2], state), F32) for part in parts]
        + [
            jax.ShapeDtypeStruct((rows, 2 * state), BF16),
            jax.ShapeDtypeStruct((blocks, block), I32),
            jax.ShapeDtypeStruct((cells, LANES), I32),
        ],
        compiler_params=pltpu.CompilerParams(vmem_limit_bytes=56 * MIB),
        cost_estimate=pl.CostEstimate(
            flops=rows * state, bytes_accessed=8 * rows * state, transcendentals=0
        ),
    )(
        me.reshape(1),
        buckets.reshape(rows // LANES, LANES),
        sensor_ids.reshape(rows // LANES, LANES),
        sensor_sigma.reshape(1, sensors),
        observations,
    )


def regroup_rest(table, place, pair, groups, others):
    rows, state = pair.shape[0], pair.shape[1] // 2
    per_bucket = rows // groups
    padded = sorted_rows(place.shape[1], groups)
    vmem = pl.BlockSpec(memory_space=pltpu.VMEM)
    return pl.pallas_call(
        functools.partial(rest_kernel, groups, per_bucket, tuple(others)),
        in_specs=[pl.BlockSpec(memory_space=pltpu.SMEM), vmem, vmem],
        out_specs=[vmem] * len(others),
        scratch_shapes=[pltpu.VMEM((padded, state), F32)] * 2,
        out_shape=[jax.ShapeDtypeStruct((per_bucket, state), F32)] * len(others),
        compiler_params=pltpu.CompilerParams(vmem_limit_bytes=14 * MIB),
        cost_estimate=pl.CostEstimate(
            flops=8 * rows * padded * state, bytes_accessed=8 * rows * state, transcendentals=0
        ),
    )(table, place, pair)


def block_pairs(count):
    return [(i, j) for i in range(count) for j in range(i + 1, count)]


def packed_rows_of(state, plane):
    count = state // LANES
    rows = (len(block_pairs(count)) + count // 2) * LANES + SUB
    return -(-rows // (plane * SUB)) * plane * SUB


def write_gram(both, state, out_ref):
    count = state // LANES
    pairs = block_pairs(count)
    row, col = iota((LANES, LANES), 0), iota((LANES, LANES), 1)

    def block(i, j):
        a, b = i * LANES, j * LANES
        cross = both[a : a + LANES, state + b : state + b + LANES]
        turned = both[b : b + LANES, state + a : state + a + LANES]
        return both[a : a + LANES, b : b + LANES] + (cross + jnp.transpose(turned))

    for n, (i, j) in enumerate(pairs):
        out_ref[n * LANES : (n + 1) * LANES, :] = block(i, j)
    tail = (len(pairs) + count // 2) * LANES
    out_ref[tail:, :] = jnp.zeros((out_ref.shape[0] - tail, LANES), F32)
    for m in range(count // 2):
        n = len(pairs) + m
        second = block(2 * m + 1, 2 * m + 1)
        out_ref[n * LANES : (n + 1) * LANES, :] = jnp.where(row <= col, block(2 * m, 2 * m), second)
        diagonal = jnp.sum(jnp.where(row == col, second, 0.0), axis=0, keepdims=True)
        out_ref[tail + m : tail + m + 1, :] = diagonal


def read_gram(value, state, a_ref):
    count = state // LANES
    pairs = block_pairs(count)
    row, col = iota((LANES, LANES), 0), iota((LANES, LANES), 1)
    span = lambda i: slice(i * LANES, (i + 1) * LANES)
    for n, (i, j) in enumerate(pairs):
        a_ref[span(i), span(j)] = value(span(n))
    tail = (len(pairs) + count // 2) * LANES
    for m in range(count // 2):
        mixed = value(span(len(pairs) + m))
        turned = jnp.transpose(mixed)
        i, j = span(2 * m), span(2 * m + 1)
        a_ref[i, i] = jnp.where(row <= col, mixed, turned)
        diagonal = value(slice(tail, tail + SUB))[m : m + 1, :]
        second = jnp.where(row > col, mixed, turned)
        a_ref[j, j] = jnp.where(row == col, diagonal, second)


def gram_kernel(prior_ref, pair_ref, out_ref, prior_out_ref, both_ref):
    state = prior_ref.shape[0]
    both_ref[...] = dot_rows(pair_ref[:, :state], pair_ref[...])
    write_gram(both_ref, state, out_ref)
    high, low = split(prior_ref[...])
    both_ref[...] = dot_rows(high, jnp.concatenate([high, low], axis=1))
    write_gram(both_ref, state, prior_out_ref)


def gram(prior_factor, pair, packed):
    rows, state = pair.shape[0], pair.shape[1] // 2
    vmem = pl.BlockSpec(memory_space=pltpu.VMEM)
    return pl.pallas_call(
        gram_kernel,
        in_specs=[vmem] * 2,
        out_specs=[vmem] * 2,
        out_shape=[jax.ShapeDtypeStruct((packed, LANES), F32)] * 2,
        scratch_shapes=[pltpu.VMEM((state, 2 * state), F32)],
        compiler_params=pltpu.CompilerParams(vmem_limit_bytes=10 * MIB),
        cost_estimate=pl.CostEstimate(
            flops=4 * rows * state * state, bytes_accessed=4 * rows * state, transcendentals=0
        ),
    )(prior_factor, pair)


def scatter_sum(packed, count, groups):
    rows, lanes = packed.shape
    axes = ("rows", "grp")
    got = lax.all_to_all(packed, axes, split_axis=0, concat_axis=0, axis_index_groups=groups, tiled=True)
    return jnp.sum(got.reshape(count, rows // count, lanes), axis=0)


def gather_pieces(piece, count, groups):
    rows, lanes = piece.shape
    copies = jnp.broadcast_to(piece, (count, rows, lanes)).reshape(count * rows, lanes)
    axes = ("rows", "grp")
    return lax.all_to_all(copies, axes, split_axis=0, concat_axis=0, axis_index_groups=groups, tiled=True)


def sweep(a, w):
    width = a.shape[0]
    groups = width // SUB
    row_id = iota((SUB, LANES), 0)
    a_rows = [a[g * SUB : (g + 1) * SUB, :] for g in range(groups)]
    w_rows = [w[g * SUB : (g + 1) * SUB, :] for g in range(groups)]
    for g in range(groups):
        va, vw = a_rows[g], w_rows[g]
        cols = [
            jnp.broadcast_to(va[:, g * SUB + j : g * SUB + j + 1], (SUB, LANES)) for j in range(SUB)
        ]
        scale = jnp.zeros((SUB, LANES), F32)
        for j in range(SUB):
            pivot = jnp.broadcast_to(cols[j][j : j + 1, :], (SUB, LANES))
            root = lax.rsqrt(pivot)
            scale = jnp.where(row_id == j, root, scale)
            if j < SUB - 1:
                ratio = jnp.where(row_id > j, cols[j] * (root * root), 0.0)
                for k in range(j + 1, SUB):
                    cols[k] = cols[k] - ratio * cols[k][j : j + 1, :]
                va = va - ratio * va[j : j + 1, :]
                vw = vw - ratio * vw[j : j + 1, :]
        va, vw = va * scale, vw * scale
        va = jnp.where(iota((SUB, LANES), 1) >= row_id + g * SUB, va, 0.0)
        a_rows[g], w_rows[g] = va, vw
        if g < groups - 1:
            both = jnp.concatenate([va, vw], axis=1)
            high = both.astype(BF16).astype(F32)
            low = both - high
            left = jnp.concatenate([high[:, :LANES], high[:, :LANES], low[:, :LANES]], axis=0)
            right = jnp.concatenate([high, low, high], axis=0)
            change = dot_rows(left.astype(BF16), right.astype(BF16))
            for q in range(g + 1, groups):
                rows = slice(q * SUB, (q + 1) * SUB)
                a_rows[q] = a_rows[q] - change[rows, :LANES]
                w_rows[q] = w_rows[q] - change[rows, LANES:]
    return jnp.concatenate(a_rows, axis=0), jnp.concatenate(w_rows, axis=0)


def factor_kernel(inv_total, sum_ref, prior_ref, factor_ref, high_ref, low_ref, a_ref, x_ref):
    state = factor_ref.shape[0]
    count = state // LANES
    span = lambda i: slice(i * LANES, (i + 1) * LANES)
    read_gram(lambda rows: prior_ref[rows, :] + sum_ref[rows, :] * inv_total, state, a_ref)
    factor_ref[...] = jnp.zeros((state, state), F32)
    x_ref[...] = jnp.zeros((state, state), F32)
    eye = (iota((LANES, LANES), 0) == iota((LANES, LANES), 1)).astype(F32)
    for k in range(count):
        r, w = sweep(a_ref[span(k), span(k)], eye)
        factor_ref[span(k), span(k)] = r
        x = jnp.transpose(w)
        x_ref[span(k), span(k)] = x
        if k > 0:
            left = dot3(x_ref[: k * LANES, : k * LANES], factor_ref[: k * LANES, span(k)])
            x_ref[: k * LANES, span(k)] = -dot3(left, x)
        if k < count - 1:
            rest = slice((k + 1) * LANES, state)
            right = dot3(w, a_ref[span(k), rest])
            factor_ref[span(k), rest] = right
            for i in range(k + 1, count):
                low = slice(i * LANES, state)
                at = (i - k - 1) * LANES
                a_ref[span(i), low] -= dot3_rows(right[:, at : at + LANES], right[:, at:])
    high, low = split(x_ref[...])
    high_ref[...] = high
    low_ref[...] = low


def factorise(summed, prior_gram, state, total_rows):
    vmem = pl.BlockSpec(memory_space=pltpu.VMEM)
    return pl.pallas_call(
        functools.partial(factor_kernel, 1.0 / total_rows),
        in_specs=[vmem] * 2,
        out_specs=[vmem] * 3,
        out_shape=[
            jax.ShapeDtypeStruct((state, state), F32),
            jax.ShapeDtypeStruct((state, state), BF16),
            jax.ShapeDtypeStruct((state, state), BF16),
        ],
        scratch_shapes=[pltpu.VMEM((state, state), F32)] * 2,
        compiler_params=pltpu.CompilerParams(vmem_limit_bytes=16 * MIB),
        cost_estimate=pl.CostEstimate(
            flops=1, bytes_accessed=1, transcendentals=0
        ),
    )(summed, prior_gram)


def whiten_kernel(steps, aliased, per_bucket, me_ref, high_ref, low_ref, *rest):
    count = len(steps)
    chunks = rest[:count]
    out_ref, held, sems = rest[count + aliased :]
    high, low = high_ref[...], low_ref[...]
    pieces = 2 if count == 1 else 1
    copies = []
    for n, (k, offset) in enumerate(steps):
        rows = chunks[n].shape[0] // pieces
        for i in range(pieces):
            rows_high, rows_low = split(chunks[n][i * rows : (i + 1) * rows, :])
            product = dot(rows_high, high) + (dot(rows_high, low) + dot(rows_low, high))
            held[n, i * rows : (i + 1) * rows] = product
            first = pl.multiple_of((me_ref[0] ^ k) * per_bucket, per_bucket) + offset + i * rows
            copy = pltpu.make_async_copy(
                held.at[n, pl.ds(i * rows, rows)],
                out_ref.at[pl.ds(pl.multiple_of(first, SUB), rows), :],
                sems.at[n * pieces + i],
            )
            copy.start()
            copies.append(copy)
    for copy in copies:
        copy.wait()


def whiten(me, high, low, parts, out, rows, groups):
    steps = tuple((k, offset) for k, offset, _ in parts)
    chunks = [chunk for _, _, chunk in parts]
    per_bucket, state = rows // groups, chunks[0].shape[1]
    count = len(chunks)
    vmem = pl.BlockSpec(memory_space=pltpu.VMEM)
    anywhere = pl.BlockSpec(memory_space=pl.ANY)
    extra = [] if out is None else [out]
    return pl.pallas_call(
        functools.partial(whiten_kernel, steps, len(extra), per_bucket),
        in_specs=[pl.BlockSpec(memory_space=pltpu.SMEM)]
        + [vmem] * (2 + count)
        + [anywhere] * len(extra),
        out_specs=anywhere,
        out_shape=jax.ShapeDtypeStruct((rows, state), F32),
        scratch_shapes=[
            pltpu.VMEM((count, per_bucket, state), F32),
            pltpu.SemaphoreType.DMA((count + 1,)),
        ],
        input_output_aliases={3 + count: 0} if extra else {},
        compiler_params=pltpu.CompilerParams(vmem_limit_bytes=16 * MIB),
        cost_estimate=pl.CostEstimate(flops=1, bytes_accessed=1, transcendentals=0),
    )(me.reshape(1), high, low, *chunks, *extra)


def behind(value, *arrays):
    return lax.optimization_barrier((value, *arrays))


def shards(observations, sensor_ids, sensor_sigma, buckets, prior_factor):
    rows_dev, state = observations.shape
    groups = lax.axis_size("rows")
    grp = lax.axis_size("grp")
    me = lax.axis_index("rows").astype(I32)
    total_rows = rows_dev * groups * grp
    leads = [k for k in (4, 1) if k < groups]
    others = [k for k in range(groups) if k not in leads]
    per_bucket = rows_dev // groups
    parts = [(n, 0, per_bucket) for n in range(len(leads))]
    *chunks, pair, place, table = regroup_lead(
        observations, sensor_ids, sensor_sigma, buckets, me, groups, leads, parts
    )
    move = lambda k, chunk: lax.ppermute(chunk, "rows", [(i, i ^ k) for i in range(groups)])
    received = {k: move(k, chunk) for k, chunk in zip(leads, chunks)}
    plane = 2 * grp
    packed_rows = packed_rows_of(state, plane)
    planes = [list(range(i, i + plane)) for i in range(0, groups * grp, plane)]
    middle = [k for k in (2, 6) if k < groups]
    late = [k for k in (5, *range(7, groups), 3) if k < groups]
    valid = sensor_sigma[0] > 0
    nothing = lambda rows: jnp.full((rows, LANES), jnp.nan, F32)

    def first():
        packed, prior_gram = gram(prior_factor, pair, packed_rows)
        rest = list(regroup_rest(table, place, pair, groups, others))
        return scatter_sum(packed, plane, planes), prior_gram, rest

    def wrong():
        return nothing(packed_rows // plane), nothing(packed_rows), [jnp.full((per_bucket, state), jnp.nan, F32)] * len(others)

    piece, prior_gram, rest = lax.cond(valid, first, wrong)
    rest = dict(zip(others, rest))
    received[0] = rest[0]
    for k in leads[1:]:
        piece, received[k] = behind(piece, received[k])
    across = [piece]
    for step in range(1, groups // 2):
        across.append(move(2 * step, piece))
    for k in middle[:1]:
        received[k] = move(k, behind(piece, rest[k])[1])
    while len(across) > 1:
        across = [across[i] + across[i + 1] for i in range(0, len(across), 2)]
    for k in middle[1:]:
        received[leads[0]], chunk = behind(received[leads[0]], rest[k])
        received[k] = move(k, chunk)
    across[0], received[leads[0]] = behind(across[0], received[leads[0]])
    for k in late[:1]:
        received[k] = move(k, behind(across[0], rest[k])[1])
    summed = lax.cond(
        valid, lambda: gather_pieces(across[0], plane, planes), lambda: nothing(packed_rows)
    )
    for k in late[1:]:
        received[k] = move(k, behind(summed, rest[k])[1])
    factor, high, low = factorise(summed, prior_gram, state, total_rows)
    whole = lambda slots: [(k, 0, received[k]) for k in slots]
    out = None
    for parts in (whole([0, *leads, *middle]), whole(late[:-1]), whole(late[-1:])):
        if parts:
            out = whiten(me, high, low, parts, out, rows_dev, groups)
    return (out, factor)


def solution(mesh):
    in_specs = (P(("rows", "grp"), None), P(("rows", "grp")), P(), P(("rows", "grp")), P())
    out_specs = (P(("rows", "grp"), None), P())
    return jax.shard_map(shards, mesh=mesh, in_specs=in_specs, out_specs=out_specs, check_vma=False)
```
